32 devices in a mesh: fsdp: 32 (over z, y, x, core).
Axes of the slice: x: 2, y: 2, z: 4, core: 2. Of those that a mesh axis runs over, the one named last changes fastest.
Arguments:
- tokens: bfloat16 [16384, 1024], P('fsdp'), may hold values from -6 to 6
- lengths: int32 [32], P('fsdp'), may hold values from 1 to 512, 10240 in all
- routes: int32 [16384, 8], P('fsdp'), may hold values from 0 to 15, all different within a row; in each aligned block of 512 rows (0 to 511, 512 to 1023, ...) at most 384 rows name the same one
- attention_gain: bfloat16 [1024], P('fsdp'), may hold values from 0.25 to 1.75
- query_weight: bfloat16 [1024, 1024], P('fsdp'), may hold values from -1.75 to 1.75
- key_weight: bfloat16 [1024, 512], P('fsdp'), may hold values from -1.75 to 1.75
- value_weight: bfloat16 [1024, 512], P('fsdp'), may hold values from -0.1875 to 0.1875
- output_weight: bfloat16 [1024, 1024], P(None, 'fsdp'), may hold values from -6 to 6
- expert_gain: bfloat16 [1024], P('fsdp'), may hold values from 0.25 to 1.75
- router_weight: bfloat16 [1024, 16], P('fsdp'), may hold values from -0.25 to 0.25
- gate_weight: bfloat16 [16, 1024, 512], P(None, 'fsdp'), may hold values from -0.1875 to 0.1875
- up_weight: bfloat16 [16, 1024, 512], P(None, 'fsdp'), may hold values from -0.1875 to 0.1875
- down_weight: bfloat16 [16, 512, 1024], P(None, None, 'fsdp'), may hold values from -6 to 6
- cotangent: bfloat16 [16384, 1024], P('fsdp'), may hold values from -6 to 6
Outputs:
- layer_out: bfloat16 [16384, 1024], P('fsdp')
- grad_tokens: float32 [16384, 1024], P('fsdp')
- grad_attention_gain: float32 [1024], P('fsdp')
- grad_query_weight: float32 [1024, 1024], P('fsdp')
- grad_key_weight: float32 [1024, 512], P('fsdp')
- grad_value_weight: float32 [1024, 512], P('fsdp')
- grad_output_weight: float32 [1024, 1024], P(None, 'fsdp')
- grad_expert_gain: float32 [1024], P('fsdp')
- grad_router_weight: float32 [1024, 16], P('fsdp')
- grad_gate_weight: float32 [16, 1024, 512], P(None, 'fsdp')
- grad_up_weight: float32 [16, 1024, 512], P(None, 'fsdp')
- grad_down_weight: float32 [16, 512, 1024], P(None, None, 'fsdp')
The draws below stay inside these ranges and needn't reach their ends.
Inputs may be any that keep to these rules, and one draw needn't show every extreme that they name: `lengths`: each device's 512 rows hold one sequence of this length, followed by padding rows. The longest is exactly 512, and they sum to 10240. `routes`: each row names 8 different experts. Among the 512 rows of one device no expert is named by more than 384 rows, a bound that some block reaches.
All inputs are finite; a program needn't handle non-finite values.
Results may differ from the reference program's by a relative error of at most 0.015.
The reference program's roundings to bfloat16 on the way count: a program that leaves them out, or rounds other values in their place, can miss the bound.
Values may be sent and summed in bfloat16 or wider, within the bound.
No kernel may reach another device: no remote copies, remote signals or barrier semaphores. Data moves between devices by JAX's collectives and lax.ppermute only.
A program may use at most 384 MiB of HBM per device.

```python
import math
import jax
import jax.numpy as jnp
import numpy as np
from jax import lax

D = 1024
FF = 512
HEADS = 16
KV_HEADS = 8
HEAD_DIM = 64
TOP = 8
EXPERTS = 16
TOK_DEV = 512
CAP = 384
TOKENS = 16384
N_FSDP = 32


def shard_levels(own_key, shape, cuts, low, high):
    def one(axis_at, shards_of):
        draws = jax.random.uniform(jax.random.fold_in(jax.random.fold_in(own_key, 6), axis_at), (shards_of,), jnp.float32, low / len(cuts), high / len(cuts))
        return jnp.repeat(jnp.exp(draws), shape[axis_at] // shards_of).reshape((-1,) + (1,) * (len(shape) - axis_at - 1))

    factor_of = one(*cuts[0])
    for cut in cuts[1:]:
        factor_of = factor_of * one(*cut)
    return factor_of


def length_profile(number_of, total, limit, slope):
    portions = [(1 << 20) // math.isqrt(standing ** slope) + 1 for standing in range(2, number_of + 1)]
    spare, given = total - limit - (number_of - 1), [1] * (number_of - 1)
    while spare > 0:
        free = [i for i in range(number_of - 1) if given[i] < limit]
        whole, remaining = sum([portions[i] for i in free]), spare
        for i in free:
            addition = min(limit - given[i], max(1, remaining * portions[i] // whole), spare)
            given[i] = given[i] + addition
            spare = spare - addition
    return np.array([limit] + given)


def uneven_parts(key, amount, total, most, slope):
    if amount == 2:
        one = jax.random.randint(key, (), max(1, total - most), min(most, total - 1) + 1)
        return jnp.stack([one, total - one])
    sizes = jnp.asarray(length_profile(amount, total, most, slope), jnp.int32)
    twos = (amount - 1) // 2
    donor, receiver = sizes[1:1 + 2 * twos:2], sizes[2:2 + 2 * twos:2]
    margin = jnp.minimum(donor - 1, most - receiver)
    shifted = jax.random.randint(jax.random.fold_in(key, 1), (twos,), 0, 1 << 20) % (margin + 1)
    sizes = sizes.at[1:1 + 2 * twos:2].set(donor - shifted).at[2:2 + 2 * twos:2].set(receiver + shifted)
    return sizes[jax.random.permutation(jax.random.fold_in(key, 2), amount)]


def routed_block(rng, own, number, rows, amount, top, reach, slope):
    ranking = jax.random.permutation(rng, amount)
    heavy_load, usual = load_shares(amount, rows * top, reach, slope, True), load_shares(amount, rows * top, reach, slope, False)
    places = jnp.arange(amount)

    def named(tallies, turn):
        used = int((tallies > 0).sum())
        fixed = max(1, used // 4)
        moved = fixed + (places - fixed + turn * (used - fixed)) % max(1, amount - fixed)
        return jnp.zeros((amount,), jnp.int32).at[ranking[jnp.where(places < fixed, places, moved)]].set(jnp.asarray(tallies, jnp.int32))

    tallies = jnp.where(number % 4 == 0, named(heavy_load, number // 4), named(usual, number - number // 4 - 1))
    mixed = jax.random.permutation(jax.random.fold_in(own, 3), amount)
    source_of, sink = mixed[0:amount // 2 * 2:2], mixed[1:amount // 2 * 2:2]
    slack = jnp.minimum(tallies[source_of] - 1, reach - tallies[sink]) // 2
    slack = jnp.where((source_of == ranking[0]) | (sink == ranking[0]) | (tallies[sink] == 0), 0, jnp.maximum(slack, 0))
    moved = jax.random.randint(jax.random.fold_in(own, 4), (amount // 2,), 0, 1 << 20) % (slack + 1)
    tallies = tallies.at[source_of].add(-moved).at[sink].add(moved)
    labels = jnp.searchsorted(jnp.cumsum(tallies), jnp.arange(rows * top), side="right").astype(jnp.int32)
    grid = labels.reshape(top, rows).T
    grid = grid[jax.random.permutation(jax.random.fold_in(own, 1), rows)]
    turn = jax.random.randint(jax.random.fold_in(own, 2), (rows, 1), 0, top)
    return jnp.take_along_axis(grid, (jnp.arange(top)[None, :] + turn) % top, axis=1)


def load_shares(amount, total, most, skew, full):
    weights = [(1 << 20) // math.isqrt(grade ** skew) + 1 for grade in range(1, amount + 1)]
    largest = most if full else min(most, max(-(-total // amount), total * weights[0] // sum(weights)))
    least = 1 if total - largest >= amount - 1 else 0
    given, spare = [largest] + [least] * (amount - 1), total - largest - least * (amount - 1)
    while spare > 0:
        candidates = [i for i in range(1, amount) if given[i] < largest] or [i for i in range(1, amount) if given[i] < most]
        whole, remaining = sum([weights[i] for i in candidates]), spare
        for i in candidates:
            more = min(most - given[i], max(1, remaining * weights[i] // whole), spare)
            given[i] = given[i] + more
            spare = spare - more
    return np.array(given)


def centred(key, dims, spread, bound, cuts=(), held_as=jnp.bfloat16):
    entries = spread * jax.random.normal(key, dims, jnp.float32)
    if cuts:
        entries = entries * shard_levels(key, dims, cuts, -0.22, 0.18)
    return jnp.clip(entries, -bound, bound).astype(held_as)


def setup_inputs(seed: int = 0) -> dict:
    arg_keys = jax.random.split(jax.random.key(seed), 15)
    tokens = centred(arg_keys[0], (TOKENS, D), 1.0, 6.0, ((0, 32),))
    lengths = uneven_parts(arg_keys[1], N_FSDP, TOKENS * 5 // 8, TOK_DEV, 2).astype(jnp.int32)
    routes_keys = jax.random.split(jax.random.fold_in(arg_keys[2], 1), TOKENS // TOK_DEV)
    routes_turns = jax.random.permutation(jax.random.fold_in(arg_keys[2], 3), TOKENS // TOK_DEV)
    routes = jax.vmap(lambda own, number: routed_block(jax.random.fold_in(arg_keys[2], 2), own, number, TOK_DEV, EXPERTS, TOP, CAP, 1))(routes_keys, routes_turns).reshape((TOKENS, TOP))
    attention_gain = jnp.clip(1.0 + 0.15 * jax.random.normal(arg_keys[3], (D,), jnp.float32), 0.25, 1.75).astype(jnp.bfloat16)
    query_weight = centred(arg_keys[4], (D, HEADS * HEAD_DIM), 0.11, 1.75, ((0, 32),))
    key_weight = centred(arg_keys[5], (D, KV_HEADS * HEAD_DIM), 0.11, 1.75, ((0, 32),))
    value_weight = centred(arg_keys[6], (D, KV_HEADS * HEAD_DIM), D ** -0.5, 0.1875, ((0, 32),))
    output_weight = centred(arg_keys[7], (HEADS * HEAD_DIM, D), 0.5, 6.0, ((1, 32),))
    expert_gain = jnp.clip(1.0 + 0.15 * jax.random.normal(arg_keys[8], (D,), jnp.float32), 0.25, 1.75).astype(jnp.bfloat16)
    router_weight = centred(arg_keys[9], (D, EXPERTS), 0.015625, 0.25, ((0, 32),))
    gate_weight = centred(arg_keys[10], (EXPERTS, D, FF), D ** -0.5, 0.1875, ((1, 32),))
    up_weight = centred(arg_keys[11], (EXPERTS, D, FF), D ** -0.5, 0.1875, ((1, 32),))
    down_weight = centred(arg_keys[12], (EXPERTS, FF, D), 0.9, 6.0, ((2, 32),))
    cotangent = centred(arg_keys[13], (TOKENS, D), 1.0, 6.0, ((0, 32),))
    return dict(tokens=tokens, lengths=lengths, routes=routes, attention_gain=attention_gain, query_weight=query_weight, key_weight=key_weight, value_weight=value_weight, output_weight=output_weight, expert_gain=expert_gain, router_weight=router_weight, gate_weight=gate_weight, up_weight=up_weight, down_weight=down_weight, cotangent=cotangent)


norm_eps = 1e-06
attention_scale = 0.015625
residual_scale = 0.22
rope_base = 10000.0
masked_value = -1e+30

@jax.custom_vjp
def low(v):
    return lax.optimization_barrier(v.astype(jnp.bfloat16)).astype(jnp.float32)

@jax.custom_vjp
def low_back(v):
    return v

def low_keep(v):
    return (low(v), None)

def low_pass(kept, grad):
    return (grad,)

def back_keep(v):
    return (v, None)

def back_low(kept, grad):
    return (low(grad),)
low.defvjp(low_keep, low_pass)
low_back.defvjp(back_keep, back_low)

def rope_tables(row_count):
    half_dim = HEAD_DIM // 2
    frequency = rope_base ** (-2.0 * jnp.arange(half_dim, dtype=jnp.float32) / HEAD_DIM)
    angles = jnp.arange(row_count, dtype=jnp.float32)[:, None] * frequency[None, :]
    angles = jnp.concatenate([angles, angles], axis=1)
    return (jnp.cos(angles), jnp.sin(angles))

def rotate_apply(values, cosine_table, sine_table):
    half_dim = values.shape[-1] // 2
    turned = jnp.concatenate([-values[..., half_dim:], values[..., :half_dim]], axis=-1)
    return values * cosine_table + turned * sine_table

def layer_group(hidden_in, lengths, routes, attention_gain, query_weight, key_weight, value_weight, output_weight, expert_gain, router_weight, gate_weight, up_weight, down_weight):
    precise = lax.Precision.HIGHEST
    seq_count, row_count, width = hidden_in.shape
    group_size = HEADS // KV_HEADS
    cosine_table, sine_table = rope_tables(row_count)
    scale_one = lax.rsqrt(lax.optimization_barrier(jnp.mean(hidden_in * hidden_in, axis=-1, keepdims=True)) + norm_eps)
    normed_one = low(hidden_in * scale_one * attention_gain)
    queries = low_back(jnp.einsum('std,dh->sth', normed_one, query_weight, precision=precise))
    key_rows = low_back(jnp.einsum('std,dh->sth', normed_one, key_weight, precision=precise))
    value_rows = low(low_back(jnp.einsum('std,dh->sth', normed_one, value_weight, precision=precise)))
    queries = queries.reshape(seq_count, row_count, KV_HEADS, group_size, HEAD_DIM)
    key_rows = key_rows.reshape(seq_count, row_count, KV_HEADS, HEAD_DIM)
    value_rows = value_rows.reshape(seq_count, row_count, KV_HEADS, HEAD_DIM)
    query_rot = low(rotate_apply(queries, cosine_table[:, None, None, :], sine_table[:, None, None, :]))
    key_rot = low(rotate_apply(key_rows, cosine_table[:, None, :], sine_table[:, None, :]))
    raw_scores = low_back(jnp.einsum('sqkgd,spkd->skgqp', query_rot, key_rot, precision=precise))
    position = jnp.arange(row_count, dtype=jnp.int32)
    allowed = (position[None, :] <= position[:, None])[None, :, :] & (position[None, None, :] < lengths[:, None, None])
    scores = jnp.where(allowed[:, None, None, :, :], attention_scale * raw_scores, masked_value)
    softmax_rows = jax.nn.softmax(scores, axis=-1)
    mixed = low(low_back(jnp.einsum('skgqp,spkd->sqkgd', low(softmax_rows), value_rows, precision=precise)))
    mixed = mixed.reshape(seq_count, row_count, HEADS * HEAD_DIM)
    branch = low_back(jnp.einsum('sth,hd->std', mixed, output_weight, precision=precise))
    middle = hidden_in + residual_scale * branch
    scale_two = lax.rsqrt(lax.optimization_barrier(jnp.mean(middle * middle, axis=-1, keepdims=True)) + norm_eps)
    normed_two = low(middle * scale_two * expert_gain)
    logits = low_back(jnp.einsum('std,de->ste', normed_two, router_weight, precision=precise))
    chosen = jnp.take_along_axis(logits, routes, axis=-1)
    gate_values = jax.nn.softmax(chosen, axis=-1)
    combine = lax.optimization_barrier(jnp.sum(jax.nn.one_hot(routes, EXPERTS, dtype=logits.dtype) * gate_values[..., None], axis=-2))
    gate_pre = low_back(jnp.einsum('std,edf->stef', normed_two, gate_weight, precision=precise))
    up_pre = low_back(jnp.einsum('std,edf->stef', normed_two, up_weight, precision=precise))
    inner = low(jax.nn.silu(gate_pre) * up_pre)
    expert_out = low_back(jnp.einsum('stef,efd->sted', inner, down_weight, precision=precise))
    mixture = jnp.einsum('ste,sted->std', combine, expert_out, precision=precise)
    return middle + residual_scale * mixture

def reference(tokens, lengths, routes, attention_gain, query_weight, key_weight, value_weight, output_weight, expert_gain, router_weight, gate_weight, up_weight, down_weight, cotangent):
    group_size = math.gcd(N_FSDP, max(1, 4096 // TOK_DEV))
    step_count = N_FSDP // group_size
    inputs = tokens.astype(jnp.float32).reshape(step_count, group_size, TOK_DEV, D)
    length_groups = lengths.reshape(step_count, group_size)
    route_groups = routes.reshape(step_count, group_size, TOK_DEV, TOP)
    weights = tuple((weight_item.astype(jnp.float32) for weight_item in (attention_gain, query_weight, key_weight, value_weight, output_weight, expert_gain, router_weight, gate_weight, up_weight, down_weight)))
    block = jax.checkpoint(layer_group)

    def forward(hidden_all, weight_list):

        def step_fn(carried, slices):
            return (carried, block(slices[0], slices[1], slices[2], *weight_list))
        unused, outputs = lax.scan(step_fn, None, (hidden_all, length_groups, route_groups))
        return outputs
    result, pullback = jax.vjp(forward, inputs, weights)
    grad_inputs, grad_weights = pullback(cotangent.astype(jnp.float32).reshape(result.shape))
    layer_out = result.reshape(TOKENS, D).astype(jnp.bfloat16)
    return (layer_out, grad_inputs.reshape(TOKENS, D), grad_weights[0], grad_weights[1], grad_weights[2], grad_weights[3], grad_weights[4], grad_weights[5], grad_weights[6], grad_weights[7], grad_weights[8], grad_weights[9])
```

```python
import jax
import jax.numpy as jnp
from jax import lax
from jax.experimental import pallas as pl
from jax.experimental.pallas import tpu as pltpu
from jax.sharding import PartitionSpec as P

HEADS = 16
KV_HEADS = 8
HEAD_DIM = 64
EXPERTS = 16
MEMBERS = 8
LOCAL_EXPERTS = EXPERTS // MEMBERS
EXTRA = 128

norm_eps = 1e-06
attention_scale = 0.015625
residual_scale = 0.22
rope_base = 10000.0
masked_value = -1e30
f32 = jnp.float32
bf16 = jnp.bfloat16


def rope_tables(row_count):
    half_dim = HEAD_DIM // 2
    frequency = rope_base ** (-2.0 * jnp.arange(half_dim, dtype=jnp.float32) / HEAD_DIM)
    angles = jnp.arange(row_count, dtype=jnp.float32)[:, None] * frequency[None, :]
    angles = jnp.concatenate([angles, angles], axis=1)
    return (jnp.cos(angles), jnp.sin(angles))


def rotate_apply(values, cosine_table, sine_table):
    half_dim = values.shape[-1] // 2
    turned = jnp.concatenate([-values[..., half_dim:], values[..., :half_dim]], axis=-1)
    return values * cosine_table + turned * sine_table


def rotate_back(grads, cosine_table, sine_table):
    half_dim = grads.shape[-1] // 2
    scaled = grads * sine_table
    turned = jnp.concatenate([scaled[..., half_dim:], -scaled[..., :half_dim]], axis=-1)
    return grads * cosine_table + turned


def norm_rows(values, gain_row):
    row_scale = lax.rsqrt(jnp.mean(values * values, axis=-1, keepdims=True) + norm_eps)
    return (row_scale, values * row_scale * gain_row)


def norm_back(values, row_scale, gain_row, normed_grad):
    weighted = normed_grad * gain_row
    grad_gain = jnp.sum(normed_grad * values * row_scale, axis=0)
    correction = jnp.mean(weighted * values, axis=-1, keepdims=True)
    return (row_scale * weighted - values * row_scale**3 * correction, grad_gain)


def attention_scores(query_rot, key_rot, allowed):
    raw_scores = jnp.einsum("qkgd,pkd->kgqp", query_rot, key_rot, preferred_element_type=f32)
    return jnp.where(allowed, attention_scale * raw_scores, masked_value)


class Exchange:
    def __init__(self, count):
        self.count = count
        self.groups = count // MEMBERS
        index = lax.axis_index("fsdp")
        self.member = index % MEMBERS
        self.group = index // MEMBERS

    def swap(self, value, bits):
        return lax.ppermute(value, "fsdp", [(i, i ^ bits) for i in range(self.count)])

    def shift(self, value, senders, step):
        pairs = [
            (g * MEMBERS + m, (g + step) * MEMBERS + m) for g in senders for m in range(MEMBERS)
        ]
        return lax.ppermute(value, "fsdp", pairs)

    def line_gather(self, piece):
        groups = self.groups
        rising, falling = [piece], [piece]
        for step in range(1, groups):
            rising.append(self.shift(rising[-1], range(step - 1, groups - 1), 1))
            falling.append(self.shift(falling[-1], range(1, groups - step + 1), -1))
        found = [piece]
        for step in range(1, groups):
            found.append(jnp.where(self.group >= step, rising[step], falling[groups - step]))
        return found

    def line_reduce(self, pick):
        groups = self.groups
        rising = falling = None
        for step in range(1, groups):
            up = pick((self.group + groups - step) % groups)
            down = pick((self.group + step) % groups)
            up_owner = self.group + groups - step
            down_owner = self.group - groups + step
            if rising is not None:
                up = up + rising.astype(f32)
                down = down + falling.astype(f32)
            del up_owner, down_owner
            rising = self.shift(up.astype(bf16), range(0, step), 1)
            falling = self.shift(down.astype(bf16), range(groups - step, groups), -1)
        own = pick(self.group)
        if rising is None:
            return own
        return own + rising.astype(f32) + falling.astype(f32)

    def group_gather(self, block):
        half = block.shape[0] // 2
        top, low = block[:half], block[half:]
        near_top = self.swap(top, 2)
        far_low = self.swap(low, 4)
        near_low = self.swap(low, 2)
        far_top = self.swap(top, 4)
        cross_top = self.swap(near_top, 4)
        cross_low = self.swap(far_low, 2)
        found = {0: (top, low), 2: (near_top, near_low), 4: (far_top, far_low), 6: (cross_top, cross_low)}
        found[1] = (self.swap(top, 1), self.swap(low, 1))
        for k in (2, 4, 6):
            found[k + 1] = tuple(self.swap(part, 1) for part in found[k])
        return found

    def group_reduce(self, blocks):
        half = blocks[0].shape[0] // 2
        joined = {}
        for k in (6, 2, 4, 0):
            joined[k] = blocks[k].astype(f32) + self.swap(blocks[k ^ 1], 1).astype(f32)
        cross_top = self.swap(joined[6][:half].astype(bf16), 2).astype(f32)
        cross_low = self.swap(joined[6][half:].astype(bf16), 4).astype(f32)
        near_top = self.swap(joined[2][:half].astype(bf16), 2).astype(f32)
        far_low = self.swap(joined[4][half:].astype(bf16), 4).astype(f32)
        near_low = self.swap((joined[2][half:] + cross_low).astype(bf16), 2).astype(f32)
        far_top = self.swap((joined[4][:half] + cross_top).astype(bf16), 4).astype(f32)
        return jnp.concatenate(
            [joined[0][:half] + near_top + far_top, joined[0][half:] + near_low + far_low], axis=0
        )


def dot(left, right):
    return jnp.dot(left, right, preferred_element_type=f32)


def dot_turned(left, right):
    return lax.dot_general(left, right, (((1,), (1,)), ((), ())), preferred_element_type=f32)


def expert_kernel(first_ref, packet_ref, cotangent_ref, weight_ref, out_ref, back_ref, grad_ref,
                  packet_turned, cotangent_turned, out_sum, back_sum, extra_sum):
    width = cotangent_ref.shape[-1]
    rows = cotangent_ref.shape[1]
    first = first_ref[0]

    @pl.when(pl.program_id(0) == 0)
    def _():
        grad_ref[...] = jnp.zeros_like(grad_ref)

    packet_turned[...] = packet_ref[0, :, :width].T
    cotangent_turned[...] = cotangent_ref[0].T
    out_sum[...] = jnp.zeros_like(out_sum)
    back_sum[...] = jnp.zeros_like(back_sum)
    extra_sum[...] = jnp.zeros_like(extra_sum)
    lane = lax.broadcasted_iota(jnp.int32, (rows, EXTRA), 1)

    def one_expert(local, carry):
        expert = first + local
        shares = packet_ref[0, :, width:].astype(f32)
        is_high, is_low = lane == expert, lane == expert + EXPERTS
        share = jnp.sum(jnp.where(is_high | is_low, shares, 0.0), axis=1, keepdims=True)
        normed = packet_ref[0, :, :width]
        upstream = cotangent_ref[0]
        gate_pre = dot(normed, weight_ref[local, 0])
        up_pre = dot(normed, weight_ref[local, 1])
        inner_raw = dot(upstream, weight_ref[local, 2]) * residual_scale
        sigmoid_gate = jax.nn.sigmoid(gate_pre)
        activated = gate_pre * sigmoid_gate
        inner = (activated * up_pre).astype(bf16).astype(f32)
        share_grad = jnp.sum(inner * inner_raw, axis=1, keepdims=True)
        inner_grad = inner_raw * share
        gate_grad = (
            inner_grad * up_pre * sigmoid_gate * (1.0 + gate_pre * (1.0 - sigmoid_gate))
        ).astype(bf16)
        up_grad = (inner_grad * activated).astype(bf16)
        inner_shared = (inner * (share * residual_scale)).astype(bf16)
        out_sum[...] += dot_turned(inner_shared, weight_ref[local, 2])
        back_sum[...] += dot_turned(gate_grad, weight_ref[local, 0]) + dot_turned(
            up_grad, weight_ref[local, 1]
        )
        grad_ref[local, 0] += dot(packet_turned[...], gate_grad)
        grad_ref[local, 1] += dot(packet_turned[...], up_grad)
        grad_ref[local, 2] += dot(cotangent_turned[...], inner_shared)
        high = share_grad.astype(bf16).astype(f32)
        extra_sum[...] += jnp.where(is_high, high, 0.0) + jnp.where(is_low, share_grad - high, 0.0)
        return carry

    lax.fori_loop(0, LOCAL_EXPERTS, one_expert, 0)
    out_ref[0] = out_sum[...].astype(bf16)
    back_ref[0, :, :width] = back_sum[...].astype(bf16)
    back_ref[0, :, width:] = extra_sum[...].astype(bf16)


def run_experts(first, packets, cotangents, weights):
    block_count, rows, wide = packets.shape
    width = cotangents.shape[-1]
    hidden = weights.shape[-1]
    grad_shape = (LOCAL_EXPERTS, 3, width, hidden)
    return pl.pallas_call(
        expert_kernel,
        grid_spec=pltpu.PrefetchScalarGridSpec(
            num_scalar_prefetch=1,
            grid=(block_count,),
            in_specs=[
                pl.BlockSpec((1, rows, wide), lambda i, s: (i, 0, 0)),
                pl.BlockSpec((1, rows, width), lambda i, s: (i, 0, 0)),
                pl.BlockSpec(grad_shape, lambda i, s: (0, 0, 0, 0), pipeline_mode=pl.Buffered(1)),
            ],
            out_specs=[
                pl.BlockSpec((1, rows, width), lambda i, s: (i, 0, 0)),
                pl.BlockSpec((1, rows, wide), lambda i, s: (i, 0, 0)),
                pl.BlockSpec(grad_shape, lambda i, s: (0, 0, 0, 0), pipeline_mode=pl.Buffered(1)),
            ],
            scratch_shapes=[
                pltpu.VMEM((width, rows), bf16),
                pltpu.VMEM((width, rows), bf16),
                pltpu.VMEM((rows, width), f32),
                pltpu.VMEM((rows, width), f32),
                pltpu.VMEM((rows, EXTRA), f32),
            ],
        ),
        out_shape=[
            jax.ShapeDtypeStruct((block_count, rows, width), bf16),
            jax.ShapeDtypeStruct((block_count, rows, wide), bf16),
            jax.ShapeDtypeStruct(grad_shape, f32),
        ],
        compiler_params=pltpu.CompilerParams(vmem_limit_bytes=60 * 1024 * 1024),
        cost_estimate=pl.CostEstimate(
            flops=block_count * LOCAL_EXPERTS * 9 * 2 * rows * width * hidden,
            bytes_accessed=block_count * rows * width * 8 + 36 * width * hidden,
            transcendentals=block_count * LOCAL_EXPERTS * rows * hidden,
        ),
        name="experts",
    )(first, packets, cotangents, weights)


def local(
    tokens,
    lengths,
    routes,
    attention_gain,
    query_weight,
    key_weight,
    value_weight,
    output_weight,
    expert_gain,
    router_weight,
    gate_weight,
    up_weight,
    down_weight,
    cotangent,
    *,
    count,
):
    links = Exchange(count)
    member, group, groups = links.member, links.group, links.groups
    row_count, width = tokens.shape
    shard = query_weight.shape[0]
    hidden = gate_weight.shape[2]
    head_columns, kv_columns = HEADS * HEAD_DIM, KV_HEADS * HEAD_DIM
    group_size = HEADS // KV_HEADS

    packed = jnp.concatenate(
        [
            query_weight,
            key_weight,
            value_weight,
            output_weight.T,
            router_weight,
            attention_gain[:, None],
            expert_gain[:, None],
            jnp.zeros((shard, EXTRA - EXPERTS - 2), bf16),
        ],
        axis=1,
    )
    pack_width = packed.shape[1]
    line = links.line_gather(packed)
    column = jnp.zeros((groups, shard, pack_width), bf16)
    for back, piece in enumerate(line):
        column = lax.dynamic_update_index_in_dim(column, piece, (group + groups - back) % groups, 0)
    spread = links.group_gather(column.reshape(groups * shard, pack_width))
    whole = jnp.zeros((groups, MEMBERS, shard, pack_width), bf16)
    for k in range(MEMBERS):
        part = jnp.concatenate(spread[k], axis=0).reshape(groups, shard, pack_width)
        whole = lax.dynamic_update_index_in_dim(whole, part, member ^ k, 1)
    whole = whole.reshape(width, pack_width)
    at_output = head_columns + 2 * kv_columns
    at_extra = at_output + head_columns
    qkv_full = whole[:, :at_output]
    output_turned = whole[:, at_output:at_extra]
    router_full = whole[:, at_extra : at_extra + EXPERTS]
    gain_one = whole[:, at_extra + EXPERTS].astype(f32)
    gain_two = whole[:, at_extra + EXPERTS + 1].astype(f32)

    mine = jnp.stack([gate_weight, up_weight, down_weight.transpose(0, 2, 1)], axis=1)
    mine = mine.reshape(MEMBERS, LOCAL_EXPERTS, 3, shard, hidden)
    shelf = jnp.zeros((LOCAL_EXPERTS, 3, MEMBERS, shard, hidden), bf16)
    for k in range(MEMBERS):
        part = lax.dynamic_index_in_dim(mine, member ^ k, 0, keepdims=False)
        if k:
            part = links.swap(part, k)
        shelf = lax.dynamic_update_index_in_dim(shelf, part, member ^ k, 2)
    shelf = shelf.reshape(LOCAL_EXPERTS, 3, MEMBERS * shard, hidden)
    expert_full = jnp.zeros((LOCAL_EXPERTS, 3, groups, MEMBERS * shard, hidden), bf16)
    for back, piece in enumerate(links.line_gather(shelf)):
        expert_full = lax.dynamic_update_index_in_dim(
            expert_full, piece, (group + groups - back) % groups, 2
        )
    expert_full = expert_full.reshape(LOCAL_EXPERTS, 3, width, hidden)
    cotangents = links.group_gather(cotangent)

    inputs = tokens.astype(f32)
    cosine_table, sine_table = rope_tables(row_count)
    scale_one, normed_raw = norm_rows(inputs, gain_one)
    normed_one = normed_raw.astype(bf16)
    projected = dot(normed_one, qkv_full)
    queries = projected[:, :head_columns].reshape(row_count, KV_HEADS, group_size, HEAD_DIM)
    key_rows = projected[:, head_columns : head_columns + kv_columns].reshape(
        row_count, KV_HEADS, HEAD_DIM
    )
    value_rows = (
        projected[:, head_columns + kv_columns :].astype(bf16).reshape(row_count, KV_HEADS, HEAD_DIM)
    )
    query_rot = rotate_apply(
        queries, cosine_table[:, None, None, :], sine_table[:, None, None, :]
    ).astype(bf16)
    key_rot = rotate_apply(key_rows, cosine_table[:, None, :], sine_table[:, None, :]).astype(bf16)
    position = jnp.arange(row_count, dtype=jnp.int32)
    allowed = (position[None, :] <= position[:, None]) & (position[None, :] < lengths[0])
    scores = attention_scores(query_rot, key_rot, allowed)
    maxima = jnp.max(scores, axis=-1, keepdims=True)
    exponent = jnp.exp(scores - maxima)
    totals = jnp.sum(exponent, axis=-1, keepdims=True)
    log_total = maxima + jnp.log(totals)
    softmax_rows = exponent / totals
    mixed = (
        jnp.einsum("kgqp,pkd->qkgd", softmax_rows.astype(bf16), value_rows, preferred_element_type=f32)
        .astype(bf16)
        .reshape(row_count, head_columns)
    )
    middle = inputs + residual_scale * dot_turned(mixed, output_turned)
    scale_two, normed_raw_two = norm_rows(middle, gain_two)
    normed_two = normed_raw_two.astype(bf16)
    logits = dot(normed_two, router_full)
    expert_ids = jnp.arange(EXPERTS, dtype=jnp.int32)
    routed = jnp.any(routes[:, :, None] == expert_ids[None, None, :], axis=1)
    best = jnp.max(jnp.where(routed, logits, masked_value), axis=1, keepdims=True)
    weights = jnp.where(routed, jnp.exp(jnp.where(routed, logits, best) - best), 0.0)
    shares = weights / jnp.sum(weights, axis=1, keepdims=True)
    share_high = lax.reduce_precision(shares, 8, 7)
    packet = jnp.concatenate(
        [
            normed_two,
            share_high.astype(bf16),
            (shares - share_high).astype(bf16),
            jnp.zeros((row_count, EXTRA - 2 * EXPERTS), bf16),
        ],
        axis=1,
    )
    packets = links.group_gather(packet)

    order = (0, 1, 2, 3, 6, 7, 4, 5)
    first = (member * LOCAL_EXPERTS).astype(jnp.int32).reshape(1)
    out_terms, back_terms, expert_grads = {}, {}, []
    for turn in (order[:4], order[4:]):
        packet_stack = jnp.concatenate([part for k in turn for part in packets[k]], axis=0)
        cotangent_stack = jnp.concatenate([part for k in turn for part in cotangents[k]], axis=0)
        outs, backs, grads = run_experts(
            first,
            packet_stack.reshape(len(turn), row_count, width + EXTRA),
            cotangent_stack.reshape(len(turn), row_count, width),
            expert_full,
        )
        expert_grads.append(grads)
        for at, k in enumerate(turn):
            out_terms[k], back_terms[k] = outs[at], backs[at]

    back_total = links.group_reduce(back_terms)

    def pick(owner):
        parts = [
            lax.dynamic_index_in_dim(
                grads.reshape(LOCAL_EXPERTS, 3, groups, MEMBERS, shard, hidden), owner, 2, keepdims=False
            )
            for grads in expert_grads
        ]
        return parts[0] + parts[1]

    shelf_grad = links.line_reduce(pick).astype(bf16)
    expert_shards = jnp.zeros((MEMBERS, LOCAL_EXPERTS, 3, shard, hidden), f32)
    for k in range(MEMBERS):
        part = lax.dynamic_index_in_dim(shelf_grad, member ^ k, 2, keepdims=False)
        if k:
            part = links.swap(part, k)
        expert_shards = lax.dynamic_update_index_in_dim(
            expert_shards, part.astype(f32), member ^ k, 0
        )
    expert_shards = expert_shards.reshape(EXPERTS, 3, shard, hidden)

    mixture = links.group_reduce(out_terms)
    layer_out = (middle + mixture).astype(bf16)

    upstream = cotangent.astype(f32)
    share_grad = (
        back_total[:, width : width + EXPERTS] + back_total[:, width + EXPERTS : width + 2 * EXPERTS]
    )
    share_grad = jnp.where(routed, share_grad, 0.0)
    logit_grad = (
        shares * (share_grad - jnp.sum(shares * share_grad, axis=1, keepdims=True))
    ).astype(bf16)
    normed_two_grad = back_total[:, :width] + dot_turned(logit_grad, router_full)
    grad_router = dot(normed_two.T, logit_grad)
    middle_norm_grad, grad_gain_two = norm_back(middle, scale_two, gain_two, normed_two_grad)
    middle_grad = upstream + middle_norm_grad
    branch_grad = (residual_scale * middle_grad).astype(bf16)
    grad_output_turned = dot(branch_grad.T, mixed)
    mixed_grad = (
        dot(branch_grad, output_turned)
        .astype(bf16)
        .reshape(row_count, KV_HEADS, group_size, HEAD_DIM)
    )
    scores_again = attention_scores(query_rot, key_rot, allowed)
    softmax_again = jnp.exp(scores_again - log_total)
    prob_grad = jnp.einsum("qkgd,pkd->kgqp", mixed_grad, value_rows, preferred_element_type=f32)
    row_delta = jnp.sum(prob_grad * softmax_again, axis=-1, keepdims=True)
    score_grad = (attention_scale * softmax_again * (prob_grad - row_delta)).astype(bf16)
    value_grad = (
        jnp.einsum("kgqp,qkgd->pkd", softmax_again.astype(bf16), mixed_grad, preferred_element_type=f32)
        .astype(bf16)
        .reshape(row_count, kv_columns)
    )
    query_rot_grad = jnp.einsum("kgqp,pkd->qkgd", score_grad, key_rot, preferred_element_type=f32)
    key_rot_grad = jnp.einsum("kgqp,qkgd->pkd", score_grad, query_rot, preferred_element_type=f32)
    query_grad = (
        rotate_back(query_rot_grad, cosine_table[:, None, None, :], sine_table[:, None, None, :])
        .astype(bf16)
        .reshape(row_count, head_columns)
    )
    key_grad = (
        rotate_back(key_rot_grad, cosine_table[:, None, :], sine_table[:, None, :])
        .astype(bf16)
        .reshape(row_count, kv_columns)
    )
    qkv_grad = jnp.concatenate([query_grad, key_grad, value_grad], axis=1)
    grad_qkv = dot(normed_one.T, qkv_grad)
    normed_one_grad = dot_turned(qkv_grad, qkv_full)
    input_norm_grad, grad_gain_one = norm_back(inputs, scale_one, gain_one, normed_one_grad)
    grad_tokens = middle_grad + input_norm_grad

    grad_pack = jnp.concatenate(
        [
            grad_qkv,
            grad_output_turned,
            grad_router,
            grad_gain_one[:, None],
            grad_gain_two[:, None],
            jnp.zeros((width, EXTRA - EXPERTS - 2), f32),
        ],
        axis=1,
    ).astype(bf16)
    grad_pack = grad_pack.reshape(groups, MEMBERS, shard, pack_width)
    terms = {
        k: lax.dynamic_index_in_dim(grad_pack, member ^ k, 1, keepdims=False).reshape(
            groups * shard, pack_width
        )
        for k in range(MEMBERS)
    }
    group_total = links.group_reduce(terms).reshape(groups, shard, pack_width)
    total = links.line_reduce(
        lambda owner: lax.dynamic_index_in_dim(group_total, owner, 0, keepdims=False)
    )
    return (
        layer_out,
        grad_tokens,
        total[:, at_extra + EXPERTS],
        total[:, :head_columns],
        total[:, head_columns : head_columns + kv_columns],
        total[:, head_columns + kv_columns : at_output],
        total[:, at_output:at_extra].T,
        total[:, at_extra + EXPERTS + 1],
        total[:, at_extra : at_extra + EXPERTS],
        expert_shards[:, 0],
        expert_shards[:, 1],
        expert_shards[:, 2].transpose(0, 2, 1),
    )


def solution(mesh):
    count = mesh.shape["fsdp"]
    placed = (
        P("fsdp", None),
        P("fsdp"),
        P("fsdp", None),
        P("fsdp"),
        P("fsdp", None),
        P("fsdp", None),
        P("fsdp", None),
        P(None, "fsdp"),
        P("fsdp"),
        P("fsdp", None),
        P(None, "fsdp", None),
        P(None, "fsdp", None),
        P(None, None, "fsdp"),
        P("fsdp", None),
    )

    def body(*args):
        return local(*args, count=count)

    return jax.shard_map(
        body,
        mesh=mesh,
        in_specs=placed,
        out_specs=(
            P("fsdp", None),
            P("fsdp", None),
            P("fsdp"),
            P("fsdp", None),
            P("fsdp", None),
            P("fsdp", None),
            P(None, "fsdp"),
            P("fsdp"),
            P("fsdp", None),
            P(None, "fsdp", None),
            P(None, "fsdp", None),
            P(None, None, "fsdp"),
        ),
        check_vma=False,
    )
```

```python
import functools

import jax
import jax.numpy as jnp
from jax import lax
from jax.experimental import pallas as pl
from jax.experimental.pallas import tpu as pltpu
from jax.sharding import PartitionSpec as P

HEADS = 16
KV_HEADS = 8
HEAD_DIM = 64
EXPERTS = 16
MEMBERS = 8
LOCAL_EXPERTS = EXPERTS // MEMBERS
EXTRA = 128

norm_eps = 1e-06
attention_scale = 0.015625
residual_scale = 0.22
rope_base = 10000.0
masked_value = -1e30
f32 = jnp.float32
bf16 = jnp.bfloat16


def rope_tables(row_count):
    half_dim = HEAD_DIM // 2
    frequency = rope_base ** (-2.0 * jnp.arange(half_dim, dtype=jnp.float32) / HEAD_DIM)
    angles = jnp.arange(row_count, dtype=jnp.float32)[:, None] * frequency[None, :]
    angles = jnp.concatenate([angles, angles], axis=1)
    return (jnp.cos(angles), jnp.sin(angles))


def rotate_apply(values, cosine_table, sine_table):
    half_dim = values.shape[-1] // 2
    turned = jnp.concatenate([-values[..., half_dim:], values[..., :half_dim]], axis=-1)
    return values * cosine_table + turned * sine_table


def rotate_back(grads, cosine_table, sine_table):
    half_dim = grads.shape[-1] // 2
    scaled = grads * sine_table
    turned = jnp.concatenate([scaled[..., half_dim:], -scaled[..., :half_dim]], axis=-1)
    return grads * cosine_table + turned


def norm_rows(values, gain_row):
    row_scale = lax.rsqrt(jnp.mean(values * values, axis=-1, keepdims=True) + norm_eps)
    return (row_scale, values * row_scale * gain_row)


def norm_back(values, row_scale, gain_row, normed_grad):
    weighted = normed_grad * gain_row
    grad_gain = jnp.sum(normed_grad * values * row_scale, axis=0)
    correction = jnp.mean(weighted * values, axis=-1, keepdims=True)
    return (row_scale * weighted - values * row_scale**3 * correction, grad_gain)


def attention_scores(query_rot, key_rot, allowed):
    raw_scores = jnp.einsum("qkgd,pkd->kgqp", query_rot, key_rot, preferred_element_type=f32)
    return jnp.where(allowed, attention_scale * raw_scores, masked_value)


class Exchange:
    def __init__(self, count):
        self.count = count
        self.groups = count // MEMBERS
        index = lax.axis_index("fsdp")
        self.member = index % MEMBERS
        self.group = index // MEMBERS

    def swap(self, value, bits):
        return lax.ppermute(value, "fsdp", [(i, i ^ bits) for i in range(self.count)])

    def shift(self, value, senders, step):
        pairs = [
            (g * MEMBERS + m, (g + step) * MEMBERS + m) for g in senders for m in range(MEMBERS)
        ]
        return lax.ppermute(value, "fsdp", pairs)

    def line_gather(self, piece):
        groups = self.groups
        rising, falling = [piece], [piece]
        for step in range(1, groups):
            rising.append(self.shift(rising[-1], range(step - 1, groups - 1), 1))
            falling.append(self.shift(falling[-1], range(1, groups - step + 1), -1))
        found = [piece]
        for step in range(1, groups):
            found.append(jnp.where(self.group >= step, rising[step], falling[groups - step]))
        return found

    def line_reduce(self, pick):
        groups = self.groups
        rising = falling = None
        for step in range(1, groups):
            up = pick((self.group + groups - step) % groups)
            down = pick((self.group + step) % groups)
            up_owner = self.group + groups - step
            down_owner = self.group - groups + step
            if rising is not None:
                up = up + rising.astype(f32)
                down = down + falling.astype(f32)
            del up_owner, down_owner
            rising = self.shift(up.astype(bf16), range(0, step), 1)
            falling = self.shift(down.astype(bf16), range(groups - step, groups), -1)
        own = pick(self.group)
        if rising is None:
            return own
        return own + rising.astype(f32) + falling.astype(f32)

    def direct_gather(self, piece):
        stack = jnp.zeros((self.groups,) + piece.shape, piece.dtype)
        for bits in range(self.groups):
            part = self.swap(piece, bits * MEMBERS) if bits else piece
            stack = lax.dynamic_update_index_in_dim(stack, part, self.group ^ bits, 0)
        return stack

    def direct_reduce(self, terms):
        total = lax.dynamic_index_in_dim(terms, self.group, 0, keepdims=False)
        for bits in range(1, self.groups):
            part = lax.dynamic_index_in_dim(terms, self.group ^ bits, 0, keepdims=False)
            total = total + self.swap(part.astype(bf16), bits * MEMBERS).astype(f32)
        return total

    def chips_gather(self, block):
        half = block.shape[0] // 2
        top, low = block[:half], block[half:]
        near_top = self.swap(top, 2)
        far_low = self.swap(low, 4)
        near_low = self.swap(low, 2)
        far_top = self.swap(top, 4)
        cross_top = self.swap(near_top, 4)
        cross_low = self.swap(far_low, 2)
        return {0: (top, low), 2: (near_top, near_low), 4: (far_top, far_low), 6: (cross_top, cross_low)}

    def chips_reduce(self, joined):
        half = joined[0].shape[0] // 2
        cross_top = self.swap(joined[6][:half].astype(bf16), 2).astype(f32)
        cross_low = self.swap(joined[6][half:].astype(bf16), 4).astype(f32)
        near_top = self.swap(joined[2][:half].astype(bf16), 2).astype(f32)
        far_low = self.swap(joined[4][half:].astype(bf16), 4).astype(f32)
        near_low = self.swap((joined[2][half:] + cross_low).astype(bf16), 2).astype(f32)
        far_top = self.swap((joined[4][:half] + cross_top).astype(bf16), 4).astype(f32)
        return jnp.concatenate(
            [joined[0][:half] + near_top + far_top, joined[0][half:] + near_low + far_low], axis=0
        )

    def join_cores(self, own, other):
        return own.astype(f32) + self.swap(other, 1).astype(f32)

    def send_parts(self, parts):
        chips = parts.reshape((MEMBERS // 2, 2) + parts.shape[1:])
        chip, core = self.member // 2, self.member % 2
        arrived = jnp.zeros_like(chips)
        for bits in range(MEMBERS // 2):
            part = lax.dynamic_index_in_dim(chips, chip ^ bits, 0, keepdims=False)
            if bits:
                part = self.swap(part, 2 * bits)
            arrived = lax.dynamic_update_index_in_dim(arrived, part, chip ^ bits, 0)
        kept = lax.dynamic_index_in_dim(arrived, core, 1, keepdims=False)
        other = self.swap(lax.dynamic_index_in_dim(arrived, 1 - core, 1, keepdims=False), 1)
        even = jnp.where(core == 0, kept, other)
        odd = jnp.where(core == 0, other, kept)
        return jnp.stack([even, odd], axis=1).reshape(parts.shape)


def dot(left, right):
    return jnp.dot(left, right, preferred_element_type=f32)


def dot_turned(left, right):
    return lax.dot_general(left, right, (((1,), (1,)), ((), ())), preferred_element_type=f32)


def expert_kernel(first_ref, packet_ref, cotangent_ref, weight_ref, *refs, fresh, last):
    if fresh:
        (out_ref, back_ref, grad_ref, packet_turned, cotangent_turned, sums) = refs
    elif last:
        (prior_ref, out_ref, back_ref, rounded_ref, packet_turned, cotangent_turned, grad_ref, sums,
         arrival) = refs
    else:
        (prior_ref, out_ref, back_ref, grad_ref, packet_turned, cotangent_turned, sums, arrival) = refs
    width = cotangent_ref.shape[-1]
    rows = cotangent_ref.shape[1]
    first = first_ref[0]
    start = pl.program_id(0) == 0

    @pl.when(start)
    def _():
        if fresh:
            grad_ref[...] = jnp.zeros_like(grad_ref)
        else:
            copy = pltpu.make_async_copy(prior_ref, grad_ref, arrival)
            copy.start()
            copy.wait()

    lane = lax.broadcasted_iota(jnp.int32, (rows, EXTRA), 1)
    normed = packet_ref[0, :, :width]
    upstream = cotangent_ref[0]
    shares = packet_ref[0, :, width:].astype(f32)
    extra = jnp.zeros((rows, EXTRA), f32)
    packet_turned[...] = normed.T
    cotangent_turned[...] = upstream.T
    begun = []
    for local in range(LOCAL_EXPERTS):
        begun.append(
            (
                dot(normed, weight_ref[local, 0]),
                dot(normed, weight_ref[local, 1]),
                dot(upstream, weight_ref[local, 2]),
            )
        )
    for local in range(LOCAL_EXPERTS):
        gate_pre, up_pre, inner_raw = begun[local]
        expert = first + local
        is_high, is_low = lane == expert, lane == expert + EXPERTS
        share = jnp.sum(jnp.where(is_high | is_low, shares, 0.0), axis=1, keepdims=True)
        sigmoid_gate = jax.nn.sigmoid(gate_pre)
        activated = gate_pre * sigmoid_gate
        inner = (activated * up_pre).astype(bf16).astype(f32)
        share_grad = residual_scale * jnp.sum(inner * inner_raw, axis=1, keepdims=True)
        scaled = share * residual_scale
        inner_grad = inner_raw * scaled
        gate_grad = (
            inner_grad * up_pre * (sigmoid_gate + activated * (1.0 - sigmoid_gate))
        ).astype(bf16)
        up_grad = (inner_grad * activated).astype(bf16)
        inner_shared = (inner * scaled).astype(bf16)
        out_term = dot_turned(inner_shared, weight_ref[local, 2])
        back_term = dot_turned(gate_grad, weight_ref[local, 0]) + dot_turned(
            up_grad, weight_ref[local, 1]
        )
        if local == 0:
            sums[0], sums[1] = out_term, back_term
        else:
            out_ref[0] = (sums[0] + out_term).astype(bf16)
            back_ref[0, :, :width] = (sums[1] + back_term).astype(bf16)
        grad_ref[local, 0] += dot(packet_turned[...], gate_grad)
        grad_ref[local, 1] += dot(packet_turned[...], up_grad)
        grad_ref[local, 2] += dot(cotangent_turned[...], inner_shared)
        high = share_grad.astype(bf16).astype(f32)
        extra = extra + jnp.where(is_high, high, 0.0) + jnp.where(is_low, share_grad - high, 0.0)
    back_ref[0, :, width:] = extra.astype(bf16)
    if last:
        @pl.when(pl.program_id(0) == pl.num_programs(0) - 1)
        def _():
            rounded_ref[...] = grad_ref[...].astype(bf16)


def run_experts(first, packets, cotangents, weights, prior, last):
    block_count, rows, wide = packets.shape
    width = cotangents.shape[-1]
    hidden = weights.shape[-1]
    grad_shape = (LOCAL_EXPERTS, 3, width, hidden)
    fresh = prior is None
    in_specs = [
        pl.BlockSpec((1, rows, wide), lambda i, s: (i, 0, 0)),
        pl.BlockSpec((1, rows, width), lambda i, s: (i, 0, 0)),
        pl.BlockSpec(grad_shape, lambda i, s: (0, 0, 0, 0), pipeline_mode=pl.Buffered(1)),
    ]
    scratch = [pltpu.VMEM((width, rows), bf16), pltpu.VMEM((width, rows), bf16)]
    if last:
        scratch.append(pltpu.VMEM(grad_shape, f32))
    scratch.append(pltpu.VMEM((2, rows, width), f32))
    if not fresh:
        in_specs.append(pl.BlockSpec(memory_space=pl.ANY))
        scratch.append(pltpu.SemaphoreType.DMA)
    return pl.pallas_call(
        functools.partial(expert_kernel, fresh=fresh, last=last),
        grid_spec=pltpu.PrefetchScalarGridSpec(
            num_scalar_prefetch=1,
            grid=(block_count,),
            in_specs=in_specs,
            out_specs=[
                pl.BlockSpec((1, rows, width), lambda i, s: (i, 0, 0)),
                pl.BlockSpec((1, rows, wide), lambda i, s: (i, 0, 0)),
                pl.BlockSpec(grad_shape, lambda i, s: (0, 0, 0, 0), pipeline_mode=pl.Buffered(1)),
            ],
            scratch_shapes=scratch,
        ),
        out_shape=[
            jax.ShapeDtypeStruct((block_count, rows, width), bf16),
            jax.ShapeDtypeStruct((block_count, rows, wide), bf16),
            jax.ShapeDtypeStruct(grad_shape, bf16 if last else f32),
        ],
        compiler_params=pltpu.CompilerParams(vmem_limit_bytes=60 * 1024 * 1024),
        cost_estimate=pl.CostEstimate(
            flops=block_count * LOCAL_EXPERTS * 9 * 2 * rows * width * hidden,
            bytes_accessed=block_count * rows * width * 8 + 36 * width * hidden,
            transcendentals=block_count * LOCAL_EXPERTS * rows * hidden,
        ),
        name="experts",
    )(first, packets, cotangents, weights, *(() if fresh else (prior,)))


def local(
    tokens,
    lengths,
    routes,
    attention_gain,
    query_weight,
    key_weight,
    value_weight,
    output_weight,
    expert_gain,
    router_weight,
    gate_weight,
    up_weight,
    down_weight,
    cotangent,
    *,
    count,
):
    links = Exchange(count)
    member, group, groups = links.member, links.group, links.groups
    row_count, width = tokens.shape
    shard = query_weight.shape[0]
    hidden = gate_weight.shape[2]
    head_columns, kv_columns = HEADS * HEAD_DIM, KV_HEADS * HEAD_DIM
    group_size = HEADS // KV_HEADS

    packed = jnp.concatenate(
        [
            query_weight,
            key_weight,
            value_weight,
            output_weight.T,
            router_weight,
            attention_gain[:, None],
            expert_gain[:, None],
            jnp.zeros((shard, EXTRA - EXPERTS - 2), bf16),
        ],
        axis=1,
    )
    pack_width = packed.shape[1]
    column = links.direct_gather(packed).reshape(groups * shard, pack_width)
    spread = links.chips_gather(column)
    even = jnp.stack([jnp.concatenate(spread[k], axis=0) for k in (0, 2, 4, 6)])
    odd = links.swap(even, 1)
    whole = jnp.zeros((groups, MEMBERS, shard, pack_width), bf16)
    for k in range(MEMBERS):
        part = (odd if k % 2 else even)[k // 2].reshape(groups, shard, pack_width)
        whole = lax.dynamic_update_index_in_dim(whole, part, member ^ k, 1)
    whole = whole.reshape(width, pack_width)
    at_output = head_columns + 2 * kv_columns
    at_extra = at_output + head_columns
    qkv_full = whole[:, :at_output]
    output_turned = whole[:, at_output:at_extra]
    router_full = whole[:, at_extra : at_extra + EXPERTS]
    gain_one = whole[:, at_extra + EXPERTS].astype(f32)
    gain_two = whole[:, at_extra + EXPERTS + 1].astype(f32)

    mine = jnp.stack([gate_weight, up_weight, down_weight.transpose(0, 2, 1)], axis=1)
    mine = mine.reshape(MEMBERS, LOCAL_EXPERTS, 3, shard, hidden)
    shelf = links.send_parts(mine).transpose(1, 2, 0, 3, 4)
    shelf = shelf.reshape(LOCAL_EXPERTS, 3, MEMBERS * shard, hidden)
    expert_full = jnp.zeros((LOCAL_EXPERTS, 3, groups, MEMBERS * shard, hidden), bf16)
    for back, piece in enumerate(links.line_gather(shelf)):
        expert_full = lax.dynamic_update_index_in_dim(
            expert_full, piece, (group + groups - back) % groups, 2
        )
    expert_full = expert_full.reshape(LOCAL_EXPERTS, 3, width, hidden)
    late_cotangent, whole = lax.optimization_barrier((cotangent, whole))
    cotangents = links.chips_gather(late_cotangent)

    inputs = tokens.astype(f32)
    cosine_table, sine_table = rope_tables(row_count)
    scale_one, normed_raw = norm_rows(inputs, gain_one)
    normed_one = normed_raw.astype(bf16)
    projected = dot(normed_one, qkv_full)
    queries = projected[:, :head_columns].reshape(row_count, KV_HEADS, group_size, HEAD_DIM)
    key_rows = projected[:, head_columns : head_columns + kv_columns].reshape(
        row_count, KV_HEADS, HEAD_DIM
    )
    value_rows = (
        projected[:, head_columns + kv_columns :].astype(bf16).reshape(row_count, KV_HEADS, HEAD_DIM)
    )
    query_rot = rotate_apply(
        queries, cosine_table[:, None, None, :], sine_table[:, None, None, :]
    ).astype(bf16)
    key_rot = rotate_apply(key_rows, cosine_table[:, None, :], sine_table[:, None, :]).astype(bf16)
    position = jnp.arange(row_count, dtype=jnp.int32)
    allowed = (position[None, :] <= position[:, None]) & (position[None, :] < lengths[0])
    scores = attention_scores(query_rot, key_rot, allowed)
    maxima = jnp.max(scores, axis=-1, keepdims=True)
    exponent = jnp.exp(scores - maxima)
    totals = jnp.sum(exponent, axis=-1, keepdims=True)
    log_total = maxima + jnp.log(totals)
    softmax_rows = exponent / totals
    mixed = (
        jnp.einsum("kgqp,pkd->qkgd", softmax_rows.astype(bf16), value_rows, preferred_element_type=f32)
        .astype(bf16)
        .reshape(row_count, head_columns)
    )
    middle = inputs + residual_scale * dot_turned(mixed, output_turned)
    scale_two, normed_raw_two = norm_rows(middle, gain_two)
    normed_two = normed_raw_two.astype(bf16)
    logits = dot(normed_two, router_full)
    expert_ids = jnp.arange(EXPERTS, dtype=jnp.int32)
    routed = jnp.any(routes[:, :, None] == expert_ids[None, None, :], axis=1)
    best = jnp.max(jnp.where(routed, logits, masked_value), axis=1, keepdims=True)
    weights = jnp.where(routed, jnp.exp(jnp.where(routed, logits, best) - best), 0.0)
    shares = weights / jnp.sum(weights, axis=1, keepdims=True)
    share_high = lax.reduce_precision(shares, 8, 7)
    packet = jnp.concatenate(
        [
            normed_two,
            share_high.astype(bf16),
            (shares - share_high).astype(bf16),
            jnp.zeros((row_count, EXTRA - 2 * EXPERTS), bf16),
        ],
        axis=1,
    )
    packets = links.chips_gather(packet)

    first = (member * LOCAL_EXPERTS).astype(jnp.int32).reshape(1)
    out_terms, back_terms = {}, {}
    grads = None
    turns = ((0,), (2, 6), (4,))
    for turn in turns:
        stacks = []
        for blocks in (packets, cotangents):
            even = jnp.concatenate([part for k in turn for part in blocks[k]], axis=0)
            even = even.reshape(len(turn), row_count, even.shape[-1])
            stacks.append(jnp.concatenate([even, links.swap(even, 1)], axis=0))
        outs, backs, grads = run_experts(
            first, stacks[0], stacks[1], expert_full, grads, turn == turns[-1]
        )
        for at, k in enumerate(turn):
            out_terms[k], out_terms[k + 1] = outs[at], outs[len(turn) + at]
            back_terms[k] = links.join_cores(backs[at], backs[len(turn) + at])

    back_total = links.chips_reduce(back_terms)

    grads = grads.reshape(LOCAL_EXPERTS, 3, groups, MEMBERS, shard, hidden)
    shelf_grad = links.line_reduce(
        lambda owner: lax.dynamic_index_in_dim(grads, owner, 2, keepdims=False).astype(f32)
    ).astype(bf16)
    expert_shards = links.send_parts(shelf_grad.transpose(2, 0, 1, 3, 4)).astype(f32)
    expert_shards = expert_shards.reshape(EXPERTS, 3, shard, hidden)

    out_terms, back_total = lax.optimization_barrier((out_terms, back_total))
    mixture = links.chips_reduce(
        {k: links.join_cores(out_terms[k], out_terms[k + 1]) for k in (6, 2, 4, 0)}
    )
    layer_out = (middle + mixture).astype(bf16)

    def reduce_pack(parts):
        spare = -sum(part.shape[1] for part in parts) % EXTRA
        pack = jnp.concatenate(parts + [jnp.zeros((width, spare), f32)], axis=1).astype(bf16)
        columns = pack.shape[1]
        pack = pack.reshape(groups, MEMBERS // 2, 2, shard, columns)
        core, chip = member % 2, member // 2
        own = lax.dynamic_index_in_dim(pack, core, 2, keepdims=False)
        other = lax.dynamic_index_in_dim(pack, 1 - core, 2, keepdims=False)
        joined = links.join_cores(own, other)
        terms = {
            2 * bits: lax.dynamic_index_in_dim(joined, chip ^ bits, 1, keepdims=False).reshape(
                groups * shard, columns
            )
            for bits in range(MEMBERS // 2)
        }
        return links.direct_reduce(links.chips_reduce(terms).reshape(groups, shard, columns))

    upstream = cotangent.astype(f32)
    share_grad = (
        back_total[:, width : width + EXPERTS] + back_total[:, width + EXPERTS : width + 2 * EXPERTS]
    )
    share_grad = jnp.where(routed, share_grad, 0.0)
    logit_grad = (
        shares * (share_grad - jnp.sum(shares * share_grad, axis=1, keepdims=True))
    ).astype(bf16)
    normed_two_grad = back_total[:, :width] + dot_turned(logit_grad, router_full)
    grad_router = dot(normed_two.T, logit_grad)
    middle_norm_grad, grad_gain_two = norm_back(middle, scale_two, gain_two, normed_two_grad)
    middle_grad = upstream + middle_norm_grad
    branch_grad = (residual_scale * middle_grad).astype(bf16)
    grad_output_turned = dot(branch_grad.T, mixed)
    mixed_grad = (
        dot(branch_grad, output_turned)
        .astype(bf16)
        .reshape(row_count, KV_HEADS, group_size, HEAD_DIM)
    )
    scores_again = attention_scores(query_rot, key_rot, allowed)
    softmax_again = jnp.exp(scores_again - log_total)
    prob_grad = jnp.einsum("qkgd,pkd->kgqp", mixed_grad, value_rows, preferred_element_type=f32)
    row_delta = jnp.sum(prob_grad * softmax_again, axis=-1, keepdims=True)
    score_grad = (attention_scale * softmax_again * (prob_grad - row_delta)).astype(bf16)
    value_grad = (
        jnp.einsum("kgqp,qkgd->pkd", softmax_again.astype(bf16), mixed_grad, preferred_element_type=f32)
        .astype(bf16)
        .reshape(row_count, kv_columns)
    )
    query_rot_grad = jnp.einsum("kgqp,pkd->qkgd", score_grad, key_rot, preferred_element_type=f32)
    key_rot_grad = jnp.einsum("kgqp,qkgd->pkd", score_grad, query_rot, preferred_element_type=f32)
    query_grad = (
        rotate_back(query_rot_grad, cosine_table[:, None, None, :], sine_table[:, None, None, :])
        .astype(bf16)
        .reshape(row_count, head_columns)
    )
    key_grad = (
        rotate_back(key_rot_grad, cosine_table[:, None, :], sine_table[:, None, :])
        .astype(bf16)
        .reshape(row_count, kv_columns)
    )
    qkv_grad = jnp.concatenate([query_grad, key_grad, value_grad], axis=1)
    grad_qkv = dot(normed_one.T, qkv_grad)
    normed_one_grad = dot_turned(qkv_grad, qkv_full)
    input_norm_grad, grad_gain_one = norm_back(inputs, scale_one, gain_one, normed_one_grad)
    grad_tokens = middle_grad + input_norm_grad

    first_total = reduce_pack([grad_output_turned, grad_router, grad_gain_two[:, None]])
    second_total = reduce_pack([grad_qkv, grad_gain_one[:, None]])
    return (
        layer_out,
        grad_tokens,
        second_total[:, at_output],
        second_total[:, :head_columns],
        second_total[:, head_columns : head_columns + kv_columns],
        second_total[:, head_columns + kv_columns : at_output],
        first_total[:, :head_columns].T,
        first_total[:, head_columns + EXPERTS],
        first_total[:, head_columns : head_columns + EXPERTS],
        expert_shards[:, 0],
        expert_shards[:, 1],
        expert_shards[:, 2].transpose(0, 2, 1),
    )


def solution(mesh):
    count = mesh.shape["fsdp"]
    placed = (
        P("fsdp", None),
        P("fsdp"),
        P("fsdp", None),
        P("fsdp"),
        P("fsdp", None),
        P("fsdp", None),
        P("fsdp", None),
        P(None, "fsdp"),
        P("fsdp"),
        P("fsdp", None),
        P(None, "fsdp", None),
        P(None, "fsdp", None),
        P(None, None, "fsdp"),
        P("fsdp", None),
    )

    def body(*args):
        return local(*args, count=count)

    return jax.shard_map(
        body,
        mesh=mesh,
        in_specs=placed,
        out_specs=(
            P("fsdp", None),
            P("fsdp", None),
            P("fsdp"),
            P("fsdp", None),
            P("fsdp", None),
            P("fsdp", None),
            P(None, "fsdp"),
            P("fsdp"),
            P("fsdp", None),
            P(None, "fsdp", None),
            P(None, "fsdp", None),
            P(None, None, "fsdp"),
        ),
        check_vma=False,
    )
```

```python
import functools

import jax
import jax.numpy as jnp
from jax import lax
from jax.experimental import pallas as pl
from jax.experimental.pallas import tpu as pltpu
from jax.sharding import PartitionSpec as P

HEADS = 16
KV_HEADS = 8
HEAD_DIM = 64
EXPERTS = 16
MEMBERS = 8
LOCAL_EXPERTS = EXPERTS // MEMBERS
EXTRA = 128

norm_eps = 1e-06
attention_scale = 0.015625
residual_scale = 0.22
rope_base = 10000.0
masked_value = -1e30
f32 = jnp.float32
bf16 = jnp.bfloat16


def rope_tables(row_count):
    half_dim = HEAD_DIM // 2
    frequency = rope_base ** (-2.0 * jnp.arange(half_dim, dtype=jnp.float32) / HEAD_DIM)
    angles = jnp.arange(row_count, dtype=jnp.float32)[:, None] * frequency[None, :]
    angles = jnp.concatenate([angles, angles], axis=1)
    return (jnp.cos(angles), jnp.sin(angles))


def rotate_apply(values, cosine_table, sine_table):
    half_dim = values.shape[-1] // 2
    turned = jnp.concatenate([-values[..., half_dim:], values[..., :half_dim]], axis=-1)
    return values * cosine_table + turned * sine_table


def rotate_back(grads, cosine_table, sine_table):
    half_dim = grads.shape[-1] // 2
    scaled = grads * sine_table
    turned = jnp.concatenate([scaled[..., half_dim:], -scaled[..., :half_dim]], axis=-1)
    return grads * cosine_table + turned


def norm_rows(values, gain_row):
    row_scale = lax.rsqrt(jnp.mean(values * values, axis=-1, keepdims=True) + norm_eps)
    return (row_scale, values * row_scale * gain_row)


def norm_back(values, row_scale, gain_row, normed_grad):
    weighted = normed_grad * gain_row
    grad_gain = jnp.sum(normed_grad * values * row_scale, axis=0)
    correction = jnp.mean(weighted * values, axis=-1, keepdims=True)
    return (row_scale * weighted - values * row_scale**3 * correction, grad_gain)


def attention_scores(query_rot, key_rot, allowed):
    raw_scores = jnp.einsum("qkgd,pkd->kgqp", query_rot, key_rot, preferred_element_type=f32)
    return jnp.where(allowed, attention_scale * raw_scores, masked_value)


class Exchange:
    def __init__(self, count):
        self.count = count
        self.groups = count // MEMBERS
        index = lax.axis_index("fsdp")
        self.member = index % MEMBERS
        self.group = index // MEMBERS

    def swap(self, value, bits):
        return lax.ppermute(value, "fsdp", [(i, i ^ bits) for i in range(self.count)])

    def shift(self, value, senders, step):
        pairs = [
            (g * MEMBERS + m, (g + step) * MEMBERS + m) for g in senders for m in range(MEMBERS)
        ]
        return lax.ppermute(value, "fsdp", pairs)

    def line_gather(self, piece):
        groups = self.groups
        rising, falling = [piece], [piece]
        for step in range(1, groups):
            rising.append(self.shift(rising[-1], range(step - 1, groups - 1), 1))
            falling.append(self.shift(falling[-1], range(1, groups - step + 1), -1))
        found = [piece]
        for step in range(1, groups):
            found.append(jnp.where(self.group >= step, rising[step], falling[groups - step]))
        return found

    def line_reduce(self, pick):
        groups = self.groups
        rising = falling = None
        for step in range(1, groups):
            up = pick((self.group + groups - step) % groups)
            down = pick((self.group + step) % groups)
            up_owner = self.group + groups - step
            down_owner = self.group - groups + step
            if rising is not None:
                up = up + rising.astype(f32)
                down = down + falling.astype(f32)
            del up_owner, down_owner
            rising = self.shift(up.astype(bf16), range(0, step), 1)
            falling = self.shift(down.astype(bf16), range(groups - step, groups), -1)
        own = pick(self.group)
        if rising is None:
            return own
        return own + rising.astype(f32) + falling.astype(f32)

    def direct_gather(self, piece):
        stack = jnp.zeros((self.groups,) + piece.shape, piece.dtype)
        for bits in range(self.groups):
            part = self.swap(piece, bits * MEMBERS) if bits else piece
            stack = lax.dynamic_update_index_in_dim(stack, part, self.group ^ bits, 0)
        return stack

    def direct_reduce(self, terms):
        total = lax.dynamic_index_in_dim(terms, self.group, 0, keepdims=False)
        for bits in range(1, self.groups):
            part = lax.dynamic_index_in_dim(terms, self.group ^ bits, 0, keepdims=False)
            total = total + self.swap(part.astype(bf16), bits * MEMBERS).astype(f32)
        return total

    def chips_gather(self, block):
        half = block.shape[0] // 2
        top, low = block[:half], block[half:]
        near_top = self.swap(top, 2)
        far_low = self.swap(low, 4)
        near_low = self.swap(low, 2)
        far_top = self.swap(top, 4)
        cross_top = self.swap(near_top, 4)
        cross_low = self.swap(far_low, 2)
        return {0: (top, low), 2: (near_top, near_low), 4: (far_top, far_low), 6: (cross_top, cross_low)}

    def chips_reduce(self, joined):
        half = joined[0].shape[0] // 2
        cross_top = self.swap(joined[6][:half].astype(bf16), 2).astype(f32)
        cross_low = self.swap(joined[6][half:].astype(bf16), 4).astype(f32)
        near_top = self.swap(joined[2][:half].astype(bf16), 2).astype(f32)
        far_low = self.swap(joined[4][half:].astype(bf16), 4).astype(f32)
        near_low = self.swap((joined[2][half:] + cross_low).astype(bf16), 2).astype(f32)
        far_top = self.swap((joined[4][:half] + cross_top).astype(bf16), 4).astype(f32)
        return jnp.concatenate(
            [joined[0][:half] + near_top + far_top, joined[0][half:] + near_low + far_low], axis=0
        )

    def join_cores(self, own, other):
        return own.astype(f32) + self.swap(other, 1).astype(f32)

    def send_parts(self, parts):
        chips = parts.reshape((MEMBERS // 2, 2) + parts.shape[1:])
        chip, core = self.member // 2, self.member % 2
        arrived = jnp.zeros_like(chips)
        for bits in range(MEMBERS // 2):
            part = lax.dynamic_index_in_dim(chips, chip ^ bits, 0, keepdims=False)
            if bits:
                part = self.swap(part, 2 * bits)
            arrived = lax.dynamic_update_index_in_dim(arrived, part, chip ^ bits, 0)
        kept = lax.dynamic_index_in_dim(arrived, core, 1, keepdims=False)
        other = self.swap(lax.dynamic_index_in_dim(arrived, 1 - core, 1, keepdims=False), 1)
        even = jnp.where(core == 0, kept, other)
        odd = jnp.where(core == 0, other, kept)
        return jnp.stack([even, odd], axis=1).reshape(parts.shape)


def dot(left, right):
    return jnp.dot(left, right, preferred_element_type=f32)


def dot_turned(left, right):
    return lax.dot_general(left, right, (((1,), (1,)), ((), ())), preferred_element_type=f32)


def expert_kernel(first_ref, *refs, layout, fresh, last):
    refs = list(refs)
    packet_parts = [[refs.pop(0) for _ in range(number)] for number in layout]
    cotangent_parts = [[refs.pop(0) for _ in range(number)] for number in layout]
    weight_parts = refs.pop(0)
    prior_ref = None if fresh else refs.pop(0)
    out_refs, back_refs = (refs.pop(0), refs.pop(0)), (refs.pop(0), refs.pop(0))
    if last:
        rounded_ref = refs.pop(0)
        grad_ref = refs.pop(0)
    else:
        grad_ref = refs.pop(0)
    packet_buffer, cotangent_buffer, weight_ref, packet_turned, cotangent_turned, sums = refs[:6]
    block_sem, weight_sem, prior_sem = refs[6:]
    rows, width = cotangent_buffer.shape[1:]
    groups, _, _, depth, _ = weight_parts.shape
    blocks = len(layout)
    at = pl.program_id(0)
    first = first_ref[0]

    def block_copies(block):
        copies = []
        for kind, (parts, buffer) in enumerate(
            ((packet_parts, packet_buffer), (cotangent_parts, cotangent_buffer))
        ):
            size = rows // layout[block]
            for number, part in enumerate(parts[block]):
                place = buffer.at[block, pl.ds(number * size, size)]
                copies.append(
                    pltpu.make_async_copy(part, place, block_sem.at[block, 2 * kind + number])
                )
        return copies

    def weight_copies():
        return [
            pltpu.make_async_copy(
                weight_parts.at[g], weight_ref.at[:, :, pl.ds(g * depth, depth)], weight_sem.at[g]
            )
            for g in range(groups)
        ]

    def prior_copy():
        return pltpu.make_async_copy(prior_ref, grad_ref, prior_sem)

    @pl.when(at == 0)
    def _():
        for copy in block_copies(0) + weight_copies():
            copy.start()
        if fresh:
            grad_ref[...] = jnp.zeros_like(grad_ref)
        else:
            prior_copy().start()
        for block in range(1, blocks):
            for copy in block_copies(block):
                copy.start()
        for copy in weight_copies():
            copy.wait()

    for block in range(blocks):

        @pl.when(at == block)
        def _():
            for copy in block_copies(block):
                copy.wait()

    lane = lax.broadcasted_iota(jnp.int32, (rows, EXTRA), 1)
    normed = packet_buffer[at, :, :width]
    upstream = cotangent_buffer[at]
    shares = packet_buffer[at, :, width:].astype(f32)
    extra = jnp.zeros((rows, EXTRA), f32)
    packet_turned[...] = normed.T
    cotangent_turned[...] = upstream.T
    begun = []
    for local in range(LOCAL_EXPERTS):
        begun.append(
            (
                dot(normed, weight_ref[local, 0]),
                dot(normed, weight_ref[local, 1]),
                dot(upstream, weight_ref[local, 2]),
            )
        )
    if not fresh:

        @pl.when(at == 0)
        def _():
            prior_copy().wait()

    for local in range(LOCAL_EXPERTS):
        gate_pre, up_pre, inner_raw = begun[local]
        expert = first + local
        is_high, is_low = lane == expert, lane == expert + EXPERTS
        share = jnp.sum(jnp.where(is_high | is_low, shares, 0.0), axis=1, keepdims=True)
        sigmoid_gate = jax.nn.sigmoid(gate_pre)
        activated = gate_pre * sigmoid_gate
        inner = (activated * up_pre).astype(bf16).astype(f32)
        share_grad = residual_scale * jnp.sum(inner * inner_raw, axis=1, keepdims=True)
        scaled = share * residual_scale
        inner_grad = inner_raw * scaled
        gate_grad = (
            inner_grad * up_pre * (sigmoid_gate + activated * (1.0 - sigmoid_gate))
        ).astype(bf16)
        up_grad = (inner_grad * activated).astype(bf16)
        inner_shared = (inner * scaled).astype(bf16)
        out_term = dot_turned(inner_shared, weight_ref[local, 2])
        back_term = dot_turned(gate_grad, weight_ref[local, 0]) + dot_turned(
            up_grad, weight_ref[local, 1]
        )
        if local == 0:
            sums[0], sums[1] = out_term, back_term
        else:
            sums[0] += out_term
            sums[1] += back_term
        grad_ref[local, 0] += dot(packet_turned[...], gate_grad)
        grad_ref[local, 1] += dot(packet_turned[...], up_grad)
        grad_ref[local, 2] += dot(cotangent_turned[...], inner_shared)
        high = share_grad.astype(bf16).astype(f32)
        extra = extra + jnp.where(is_high, high, 0.0) + jnp.where(is_low, share_grad - high, 0.0)
    for side in range(2):

        @pl.when((at < blocks // 2) == (side == 0))
        def _():
            out_refs[side][0] = sums[0].astype(bf16)
            back_refs[side][0, :, :width] = sums[1].astype(bf16)
            back_refs[side][0, :, width:] = extra.astype(bf16)

    if last:

        @pl.when(at == blocks - 1)
        def _():
            for g in range(groups):
                rounded_ref[g] = grad_ref[:, :, pl.ds(g * depth, depth)].astype(bf16)


def run_experts(first, packets, cotangents, weights, prior, last):
    layout = tuple(len(parts) for parts in packets)
    blocks = len(layout)
    rows = sum(part.shape[0] for part in packets[0])
    wide, width = packets[0][0].shape[1], cotangents[0][0].shape[1]
    groups, _, _, depth, hidden = weights.shape
    grad_shape = (LOCAL_EXPERTS, 3, width, hidden)
    fresh = prior is None
    operands = [part for parts in packets for part in parts]
    operands += [part for parts in cotangents for part in parts]
    operands += [weights] + ([] if fresh else [prior])
    half = blocks // 2

    def own_side(i, s):
        return (jnp.minimum(i, half - 1), 0, 0)

    def other_side(i, s):
        return (jnp.maximum(i - half, 0), 0, 0)

    def whole(i, s):
        return (0, 0, 0, 0, 0) if last else (0, 0, 0, 0)

    last_shape = weights.shape if last else grad_shape
    scratch = [pltpu.VMEM(grad_shape, f32)] if last else []
    scratch += [
        pltpu.VMEM((blocks, rows, wide), bf16),
        pltpu.VMEM((blocks, rows, width), bf16),
        pltpu.VMEM(grad_shape, bf16),
        pltpu.VMEM((width, rows), bf16),
        pltpu.VMEM((width, rows), bf16),
        pltpu.VMEM((2, rows, width), f32),
        pltpu.SemaphoreType.DMA((blocks, 4)),
        pltpu.SemaphoreType.DMA((groups,)),
        pltpu.SemaphoreType.DMA,
    ]
    return pl.pallas_call(
        functools.partial(expert_kernel, layout=layout, fresh=fresh, last=last),
        grid_spec=pltpu.PrefetchScalarGridSpec(
            num_scalar_prefetch=1,
            grid=(blocks,),
            in_specs=[pl.BlockSpec(memory_space=pl.ANY)] * len(operands),
            out_specs=[
                pl.BlockSpec((1, rows, width), own_side),
                pl.BlockSpec((1, rows, width), other_side),
                pl.BlockSpec((1, rows, wide), own_side),
                pl.BlockSpec((1, rows, wide), other_side),
                pl.BlockSpec(last_shape, whole, pipeline_mode=pl.Buffered(1)),
            ],
            scratch_shapes=scratch,
        ),
        out_shape=[
            jax.ShapeDtypeStruct((half, rows, width), bf16),
            jax.ShapeDtypeStruct((half, rows, width), bf16),
            jax.ShapeDtypeStruct((half, rows, wide), bf16),
            jax.ShapeDtypeStruct((half, rows, wide), bf16),
            jax.ShapeDtypeStruct(last_shape, bf16 if last else f32),
        ],
        compiler_params=pltpu.CompilerParams(vmem_limit_bytes=62 * 1024 * 1024),
        cost_estimate=pl.CostEstimate(
            flops=blocks * LOCAL_EXPERTS * 9 * 2 * rows * width * hidden,
            bytes_accessed=blocks * rows * width * 8 + 36 * width * hidden,
            transcendentals=blocks * LOCAL_EXPERTS * rows * hidden,
        ),
        name="experts",
    )(first, *operands)


def local(
    tokens,
    lengths,
    routes,
    attention_gain,
    query_weight,
    key_weight,
    value_weight,
    output_weight,
    expert_gain,
    router_weight,
    gate_weight,
    up_weight,
    down_weight,
    cotangent,
    *,
    count,
):
    links = Exchange(count)
    member, group, groups = links.member, links.group, links.groups
    row_count, width = tokens.shape
    shard = query_weight.shape[0]
    hidden = gate_weight.shape[2]
    head_columns, kv_columns = HEADS * HEAD_DIM, KV_HEADS * HEAD_DIM
    group_size = HEADS // KV_HEADS

    packed = jnp.concatenate(
        [
            query_weight,
            key_weight,
            value_weight,
            output_weight.T,
            router_weight,
            attention_gain[:, None],
            expert_gain[:, None],
            jnp.zeros((shard, EXTRA - EXPERTS - 2), bf16),
        ],
        axis=1,
    )
    pack_width = packed.shape[1]
    column = links.direct_gather(packed).reshape(groups * shard, pack_width)
    spread = links.chips_gather(column)
    even = jnp.stack([jnp.concatenate(spread[k], axis=0) for k in (0, 2, 4, 6)])
    odd = links.swap(even, 1)
    whole = jnp.zeros((groups, MEMBERS, shard, pack_width), bf16)
    for k in range(MEMBERS):
        part = (odd if k % 2 else even)[k // 2].reshape(groups, shard, pack_width)
        whole = lax.dynamic_update_index_in_dim(whole, part, member ^ k, 1)
    whole = whole.reshape(width, pack_width)
    at_output = head_columns + 2 * kv_columns
    at_extra = at_output + head_columns
    qkv_full = whole[:, :at_output]
    output_turned = whole[:, at_output:at_extra]
    router_full = whole[:, at_extra : at_extra + EXPERTS]
    gain_one = whole[:, at_extra + EXPERTS].astype(f32)
    gain_two = whole[:, at_extra + EXPERTS + 1].astype(f32)

    mine = jnp.stack([gate_weight, up_weight, down_weight.transpose(0, 2, 1)], axis=1)
    mine = mine.reshape(MEMBERS, LOCAL_EXPERTS, 3, shard, hidden)
    shelf = links.send_parts(mine).transpose(1, 2, 0, 3, 4)
    shelf = shelf.reshape(LOCAL_EXPERTS, 3, MEMBERS * shard, hidden)
    lines = [[m + MEMBERS * g for g in range(groups)] for m in range(MEMBERS)]
    expert_full = lax.all_gather(shelf, "fsdp", axis_index_groups=lines)
    late_cotangent, whole = lax.optimization_barrier((cotangent, whole))
    cotangents = links.chips_gather(late_cotangent)

    inputs = tokens.astype(f32)
    cosine_table, sine_table = rope_tables(row_count)
    scale_one, normed_raw = norm_rows(inputs, gain_one)
    normed_one = normed_raw.astype(bf16)
    projected = dot(normed_one, qkv_full)
    queries = projected[:, :head_columns].reshape(row_count, KV_HEADS, group_size, HEAD_DIM)
    key_rows = projected[:, head_columns : head_columns + kv_columns].reshape(
        row_count, KV_HEADS, HEAD_DIM
    )
    value_rows = (
        projected[:, head_columns + kv_columns :].astype(bf16).reshape(row_count, KV_HEADS, HEAD_DIM)
    )
    query_rot = rotate_apply(
        queries, cosine_table[:, None, None, :], sine_table[:, None, None, :]
    ).astype(bf16)
    key_rot = rotate_apply(key_rows, cosine_table[:, None, :], sine_table[:, None, :]).astype(bf16)
    position = jnp.arange(row_count, dtype=jnp.int32)
    allowed = (position[None, :] <= position[:, None]) & (position[None, :] < lengths[0])
    scores = attention_scores(query_rot, key_rot, allowed)
    maxima = jnp.max(scores, axis=-1, keepdims=True)
    exponent = jnp.exp(scores - maxima)
    totals = jnp.sum(exponent, axis=-1, keepdims=True)
    log_total = maxima + jnp.log(totals)
    softmax_rows = exponent / totals
    mixed = (
        jnp.einsum("kgqp,pkd->qkgd", softmax_rows.astype(bf16), value_rows, preferred_element_type=f32)
        .astype(bf16)
        .reshape(row_count, head_columns)
    )
    middle = inputs + residual_scale * dot_turned(mixed, output_turned)
    scale_two, normed_raw_two = norm_rows(middle, gain_two)
    normed_two = normed_raw_two.astype(bf16)
    logits = dot(normed_two, router_full)
    expert_ids = jnp.arange(EXPERTS, dtype=jnp.int32)
    routed = jnp.any(routes[:, :, None] == expert_ids[None, None, :], axis=1)
    best = jnp.max(jnp.where(routed, logits, masked_value), axis=1, keepdims=True)
    weights = jnp.where(routed, jnp.exp(jnp.where(routed, logits, best) - best), 0.0)
    shares = weights / jnp.sum(weights, axis=1, keepdims=True)
    share_high = lax.reduce_precision(shares, 8, 7)
    packet = jnp.concatenate(
        [
            normed_two,
            share_high.astype(bf16),
            (shares - share_high).astype(bf16),
            jnp.zeros((row_count, EXTRA - 2 * EXPERTS), bf16),
        ],
        axis=1,
    )
    packets = links.chips_gather(packet)
    packets[0] = (packet,)
    cotangents[0] = (late_cotangent,)

    first = (member * LOCAL_EXPERTS).astype(jnp.int32).reshape(1)
    out_terms, back_terms = {}, {}
    grads = None
    turns = ((0,), (2, 6), (4,))
    for turn in turns:
        stacks = []
        for blocks in (packets, cotangents):
            even = [blocks[k] for k in turn]
            stacks.append(even + [tuple(links.swap(part, 1) for part in parts) for parts in even])
        out_own, out_other, back_own, back_other, grads = run_experts(
            first, stacks[0], stacks[1], expert_full, grads, turn == turns[-1]
        )
        back_join = links.join_cores(back_own, back_other)
        for at, k in enumerate(turn):
            out_terms[k] = (out_own[at], out_other[at])
            back_terms[k] = back_join[at]

    back_total = links.chips_reduce(back_terms)

    shelf_grad = lax.psum_scatter(grads, "fsdp", scatter_dimension=0, axis_index_groups=lines)
    shelf_grad = shelf_grad.reshape(LOCAL_EXPERTS, 3, MEMBERS, shard, hidden)
    expert_shards = links.send_parts(shelf_grad.transpose(2, 0, 1, 3, 4)).astype(f32)
    expert_shards = expert_shards.reshape(EXPERTS, 3, shard, hidden)

    out_terms, back_total = lax.optimization_barrier((out_terms, back_total))
    mixture = links.chips_reduce(
        {k: links.join_cores(*out_terms[k]) for k in (6, 2, 4, 0)}
    )
    layer_out = (middle + mixture).astype(bf16)

    def reduce_pack(parts):
        spare = -sum(part.shape[1] for part in parts) % EXTRA
        pack = jnp.concatenate(parts + [jnp.zeros((width, spare), f32)], axis=1).astype(bf16)
        columns = pack.shape[1]
        pack = pack.reshape(groups, MEMBERS // 2, 2, shard, columns)
        core, chip = member % 2, member // 2
        own = lax.dynamic_index_in_dim(pack, core, 2, keepdims=False)
        other = lax.dynamic_index_in_dim(pack, 1 - core, 2, keepdims=False)
        joined = links.join_cores(own, other)
        terms = {
            2 * bits: lax.dynamic_index_in_dim(joined, chip ^ bits, 1, keepdims=False).reshape(
                groups * shard, columns
            )
            for bits in range(MEMBERS // 2)
        }
        return links.direct_reduce(links.chips_reduce(terms).reshape(groups, shard, columns))

    upstream = cotangent.astype(f32)
    share_grad = (
        back_total[:, width : width + EXPERTS] + back_total[:, width + EXPERTS : width + 2 * EXPERTS]
    )
    share_grad = jnp.where(routed, share_grad, 0.0)
    logit_grad = (
        shares * (share_grad - jnp.sum(shares * share_grad, axis=1, keepdims=True))
    ).astype(bf16)
    normed_two_grad = back_total[:, :width] + dot_turned(logit_grad, router_full)
    grad_router = dot(normed_two.T, logit_grad)
    middle_norm_grad, grad_gain_two = norm_back(middle, scale_two, gain_two, normed_two_grad)
    middle_grad = upstream + middle_norm_grad
    branch_grad = (residual_scale * middle_grad).astype(bf16)
    grad_output_turned = dot(branch_grad.T, mixed)
    mixed_grad = (
        dot(branch_grad, output_turned)
        .astype(bf16)
        .reshape(row_count, KV_HEADS, group_size, HEAD_DIM)
    )
    scores_again = attention_scores(query_rot, key_rot, allowed)
    softmax_again = jnp.exp(scores_again - log_total)
    prob_grad = jnp.einsum("qkgd,pkd->kgqp", mixed_grad, value_rows, preferred_element_type=f32)
    row_delta = jnp.sum(prob_grad * softmax_again, axis=-1, keepdims=True)
    score_grad = (attention_scale * softmax_again * (prob_grad - row_delta)).astype(bf16)
    value_grad = (
        jnp.einsum("kgqp,qkgd->pkd", softmax_again.astype(bf16), mixed_grad, preferred_element_type=f32)
        .astype(bf16)
        .reshape(row_count, kv_columns)
    )
    query_rot_grad = jnp.einsum("kgqp,pkd->qkgd", score_grad, key_rot, preferred_element_type=f32)
    key_rot_grad = jnp.einsum("kgqp,qkgd->pkd", score_grad, query_rot, preferred_element_type=f32)
    query_grad = (
        rotate_back(query_rot_grad, cosine_table[:, None, None, :], sine_table[:, None, None, :])
        .astype(bf16)
        .reshape(row_count, head_columns)
    )
    key_grad = (
        rotate_back(key_rot_grad, cosine_table[:, None, :], sine_table[:, None, :])
        .astype(bf16)
        .reshape(row_count, kv_columns)
    )
    qkv_grad = jnp.concatenate([query_grad, key_grad, value_grad], axis=1)
    grad_qkv = dot(normed_one.T, qkv_grad)
    normed_one_grad = dot_turned(qkv_grad, qkv_full)
    input_norm_grad, grad_gain_one = norm_back(inputs, scale_one, gain_one, normed_one_grad)
    grad_tokens = middle_grad + input_norm_grad

    first_total = reduce_pack([grad_output_turned, grad_router, grad_gain_two[:, None]])
    second_total = reduce_pack([grad_qkv, grad_gain_one[:, None]])
    return (
        layer_out,
        grad_tokens,
        second_total[:, at_output],
        second_total[:, :head_columns],
        second_total[:, head_columns : head_columns + kv_columns],
        second_total[:, head_columns + kv_columns : at_output],
        first_total[:, :head_columns].T,
        first_total[:, head_columns + EXPERTS],
        first_total[:, head_columns : head_columns + EXPERTS],
        expert_shards[:, 0],
        expert_shards[:, 1],
        expert_shards[:, 2].transpose(0, 2, 1),
    )


def solution(mesh):
    count = mesh.shape["fsdp"]
    placed = (
        P("fsdp", None),
        P("fsdp"),
        P("fsdp", None),
        P("fsdp"),
        P("fsdp", None),
        P("fsdp", None),
        P("fsdp", None),
        P(None, "fsdp"),
        P("fsdp"),
        P("fsdp", None),
        P(None, "fsdp", None),
        P(None, "fsdp", None),
        P(None, None, "fsdp"),
        P("fsdp", None),
    )

    def body(*args):
        return local(*args, count=count)

    return jax.shard_map(
        body,
        mesh=mesh,
        in_specs=placed,
        out_specs=(
            P("fsdp", None),
            P("fsdp", None),
            P("fsdp"),
            P("fsdp", None),
            P("fsdp", None),
            P("fsdp", None),
            P(None, "fsdp"),
            P("fsdp"),
            P("fsdp", None),
            P(None, "fsdp", None),
            P(None, "fsdp", None),
            P(None, None, "fsdp"),
        ),
        check_vma=False,
    )
```

```python
import functools

import jax
import jax.numpy as jnp
from jax import lax
from jax.experimental import pallas as pl
from jax.experimental.pallas import tpu as pltpu
from jax.sharding import PartitionSpec as P

HEADS = 16
KV_HEADS = 8
HEAD_DIM = 64
EXPERTS = 16
MEMBERS = 8
LOCAL_EXPERTS = EXPERTS // MEMBERS
EXTRA = 128

norm_eps = 1e-06
attention_scale = 0.015625
residual_scale = 0.22
rope_base = 10000.0
masked_value = -1e30
f32 = jnp.float32
bf16 = jnp.bfloat16


def rope_tables(row_count):
    half_dim = HEAD_DIM // 2
    frequency = rope_base ** (-2.0 * jnp.arange(half_dim, dtype=jnp.float32) / HEAD_DIM)
    angles = jnp.arange(row_count, dtype=jnp.float32)[:, None] * frequency[None, :]
    angles = jnp.concatenate([angles, angles], axis=1)
    return (jnp.cos(angles), jnp.sin(angles))


class Exchange:
    def __init__(self, count):
        self.count = count
        self.groups = count // MEMBERS
        index = lax.axis_index("fsdp")
        self.member = index % MEMBERS
        self.group = index // MEMBERS

    def swap(self, value, bits):
        return lax.ppermute(value, "fsdp", [(i, i ^ bits) for i in range(self.count)])

    def shift(self, value, senders, step):
        pairs = [
            (g * MEMBERS + m, (g + step) * MEMBERS + m) for g in senders for m in range(MEMBERS)
        ]
        return lax.ppermute(value, "fsdp", pairs)

    def line_gather(self, piece):
        groups = self.groups
        rising, falling = [piece], [piece]
        for step in range(1, groups):
            rising.append(self.shift(rising[-1], range(step - 1, groups - 1), 1))
            falling.append(self.shift(falling[-1], range(1, groups - step + 1), -1))
        found = [piece]
        for step in range(1, groups):
            found.append(jnp.where(self.group >= step, rising[step], falling[groups - step]))
        return found

    def line_reduce(self, pick):
        groups = self.groups
        rising = falling = None
        for step in range(1, groups):
            up = pick((self.group + groups - step) % groups)
            down = pick((self.group + step) % groups)
            up_owner = self.group + groups - step
            down_owner = self.group - groups + step
            if rising is not None:
                up = up + rising.astype(f32)
                down = down + falling.astype(f32)
            del up_owner, down_owner
            rising = self.shift(up.astype(bf16), range(0, step), 1)
            falling = self.shift(down.astype(bf16), range(groups - step, groups), -1)
        own = pick(self.group)
        if rising is None:
            return own
        return own + rising.astype(f32) + falling.astype(f32)

    def direct_gather(self, piece):
        stack = jnp.zeros((self.groups,) + piece.shape, piece.dtype)
        for bits in range(self.groups):
            part = self.swap(piece, bits * MEMBERS) if bits else piece
            stack = lax.dynamic_update_index_in_dim(stack, part, self.group ^ bits, 0)
        return stack

    def direct_reduce(self, terms):
        total = lax.dynamic_index_in_dim(terms, self.group, 0, keepdims=False)
        for bits in range(1, self.groups):
            part = lax.dynamic_index_in_dim(terms, self.group ^ bits, 0, keepdims=False)
            total = total + self.swap(part.astype(bf16), bits * MEMBERS).astype(f32)
        return total

    def chips_gather(self, block):
        half = block.shape[0] // 2
        top, low = block[:half], block[half:]
        near_top = self.swap(top, 2)
        far_low = self.swap(low, 4)
        near_low = self.swap(low, 2)
        far_top = self.swap(top, 4)
        cross_top = self.swap(near_top, 4)
        cross_low = self.swap(far_low, 2)
        return {0: (top, low), 2: (near_top, near_low), 4: (far_top, far_low), 6: (cross_top, cross_low)}

    def chips_reduce_begin(self, joined):
        half = joined[0].shape[0] // 2
        cross_top = self.swap(joined[6][:half].astype(bf16), 2)
        cross_low = self.swap(joined[6][half:].astype(bf16), 4)
        near_top = self.swap(joined[2][:half].astype(bf16), 2)
        far_low = self.swap(joined[4][half:].astype(bf16), 4)
        return cross_top, cross_low, near_top, far_low, joined[2][half:], joined[4][:half]

    def chips_reduce_end(self, begun):
        cross_top, cross_low, near_top, far_low, near_rest, far_rest = begun
        near_low = self.swap((near_rest + cross_low.astype(f32)).astype(bf16), 2)
        far_top = self.swap((far_rest + cross_top.astype(f32)).astype(bf16), 4)
        return near_top, near_low, far_top, far_low

    @staticmethod
    def add_pieces(own, pieces):
        near_top, near_low, far_top, far_low = (piece.astype(f32) for piece in pieces)
        half = own.shape[0] // 2
        return jnp.concatenate(
            [own[:half] + near_top + far_top, own[half:] + near_low + far_low], axis=0
        )

    def chips_reduce(self, joined):
        return self.add_pieces(joined[0], self.chips_reduce_end(self.chips_reduce_begin(joined)))

    def join_cores(self, own, other):
        return own.astype(f32) + self.swap(other, 1).astype(f32)

    def send_parts(self, parts):
        chips = parts.reshape((MEMBERS // 2, 2) + parts.shape[1:])
        chip, core = self.member // 2, self.member % 2
        arrived = jnp.zeros_like(chips)
        for bits in range(MEMBERS // 2):
            part = lax.dynamic_index_in_dim(chips, chip ^ bits, 0, keepdims=False)
            if bits:
                part = self.swap(part, 2 * bits)
            arrived = lax.dynamic_update_index_in_dim(arrived, part, chip ^ bits, 0)
        kept = lax.dynamic_index_in_dim(arrived, core, 1, keepdims=False)
        other = self.swap(lax.dynamic_index_in_dim(arrived, 1 - core, 1, keepdims=False), 1)
        even = jnp.where(core == 0, kept, other)
        odd = jnp.where(core == 0, other, kept)
        return jnp.stack([even, odd], axis=1).reshape(parts.shape)


def dot(left, right):
    return jnp.dot(left, right, preferred_element_type=f32)


def dot_turned(left, right):
    return lax.dot_general(left, right, (((1,), (1,)), ((), ())), preferred_element_type=f32)


def expert_kernel(first_ref, *refs, layout, fresh, last):
    refs = list(refs)
    packet_parts = [[refs.pop(0) for _ in range(number)] for number in layout]
    cotangent_parts = [[refs.pop(0) for _ in range(number)] for number in layout]
    weight_parts = refs.pop(0)
    prior_ref = None if fresh else refs.pop(0)
    out_refs, back_refs = (refs.pop(0), refs.pop(0)), (refs.pop(0), refs.pop(0))
    if last:
        rounded_ref = refs.pop(0)
        grad_ref = refs.pop(0)
    else:
        grad_ref = refs.pop(0)
    packet_buffer, cotangent_buffer, weight_ref, packet_turned, cotangent_turned, sums = refs[:6]
    block_sem, weight_sem, prior_sem = refs[6:]
    rows, width = cotangent_buffer.shape[1:]
    groups, _, _, depth, _ = weight_parts.shape
    blocks = len(layout)
    at = pl.program_id(0)
    first = first_ref[0]

    def block_copies(block):
        copies = []
        for kind, (parts, buffer) in enumerate(
            ((packet_parts, packet_buffer), (cotangent_parts, cotangent_buffer))
        ):
            size = rows // layout[block]
            for number, part in enumerate(parts[block]):
                place = buffer.at[block, pl.ds(number * size, size)]
                copies.append(
                    pltpu.make_async_copy(part, place, block_sem.at[block, 2 * kind + number])
                )
        return copies

    def weight_copies():
        return [
            pltpu.make_async_copy(
                weight_parts.at[g], weight_ref.at[:, :, pl.ds(g * depth, depth)], weight_sem.at[g]
            )
            for g in range(groups)
        ]

    def prior_copy():
        return pltpu.make_async_copy(prior_ref, grad_ref, prior_sem)

    @pl.when(at == 0)
    def _():
        for copy in block_copies(0) + weight_copies():
            copy.start()
        if fresh:
            grad_ref[...] = jnp.zeros_like(grad_ref)
        else:
            prior_copy().start()
        for block in range(1, blocks):
            for copy in block_copies(block):
                copy.start()
        for copy in weight_copies():
            copy.wait()

    for block in range(blocks):

        @pl.when(at == block)
        def _():
            for copy in block_copies(block):
                copy.wait()

    lane = lax.broadcasted_iota(jnp.int32, (rows, EXTRA), 1)
    normed = packet_buffer[at, :, :width]
    upstream = cotangent_buffer[at]
    shares = packet_buffer[at, :, width:].astype(f32)
    extra = jnp.zeros((rows, EXTRA), f32)
    packet_turned[...] = normed.T
    cotangent_turned[...] = upstream.T
    begun = []
    for local in range(LOCAL_EXPERTS):
        begun.append(
            (
                dot(normed, weight_ref[local, 0]),
                dot(normed, weight_ref[local, 1]),
                dot(upstream, weight_ref[local, 2]),
            )
        )
    if not fresh:

        @pl.when(at == 0)
        def _():
            prior_copy().wait()

    for local in range(LOCAL_EXPERTS):
        gate_pre, up_pre, inner_raw = begun[local]
        expert = first + local
        is_high, is_low = lane == expert, lane == expert + EXPERTS
        share = jnp.sum(jnp.where(is_high | is_low, shares, 0.0), axis=1, keepdims=True)
        sigmoid_gate = jax.nn.sigmoid(gate_pre)
        activated = gate_pre * sigmoid_gate
        inner = (activated * up_pre).astype(bf16).astype(f32)
        share_grad = residual_scale * jnp.sum(inner * inner_raw, axis=1, keepdims=True)
        scaled = share * residual_scale
        inner_grad = inner_raw * scaled
        gate_grad = (
            inner_grad * up_pre * (sigmoid_gate + activated * (1.0 - sigmoid_gate))
        ).astype(bf16)
        up_grad = (inner_grad * activated).astype(bf16)
        inner_shared = (inner * scaled).astype(bf16)
        out_term = dot_turned(inner_shared, weight_ref[local, 2])
        back_term = dot_turned(gate_grad, weight_ref[local, 0]) + dot_turned(
            up_grad, weight_ref[local, 1]
        )
        if local == 0:
            sums[0], sums[1] = out_term, back_term
        else:
            sums[0] += out_term
            sums[1] += back_term
        grad_ref[local, 0] += dot(packet_turned[...], gate_grad)
        grad_ref[local, 1] += dot(packet_turned[...], up_grad)
        grad_ref[local, 2] += dot(cotangent_turned[...], inner_shared)
        high = share_grad.astype(bf16).astype(f32)
        extra = extra + jnp.where(is_high, high, 0.0) + jnp.where(is_low, share_grad - high, 0.0)
    for side in range(2):

        @pl.when((at < blocks // 2) == (side == 0))
        def _():
            out_refs[side][0] = sums[0].astype(bf16)
            back_refs[side][0, :, :width] = sums[1].astype(bf16)
            back_refs[side][0, :, width:] = extra.astype(bf16)

    if last:

        @pl.when(at == blocks - 1)
        def _():
            for g in range(groups):
                rounded_ref[g] = grad_ref[:, :, pl.ds(g * depth, depth)].astype(bf16)


def run_experts(first, packets, cotangents, weights, prior, last):
    layout = tuple(len(parts) for parts in packets)
    blocks = len(layout)
    rows = sum(part.shape[0] for part in packets[0])
    wide, width = packets[0][0].shape[1], cotangents[0][0].shape[1]
    groups, _, _, depth, hidden = weights.shape
    grad_shape = (LOCAL_EXPERTS, 3, width, hidden)
    fresh = prior is None
    operands = [part for parts in packets for part in parts]
    operands += [part for parts in cotangents for part in parts]
    operands += [weights] + ([] if fresh else [prior])
    half = blocks // 2

    def own_side(i, s):
        return (jnp.minimum(i, half - 1), 0, 0)

    def other_side(i, s):
        return (jnp.maximum(i - half, 0), 0, 0)

    def whole(i, s):
        return (0, 0, 0, 0, 0) if last else (0, 0, 0, 0)

    last_shape = weights.shape if last else grad_shape
    scratch = [pltpu.VMEM(grad_shape, f32)] if last else []
    scratch += [
        pltpu.VMEM((blocks, rows, wide), bf16),
        pltpu.VMEM((blocks, rows, width), bf16),
        pltpu.VMEM(grad_shape, bf16),
        pltpu.VMEM((width, rows), bf16),
        pltpu.VMEM((width, rows), bf16),
        pltpu.VMEM((2, rows, width), f32),
        pltpu.SemaphoreType.DMA((blocks, 4)),
        pltpu.SemaphoreType.DMA((groups,)),
        pltpu.SemaphoreType.DMA,
    ]
    return pl.pallas_call(
        functools.partial(expert_kernel, layout=layout, fresh=fresh, last=last),
        grid_spec=pltpu.PrefetchScalarGridSpec(
            num_scalar_prefetch=1,
            grid=(blocks,),
            in_specs=[pl.BlockSpec(memory_space=pl.ANY)] * len(operands),
            out_specs=[
                pl.BlockSpec((1, rows, width), own_side),
                pl.BlockSpec((1, rows, width), other_side),
                pl.BlockSpec((1, rows, wide), own_side),
                pl.BlockSpec((1, rows, wide), other_side),
                pl.BlockSpec(last_shape, whole, pipeline_mode=pl.Buffered(1)),
            ],
            scratch_shapes=scratch,
        ),
        out_shape=[
            jax.ShapeDtypeStruct((half, rows, width), bf16),
            jax.ShapeDtypeStruct((half, rows, width), bf16),
            jax.ShapeDtypeStruct((half, rows, wide), bf16),
            jax.ShapeDtypeStruct((half, rows, wide), bf16),
            jax.ShapeDtypeStruct(last_shape, bf16 if last else f32),
        ],
        compiler_params=pltpu.CompilerParams(vmem_limit_bytes=62 * 1024 * 1024),
        cost_estimate=pl.CostEstimate(
            flops=blocks * LOCAL_EXPERTS * 9 * 2 * rows * width * hidden,
            bytes_accessed=blocks * rows * width * 8 + 36 * width * hidden,
            transcendentals=blocks * LOCAL_EXPERTS * rows * hidden,
        ),
        name="experts",
    )(first, *operands)


TILE = 256
PAIR = 2 * HEAD_DIM


def columns_at(index, size):
    return pl.ds(pl.multiple_of(index * size, size), size)


def swap_halves(values):
    width, half_dim = values.shape[1], HEAD_DIM // 2
    lane = lax.broadcasted_iota(jnp.int32, values.shape, 1)
    return jnp.where(
        lane % HEAD_DIM < half_dim,
        pltpu.roll(values, width - half_dim, 1),
        pltpu.roll(values, half_dim, 1),
    )


def row_scale_of(values):
    return lax.rsqrt(jnp.mean(values * values, axis=1, keepdims=True) + norm_eps)


def scores_of(keys, queries, length, first_query):
    scores = attention_scale * dot_turned(keys, queries)
    key_at = lax.broadcasted_iota(jnp.int32, scores.shape, 0)
    query_at = lax.broadcasted_iota(jnp.int32, scores.shape, 1) + first_query
    return jnp.where((key_at <= query_at) & (key_at < length), scores, masked_value)


def head_of(block, index):
    return block[:, index * HEAD_DIM : (index + 1) * HEAD_DIM]


def forward_kernel(
    length_ref, tokens_ref, routes_ref, cosine_ref, sine_ref, gains_ref, weight_ref,
    packet_ref, middle_ref, rotated_ref, mixed_ref, log_ref, share_ref, normed_ref,
):
    rows, width = tokens_ref.shape
    head_columns, kv_columns = HEADS * HEAD_DIM, KV_HEADS * HEAD_DIM
    at_value = head_columns + kv_columns
    at_output = at_value + kv_columns
    at_extra = at_output + head_columns
    length = length_ref[0]
    group = HEADS // KV_HEADS

    inputs = tokens_ref[...].astype(f32)
    normed_ref[...] = (inputs * row_scale_of(inputs) * gains_ref[0:1, :]).astype(bf16)

    def project_turned(c, carry):
        where = columns_at(c, TILE)
        value = dot(normed_ref[...], weight_ref[:, where])
        value = value * cosine_ref[...] + swap_halves(value) * sine_ref[...]
        rotated_ref[:, where] = value.astype(bf16)
        return carry

    def project(c, carry):
        where = columns_at(c, TILE)
        rotated_ref[:, where] = dot(normed_ref[...], weight_ref[:, where]).astype(bf16)
        return carry

    lax.fori_loop(0, at_value // TILE, project_turned, 0)
    lax.fori_loop(at_value // TILE, at_output // TILE, project, 0)

    block = rows // 2

    def attend(j, carry):
        queries = rotated_ref[:, columns_at(j, group * PAIR)]
        keys = rotated_ref[:, columns_at(j + head_columns // PAIR, PAIR)]
        values_turned = rotated_ref[:, columns_at(j + at_value // PAIR, PAIR)].T
        outs = []
        for head in range(2 * group):
            kv = head // group
            key, query = head_of(keys, kv), head_of(queries, head)
            value = values_turned[kv * HEAD_DIM : (kv + 1) * HEAD_DIM]
            parts, logs = [], []
            for b in range(2):
                reach = (b + 1) * block
                scores = scores_of(key[:reach], query[b * block : reach], length, b * block)
                best = jnp.max(scores, axis=0, keepdims=True)
                exponent = jnp.exp(scores - best)
                total = jnp.sum(exponent, axis=0, keepdims=True)
                chance = (exponent * (1.0 / total)).astype(bf16)
                parts.append(dot(value[:, :reach], chance))
                logs.append(best + jnp.log(total))
            outs.append(jnp.concatenate(parts, axis=1))
            log_ref[j, head : head + 1, :] = jnp.concatenate(logs, axis=1)
        mixed_ref[:, columns_at(j, group * PAIR)] = jnp.concatenate(outs, axis=0).T.astype(bf16)
        return carry

    lax.fori_loop(0, KV_HEADS // 2, attend, 0)

    def mix(c, carry):
        where = columns_at(c, TILE)
        branch = dot_turned(mixed_ref[...], weight_ref[where, at_output:at_extra])
        middle_ref[:, where] = tokens_ref[:, where].astype(f32) + residual_scale * branch
        return carry

    lax.fori_loop(0, width // TILE, mix, 0)
    middle = middle_ref[...]
    normed_two = (middle * row_scale_of(middle) * gains_ref[1:2, :]).astype(bf16)
    packet_ref[:, :width] = normed_two
    logits = dot(normed_two, weight_ref[:, at_extra:])
    lane = lax.broadcasted_iota(jnp.int32, logits.shape, 1)
    routed = lane == routes_ref[:, 0:1]
    for k in range(1, routes_ref.shape[1]):
        routed = routed | (lane == routes_ref[:, k : k + 1])
    best = jnp.max(jnp.where(routed, logits, masked_value), axis=1, keepdims=True)
    weights = jnp.where(routed, jnp.exp(jnp.where(routed, logits, best) - best), 0.0)
    shares = weights / jnp.sum(weights, axis=1, keepdims=True)
    share_ref[...] = shares
    high = shares.astype(bf16).astype(f32)
    packet_ref[:, width:] = (high + pltpu.roll(shares - high, EXPERTS, 1)).astype(bf16)


def column_of(row, lanes):
    return jnp.broadcast_to(row, (lanes, row.shape[1])).T


def middle_kernel(
    joined_ref, near_top_ref, near_low_ref, far_top_ref, far_low_ref, packet_ref, middle_ref,
    cotangent_ref, share_ref, gains_ref, mixed_ref, output_ref, extra_ref,
    middle_grad_ref, mixed_grad_ref, pack_ref, back_ref, branch_ref, turned_ref,
):
    rows, width = cotangent_ref.shape
    half = rows // 2
    back_ref[:half] = joined_ref[:half] + near_top_ref[...].astype(f32) + far_top_ref[...].astype(f32)
    back_ref[half:] = joined_ref[half:] + near_low_ref[...].astype(f32) + far_low_ref[...].astype(f32)
    shares = share_ref[...]
    share_grad = back_ref[:, width:]
    share_grad = share_grad + pltpu.roll(share_grad, EXTRA - EXPERTS, 1)
    weighted_mean = jnp.sum(shares * share_grad, axis=1, keepdims=True)
    logit_grad = (shares * (share_grad - weighted_mean)).astype(bf16)
    normed_grad = back_ref[:, :width] + dot_turned(logit_grad, extra_ref[...])
    middle = middle_ref[...]
    scale = row_scale_of(middle)
    scaled = middle * scale
    gain_grad = jnp.sum(normed_grad * scaled, axis=0, keepdims=True)
    weighted = normed_grad * gains_ref[1:2, :]
    correction = jnp.mean(weighted * middle, axis=1, keepdims=True)
    middle_grad = cotangent_ref[...].astype(f32) + scale * weighted - scaled * (scale * scale * correction)
    middle_grad_ref[...] = middle_grad
    branch_ref[...] = (residual_scale * middle_grad).astype(bf16)
    router_grad = dot(packet_ref[:, :width].T, logit_grad)
    lane = lax.broadcasted_iota(jnp.int32, router_grad.shape, 1)
    pack_ref[:, width:] = jnp.where(
        lane == EXPERTS, column_of(gain_grad, EXTRA), router_grad
    ).astype(bf16)
    turned_ref[...] = branch_ref[...].T

    def step(c, carry):
        where = columns_at(c, TILE)
        pack_ref[:, where] = dot(turned_ref[...], mixed_ref[:, where]).astype(bf16)
        mixed_grad_ref[:, where] = dot(branch_ref[...], output_ref[:, where]).astype(bf16)
        return carry

    lax.fori_loop(0, output_ref.shape[1] // TILE, step, 0)


def attention_back_kernel(
    length_ref, rotated_ref, mixed_grad_ref, log_ref, cosine_ref, sine_ref, grad_ref
):
    rows = rotated_ref.shape[0]
    head_columns, kv_columns = HEADS * HEAD_DIM, KV_HEADS * HEAD_DIM
    at_value = head_columns + kv_columns
    length = length_ref[0]
    group = HEADS // KV_HEADS
    block = rows // 2

    def attend(j, carry):
        wide = columns_at(j, group * PAIR)
        key_place = columns_at(j + head_columns // PAIR, PAIR)
        value_place = columns_at(j + at_value // PAIR, PAIR)
        queries, grads = rotated_ref[:, wide], mixed_grad_ref[:, wide]
        keys, values = rotated_ref[:, key_place], rotated_ref[:, value_place]
        keys_turned = keys.T
        query_grads, key_grads, value_grads = [], [], []
        for kv in range(2):
            key, value = head_of(keys, kv), head_of(values, kv)
            key_turned = keys_turned[kv * HEAD_DIM : (kv + 1) * HEAD_DIM]
            key_sums, value_sums = [], []
            for member in range(group):
                head = kv * group + member
                query, grad = head_of(queries, head), head_of(grads, head)
                query_parts = []
                for b in range(2):
                    reach = (b + 1) * block
                    query_block, grad_block = query[b * block : reach], grad[b * block : reach]
                    scores = scores_of(key[:reach], query_block, length, b * block)
                    chance = jnp.exp(scores - log_ref[j, head : head + 1, b * block : reach])
                    chance_grad = dot_turned(value[:reach], grad_block)
                    delta = jnp.sum(chance * chance_grad, axis=0, keepdims=True)
                    score_grad = (attention_scale * chance * (chance_grad - delta)).astype(bf16)
                    value_sums.append(dot(chance.astype(bf16), grad_block))
                    key_sums.append(dot(score_grad, query_block))
                    query_parts.append(dot(key_turned[:, :reach], score_grad))
                query_grads.append(jnp.concatenate(query_parts, axis=1))
            for sums, into in ((key_sums, key_grads), (value_sums, value_grads)):
                short = sum(sums[2::2], sums[0])
                long = sum(sums[3::2], sums[1])
                into.append(jnp.concatenate([short + long[:block], long[block:]], axis=0))
        query_grad = jnp.concatenate(query_grads, axis=0).T
        query_grad = query_grad * cosine_ref[...] - swap_halves(query_grad) * sine_ref[...]
        grad_ref[:, wide] = query_grad.astype(bf16)
        key_grad = jnp.concatenate(key_grads, axis=1)
        key_grad = key_grad * cosine_ref[:, :PAIR] - swap_halves(key_grad) * sine_ref[:, :PAIR]
        grad_ref[:, key_place] = key_grad.astype(bf16)
        grad_ref[:, value_place] = jnp.concatenate(value_grads, axis=1).astype(bf16)
        return carry

    lax.fori_loop(0, KV_HEADS // 2, attend, 0)


def inputs_kernel(
    tokens_ref, gains_ref, projected_ref, weight_ref, middle_grad_ref,
    grad_ref, pack_ref, normed_grad_ref, turned_ref,
):
    width = tokens_ref.shape[1]
    projections = projected_ref.shape[1]
    inputs = tokens_ref[...].astype(f32)
    scale = row_scale_of(inputs)
    scaled = inputs * scale
    turned_ref[...] = (scaled * gains_ref[0:1, :]).astype(bf16).T

    def to_weight(c, carry):
        where = columns_at(c, TILE)
        pack_ref[:, where] = dot(turned_ref[...], projected_ref[:, where]).astype(bf16)
        return carry

    def to_input(c, carry):
        where = columns_at(c, TILE)
        normed_grad_ref[:, where] = dot_turned(projected_ref[...], weight_ref[where, :])
        return carry

    lax.fori_loop(0, projections // TILE, to_weight, 0)
    lax.fori_loop(0, width // TILE, to_input, 0)
    normed_grad = normed_grad_ref[...]
    gain_grad = column_of(jnp.sum(normed_grad * scaled, axis=0, keepdims=True), EXTRA)
    lane = lax.broadcasted_iota(jnp.int32, gain_grad.shape, 1)
    pack_ref[:, projections:] = jnp.where(lane == 0, gain_grad, 0.0).astype(bf16)
    weighted = normed_grad * gains_ref[0:1, :]
    correction = jnp.mean(weighted * inputs, axis=1, keepdims=True)
    grad_ref[...] = middle_grad_ref[...] + scale * weighted - scaled * (scale * scale * correction)


def call_kernel(body, name, operands, out_shape, scratch, flops):
    specs, arrays = [], []
    for operand in operands:
        array, shape, index = operand
        if shape == "scalar":
            specs.append(pl.BlockSpec(memory_space=pltpu.SMEM))
        else:
            shape = array.shape if shape is None else shape
            index = (0,) * len(shape) if index is None else index
            specs.append(pl.BlockSpec(shape, lambda i, index=index: index))
        arrays.append(array)
    outs = [jax.ShapeDtypeStruct(shape, dtype) for shape, dtype in out_shape]
    return pl.pallas_call(
        body,
        grid=(1,),
        in_specs=specs,
        out_specs=[
            pl.BlockSpec(out.shape, lambda i, rank=len(out.shape): (0,) * rank) for out in outs
        ],
        out_shape=outs,
        scratch_shapes=[pltpu.VMEM(shape, dtype) for shape, dtype in scratch],
        compiler_params=pltpu.CompilerParams(vmem_limit_bytes=62 * 1024 * 1024),
        cost_estimate=pl.CostEstimate(
            flops=flops,
            bytes_accessed=sum(a.size * a.dtype.itemsize for a in arrays)
            + sum(o.size * o.dtype.itemsize for o in outs),
            transcendentals=0,
        ),
        name=name,
    )(*arrays)


def rope_lanes(row_count):
    cosine_table, sine_table = rope_tables(row_count)
    half_dim = HEAD_DIM // 2
    signed = jnp.concatenate([-sine_table[:, :half_dim], sine_table[:, half_dim:]], axis=1)
    repeats = TILE // HEAD_DIM
    return jnp.tile(cosine_table, (1, repeats)), jnp.tile(signed, (1, repeats))


def attention_forward(tokens, lengths, routes, tables, gains, whole):
    rows, width = tokens.shape
    head_columns, kv_columns = HEADS * HEAD_DIM, KV_HEADS * HEAD_DIM
    return call_kernel(
        forward_kernel,
        "attention_forward",
        [
            (lengths, "scalar", None), (tokens, None, None), (routes, None, None),
            (tables[0], None, None), (tables[1], None, None), (gains, None, None),
            (whole, None, None),
        ],
        [
            ((rows, width + EXTRA), bf16), ((rows, width), f32),
            ((rows, head_columns + 2 * kv_columns), bf16), ((rows, head_columns), bf16),
            ((KV_HEADS // 2, 2 * HEADS // KV_HEADS, rows), f32), ((rows, EXTRA), f32),
        ],
        [((rows, width), bf16)],
        8 * rows * width * head_columns,
    )


def middle_back(joined, pieces, packet, middle, cotangent, shares, gains, mixed, whole):
    rows, width = cotangent.shape
    head_columns, kv_columns = HEADS * HEAD_DIM, KV_HEADS * HEAD_DIM
    at_output = head_columns + 2 * kv_columns
    return call_kernel(
        middle_kernel,
        "middle_back",
        [(a, None, None) for a in (joined, *pieces, packet, middle, cotangent, shares, gains, mixed)]
        + [
            (whole, (width, head_columns), (0, at_output // head_columns)),
            (whole, (width, EXTRA), (0, (at_output + head_columns) // EXTRA)),
        ],
        [((rows, width), f32), ((rows, head_columns), bf16), ((width, head_columns + EXTRA), bf16)],
        [((rows, width + EXTRA), f32), ((rows, width), bf16), ((width, rows), bf16)],
        4 * rows * width * head_columns,
    )


def attention_back(lengths, rotated, mixed_grad, logs, tables):
    return call_kernel(
        attention_back_kernel,
        "attention_back",
        [
            (lengths, "scalar", None), (rotated, None, None), (mixed_grad, None, None),
            (logs, None, None), (tables[0], None, None), (tables[1], None, None),
        ],
        [(rotated.shape, bf16)],
        [],
        10 * rotated.shape[0] ** 2 * HEADS * HEAD_DIM,
    )[0]


def inputs_back(tokens, gains, projected_grad, whole, middle_grad):
    rows, width = tokens.shape
    projections = projected_grad.shape[1]
    return call_kernel(
        inputs_kernel,
        "inputs_back",
        [
            (tokens, None, None), (gains, None, None), (projected_grad, None, None),
            (whole, (width, projections), (0, 0)), (middle_grad, None, None),
        ],
        [((rows, width), f32), ((width, projections + EXTRA), bf16)],
        [((rows, width), f32), ((width, rows), bf16)],
        4 * rows * width * projections,
    )


def local(
    tokens,
    lengths,
    routes,
    attention_gain,
    query_weight,
    key_weight,
    value_weight,
    output_weight,
    expert_gain,
    router_weight,
    gate_weight,
    up_weight,
    down_weight,
    cotangent,
    *,
    count,
):
    links = Exchange(count)
    member, group, groups = links.member, links.group, links.groups
    row_count, width = tokens.shape
    shard = query_weight.shape[0]
    hidden = gate_weight.shape[2]
    head_columns, kv_columns = HEADS * HEAD_DIM, KV_HEADS * HEAD_DIM

    mine = jnp.stack([gate_weight, up_weight, down_weight.transpose(0, 2, 1)], axis=1)
    mine = mine.reshape(MEMBERS, LOCAL_EXPERTS, 3, shard, hidden)
    shelf = links.send_parts(mine).transpose(1, 2, 0, 3, 4)
    shelf = shelf.reshape(LOCAL_EXPERTS, 3, MEMBERS * shard, hidden)
    lines = [[m + MEMBERS * g for g in range(groups)] for m in range(MEMBERS)]
    expert_full = lax.all_gather(shelf, "fsdp", axis_index_groups=lines)

    packed = jnp.concatenate(
        [
            query_weight,
            key_weight,
            value_weight,
            output_weight.T,
            router_weight,
            attention_gain[:, None],
            expert_gain[:, None],
            jnp.zeros((shard, EXTRA - EXPERTS - 2), bf16),
        ],
        axis=1,
    )
    pack_width = packed.shape[1]
    column = links.direct_gather(packed).reshape(groups * shard, pack_width)
    spread = links.chips_gather(column)
    spread[0] = (column,)
    whole = jnp.zeros((groups, MEMBERS, shard, pack_width), bf16)
    for k in range(MEMBERS):
        parts = spread[k & 6]
        if k & 1:
            parts = [links.swap(part, 1) for part in parts]
        part = jnp.concatenate(parts, axis=0).reshape(groups, shard, pack_width)
        whole = lax.dynamic_update_index_in_dim(whole, part, member ^ k, 1)
    whole = whole.reshape(width, pack_width)
    at_output = head_columns + 2 * kv_columns
    at_extra = at_output + head_columns
    gains = whole[:, at_extra + EXPERTS : at_extra + EXPERTS + 2].astype(f32).T

    late_cotangent, whole = lax.optimization_barrier((cotangent, whole))
    cotangents = links.chips_gather(late_cotangent)

    tables = rope_lanes(row_count)
    packet, middle, rotated, mixed, logs, shares = attention_forward(
        tokens, lengths, routes, tables, gains, whole
    )
    packets = links.chips_gather(packet)
    packets[0] = (packet,)
    cotangents[0] = (late_cotangent,)

    first = (member * LOCAL_EXPERTS).astype(jnp.int32).reshape(1)
    out_terms, back_terms = {}, {}
    grads = None
    turns = ((0,), (2, 6), (4,))
    for turn in turns:
        stacks = []
        for blocks in (packets, cotangents):
            even = [blocks[k] for k in turn]
            stacks.append(even + [tuple(links.swap(part, 1) for part in parts) for parts in even])
        out_own, out_other, back_own, back_other, grads = run_experts(
            first, stacks[0], stacks[1], expert_full, grads, turn == turns[-1]
        )
        back_join = links.join_cores(back_own, back_other)
        for at, k in enumerate(turn):
            out_terms[k] = (out_own[at], out_other[at])
            back_terms[k] = back_join[at]

    back_pieces = links.chips_reduce_end(links.chips_reduce_begin(back_terms))
    out_join = {k: links.join_cores(*out_terms[k]) for k in (6, 2, 4, 0)}

    shelf_grad = lax.psum_scatter(grads, "fsdp", scatter_dimension=0, axis_index_groups=lines)
    shelf_grad = shelf_grad.reshape(LOCAL_EXPERTS, 3, MEMBERS, shard, hidden)
    expert_shards = links.send_parts(shelf_grad.transpose(2, 0, 1, 3, 4)).astype(f32)
    expert_shards = expert_shards.reshape(EXPERTS, 3, shard, hidden)

    def pack_begin(pack):
        columns = pack.shape[1]
        pack = pack.reshape(groups, MEMBERS // 2, 2, shard, columns)
        core, chip = member % 2, member // 2
        own = lax.dynamic_index_in_dim(pack, core, 2, keepdims=False)
        other = lax.dynamic_index_in_dim(pack, 1 - core, 2, keepdims=False)
        joined = links.join_cores(own, other)
        return {
            2 * bits: lax.dynamic_index_in_dim(joined, chip ^ bits, 1, keepdims=False).reshape(
                groups * shard, columns
            )
            for bits in range(MEMBERS // 2)
        }

    def pack_end(terms):
        total = links.chips_reduce(terms)
        return links.direct_reduce(total.reshape(groups, shard, total.shape[1]))

    middle_grad, mixed_grad, first_pack = middle_back(
        back_terms[0], back_pieces, packet, middle, cotangent, shares, gains, mixed, whole
    )
    out_join, middle_grad = lax.optimization_barrier((out_join, middle_grad))
    out_begun = links.chips_reduce_begin(out_join)
    projected_grad = attention_back(lengths, rotated, mixed_grad, logs, tables)
    out_begun, projected_grad = lax.optimization_barrier((out_begun, projected_grad))
    out_pieces = links.chips_reduce_end(out_begun)
    first_terms = pack_begin(first_pack)
    grad_tokens, second_pack = inputs_back(tokens, gains, projected_grad, whole, middle_grad)
    second_terms = pack_begin(second_pack)
    first_total = pack_end(first_terms)
    second_total = pack_end(second_terms)
    layer_out = (middle + links.add_pieces(out_join[0], out_pieces)).astype(bf16)
    return (
        layer_out,
        grad_tokens,
        second_total[:, at_output],
        second_total[:, :head_columns],
        second_total[:, head_columns : head_columns + kv_columns],
        second_total[:, head_columns + kv_columns : at_output],
        first_total[:, :head_columns].T,
        first_total[:, head_columns + EXPERTS],
        first_total[:, head_columns : head_columns + EXPERTS],
        expert_shards[:, 0],
        expert_shards[:, 1],
        expert_shards[:, 2].transpose(0, 2, 1),
    )


def solution(mesh):
    count = mesh.shape["fsdp"]
    placed = (
        P("fsdp", None),
        P("fsdp"),
        P("fsdp", None),
        P("fsdp"),
        P("fsdp", None),
        P("fsdp", None),
        P("fsdp", None),
        P(None, "fsdp"),
        P("fsdp"),
        P("fsdp", None),
        P(None, "fsdp", None),
        P(None, "fsdp", None),
        P(None, None, "fsdp"),
        P("fsdp", None),
    )

    def body(*args):
        return local(*args, count=count)

    return jax.shard_map(
        body,
        mesh=mesh,
        in_specs=placed,
        out_specs=(
            P("fsdp", None),
            P("fsdp", None),
            P("fsdp"),
            P("fsdp", None),
            P("fsdp", None),
            P("fsdp", None),
            P(None, "fsdp"),
            P("fsdp"),
            P("fsdp", None),
            P(None, "fsdp", None),
            P(None, "fsdp", None),
            P(None, None, "fsdp"),
        ),
        check_vma=False,
    )
```

```python
import functools

import jax
import jax.numpy as jnp
from jax import lax
from jax.experimental import pallas as pl
from jax.experimental.pallas import tpu as pltpu
from jax.sharding import PartitionSpec as P

HEADS = 16
KV_HEADS = 8
HEAD_DIM = 64
EXPERTS = 16
MEMBERS = 8
LOCAL_EXPERTS = EXPERTS // MEMBERS
EXTRA = 128

norm_eps = 1e-06
attention_scale = 0.015625
residual_scale = 0.22
rope_base = 10000.0
masked_value = -1e30
f32 = jnp.float32
bf16 = jnp.bfloat16


def rope_tables(row_count):
    half_dim = HEAD_DIM // 2
    frequency = rope_base ** (-2.0 * jnp.arange(half_dim, dtype=jnp.float32) / HEAD_DIM)
    angles = jnp.arange(row_count, dtype=jnp.float32)[:, None] * frequency[None, :]
    angles = jnp.concatenate([angles, angles], axis=1)
    return (jnp.cos(angles), jnp.sin(angles))


class Exchange:
    def __init__(self, count):
        self.count = count
        self.groups = count // MEMBERS
        index = lax.axis_index("fsdp")
        self.member = index % MEMBERS
        self.group = index // MEMBERS

    def swap(self, value, bits):
        return lax.ppermute(value, "fsdp", [(i, i ^ bits) for i in range(self.count)])

    def direct_gather(self, piece):
        stack = jnp.zeros((self.groups,) + piece.shape, piece.dtype)
        for bits in range(self.groups):
            part = self.swap(piece, bits * MEMBERS) if bits else piece
            stack = lax.dynamic_update_index_in_dim(stack, part, self.group ^ bits, 0)
        return stack

    def direct_reduce(self, terms):
        total = lax.dynamic_index_in_dim(terms, self.group, 0, keepdims=False)
        for bits in range(1, self.groups):
            part = lax.dynamic_index_in_dim(terms, self.group ^ bits, 0, keepdims=False)
            total = total + self.swap(part.astype(bf16), bits * MEMBERS).astype(f32)
        return total

    def chips_gather(self, block):
        near, far = self.swap(block, 2), self.swap(block, 4)
        return {0: (block,), 2: (near,), 4: (far,), 6: self.cross_of(near, far)}

    def cross_of(self, near, far):
        half = near.shape[0] // 2
        return self.swap(near[:half], 4), self.swap(far[half:], 2)

    def send_cross(self, own, other):
        half = own.shape[0] // 2
        top = (own[:half].astype(f32) + other[:half].astype(f32)).astype(bf16)
        low = (own[half:].astype(f32) + other[half:].astype(f32)).astype(bf16)
        return top, low

    def send_sides(self, near, far, cross):
        half = near[0].shape[0] // 2
        cross_top, cross_low = cross
        near_sum = near[0].astype(f32) + near[1].astype(f32)
        far_sum = far[0].astype(f32) + far[1].astype(f32)
        near_all = jnp.concatenate([near_sum[:half], near_sum[half:] + cross_low.astype(f32)], axis=0)
        far_all = jnp.concatenate([far_sum[:half] + cross_top.astype(f32), far_sum[half:]], axis=0)
        return near_all.astype(bf16), far_all.astype(bf16)

    def send_parts(self, parts):
        chips = parts.reshape((MEMBERS // 2, 2) + parts.shape[1:])
        chip, core = self.member // 2, self.member % 2
        arrived = jnp.zeros_like(chips)
        for bits in range(MEMBERS // 2):
            part = lax.dynamic_index_in_dim(chips, chip ^ bits, 0, keepdims=False)
            if bits:
                part = self.swap(part, 2 * bits)
            arrived = lax.dynamic_update_index_in_dim(arrived, part, chip ^ bits, 0)
        kept = lax.dynamic_index_in_dim(arrived, core, 1, keepdims=False)
        other = self.swap(lax.dynamic_index_in_dim(arrived, 1 - core, 1, keepdims=False), 1)
        even = jnp.where(core == 0, kept, other)
        odd = jnp.where(core == 0, other, kept)
        return jnp.stack([even, odd], axis=1).reshape(parts.shape)


def dot(left, right):
    return jnp.dot(left, right, preferred_element_type=f32)


def dot_turned(left, right):
    return lax.dot_general(left, right, (((1,), (1,)), ((), ())), preferred_element_type=f32)


def expert_kernel(first_ref, *refs, layout, experts, fresh, last, carried):
    refs = list(refs)
    packet_parts = [[refs.pop(0) for _ in range(number)] for number in layout]
    cotangent_parts = [[refs.pop(0) for _ in range(number)] for number in layout]
    weight_parts = [refs.pop(0) for _ in experts]
    prior_refs = [None if new else refs.pop(0) for new in fresh]
    carried_out = (refs.pop(0), refs.pop(0)) if carried else None
    carried_back = (refs.pop(0), refs.pop(0)) if carried else None
    out_refs, back_refs = (refs.pop(0), refs.pop(0)), (refs.pop(0), refs.pop(0))
    result_refs = [refs.pop(0) for _ in experts]
    grad_refs = [refs.pop(0) if end else result for end, result in zip(last, result_refs)]
    packet_buffer, cotangent_buffer, weight_ref, packet_turned, cotangent_turned, sums = refs[:6]
    block_sem, weight_sem, prior_sem = refs[6:]
    rows, width = cotangent_buffer.shape[1:]
    groups, _, depth, _ = weight_parts[0].shape
    blocks = len(layout)
    at = pl.program_id(0)
    first = first_ref[0]

    def block_copies(block):
        copies = []
        for kind, (parts, buffer) in enumerate(
            ((packet_parts, packet_buffer), (cotangent_parts, cotangent_buffer))
        ):
            size = rows // layout[block]
            for number, part in enumerate(parts[block]):
                place = buffer.at[block, pl.ds(number * size, size)]
                copies.append(
                    pltpu.make_async_copy(part, place, block_sem.at[block, 2 * kind + number])
                )
        return copies

    def weight_copies(n):
        return [
            pltpu.make_async_copy(
                weight_parts[n].at[g], weight_ref.at[n, :, pl.ds(g * depth, depth)], weight_sem.at[n, g]
            )
            for g in range(groups)
        ]

    def prior_copy(n):
        return pltpu.make_async_copy(prior_refs[n], grad_refs[n], prior_sem.at[n])

    @pl.when(at == 0)
    def _():
        for copy in block_copies(0):
            copy.start()
        for n in range(len(experts)):
            for copy in weight_copies(n):
                copy.start()
        for n, new in enumerate(fresh):
            if new:
                grad_refs[n][...] = jnp.zeros_like(grad_refs[n])
            else:
                prior_copy(n).start()
        for block in range(1, blocks):
            for copy in block_copies(block):
                copy.start()
        for n in range(len(experts)):
            for copy in weight_copies(n):
                copy.wait()

    for block in range(blocks):

        @pl.when(at == block)
        def _():
            for copy in block_copies(block):
                copy.wait()

    lane = lax.broadcasted_iota(jnp.int32, (rows, EXTRA), 1)
    normed = packet_buffer[at, :, :width]
    upstream = cotangent_buffer[at]
    shares = packet_buffer[at, :, width:].astype(f32)
    extra = jnp.zeros((rows, EXTRA), f32)
    packet_turned[...] = normed.T
    cotangent_turned[...] = upstream.T
    begun = []
    for n in range(len(experts)):
        begun.append(
            (
                dot(normed, weight_ref[n, 0]),
                dot(normed, weight_ref[n, 1]),
                dot(upstream, weight_ref[n, 2]),
            )
        )
    if not all(fresh):

        @pl.when(at == 0)
        def _():
            for n, new in enumerate(fresh):
                if not new:
                    prior_copy(n).wait()

    for n, local in enumerate(experts):
        gate_pre, up_pre, inner_raw = begun[n]
        expert = first + local
        is_high, is_low = lane == expert, lane == expert + EXPERTS
        share = jnp.sum(jnp.where(is_high | is_low, shares, 0.0), axis=1, keepdims=True)
        sigmoid_gate = jax.nn.sigmoid(gate_pre)
        activated = gate_pre * sigmoid_gate
        inner = (activated * up_pre).astype(bf16).astype(f32)
        share_grad = residual_scale * jnp.sum(inner * inner_raw, axis=1, keepdims=True)
        scaled = share * residual_scale
        inner_grad = inner_raw * scaled
        gate_grad = (
            inner_grad * up_pre * (sigmoid_gate + activated * (1.0 - sigmoid_gate))
        ).astype(bf16)
        up_grad = (inner_grad * activated).astype(bf16)
        inner_shared = (inner * scaled).astype(bf16)
        out_term = dot_turned(inner_shared, weight_ref[n, 2])
        back_term = dot_turned(gate_grad, weight_ref[n, 0]) + dot_turned(up_grad, weight_ref[n, 1])
        if n == 0:
            sums[0], sums[1] = out_term, back_term
        else:
            sums[0] += out_term
            sums[1] += back_term
        grad_refs[n][0] += dot(packet_turned[...], gate_grad)
        grad_refs[n][1] += dot(packet_turned[...], up_grad)
        grad_refs[n][2] += dot(cotangent_turned[...], inner_shared)
        high = share_grad.astype(bf16).astype(f32)
        extra = extra + jnp.where(is_high, high, 0.0) + jnp.where(is_low, share_grad - high, 0.0)
    for side in range(2):

        @pl.when((at < blocks // 2) == (side == 0))
        def _():
            out_total, back_total, extra_total = sums[0], sums[1], extra
            if carried:
                out_total = out_total + carried_out[side][0].astype(f32)
                back_total = back_total + carried_back[side][0, :, :width].astype(f32)
                extra_total = extra_total + carried_back[side][0, :, width:].astype(f32)
            out_refs[side][0] = out_total.astype(bf16)
            back_refs[side][0, :, :width] = back_total.astype(bf16)
            back_refs[side][0, :, width:] = extra_total.astype(bf16)

    if any(last):

        @pl.when(at == blocks - 1)
        def _():
            for n, end in enumerate(last):
                if end:
                    for g in range(groups):
                        result_refs[n][g] = grad_refs[n][:, pl.ds(g * depth, depth)].astype(bf16)


def run_experts(first, packets, cotangents, experts, weights, priors, last, carried=None):
    layout = tuple(len(parts) for parts in packets)
    blocks = len(layout)
    rows = sum(part.shape[0] for part in packets[0])
    wide, width = packets[0][0].shape[1], cotangents[0][0].shape[1]
    groups, _, depth, hidden = weights[0].shape
    grad_shape = (3, width, hidden)
    fresh = tuple(prior is None for prior in priors)
    operands = [part for parts in packets for part in parts]
    operands += [part for parts in cotangents for part in parts]
    operands += list(weights) + [prior for prior in priors if prior is not None]
    half = blocks // 2

    def own_side(i, s):
        return (jnp.minimum(i, half - 1), 0, 0)

    def other_side(i, s):
        return (jnp.maximum(i - half, 0), 0, 0)

    def whole(shape):
        return pl.BlockSpec(
            shape, lambda i, s, rank=len(shape): (0,) * rank, pipeline_mode=pl.Buffered(1)
        )

    term_specs = [
        pl.BlockSpec((1, rows, columns), side)
        for columns in (width, wide)
        for side in (own_side, other_side)
    ]
    in_specs = [pl.BlockSpec(memory_space=pl.ANY)] * len(operands)
    if carried is not None:
        in_specs += term_specs
        operands += list(carried)
    grads = [((groups, 3, depth, hidden), bf16) if end else (grad_shape, f32) for end in last]
    scratch = [pltpu.VMEM(grad_shape, f32) for end in last if end]
    scratch += [
        pltpu.VMEM((blocks, rows, wide), bf16),
        pltpu.VMEM((blocks, rows, width), bf16),
        pltpu.VMEM((len(experts),) + grad_shape, bf16),
        pltpu.VMEM((width, rows), bf16),
        pltpu.VMEM((width, rows), bf16),
        pltpu.VMEM((2, rows, width), f32),
        pltpu.SemaphoreType.DMA((blocks, 4)),
        pltpu.SemaphoreType.DMA((len(experts), groups)),
        pltpu.SemaphoreType.DMA((len(experts),)),
    ]
    return pl.pallas_call(
        functools.partial(
            expert_kernel, layout=layout, experts=experts, fresh=fresh, last=last,
            carried=carried is not None,
        ),
        grid_spec=pltpu.PrefetchScalarGridSpec(
            num_scalar_prefetch=1,
            grid=(blocks,),
            in_specs=in_specs,
            out_specs=term_specs + [whole(shape) for shape, _ in grads],
            scratch_shapes=scratch,
        ),
        out_shape=[
            jax.ShapeDtypeStruct((half, rows, columns), bf16)
            for columns in (width, width, wide, wide)
        ]
        + [jax.ShapeDtypeStruct(shape, dtype) for shape, dtype in grads],
        compiler_params=pltpu.CompilerParams(vmem_limit_bytes=62 * 1024 * 1024),
        cost_estimate=pl.CostEstimate(
            flops=blocks * len(experts) * 9 * 2 * rows * width * hidden,
            bytes_accessed=blocks * rows * width * 8 + 18 * len(experts) * width * hidden,
            transcendentals=blocks * len(experts) * rows * hidden,
        ),
        name="experts",
    )(first, *operands)


TILE = 256
PAIR = 2 * HEAD_DIM


def columns_at(index, size):
    return pl.ds(pl.multiple_of(index * size, size), size)


def swap_halves(values):
    width, half_dim = values.shape[1], HEAD_DIM // 2
    lane = lax.broadcasted_iota(jnp.int32, values.shape, 1)
    return jnp.where(
        lane % HEAD_DIM < half_dim,
        pltpu.roll(values, width - half_dim, 1),
        pltpu.roll(values, half_dim, 1),
    )


def row_scale_of(values):
    return lax.rsqrt(jnp.mean(values * values, axis=1, keepdims=True) + norm_eps)


def scores_of(keys, queries, length, first_query):
    scores = attention_scale * dot_turned(keys, queries)
    key_at = lax.broadcasted_iota(jnp.int32, scores.shape, 0)
    query_at = lax.broadcasted_iota(jnp.int32, scores.shape, 1) + first_query
    return jnp.where((key_at <= query_at) & (key_at < length), scores, masked_value)


def head_of(block, index):
    return block[:, index * HEAD_DIM : (index + 1) * HEAD_DIM]


def forward_kernel(
    length_ref, tokens_ref, routes_ref, cosine_ref, sine_ref, gains_ref, weight_ref,
    packet_ref, middle_ref, rotated_ref, mixed_ref, log_ref, share_ref, normed_ref,
):
    rows, width = tokens_ref.shape
    head_columns, kv_columns = HEADS * HEAD_DIM, KV_HEADS * HEAD_DIM
    at_value = head_columns + kv_columns
    at_output = at_value + kv_columns
    at_extra = at_output + head_columns
    length = length_ref[0]
    group = HEADS // KV_HEADS

    inputs = tokens_ref[...].astype(f32)
    normed_ref[...] = (inputs * row_scale_of(inputs) * gains_ref[0:1, :]).astype(bf16)

    def project_turned(c, carry):
        where = columns_at(c, TILE)
        value = dot(normed_ref[...], weight_ref[:, where])
        value = value * cosine_ref[...] + swap_halves(value) * sine_ref[...]
        rotated_ref[:, where] = value.astype(bf16)
        return carry

    def project(c, carry):
        where = columns_at(c, TILE)
        rotated_ref[:, where] = dot(normed_ref[...], weight_ref[:, where]).astype(bf16)
        return carry

    lax.fori_loop(0, at_value // TILE, project_turned, 0)
    lax.fori_loop(at_value // TILE, at_output // TILE, project, 0)

    block = rows // 2

    def attend(j, carry):
        queries = rotated_ref[:, columns_at(j, group * PAIR)]
        keys = rotated_ref[:, columns_at(j + head_columns // PAIR, PAIR)]
        values_turned = rotated_ref[:, columns_at(j + at_value // PAIR, PAIR)].T
        outs = []
        for head in range(2 * group):
            kv = head // group
            key, query = head_of(keys, kv), head_of(queries, head)
            value = values_turned[kv * HEAD_DIM : (kv + 1) * HEAD_DIM]
            parts, logs = [], []
            for b in range(2):
                reach = (b + 1) * block
                scores = scores_of(key[:reach], query[b * block : reach], length, b * block)
                best = jnp.max(scores, axis=0, keepdims=True)
                exponent = jnp.exp(scores - best)
                total = jnp.sum(exponent, axis=0, keepdims=True)
                chance = (exponent * (1.0 / total)).astype(bf16)
                parts.append(dot(value[:, :reach], chance))
                logs.append(best + jnp.log(total))
            outs.append(jnp.concatenate(parts, axis=1))
            log_ref[j, head : head + 1, :] = jnp.concatenate(logs, axis=1)
        mixed_ref[:, columns_at(j, group * PAIR)] = jnp.concatenate(outs, axis=0).T.astype(bf16)
        return carry

    lax.fori_loop(0, KV_HEADS // 2, attend, 0)

    def mix(c, carry):
        where = columns_at(c, TILE)
        branch = dot_turned(mixed_ref[...], weight_ref[where, at_output:at_extra])
        middle_ref[:, where] = tokens_ref[:, where].astype(f32) + residual_scale * branch
        return carry

    lax.fori_loop(0, width // TILE, mix, 0)
    middle = middle_ref[...]
    normed_two = (middle * row_scale_of(middle) * gains_ref[1:2, :]).astype(bf16)
    packet_ref[:, :width] = normed_two
    logits = dot(normed_two, weight_ref[:, at_extra:])
    lane = lax.broadcasted_iota(jnp.int32, logits.shape, 1)
    routed = lane == routes_ref[:, 0:1]
    for k in range(1, routes_ref.shape[1]):
        routed = routed | (lane == routes_ref[:, k : k + 1])
    best = jnp.max(jnp.where(routed, logits, masked_value), axis=1, keepdims=True)
    weights = jnp.where(routed, jnp.exp(jnp.where(routed, logits, best) - best), 0.0)
    shares = weights / jnp.sum(weights, axis=1, keepdims=True)
    share_ref[...] = shares
    high = shares.astype(bf16).astype(f32)
    packet_ref[:, width:] = (high + pltpu.roll(shares - high, EXPERTS, 1)).astype(bf16)


def column_of(row, lanes):
    return jnp.broadcast_to(row, (lanes, row.shape[1])).T


def middle_kernel(
    own_ref, other_ref, near_ref, far_ref, packet_ref, middle_ref, cotangent_ref, share_ref, gains_ref, mixed_ref, output_ref, extra_ref,
    middle_grad_ref, mixed_grad_ref, pack_ref, back_ref, branch_ref, turned_ref,
):
    width = cotangent_ref.shape[1]
    back_ref[...] = (own_ref[...].astype(f32) + other_ref[...].astype(f32)) + (
        near_ref[...].astype(f32) + far_ref[...].astype(f32)
    )
    shares = share_ref[...]
    share_grad = back_ref[:, width:]
    share_grad = share_grad + pltpu.roll(share_grad, EXTRA - EXPERTS, 1)
    weighted_mean = jnp.sum(shares * share_grad, axis=1, keepdims=True)
    logit_grad = (shares * (share_grad - weighted_mean)).astype(bf16)
    normed_grad = back_ref[:, :width] + dot_turned(logit_grad, extra_ref[...])
    middle = middle_ref[...]
    scale = row_scale_of(middle)
    scaled = middle * scale
    gain_grad = jnp.sum(normed_grad * scaled, axis=0, keepdims=True)
    weighted = normed_grad * gains_ref[1:2, :]
    correction = jnp.mean(weighted * middle, axis=1, keepdims=True)
    middle_grad = cotangent_ref[...].astype(f32) + scale * weighted - scaled * (scale * scale * correction)
    middle_grad_ref[...] = middle_grad
    branch_ref[...] = (residual_scale * middle_grad).astype(bf16)
    router_grad = dot(packet_ref[:, :width].T, logit_grad)
    lane = lax.broadcasted_iota(jnp.int32, router_grad.shape, 1)
    pack_ref[:, width:] = jnp.where(
        lane == EXPERTS, column_of(gain_grad, EXTRA), router_grad
    ).astype(bf16)
    turned_ref[...] = branch_ref[...].T

    def step(c, carry):
        where = columns_at(c, TILE)
        pack_ref[:, where] = dot(turned_ref[...], mixed_ref[:, where]).astype(bf16)
        mixed_grad_ref[:, where] = dot(branch_ref[...], output_ref[:, where]).astype(bf16)
        return carry

    lax.fori_loop(0, output_ref.shape[1] // TILE, step, 0)


def attention_back_kernel(
    length_ref, rotated_ref, mixed_grad_ref, log_ref, cosine_ref, sine_ref, grad_ref
):
    rows = rotated_ref.shape[0]
    head_columns, kv_columns = HEADS * HEAD_DIM, KV_HEADS * HEAD_DIM
    at_value = head_columns + kv_columns
    length = length_ref[0]
    group = HEADS // KV_HEADS
    block = rows // 2

    def attend(j, carry):
        wide = columns_at(j, group * PAIR)
        key_place = columns_at(j + head_columns // PAIR, PAIR)
        value_place = columns_at(j + at_value // PAIR, PAIR)
        queries, grads = rotated_ref[:, wide], mixed_grad_ref[:, wide]
        keys, values = rotated_ref[:, key_place], rotated_ref[:, value_place]
        keys_turned = keys.T
        query_grads, key_grads, value_grads = [], [], []
        for kv in range(2):
            key, value = head_of(keys, kv), head_of(values, kv)
            key_turned = keys_turned[kv * HEAD_DIM : (kv + 1) * HEAD_DIM]
            key_sums, value_sums = [], []
            for member in range(group):
                head = kv * group + member
                query, grad = head_of(queries, head), head_of(grads, head)
                query_parts = []
                for b in range(2):
                    reach = (b + 1) * block
                    query_block, grad_block = query[b * block : reach], grad[b * block : reach]
                    scores = scores_of(key[:reach], query_block, length, b * block)
                    chance = jnp.exp(scores - log_ref[j, head : head + 1, b * block : reach])
                    chance_grad = dot_turned(value[:reach], grad_block)
                    delta = jnp.sum(chance * chance_grad, axis=0, keepdims=True)
                    score_grad = (attention_scale * chance * (chance_grad - delta)).astype(bf16)
                    value_sums.append(dot(chance.astype(bf16), grad_block))
                    key_sums.append(dot(score_grad, query_block))
                    query_parts.append(dot(key_turned[:, :reach], score_grad))
                query_grads.append(jnp.concatenate(query_parts, axis=1))
            for sums, into in ((key_sums, key_grads), (value_sums, value_grads)):
                short = sum(sums[2::2], sums[0])
                long = sum(sums[3::2], sums[1])
                into.append(jnp.concatenate([short + long[:block], long[block:]], axis=0))
        query_grad = jnp.concatenate(query_grads, axis=0).T
        query_grad = query_grad * cosine_ref[...] - swap_halves(query_grad) * sine_ref[...]
        grad_ref[:, wide] = query_grad.astype(bf16)
        key_grad = jnp.concatenate(key_grads, axis=1)
        key_grad = key_grad * cosine_ref[:, :PAIR] - swap_halves(key_grad) * sine_ref[:, :PAIR]
        grad_ref[:, key_place] = key_grad.astype(bf16)
        grad_ref[:, value_place] = jnp.concatenate(value_grads, axis=1).astype(bf16)
        return carry

    lax.fori_loop(0, KV_HEADS // 2, attend, 0)


def inputs_kernel(
    tokens_ref, gains_ref, projected_ref, weight_ref, middle_grad_ref,
    grad_ref, pack_ref, normed_grad_ref, turned_ref,
):
    width = tokens_ref.shape[1]
    projections = projected_ref.shape[1]
    inputs = tokens_ref[...].astype(f32)
    scale = row_scale_of(inputs)
    scaled = inputs * scale
    turned_ref[...] = (scaled * gains_ref[0:1, :]).astype(bf16).T

    def to_weight(c, carry):
        where = columns_at(c, TILE)
        pack_ref[:, where] = dot(turned_ref[...], projected_ref[:, where]).astype(bf16)
        return carry

    def to_input(c, carry):
        where = columns_at(c, TILE)
        normed_grad_ref[:, where] = dot_turned(projected_ref[...], weight_ref[where, :])
        return carry

    lax.fori_loop(0, projections // TILE, to_weight, 0)
    lax.fori_loop(0, width // TILE, to_input, 0)
    normed_grad = normed_grad_ref[...]
    gain_grad = column_of(jnp.sum(normed_grad * scaled, axis=0, keepdims=True), EXTRA)
    lane = lax.broadcasted_iota(jnp.int32, gain_grad.shape, 1)
    pack_ref[:, projections:] = jnp.where(lane == 0, gain_grad, 0.0).astype(bf16)
    weighted = normed_grad * gains_ref[0:1, :]
    correction = jnp.mean(weighted * inputs, axis=1, keepdims=True)
    grad_ref[...] = middle_grad_ref[...] + scale * weighted - scaled * (scale * scale * correction)


def call_kernel(body, name, operands, out_shape, scratch, flops):
    specs, arrays = [], []
    for operand in operands:
        array, shape, index = operand
        if shape == "scalar":
            specs.append(pl.BlockSpec(memory_space=pltpu.SMEM))
        else:
            shape = array.shape if shape is None else shape
            index = (0,) * len(shape) if index is None else index
            specs.append(pl.BlockSpec(shape, lambda i, index=index: index))
        arrays.append(array)
    outs = [jax.ShapeDtypeStruct(shape, dtype) for shape, dtype in out_shape]
    return pl.pallas_call(
        body,
        grid=(1,),
        in_specs=specs,
        out_specs=[
            pl.BlockSpec(out.shape, lambda i, rank=len(out.shape): (0,) * rank) for out in outs
        ],
        out_shape=outs,
        scratch_shapes=[pltpu.VMEM(shape, dtype) for shape, dtype in scratch],
        compiler_params=pltpu.CompilerParams(vmem_limit_bytes=62 * 1024 * 1024),
        cost_estimate=pl.CostEstimate(
            flops=flops,
            bytes_accessed=sum(a.size * a.dtype.itemsize for a in arrays)
            + sum(o.size * o.dtype.itemsize for o in outs),
            transcendentals=0,
        ),
        name=name,
    )(*arrays)


def rope_lanes(row_count):
    cosine_table, sine_table = rope_tables(row_count)
    half_dim = HEAD_DIM // 2
    signed = jnp.concatenate([-sine_table[:, :half_dim], sine_table[:, half_dim:]], axis=1)
    repeats = TILE // HEAD_DIM
    return jnp.tile(cosine_table, (1, repeats)), jnp.tile(signed, (1, repeats))


def attention_forward(tokens, lengths, routes, tables, gains, whole):
    rows, width = tokens.shape
    head_columns, kv_columns = HEADS * HEAD_DIM, KV_HEADS * HEAD_DIM
    return call_kernel(
        forward_kernel,
        "attention_forward",
        [
            (lengths, "scalar", None), (tokens, None, None), (routes, None, None),
            (tables[0], None, None), (tables[1], None, None), (gains, None, None),
            (whole, None, None),
        ],
        [
            ((rows, width + EXTRA), bf16), ((rows, width), f32),
            ((rows, head_columns + 2 * kv_columns), bf16), ((rows, head_columns), bf16),
            ((KV_HEADS // 2, 2 * HEADS // KV_HEADS, rows), f32), ((rows, EXTRA), f32),
        ],
        [((rows, width), bf16)],
        8 * rows * width * head_columns,
    )


def middle_back(pieces, packet, middle, cotangent, shares, gains, mixed, whole):
    rows, width = cotangent.shape
    head_columns, kv_columns = HEADS * HEAD_DIM, KV_HEADS * HEAD_DIM
    at_output = head_columns + 2 * kv_columns
    return call_kernel(
        middle_kernel,
        "middle_back",
        [(a, None, None) for a in (*pieces, packet, middle, cotangent, shares, gains, mixed)]
        + [
            (whole, (width, head_columns), (0, at_output // head_columns)),
            (whole, (width, EXTRA), (0, (at_output + head_columns) // EXTRA)),
        ],
        [((rows, width), f32), ((rows, head_columns), bf16), ((width, head_columns + EXTRA), bf16)],
        [((rows, width + EXTRA), f32), ((rows, width), bf16), ((width, rows), bf16)],
        4 * rows * width * head_columns,
    )


def attention_back(lengths, rotated, mixed_grad, logs, tables):
    return call_kernel(
        attention_back_kernel,
        "attention_back",
        [
            (lengths, "scalar", None), (rotated, None, None), (mixed_grad, None, None),
            (logs, None, None), (tables[0], None, None), (tables[1], None, None),
        ],
        [(rotated.shape, bf16)],
        [],
        10 * rotated.shape[0] ** 2 * HEADS * HEAD_DIM,
    )[0]


def inputs_back(tokens, gains, projected_grad, whole, middle_grad):
    rows, width = tokens.shape
    projections = projected_grad.shape[1]
    return call_kernel(
        inputs_kernel,
        "inputs_back",
        [
            (tokens, None, None), (gains, None, None), (projected_grad, None, None),
            (whole, (width, projections), (0, 0)), (middle_grad, None, None),
        ],
        [((rows, width), f32), ((width, projections + EXTRA), bf16)],
        [((rows, width), f32), ((width, rows), bf16)],
        4 * rows * width * projections,
    )


def local(
    tokens,
    lengths,
    routes,
    attention_gain,
    query_weight,
    key_weight,
    value_weight,
    output_weight,
    expert_gain,
    router_weight,
    gate_weight,
    up_weight,
    down_weight,
    cotangent,
    *,
    count,
):
    links = Exchange(count)
    member, group, groups = links.member, links.group, links.groups
    row_count, width = tokens.shape
    shard = query_weight.shape[0]
    hidden = gate_weight.shape[2]
    head_columns, kv_columns = HEADS * HEAD_DIM, KV_HEADS * HEAD_DIM

    mine = jnp.stack([gate_weight, up_weight, down_weight.transpose(0, 2, 1)], axis=1)
    mine = mine.reshape(MEMBERS, LOCAL_EXPERTS, 3, shard, hidden)
    shelf = links.send_parts(mine).transpose(1, 2, 0, 3, 4)
    shelf = shelf.reshape(LOCAL_EXPERTS, 3, MEMBERS * shard, hidden)
    lines = [[m + MEMBERS * g for g in range(groups)] for m in range(MEMBERS)]
    expert_full = [
        lax.all_gather(shelf[n], "fsdp", axis_index_groups=lines) for n in range(LOCAL_EXPERTS)
    ]

    packed = jnp.concatenate(
        [
            query_weight,
            key_weight,
            value_weight,
            output_weight.T,
            router_weight,
            attention_gain[:, None],
            expert_gain[:, None],
            jnp.zeros((shard, EXTRA - EXPERTS - 2), bf16),
        ],
        axis=1,
    )
    pack_width = packed.shape[1]
    column = links.direct_gather(packed).reshape(groups * shard, pack_width)
    spread = links.chips_gather(column)
    spread[0] = (column,)
    whole = jnp.zeros((groups, MEMBERS, shard, pack_width), bf16)
    for k in range(MEMBERS):
        parts = spread[k & 6]
        if k & 1:
            parts = [links.swap(part, 1) for part in parts]
        part = jnp.concatenate(parts, axis=0).reshape(groups, shard, pack_width)
        whole = lax.dynamic_update_index_in_dim(whole, part, member ^ k, 1)
    whole = whole.reshape(width, pack_width)
    at_output = head_columns + 2 * kv_columns
    at_extra = at_output + head_columns
    gains = whole[:, at_extra + EXPERTS : at_extra + EXPERTS + 2].astype(f32).T

    late_cotangent, whole = lax.optimization_barrier((cotangent, whole))
    cotangents = links.chips_gather(late_cotangent)

    tables = rope_lanes(row_count)
    packet, middle, rotated, mixed, logs, shares = attention_forward(
        tokens, lengths, routes, tables, gains, whole
    )
    packets = links.chips_gather(packet)
    def both(blocks, turn):
        own = [blocks[k] for k in turn]
        return own + [tuple(links.swap(part, 1) for part in parts) for parts in own]

    first = (member * LOCAL_EXPERTS).astype(jnp.int32).reshape(1)
    chip_rows = both(packets, (0,)), both(cotangents, (0,))
    side_rows = both(packets, (2, 4)), both(cotangents, (2, 4))
    cross_rows = both(packets, (6,)), both(cotangents, (6,))
    *chip_terms, zero = run_experts(first, *chip_rows, (0,), expert_full[:1], [None], (False,))
    *side_terms, zero = run_experts(first, *side_rows, (0,), expert_full[:1], [zero], (False,))
    *cross_terms, zero, one = run_experts(
        first, *cross_rows, (0, 1), expert_full, [zero, None], (True, False)
    )

    def reduce_groups(grads):
        return lax.psum_scatter(grads, "fsdp", scatter_dimension=0, axis_index_groups=lines)

    shelf_zero = reduce_groups(zero)
    out_cross = links.send_cross(cross_terms[0][0], links.swap(cross_terms[1], 1)[0])
    back_cross = links.send_cross(cross_terms[2][0], links.swap(cross_terms[3], 1)[0])
    out_cross, back_cross, side_terms = lax.optimization_barrier((out_cross, back_cross, side_terms))
    back_cross = links.swap(back_cross[0], 2), links.swap(back_cross[1], 4)
    out_cross = links.swap(out_cross[0], 2), links.swap(out_cross[1], 4)
    *side_terms, one = run_experts(
        first, *side_rows, (1,), expert_full[1:], [one], (False,), side_terms
    )
    back_other = links.swap(side_terms[3], 1)
    out_other = links.swap(side_terms[1], 1)
    back_near, back_far = links.send_sides(
        (side_terms[2][0], back_other[0]), (side_terms[2][1], back_other[1]), back_cross
    )
    back_near, back_far, chip_terms = lax.optimization_barrier((back_near, back_far, chip_terms))
    back_near, back_far = links.swap(back_near, 2), links.swap(back_far, 4)
    *chip_terms, one = run_experts(
        first, *chip_rows, (1,), expert_full[1:], [one], (True,), chip_terms
    )
    shelf_one = reduce_groups(one)
    back_pieces = (chip_terms[2][0], links.swap(chip_terms[3], 1)[0], back_near, back_far)
    out_near, out_far = links.send_sides(
        (side_terms[0][0], out_other[0]), (side_terms[0][1], out_other[1]), out_cross
    )
    out_near, out_far, back_pieces = lax.optimization_barrier((out_near, out_far, back_pieces))
    out_near, out_far = links.swap(out_near, 2), links.swap(out_far, 4)
    out_pieces = chip_terms[0][0], links.swap(chip_terms[1], 1)[0], out_near, out_far

    core, chip = member % 2, member // 2

    def pack_cores(pack):
        columns = pack.shape[1]
        pack = pack.reshape(groups, MEMBERS // 2, 2, shard, columns)
        own = lax.dynamic_index_in_dim(pack, core, 2, keepdims=False)
        other = links.swap(lax.dynamic_index_in_dim(pack, 1 - core, 2, keepdims=False), 1)

        def part(bits):
            return tuple(
                lax.dynamic_index_in_dim(side, chip ^ bits, 1, keepdims=False).reshape(
                    groups * shard, columns
                )
                for side in (own, other)
            )

        return [part(bits) for bits in range(MEMBERS // 2)]

    def pack_cross(parts):
        top, low = links.send_cross(*parts[3])
        return links.swap(top, 2), links.swap(low, 4)

    def pack_sides(parts, cross):
        near, far = links.send_sides(parts[1], parts[2], cross)
        near, far = links.swap(near, 2), links.swap(far, 4)
        total = (parts[0][0].astype(f32) + parts[0][1].astype(f32)) + (
            near.astype(f32) + far.astype(f32)
        )
        return links.direct_reduce(total.reshape(groups, shard, total.shape[1]))

    middle_grad, mixed_grad, first_pack = middle_back(
        back_pieces, packet, middle, cotangent, shares, gains, mixed, whole
    )
    first_parts = pack_cores(first_pack)
    projected_grad = attention_back(lengths, rotated, mixed_grad, logs, tables)
    first_parts, projected_grad = lax.optimization_barrier((first_parts, projected_grad))
    first_cross = pack_cross(first_parts)
    grad_tokens, second_pack = inputs_back(tokens, gains, projected_grad, whole, middle_grad)
    second_parts = pack_cores(second_pack)
    first_total = pack_sides(first_parts, first_cross)
    second_total = pack_sides(second_parts, pack_cross(second_parts))
    layer_out = (middle + sum(piece.astype(f32) for piece in out_pieces)).astype(bf16)
    shelf_grad = jnp.stack([shelf_zero, shelf_one])
    shelf_grad = shelf_grad.reshape(LOCAL_EXPERTS, 3, MEMBERS, shard, hidden)
    expert_shards = links.send_parts(shelf_grad.transpose(2, 0, 1, 3, 4)).astype(f32)
    expert_shards = expert_shards.reshape(EXPERTS, 3, shard, hidden)
    return (
        layer_out,
        grad_tokens,
        second_total[:, at_output],
        second_total[:, :head_columns],
        second_total[:, head_columns : head_columns + kv_columns],
        second_total[:, head_columns + kv_columns : at_output],
        first_total[:, :head_columns].T,
        first_total[:, head_columns + EXPERTS],
        first_total[:, head_columns : head_columns + EXPERTS],
        expert_shards[:, 0],
        expert_shards[:, 1],
        expert_shards[:, 2].transpose(0, 2, 1),
    )


def solution(mesh):
    count = mesh.shape["fsdp"]
    placed = (
        P("fsdp", None),
        P("fsdp"),
        P("fsdp", None),
        P("fsdp"),
        P("fsdp", None),
        P("fsdp", None),
        P("fsdp", None),
        P(None, "fsdp"),
        P("fsdp"),
        P("fsdp", None),
        P(None, "fsdp", None),
        P(None, "fsdp", None),
        P(None, None, "fsdp"),
        P("fsdp", None),
    )

    def body(*args):
        return local(*args, count=count)

    return jax.shard_map(
        body,
        mesh=mesh,
        in_specs=placed,
        out_specs=(
            P("fsdp", None),
            P("fsdp", None),
            P("fsdp"),
            P("fsdp", None),
            P("fsdp", None),
            P("fsdp", None),
            P(None, "fsdp"),
            P("fsdp"),
            P("fsdp", None),
            P(None, "fsdp", None),
            P(None, "fsdp", None),
            P(None, None, "fsdp"),
        ),
        check_vma=False,
    )
```

```python
import functools

import jax
import jax.numpy as jnp
from jax import lax
from jax.experimental import pallas as pl
from jax.experimental.pallas import tpu as pltpu
from jax.sharding import PartitionSpec as P

HEADS = 16
KV_HEADS = 8
HEAD_DIM = 64
EXPERTS = 16
MEMBERS = 8
LOCAL_EXPERTS = EXPERTS // MEMBERS
EXTRA = 128

norm_eps = 1e-06
attention_scale = 0.015625
residual_scale = 0.22
rope_base = 10000.0
masked_value = -1e30
f32 = jnp.float32
bf16 = jnp.bfloat16


def rope_tables(row_count):
    half_dim = HEAD_DIM // 2
    frequency = rope_base ** (-2.0 * jnp.arange(half_dim, dtype=jnp.float32) / HEAD_DIM)
    angles = jnp.arange(row_count, dtype=jnp.float32)[:, None] * frequency[None, :]
    angles = jnp.concatenate([angles, angles], axis=1)
    return (jnp.cos(angles), jnp.sin(angles))


class Exchange:
    def __init__(self, count):
        self.count = count
        self.groups = count // MEMBERS
        index = lax.axis_index("fsdp")
        self.member = index % MEMBERS
        self.group = index // MEMBERS

    def swap(self, value, bits):
        return lax.ppermute(value, "fsdp", [(i, i ^ bits) for i in range(self.count)])

    def direct_gather(self, piece):
        stack = jnp.zeros((self.groups,) + piece.shape, piece.dtype)
        for bits in range(self.groups):
            part = self.swap(piece, bits * MEMBERS) if bits else piece
            stack = lax.dynamic_update_index_in_dim(stack, part, self.group ^ bits, 0)
        return stack

    def direct_reduce(self, terms):
        total = lax.dynamic_index_in_dim(terms, self.group, 0, keepdims=False)
        for bits in range(1, self.groups):
            part = lax.dynamic_index_in_dim(terms, self.group ^ bits, 0, keepdims=False)
            total = total + self.swap(part.astype(bf16), bits * MEMBERS).astype(f32)
        return total

    def chips_gather(self, block):
        half = block.shape[0] // 2
        top, low = block[:half], block[half:]
        near_top, far_low = self.swap(top, 2), self.swap(low, 4)
        near_low, far_top = self.swap(low, 2), self.swap(top, 4)
        cross_top, cross_low = self.swap(near_top, 4), self.swap(far_low, 2)
        return {0: (top, low), 2: (near_top, near_low), 4: (far_top, far_low), 6: (cross_top, cross_low)}

    def cross_of(self, near, far):
        half = near.shape[0] // 2
        return self.swap(near[:half], 4), self.swap(far[half:], 2)

    def send_cross(self, block):
        half = block.shape[0] // 2
        return self.swap(block[:half], 2), self.swap(block[half:], 4)

    def add_cross(self, near, far, cross):
        half = near.shape[0] // 2
        cross_top, cross_low = cross
        near_low = (near[half:].astype(f32) + cross_low.astype(f32)).astype(bf16)
        far_top = (far[:half].astype(f32) + cross_top.astype(f32)).astype(bf16)
        return (
            jnp.concatenate([near[:half], near_low], axis=0),
            jnp.concatenate([far_top, far[half:]], axis=0),
        )

    def chip_parts(self, parts):
        chips = parts.reshape((MEMBERS // 2, 2) + parts.shape[1:])
        chip = self.member // 2
        found = []
        for bits in range(MEMBERS // 2):
            part = lax.dynamic_index_in_dim(chips, chip ^ bits, 0, keepdims=False)
            found.append(self.swap(part, 2 * bits) if bits else part)
        return found

    def keep_parts(self, found):
        chip, core = self.member // 2, self.member % 2
        arrived = jnp.zeros((MEMBERS // 2,) + found[0].shape, found[0].dtype)
        for bits, part in enumerate(found):
            arrived = lax.dynamic_update_index_in_dim(arrived, part, chip ^ bits, 0)
        kept = lax.dynamic_index_in_dim(arrived, core, 1, keepdims=False)
        other = self.swap(lax.dynamic_index_in_dim(arrived, 1 - core, 1, keepdims=False), 1)
        even = jnp.where(core == 0, kept, other)
        odd = jnp.where(core == 0, other, kept)
        return jnp.stack([even, odd], axis=1).reshape((MEMBERS,) + found[0].shape[1:])


def dot(left, right):
    return jnp.dot(left, right, preferred_element_type=f32)


def dot_turned(left, right):
    return lax.dot_general(left, right, (((1,), (1,)), ((), ())), preferred_element_type=f32)


def expert_kernel(names_ref, *refs, layout, fresh, last, carried):
    refs = list(refs)
    experts = range(names_ref.shape[0])
    packet_parts = [[refs.pop(0) for _ in range(number)] for number in layout]
    cotangent_parts = [[refs.pop(0) for _ in range(number)] for number in layout]
    weight_parts = [refs.pop(0) for _ in experts]
    prior_refs = [None if fresh else refs.pop(0) for _ in experts]
    carried_out, carried_back = (refs.pop(0), refs.pop(0)) if carried else (None, None)
    out_ref, back_ref = refs.pop(0), refs.pop(0)
    result_refs = [refs.pop(0) for _ in experts]
    grad_refs = [refs.pop(0) for _ in experts] if last else result_refs
    packet_buffer, cotangent_buffer, weight_ref, packet_turned, cotangent_turned, sums = refs[:6]
    block_sem, weight_sem, prior_sem = refs[6:]
    rows, width = cotangent_buffer.shape[1:]
    groups, _, depth, _ = weight_parts[0].shape
    blocks = len(layout)
    at = pl.program_id(0)

    def block_copies(block):
        copies = []
        for kind, (parts, buffer) in enumerate(
            ((packet_parts, packet_buffer), (cotangent_parts, cotangent_buffer))
        ):
            size = rows // layout[block]
            for number, part in enumerate(parts[block]):
                place = buffer.at[block, pl.ds(number * size, size)]
                copies.append(
                    pltpu.make_async_copy(part, place, block_sem.at[block, 2 * kind + number])
                )
        return copies

    def weight_copies(n):
        return [
            pltpu.make_async_copy(
                weight_parts[n].at[g], weight_ref.at[n, :, pl.ds(g * depth, depth)], weight_sem.at[n, g]
            )
            for g in range(groups)
        ]

    def prior_copy(n):
        return pltpu.make_async_copy(prior_refs[n], grad_refs[n], prior_sem.at[n])

    @pl.when(at == 0)
    def _():
        for copy in block_copies(0):
            copy.start()
        for n in experts:
            for copy in weight_copies(n):
                copy.start()
        for n in experts:
            if fresh:
                grad_refs[n][...] = jnp.zeros_like(grad_refs[n])
            else:
                prior_copy(n).start()
        for block in range(1, blocks):
            for copy in block_copies(block):
                copy.start()
        for n in experts:
            for copy in weight_copies(n):
                copy.wait()

    for block in range(blocks):

        @pl.when(at == block)
        def _():
            for copy in block_copies(block):
                copy.wait()

    lane = lax.broadcasted_iota(jnp.int32, (rows, EXTRA), 1)
    normed = packet_buffer[at, :, :width]
    upstream = cotangent_buffer[at]
    shares = packet_buffer[at, :, width:].astype(f32)
    extra = jnp.zeros((rows, EXTRA), f32)
    packet_turned[...] = normed.T
    cotangent_turned[...] = upstream.T
    begun = []
    for n in experts:
        begun.append(
            (
                dot(normed, weight_ref[n, 0]),
                dot(normed, weight_ref[n, 1]),
                dot(upstream, weight_ref[n, 2]),
            )
        )
    if not fresh:

        @pl.when(at == 0)
        def _():
            for n in experts:
                prior_copy(n).wait()

    for n in experts:
        gate_pre, up_pre, inner_raw = begun[n]
        expert = names_ref[n]
        is_high, is_low = lane == expert, lane == expert + EXPERTS
        share = jnp.sum(jnp.where(is_high | is_low, shares, 0.0), axis=1, keepdims=True)
        sigmoid_gate = jax.nn.sigmoid(gate_pre)
        activated = gate_pre * sigmoid_gate
        inner = (activated * up_pre).astype(bf16).astype(f32)
        share_grad = residual_scale * jnp.sum(inner * inner_raw, axis=1, keepdims=True)
        scaled = share * residual_scale
        inner_grad = inner_raw * scaled
        gate_grad = (
            inner_grad * up_pre * (sigmoid_gate + activated * (1.0 - sigmoid_gate))
        ).astype(bf16)
        up_grad = (inner_grad * activated).astype(bf16)
        inner_shared = (inner * scaled).astype(bf16)
        out_term = dot_turned(inner_shared, weight_ref[n, 2])
        back_term = dot_turned(gate_grad, weight_ref[n, 0]) + dot_turned(up_grad, weight_ref[n, 1])
        if n == 0:
            sums[0], sums[1] = out_term, back_term
        else:
            sums[0] += out_term
            sums[1] += back_term
        grad_refs[n][0] += dot(packet_turned[...], gate_grad)
        grad_refs[n][1] += dot(packet_turned[...], up_grad)
        grad_refs[n][2] += dot(cotangent_turned[...], inner_shared)
        high = share_grad.astype(bf16).astype(f32)
        extra = extra + jnp.where(is_high, high, 0.0) + jnp.where(is_low, share_grad - high, 0.0)
    out_total, back_total = sums[0], sums[1]
    if carried:
        out_total = out_total + carried_out[0].astype(f32)
        back_total = back_total + carried_back[0, :, :width].astype(f32)
        extra = extra + carried_back[0, :, width:].astype(f32)
    out_ref[0] = out_total.astype(bf16)
    back_ref[0, :, :width] = back_total.astype(bf16)
    back_ref[0, :, width:] = extra.astype(bf16)

    if last:

        @pl.when(at == blocks - 1)
        def _():
            for n in experts:
                for g in range(groups):
                    result_refs[n][g] = grad_refs[n][:, pl.ds(g * depth, depth)].astype(bf16)


def run_experts(names, packets, cotangents, weights, priors=None, last=False, carried=None):
    layout = tuple(len(parts) for parts in packets)
    blocks = len(layout)
    rows = sum(part.shape[0] for part in packets[0])
    wide, width = packets[0][0].shape[1], cotangents[0][0].shape[1]
    groups, _, depth, hidden = weights[0].shape
    grad_shape = (3, width, hidden)
    fresh = priors is None
    count = len(weights)
    operands = [part for parts in packets for part in parts]
    operands += [part for parts in cotangents for part in parts]
    operands += list(weights) + list(priors or ())

    def whole(shape):
        return pl.BlockSpec(
            shape, lambda i, s, rank=len(shape): (0,) * rank, pipeline_mode=pl.Buffered(1)
        )

    term_specs = [
        pl.BlockSpec((1, rows, columns), lambda i, s: (i, 0, 0)) for columns in (width, wide)
    ]
    in_specs = [pl.BlockSpec(memory_space=pl.ANY)] * len(operands)
    if carried is not None:
        in_specs += term_specs
        operands += list(carried)
    grads = [((groups, 3, depth, hidden), bf16) if last else (grad_shape, f32)] * count
    scratch = [pltpu.VMEM(grad_shape, f32)] * (count if last else 0)
    scratch += [
        pltpu.VMEM((blocks, rows, wide), bf16),
        pltpu.VMEM((blocks, rows, width), bf16),
        pltpu.VMEM((count,) + grad_shape, bf16),
        pltpu.VMEM((width, rows), bf16),
        pltpu.VMEM((width, rows), bf16),
        pltpu.VMEM((2, rows, width), f32),
        pltpu.SemaphoreType.DMA((blocks, 4)),
        pltpu.SemaphoreType.DMA((count, groups)),
        pltpu.SemaphoreType.DMA((count,)),
    ]
    return pl.pallas_call(
        functools.partial(
            expert_kernel, layout=layout, fresh=fresh, last=last, carried=carried is not None
        ),
        grid_spec=pltpu.PrefetchScalarGridSpec(
            num_scalar_prefetch=1,
            grid=(blocks,),
            in_specs=in_specs,
            out_specs=term_specs + [whole(shape) for shape, _ in grads],
            scratch_shapes=scratch,
        ),
        out_shape=[
            jax.ShapeDtypeStruct((blocks, rows, columns), bf16) for columns in (width, wide)
        ]
        + [jax.ShapeDtypeStruct(shape, dtype) for shape, dtype in grads],
        compiler_params=pltpu.CompilerParams(vmem_limit_bytes=62 * 1024 * 1024),
        cost_estimate=pl.CostEstimate(
            flops=blocks * count * 9 * 2 * rows * width * hidden,
            bytes_accessed=blocks * rows * width * 8 + 18 * count * width * hidden,
            transcendentals=blocks * count * rows * hidden,
        ),
        name="experts",
    )(names, *operands)


TILE = 256
PAIR = 2 * HEAD_DIM


def columns_at(index, size):
    return pl.ds(pl.multiple_of(index * size, size), size)


def swap_halves(values):
    width, half_dim = values.shape[1], HEAD_DIM // 2
    lane = lax.broadcasted_iota(jnp.int32, values.shape, 1)
    return jnp.where(
        lane % HEAD_DIM < half_dim,
        pltpu.roll(values, width - half_dim, 1),
        pltpu.roll(values, half_dim, 1),
    )


def row_scale_of(values):
    return lax.rsqrt(jnp.mean(values * values, axis=1, keepdims=True) + norm_eps)


def scores_of(keys, queries, length, first_query):
    scores = attention_scale * dot_turned(keys, queries)
    key_at = lax.broadcasted_iota(jnp.int32, scores.shape, 0)
    query_at = lax.broadcasted_iota(jnp.int32, scores.shape, 1) + first_query
    return jnp.where((key_at <= query_at) & (key_at < length), scores, masked_value)


def head_of(block, index):
    return block[:, index * HEAD_DIM : (index + 1) * HEAD_DIM]


def attention_kernel(
    length_ref, tokens_ref, cosine_ref, sine_ref, gains_ref, weight_ref,
    rotated_ref, mixed_ref, log_ref, normed_ref,
):
    rows = tokens_ref.shape[0]
    head_columns, kv_columns = HEADS * HEAD_DIM, KV_HEADS * HEAD_DIM
    at_value = head_columns + kv_columns
    at_output = at_value + kv_columns
    length = length_ref[0]
    group = HEADS // KV_HEADS

    inputs = tokens_ref[...].astype(f32)
    normed_ref[...] = (inputs * row_scale_of(inputs) * gains_ref[0:1, :]).astype(bf16)

    def project_turned(c, carry):
        where = columns_at(c, TILE)
        value = dot(normed_ref[...], weight_ref[:, where])
        value = value * cosine_ref[...] + swap_halves(value) * sine_ref[...]
        rotated_ref[:, where] = value.astype(bf16)
        return carry

    def project(c, carry):
        where = columns_at(c, TILE)
        rotated_ref[:, where] = dot(normed_ref[...], weight_ref[:, where]).astype(bf16)
        return carry

    lax.fori_loop(0, at_value // TILE, project_turned, 0)
    lax.fori_loop(at_value // TILE, at_output // TILE, project, 0)

    block = rows // 2

    def attend(j, carry):
        queries = rotated_ref[:, columns_at(j, group * PAIR)]
        keys = rotated_ref[:, columns_at(j + head_columns // PAIR, PAIR)]
        values_turned = rotated_ref[:, columns_at(j + at_value // PAIR, PAIR)].T
        outs = []
        for head in range(2 * group):
            kv = head // group
            key, query = head_of(keys, kv), head_of(queries, head)
            value = values_turned[kv * HEAD_DIM : (kv + 1) * HEAD_DIM]
            parts, logs = [], []
            for b in range(2):
                reach = (b + 1) * block
                scores = scores_of(key[:reach], query[b * block : reach], length, b * block)
                best = jnp.max(scores, axis=0, keepdims=True)
                exponent = jnp.exp(scores - best)
                total = jnp.sum(exponent, axis=0, keepdims=True)
                chance = (exponent * (1.0 / total)).astype(bf16)
                parts.append(dot(value[:, :reach], chance))
                logs.append(best + jnp.log(total))
            outs.append(jnp.concatenate(parts, axis=1))
            log_ref[j, head : head + 1, :] = jnp.concatenate(logs, axis=1)
        mixed_ref[:, columns_at(j, group * PAIR)] = jnp.concatenate(outs, axis=0).T.astype(bf16)
        return carry

    lax.fori_loop(0, KV_HEADS // 2, attend, 0)


def router_kernel(
    tokens_ref, routes_ref, gains_ref, mixed_ref, output_ref, extra_ref,
    packet_ref, middle_ref, share_ref,
):
    width = tokens_ref.shape[1]

    def mix(c, carry):
        where = columns_at(c, TILE)
        branch = dot_turned(mixed_ref[...], output_ref[where, :])
        middle_ref[:, where] = tokens_ref[:, where].astype(f32) + residual_scale * branch
        return carry

    lax.fori_loop(0, width // TILE, mix, 0)
    middle = middle_ref[...]
    normed_two = (middle * row_scale_of(middle) * gains_ref[1:2, :]).astype(bf16)
    packet_ref[:, :width] = normed_two
    logits = dot(normed_two, extra_ref[...])
    lane = lax.broadcasted_iota(jnp.int32, logits.shape, 1)
    routed = lane == routes_ref[:, 0:1]
    for k in range(1, routes_ref.shape[1]):
        routed = routed | (lane == routes_ref[:, k : k + 1])
    best = jnp.max(jnp.where(routed, logits, masked_value), axis=1, keepdims=True)
    weights = jnp.where(routed, jnp.exp(jnp.where(routed, logits, best) - best), 0.0)
    shares = weights / jnp.sum(weights, axis=1, keepdims=True)
    share_ref[...] = shares
    high = shares.astype(bf16).astype(f32)
    packet_ref[:, width:] = (high + pltpu.roll(shares - high, EXPERTS, 1)).astype(bf16)


def column_of(row, lanes):
    return jnp.broadcast_to(row, (lanes, row.shape[1])).T


def middle_kernel(
    own_ref, near_ref, far_ref, packet_ref, middle_ref, cotangent_ref, share_ref, gains_ref, mixed_ref, output_ref, extra_ref,
    middle_grad_ref, mixed_grad_ref, pack_ref, back_ref, branch_ref, turned_ref,
):
    width = cotangent_ref.shape[1]
    back_ref[...] = own_ref[...].astype(f32) + near_ref[...].astype(f32) + far_ref[...].astype(f32)
    shares = share_ref[...]
    share_grad = back_ref[:, width:]
    share_grad = share_grad + pltpu.roll(share_grad, EXTRA - EXPERTS, 1)
    weighted_mean = jnp.sum(shares * share_grad, axis=1, keepdims=True)
    logit_grad = (shares * (share_grad - weighted_mean)).astype(bf16)
    normed_grad = back_ref[:, :width] + dot_turned(logit_grad, extra_ref[...])
    middle = middle_ref[...]
    scale = row_scale_of(middle)
    scaled = middle * scale
    gain_grad = jnp.sum(normed_grad * scaled, axis=0, keepdims=True)
    weighted = normed_grad * gains_ref[1:2, :]
    correction = jnp.mean(weighted * middle, axis=1, keepdims=True)
    middle_grad = cotangent_ref[...].astype(f32) + scale * weighted - scaled * (scale * scale * correction)
    middle_grad_ref[...] = middle_grad
    branch_ref[...] = (residual_scale * middle_grad).astype(bf16)
    router_grad = dot(packet_ref[:, :width].T, logit_grad)
    lane = lax.broadcasted_iota(jnp.int32, router_grad.shape, 1)
    pack_ref[:, width:] = jnp.where(
        lane == EXPERTS, column_of(gain_grad, EXTRA), router_grad
    ).astype(bf16)
    turned_ref[...] = branch_ref[...].T

    def step(c, carry):
        where = columns_at(c, TILE)
        pack_ref[:, where] = dot(turned_ref[...], mixed_ref[:, where]).astype(bf16)
        mixed_grad_ref[:, where] = dot(branch_ref[...], output_ref[:, where]).astype(bf16)
        return carry

    lax.fori_loop(0, output_ref.shape[1] // TILE, step, 0)


def attention_back_kernel(
    length_ref, rotated_ref, mixed_grad_ref, log_ref, cosine_ref, sine_ref, grad_ref
):
    rows = rotated_ref.shape[0]
    head_columns, kv_columns = HEADS * HEAD_DIM, KV_HEADS * HEAD_DIM
    at_value = head_columns + kv_columns
    length = length_ref[0]
    group = HEADS // KV_HEADS
    block = rows // 2

    def attend(j, carry):
        wide = columns_at(j, group * PAIR)
        key_place = columns_at(j + head_columns // PAIR, PAIR)
        value_place = columns_at(j + at_value // PAIR, PAIR)
        queries, grads = rotated_ref[:, wide], mixed_grad_ref[:, wide]
        keys, values = rotated_ref[:, key_place], rotated_ref[:, value_place]
        keys_turned = keys.T
        query_grads, key_grads, value_grads = [], [], []
        for kv in range(2):
            key, value = head_of(keys, kv), head_of(values, kv)
            key_turned = keys_turned[kv * HEAD_DIM : (kv + 1) * HEAD_DIM]
            key_sums, value_sums = [], []
            for member in range(group):
                head = kv * group + member
                query, grad = head_of(queries, head), head_of(grads, head)
                query_parts = []
                for b in range(2):
                    reach = (b + 1) * block
                    query_block, grad_block = query[b * block : reach], grad[b * block : reach]
                    scores = scores_of(key[:reach], query_block, length, b * block)
                    chance = jnp.exp(scores - log_ref[j, head : head + 1, b * block : reach])
                    chance_grad = dot_turned(value[:reach], grad_block)
                    delta = jnp.sum(chance * chance_grad, axis=0, keepdims=True)
                    score_grad = (attention_scale * chance * (chance_grad - delta)).astype(bf16)
                    value_sums.append(dot(chance.astype(bf16), grad_block))
                    key_sums.append(dot(score_grad, query_block))
                    query_parts.append(dot(key_turned[:, :reach], score_grad))
                query_grads.append(jnp.concatenate(query_parts, axis=1))
            for sums, into in ((key_sums, key_grads), (value_sums, value_grads)):
                short = sum(sums[2::2], sums[0])
                long = sum(sums[3::2], sums[1])
                into.append(jnp.concatenate([short + long[:block], long[block:]], axis=0))
        query_grad = jnp.concatenate(query_grads, axis=0).T
        query_grad = query_grad * cosine_ref[...] - swap_halves(query_grad) * sine_ref[...]
        grad_ref[:, wide] = query_grad.astype(bf16)
        key_grad = jnp.concatenate(key_grads, axis=1)
        key_grad = key_grad * cosine_ref[:, :PAIR] - swap_halves(key_grad) * sine_ref[:, :PAIR]
        grad_ref[:, key_place] = key_grad.astype(bf16)
        grad_ref[:, value_place] = jnp.concatenate(value_grads, axis=1).astype(bf16)
        return carry

    lax.fori_loop(0, KV_HEADS // 2, attend, 0)


def inputs_kernel(
    tokens_ref, gains_ref, projected_ref, weight_ref, middle_grad_ref,
    grad_ref, pack_ref, normed_grad_ref, turned_ref,
):
    width = tokens_ref.shape[1]
    projections = projected_ref.shape[1]
    inputs = tokens_ref[...].astype(f32)
    scale = row_scale_of(inputs)
    scaled = inputs * scale
    turned_ref[...] = (scaled * gains_ref[0:1, :]).astype(bf16).T

    def to_weight(c, carry):
        where = columns_at(c, TILE)
        pack_ref[:, where] = dot(turned_ref[...], projected_ref[:, where]).astype(bf16)
        return carry

    def to_input(c, carry):
        where = columns_at(c, TILE)
        normed_grad_ref[:, where] = dot_turned(projected_ref[...], weight_ref[where, :])
        return carry

    lax.fori_loop(0, projections // TILE, to_weight, 0)
    lax.fori_loop(0, width // TILE, to_input, 0)
    normed_grad = normed_grad_ref[...]
    gain_grad = column_of(jnp.sum(normed_grad * scaled, axis=0, keepdims=True), EXTRA)
    lane = lax.broadcasted_iota(jnp.int32, gain_grad.shape, 1)
    pack_ref[:, projections:] = jnp.where(lane == 0, gain_grad, 0.0).astype(bf16)
    weighted = normed_grad * gains_ref[0:1, :]
    correction = jnp.mean(weighted * inputs, axis=1, keepdims=True)
    grad_ref[...] = middle_grad_ref[...] + scale * weighted - scaled * (scale * scale * correction)


def call_kernel(body, name, operands, out_shape, scratch, flops):
    specs, arrays = [], []
    for operand in operands:
        array, shape, index = operand
        if shape == "scalar":
            specs.append(pl.BlockSpec(memory_space=pltpu.SMEM))
        else:
            shape = array.shape if shape is None else shape
            index = (0,) * len(shape) if index is None else index
            specs.append(pl.BlockSpec(shape, lambda i, index=index: index))
        arrays.append(array)
    outs = [jax.ShapeDtypeStruct(shape, dtype) for shape, dtype in out_shape]
    return pl.pallas_call(
        body,
        grid=(1,),
        in_specs=specs,
        out_specs=[
            pl.BlockSpec(out.shape, lambda i, rank=len(out.shape): (0,) * rank) for out in outs
        ],
        out_shape=outs,
        scratch_shapes=[pltpu.VMEM(shape, dtype) for shape, dtype in scratch],
        compiler_params=pltpu.CompilerParams(vmem_limit_bytes=62 * 1024 * 1024),
        cost_estimate=pl.CostEstimate(
            flops=flops,
            bytes_accessed=sum(a.size * a.dtype.itemsize for a in arrays)
            + sum(o.size * o.dtype.itemsize for o in outs),
            transcendentals=0,
        ),
        name=name,
    )(*arrays)


def rope_lanes(row_count):
    cosine_table, sine_table = rope_tables(row_count)
    half_dim = HEAD_DIM // 2
    signed = jnp.concatenate([-sine_table[:, :half_dim], sine_table[:, half_dim:]], axis=1)
    repeats = TILE // HEAD_DIM
    return jnp.tile(cosine_table, (1, repeats)), jnp.tile(signed, (1, repeats))


def attention_forward(tokens, lengths, tables, gains, whole):
    rows, width = tokens.shape
    head_columns, kv_columns = HEADS * HEAD_DIM, KV_HEADS * HEAD_DIM
    projections = head_columns + 2 * kv_columns
    return call_kernel(
        attention_kernel,
        "attention_forward",
        [
            (lengths, "scalar", None), (tokens, None, None), (tables[0], None, None),
            (tables[1], None, None), (gains, None, None), (whole, (width, projections), (0, 0)),
        ],
        [
            ((rows, projections), bf16), ((rows, head_columns), bf16),
            ((KV_HEADS // 2, 2 * HEADS // KV_HEADS, rows), f32),
        ],
        [((rows, width), bf16)],
        8 * rows * width * head_columns,
    )


def output_blocks(whole):
    width = whole.shape[0]
    head_columns, kv_columns = HEADS * HEAD_DIM, KV_HEADS * HEAD_DIM
    at_output = head_columns + 2 * kv_columns
    return [
        (whole, (width, head_columns), (0, at_output // head_columns)),
        (whole, (width, EXTRA), (0, (at_output + head_columns) // EXTRA)),
    ]


def router_forward(tokens, routes, gains, mixed, whole):
    rows, width = tokens.shape
    return call_kernel(
        router_kernel,
        "router_forward",
        [(a, None, None) for a in (tokens, routes, gains, mixed)] + output_blocks(whole),
        [((rows, width + EXTRA), bf16), ((rows, width), f32), ((rows, EXTRA), f32)],
        [],
        2 * rows * width * mixed.shape[1],
    )


def middle_back(pieces, packet, middle, cotangent, shares, gains, mixed, whole):
    rows, width = cotangent.shape
    head_columns = HEADS * HEAD_DIM
    return call_kernel(
        middle_kernel,
        "middle_back",
        [(a, None, None) for a in (*pieces, packet, middle, cotangent, shares, gains, mixed)]
        + output_blocks(whole),
        [((rows, width), f32), ((rows, head_columns), bf16), ((width, head_columns + EXTRA), bf16)],
        [((rows, width + EXTRA), f32), ((rows, width), bf16), ((width, rows), bf16)],
        4 * rows * width * head_columns,
    )


def attention_back(lengths, rotated, mixed_grad, logs, tables):
    return call_kernel(
        attention_back_kernel,
        "attention_back",
        [
            (lengths, "scalar", None), (rotated, None, None), (mixed_grad, None, None),
            (logs, None, None), (tables[0], None, None), (tables[1], None, None),
        ],
        [(rotated.shape, bf16)],
        [],
        10 * rotated.shape[0] ** 2 * HEADS * HEAD_DIM,
    )[0]


def inputs_back(tokens, gains, projected_grad, whole, middle_grad):
    rows, width = tokens.shape
    projections = projected_grad.shape[1]
    return call_kernel(
        inputs_kernel,
        "inputs_back",
        [
            (tokens, None, None), (gains, None, None), (projected_grad, None, None),
            (whole, (width, projections), (0, 0)), (middle_grad, None, None),
        ],
        [((rows, width), f32), ((width, projections + EXTRA), bf16)],
        [((rows, width), f32), ((width, rows), bf16)],
        4 * rows * width * projections,
    )


def local(
    tokens,
    lengths,
    routes,
    attention_gain,
    query_weight,
    key_weight,
    value_weight,
    output_weight,
    expert_gain,
    router_weight,
    gate_weight,
    up_weight,
    down_weight,
    cotangent,
    *,
    count,
):
    links = Exchange(count)
    member, group, groups = links.member, links.group, links.groups
    row_count, width = tokens.shape
    shard = query_weight.shape[0]
    hidden = gate_weight.shape[2]
    head_columns, kv_columns = HEADS * HEAD_DIM, KV_HEADS * HEAD_DIM

    mine = jnp.stack([gate_weight, up_weight, down_weight.transpose(0, 2, 1)], axis=1)
    mine = mine.reshape(MEMBERS, LOCAL_EXPERTS, 3, shard, hidden)
    arrived = links.chip_parts(mine)

    packed = jnp.concatenate(
        [
            query_weight,
            key_weight,
            value_weight,
            output_weight.T,
            router_weight,
            attention_gain[:, None],
            expert_gain[:, None],
            jnp.zeros((shard, EXTRA - EXPERTS - 2), bf16),
        ],
        axis=1,
    )
    pack_width = packed.shape[1]
    column = links.direct_gather(packed).reshape(groups * shard, pack_width)
    arrived, column = lax.optimization_barrier((arrived, column))
    spread = links.chips_gather(column)
    shelf = links.keep_parts(arrived).transpose(1, 2, 0, 3, 4)
    shelf = shelf.reshape(LOCAL_EXPERTS, 3, MEMBERS * shard, hidden)
    lines = [[m + MEMBERS * g for g in range(groups)] for m in range(MEMBERS)]
    own_full = [
        lax.all_gather(shelf[n], "fsdp", axis_index_groups=lines) for n in range(LOCAL_EXPERTS)
    ]
    whole = jnp.zeros((groups, MEMBERS, shard, pack_width), bf16)
    for k in range(MEMBERS):
        parts = spread[k & 6]
        if k & 1:
            parts = [links.swap(part, 1) for part in parts]
        part = jnp.concatenate(parts, axis=0).reshape(groups, shard, pack_width)
        whole = lax.dynamic_update_index_in_dim(whole, part, member ^ k, 1)
    whole = whole.reshape(width, pack_width)
    at_output = head_columns + 2 * kv_columns
    at_extra = at_output + head_columns
    gains = whole[:, at_extra + EXPERTS : at_extra + EXPERTS + 2].astype(f32).T

    late_cotangent, whole = lax.optimization_barrier((cotangent, whole))
    cot_near, cot_far = links.swap(late_cotangent, 2), links.swap(late_cotangent, 4)

    tables = rope_lanes(row_count)
    rotated, mixed, logs = attention_forward(tokens, lengths, tables, gains, whole)
    cot_near, cot_far, mixed = lax.optimization_barrier((cot_near, cot_far, mixed))
    packet, middle, shares = router_forward(tokens, routes, gains, mixed, whole)
    near, far = links.swap(packet, 2), links.swap(packet, 4)
    own_full[0], packet, cot_near, cot_far = lax.optimization_barrier(
        (own_full[0], packet, cot_near, cot_far)
    )
    cot_cross = links.cross_of(cot_near, cot_far)

    names = [
        jnp.stack([member, member ^ 1]).astype(jnp.int32) * LOCAL_EXPERTS + n
        for n in range(LOCAL_EXPERTS)
    ]
    rows_own = [(packet,)], [(cotangent,)]
    first_full = own_full[0], links.swap(own_full[0], 1)
    own_out, own_back, *zero = run_experts(names[0], *rows_own, first_full)
    near, far, own_back = lax.optimization_barrier((near, far, own_back))
    cross = links.cross_of(near, far)
    rows_chips = [cross, (near,), (far,)], [cot_cross, (cot_near,), (cot_far,)]
    chip_out, chip_back, *zero = run_experts(names[0], *rows_chips, first_full, zero, True)
    own_full[1], chip_back = lax.optimization_barrier((own_full[1], chip_back))
    second_full = own_full[1], links.swap(own_full[1], 1)
    chip_out, chip_back, *one = run_experts(
        names[1], *rows_chips, second_full, None, False, (chip_out, chip_back)
    )

    def join_cores(own, other):
        return (own.astype(f32) + links.swap(other, 1).astype(f32)).astype(bf16)

    def reduce_groups(total):
        return lax.psum_scatter(total, "fsdp", scatter_dimension=0, axis_index_groups=lines)

    zero = join_cores(*zero)
    back_cross = links.send_cross(chip_back[0])
    back_near, back_far = links.add_cross(chip_back[1], chip_back[2], back_cross)
    zero, back_near, back_far, own_back = lax.optimization_barrier(
        (zero, back_near, back_far, own_back)
    )
    shelf_zero = reduce_groups(zero)
    back_near, back_far = links.swap(back_near, 2), links.swap(back_far, 4)
    own_out, own_back, *one = run_experts(
        names[1], *rows_own, second_full, one, True, (own_out, own_back)
    )
    one = join_cores(*one)
    out_cross, back_near, back_far = lax.optimization_barrier((chip_out[0], back_near, back_far))
    out_cross = links.send_cross(out_cross)

    core, chip = member % 2, member // 2

    def pack_cores(pack):
        columns = pack.shape[1]
        pack = pack.reshape(groups, MEMBERS // 2, 2, shard, columns)
        own = lax.dynamic_index_in_dim(pack, core, 2, keepdims=False)
        other = links.swap(lax.dynamic_index_in_dim(pack, 1 - core, 2, keepdims=False), 1)

        joined = own.astype(f32) + other.astype(f32)
        return [
            lax.dynamic_index_in_dim(joined, chip ^ bits, 1, keepdims=False).reshape(
                groups * shard, columns
            )
            for bits in range(MEMBERS // 2)
        ]

    def pack_cross(parts):
        return links.send_cross(parts[3].astype(bf16))

    def pack_add(parts, cross):
        return links.add_cross(parts[1].astype(bf16), parts[2].astype(bf16), cross)

    def pack_end(parts, near, far):
        near, far = links.swap(near, 2), links.swap(far, 4)
        total = parts[0] + near.astype(f32) + far.astype(f32)
        return links.direct_reduce(total.reshape(groups, shard, total.shape[1]))

    middle_grad, mixed_grad, first_pack = middle_back(
        (own_back[0], back_near, back_far), packet, middle, cotangent, shares, gains, mixed, whole
    )
    out_near, out_far = links.add_cross(chip_out[1], chip_out[2], out_cross)
    out_near, out_far, one, mixed_grad = lax.optimization_barrier(
        (out_near, out_far, one, mixed_grad)
    )
    shelf_one = reduce_groups(one)
    out_near, out_far = links.swap(out_near, 2), links.swap(out_far, 4)
    first_parts = pack_cores(first_pack)
    projected_grad = attention_back(lengths, rotated, mixed_grad, logs, tables)
    out_near, first_parts, projected_grad = lax.optimization_barrier(
        (out_near, first_parts, projected_grad)
    )
    first_cross = pack_cross(first_parts)
    grad_tokens, second_pack = inputs_back(tokens, gains, projected_grad, whole, middle_grad)
    first_near, first_far = pack_add(first_parts, first_cross)
    first_near, first_far, second_pack = lax.optimization_barrier(
        (first_near, first_far, second_pack)
    )
    second_parts = pack_cores(second_pack)
    first_total = pack_end(first_parts, first_near, first_far)
    second_near, second_far = pack_add(second_parts, pack_cross(second_parts))
    second_total = pack_end(second_parts, second_near, second_far)
    out_pieces = (own_out[0], out_near, out_far)
    layer_out = (middle + sum(piece.astype(f32) for piece in out_pieces)).astype(bf16)
    shelf_grad = jnp.stack([shelf_zero, shelf_one])
    shelf_grad = shelf_grad.reshape(LOCAL_EXPERTS, 3, MEMBERS, shard, hidden)
    expert_shards = links.keep_parts(links.chip_parts(shelf_grad.transpose(2, 0, 1, 3, 4))).astype(f32)
    expert_shards = expert_shards.reshape(EXPERTS, 3, shard, hidden)
    return (
        layer_out,
        grad_tokens,
        second_total[:, at_output],
        second_total[:, :head_columns],
        second_total[:, head_columns : head_columns + kv_columns],
        second_total[:, head_columns + kv_columns : at_output],
        first_total[:, :head_columns].T,
        first_total[:, head_columns + EXPERTS],
        first_total[:, head_columns : head_columns + EXPERTS],
        expert_shards[:, 0],
        expert_shards[:, 1],
        expert_shards[:, 2].transpose(0, 2, 1),
    )


def solution(mesh):
    count = mesh.shape["fsdp"]
    placed = (
        P("fsdp", None),
        P("fsdp"),
        P("fsdp", None),
        P("fsdp"),
        P("fsdp", None),
        P("fsdp", None),
        P("fsdp", None),
        P(None, "fsdp"),
        P("fsdp"),
        P("fsdp", None),
        P(None, "fsdp", None),
        P(None, "fsdp", None),
        P(None, None, "fsdp"),
        P("fsdp", None),
    )

    def body(*args):
        return local(*args, count=count)

    return jax.shard_map(
        body,
        mesh=mesh,
        in_specs=placed,
        out_specs=(
            P("fsdp", None),
            P("fsdp", None),
            P("fsdp"),
            P("fsdp", None),
            P("fsdp", None),
            P("fsdp", None),
            P(None, "fsdp"),
            P("fsdp"),
            P("fsdp", None),
            P(None, "fsdp", None),
            P(None, "fsdp", None),
            P(None, None, "fsdp"),
        ),
        check_vma=False,
    )
```

```python
import functools

import jax
import jax.numpy as jnp
from jax import lax
from jax.experimental import pallas as pl
from jax.experimental.pallas import tpu as pltpu
from jax.sharding import PartitionSpec as P

HEADS = 16
KV_HEADS = 8
HEAD_DIM = 64
EXPERTS = 16
MEMBERS = 8
LOCAL_EXPERTS = EXPERTS // MEMBERS
EXTRA = 128

norm_eps = 1e-06
attention_scale = 0.015625
residual_scale = 0.22
rope_base = 10000.0
masked_value = -1e30
f32 = jnp.float32
bf16 = jnp.bfloat16


def rope_tables(row_count):
    half_dim = HEAD_DIM // 2
    frequency = rope_base ** (-2.0 * jnp.arange(half_dim, dtype=jnp.float32) / HEAD_DIM)
    angles = jnp.arange(row_count, dtype=jnp.float32)[:, None] * frequency[None, :]
    angles = jnp.concatenate([angles, angles], axis=1)
    return (jnp.cos(angles), jnp.sin(angles))


class Exchange:
    def __init__(self, count):
        self.count = count
        self.groups = count // MEMBERS
        index = lax.axis_index("fsdp")
        self.member = index % MEMBERS
        self.group = index // MEMBERS

    def swap(self, value, bits):
        return lax.ppermute(value, "fsdp", [(i, i ^ bits) for i in range(self.count)])

    def direct_gather(self, piece):
        stack = jnp.zeros((self.groups,) + piece.shape, piece.dtype)
        for bits in range(self.groups):
            part = self.swap(piece, bits * MEMBERS) if bits else piece
            stack = lax.dynamic_update_index_in_dim(stack, part, self.group ^ bits, 0)
        return stack

    def direct_reduce(self, terms):
        total = lax.dynamic_index_in_dim(terms, self.group, 0, keepdims=False)
        for bits in range(1, self.groups):
            part = lax.dynamic_index_in_dim(terms, self.group ^ bits, 0, keepdims=False)
            total = total + self.swap(part.astype(bf16), bits * MEMBERS).astype(f32)
        return total

    def cross_of(self, near, far):
        half = near.shape[0] // 2
        return self.swap(near[:half], 4), self.swap(far[half:], 2)

    def send_cross(self, block):
        half = block.shape[0] // 2
        return self.swap(block[:half], 2), self.swap(block[half:], 4)

    def add_cross(self, near, far, cross):
        half = near.shape[0] // 2
        cross_top, cross_low = cross
        near_low = (near[half:].astype(f32) + cross_low.astype(f32)).astype(bf16)
        far_top = (far[:half].astype(f32) + cross_top.astype(f32)).astype(bf16)
        return (
            jnp.concatenate([near[:half], near_low], axis=0),
            jnp.concatenate([far_top, far[half:]], axis=0),
        )

    def chip_parts(self, parts):
        chips = parts.reshape((MEMBERS // 2, 2) + parts.shape[1:])
        chip = self.member // 2
        found = []
        for bits in range(MEMBERS // 2):
            part = lax.dynamic_index_in_dim(chips, chip ^ bits, 0, keepdims=False)
            found.append(self.swap(part, 2 * bits) if bits else part)
        return found

    def keep_parts(self, found):
        chip, core = self.member // 2, self.member % 2
        arrived = jnp.zeros((MEMBERS // 2,) + found[0].shape, found[0].dtype)
        for bits, part in enumerate(found):
            arrived = lax.dynamic_update_index_in_dim(arrived, part, chip ^ bits, 0)
        kept = lax.dynamic_index_in_dim(arrived, core, 1, keepdims=False)
        other = self.swap(lax.dynamic_index_in_dim(arrived, 1 - core, 1, keepdims=False), 1)
        return kept, other

    def in_order(self, kept, other):
        core = self.member % 2
        even = jnp.where(core == 0, kept, other)
        odd = jnp.where(core == 0, other, kept)
        return jnp.stack([even, odd], axis=1).reshape((MEMBERS,) + kept.shape[1:])


def dot(left, right):
    return jnp.dot(left, right, preferred_element_type=f32)


def dot_turned(left, right):
    return lax.dot_general(left, right, (((1,), (1,)), ((), ())), preferred_element_type=f32)


def expert_kernel(names_ref, *refs, layout, fresh, last, carried):
    refs = list(refs)
    experts = range(names_ref.shape[0])
    packet_parts = [[refs.pop(0) for _ in range(number)] for number in layout]
    cotangent_parts = [[refs.pop(0) for _ in range(number)] for number in layout]
    weight_parts = [refs.pop(0) for _ in experts]
    prior_refs = [None if fresh else refs.pop(0) for _ in experts]
    carried_out, carried_back = (refs.pop(0), refs.pop(0)) if carried else (None, None)
    out_ref, back_ref = refs.pop(0), refs.pop(0)
    result_refs = [refs.pop(0) for _ in experts]
    grad_refs = [refs.pop(0) for _ in experts] if last else result_refs
    packet_buffer, cotangent_buffer, weight_ref, packet_turned, cotangent_turned, sums = refs[:6]
    block_sem, weight_sem, prior_sem = refs[6:]
    rows, width = cotangent_buffer.shape[1:]
    groups, _, depth, _ = weight_parts[0].shape
    blocks = len(layout)
    at = pl.program_id(0)

    def block_copies(block):
        copies = []
        for kind, (parts, buffer) in enumerate(
            ((packet_parts, packet_buffer), (cotangent_parts, cotangent_buffer))
        ):
            size = rows // layout[block]
            for number, part in enumerate(parts[block]):
                place = buffer.at[block, pl.ds(number * size, size)]
                copies.append(
                    pltpu.make_async_copy(part, place, block_sem.at[block, 2 * kind + number])
                )
        return copies

    def weight_copies(n):
        return [
            pltpu.make_async_copy(
                weight_parts[n].at[g], weight_ref.at[n, :, pl.ds(g * depth, depth)], weight_sem.at[n, g]
            )
            for g in range(groups)
        ]

    def prior_copy(n):
        return pltpu.make_async_copy(prior_refs[n], grad_refs[n], prior_sem.at[n])

    @pl.when(at == 0)
    def _():
        for copy in block_copies(0):
            copy.start()
        for n in experts:
            for copy in weight_copies(n):
                copy.start()
        for n in experts:
            if fresh:
                grad_refs[n][...] = jnp.zeros_like(grad_refs[n])
            else:
                prior_copy(n).start()
        for block in range(1, blocks):
            for copy in block_copies(block):
                copy.start()
        for n in experts:
            for copy in weight_copies(n):
                copy.wait()

    for block in range(blocks):

        @pl.when(at == block)
        def _():
            for copy in block_copies(block):
                copy.wait()

    lane = lax.broadcasted_iota(jnp.int32, (rows, EXTRA), 1)
    normed = packet_buffer[at, :, :width]
    upstream = cotangent_buffer[at]
    shares = packet_buffer[at, :, width:].astype(f32)
    extra = jnp.zeros((rows, EXTRA), f32)
    packet_turned[...] = normed.T
    cotangent_turned[...] = upstream.T
    begun = []
    for n in experts:
        begun.append(
            (
                dot(normed, weight_ref[n, 0]),
                dot(normed, weight_ref[n, 1]),
                dot(upstream, weight_ref[n, 2]),
            )
        )
    if not fresh:

        @pl.when(at == 0)
        def _():
            for n in experts:
                prior_copy(n).wait()

    for n in experts:
        gate_pre, up_pre, inner_raw = begun[n]
        expert = names_ref[n]
        is_high, is_low = lane == expert, lane == expert + EXPERTS
        share = jnp.sum(jnp.where(is_high | is_low, shares, 0.0), axis=1, keepdims=True)
        sigmoid_gate = jax.nn.sigmoid(gate_pre)
        activated = gate_pre * sigmoid_gate
        inner = (activated * up_pre).astype(bf16).astype(f32)
        share_grad = residual_scale * jnp.sum(inner * inner_raw, axis=1, keepdims=True)
        scaled = share * residual_scale
        inner_grad = inner_raw * scaled
        gate_grad = (
            inner_grad * up_pre * (sigmoid_gate + activated * (1.0 - sigmoid_gate))
        ).astype(bf16)
        up_grad = (inner_grad * activated).astype(bf16)
        inner_shared = (inner * scaled).astype(bf16)
        out_term = dot_turned(inner_shared, weight_ref[n, 2])
        back_term = dot_turned(gate_grad, weight_ref[n, 0]) + dot_turned(up_grad, weight_ref[n, 1])
        if n == 0:
            sums[0], sums[1] = out_term, back_term
        else:
            sums[0] += out_term
            sums[1] += back_term
        grad_refs[n][0] += dot(packet_turned[...], gate_grad)
        grad_refs[n][1] += dot(packet_turned[...], up_grad)
        grad_refs[n][2] += dot(cotangent_turned[...], inner_shared)
        high = share_grad.astype(bf16).astype(f32)
        extra = extra + jnp.where(is_high, high, 0.0) + jnp.where(is_low, share_grad - high, 0.0)
    out_total, back_total = sums[0], sums[1]
    if carried:
        out_total = out_total + carried_out[0].astype(f32)
        back_total = back_total + carried_back[0, :, :width].astype(f32)
        extra = extra + carried_back[0, :, width:].astype(f32)
    out_ref[0] = out_total.astype(bf16)
    back_ref[0, :, :width] = back_total.astype(bf16)
    back_ref[0, :, width:] = extra.astype(bf16)

    if last:

        @pl.when(at == blocks - 1)
        def _():
            for n in experts:
                for g in range(groups):
                    result_refs[n][g] = grad_refs[n][:, pl.ds(g * depth, depth)].astype(bf16)


def run_experts(names, packets, cotangents, weights, priors=None, last=False, carried=None):
    layout = tuple(len(parts) for parts in packets)
    blocks = len(layout)
    rows = sum(part.shape[0] for part in packets[0])
    wide, width = packets[0][0].shape[1], cotangents[0][0].shape[1]
    groups, _, depth, hidden = weights[0].shape
    grad_shape = (3, width, hidden)
    fresh = priors is None
    count = len(weights)
    operands = [part for parts in packets for part in parts]
    operands += [part for parts in cotangents for part in parts]
    operands += list(weights) + list(priors or ())

    def whole(shape):
        return pl.BlockSpec(
            shape, lambda i, s, rank=len(shape): (0,) * rank, pipeline_mode=pl.Buffered(1)
        )

    term_specs = [
        pl.BlockSpec((1, rows, columns), lambda i, s: (i, 0, 0)) for columns in (width, wide)
    ]
    in_specs = [pl.BlockSpec(memory_space=pl.ANY)] * len(operands)
    if carried is not None:
        in_specs += term_specs
        operands += list(carried)
    grads = [((groups, 3, depth, hidden), bf16) if last else (grad_shape, f32)] * count
    scratch = [pltpu.VMEM(grad_shape, f32)] * (count if last else 0)
    scratch += [
        pltpu.VMEM((blocks, rows, wide), bf16),
        pltpu.VMEM((blocks, rows, width), bf16),
        pltpu.VMEM((count,) + grad_shape, bf16),
        pltpu.VMEM((width, rows), bf16),
        pltpu.VMEM((width, rows), bf16),
        pltpu.VMEM((2, rows, width), f32),
        pltpu.SemaphoreType.DMA((blocks, 4)),
        pltpu.SemaphoreType.DMA((count, groups)),
        pltpu.SemaphoreType.DMA((count,)),
    ]
    return pl.pallas_call(
        functools.partial(
            expert_kernel, layout=layout, fresh=fresh, last=last, carried=carried is not None
        ),
        grid_spec=pltpu.PrefetchScalarGridSpec(
            num_scalar_prefetch=1,
            grid=(blocks,),
            in_specs=in_specs,
            out_specs=term_specs + [whole(shape) for shape, _ in grads],
            scratch_shapes=scratch,
        ),
        out_shape=[
            jax.ShapeDtypeStruct((blocks, rows, columns), bf16) for columns in (width, wide)
        ]
        + [jax.ShapeDtypeStruct(shape, dtype) for shape, dtype in grads],
        compiler_params=pltpu.CompilerParams(vmem_limit_bytes=62 * 1024 * 1024),
        cost_estimate=pl.CostEstimate(
            flops=blocks * count * 9 * 2 * rows * width * hidden,
            bytes_accessed=blocks * rows * width * 8 + 18 * count * width * hidden,
            transcendentals=blocks * count * rows * hidden,
        ),
        name="experts",
    )(names, *operands)


TILE = 256
PAIR = 2 * HEAD_DIM


def columns_at(index, size):
    return pl.ds(pl.multiple_of(index * size, size), size)


def swap_halves(values):
    width, half_dim = values.shape[1], HEAD_DIM // 2
    lane = lax.broadcasted_iota(jnp.int32, values.shape, 1)
    return jnp.where(
        lane % HEAD_DIM < half_dim,
        pltpu.roll(values, width - half_dim, 1),
        pltpu.roll(values, half_dim, 1),
    )


def row_scale_of(values):
    return lax.rsqrt(jnp.mean(values * values, axis=1, keepdims=True) + norm_eps)


def scores_of(keys, queries, length, first_query):
    scores = attention_scale * dot_turned(keys, queries)
    key_at = lax.broadcasted_iota(jnp.int32, scores.shape, 0)
    query_at = lax.broadcasted_iota(jnp.int32, scores.shape, 1) + first_query
    return jnp.where((key_at <= query_at) & (key_at < length), scores, masked_value)


def head_of(block, index):
    return block[:, index * HEAD_DIM : (index + 1) * HEAD_DIM]


def attention_kernel(
    length_ref, tokens_ref, cosine_ref, sine_ref, gains_ref, weight_ref,
    rotated_ref, mixed_ref, log_ref, normed_ref,
):
    rows = tokens_ref.shape[0]
    head_columns, kv_columns = HEADS * HEAD_DIM, KV_HEADS * HEAD_DIM
    at_value = head_columns + kv_columns
    at_output = at_value + kv_columns
    length = length_ref[0]
    group = HEADS // KV_HEADS

    inputs = tokens_ref[...].astype(f32)
    normed_ref[...] = (inputs * row_scale_of(inputs) * gains_ref[0:1, :]).astype(bf16)

    def project_turned(c, carry):
        where = columns_at(c, TILE)
        value = dot(normed_ref[...], weight_ref[:, where])
        value = value * cosine_ref[...] + swap_halves(value) * sine_ref[...]
        rotated_ref[:, where] = value.astype(bf16)
        return carry

    def project(c, carry):
        where = columns_at(c, TILE)
        rotated_ref[:, where] = dot(normed_ref[...], weight_ref[:, where]).astype(bf16)
        return carry

    lax.fori_loop(0, at_value // TILE, project_turned, 0)
    lax.fori_loop(at_value // TILE, at_output // TILE, project, 0)

    block = rows // 2

    def attend(j, carry):
        queries = rotated_ref[:, columns_at(j, group * PAIR)]
        keys = rotated_ref[:, columns_at(j + head_columns // PAIR, PAIR)]
        values_turned = rotated_ref[:, columns_at(j + at_value // PAIR, PAIR)].T
        outs = []
        for head in range(2 * group):
            kv = head // group
            key, query = head_of(keys, kv), head_of(queries, head)
            value = values_turned[kv * HEAD_DIM : (kv + 1) * HEAD_DIM]
            parts, logs = [], []
            for b in range(2):
                reach = (b + 1) * block
                scores = scores_of(key[:reach], query[b * block : reach], length, b * block)
                best = jnp.max(scores, axis=0, keepdims=True)
                exponent = jnp.exp(scores - best)
                total = jnp.sum(exponent, axis=0, keepdims=True)
                chance = (exponent * (1.0 / total)).astype(bf16)
                parts.append(dot(value[:, :reach], chance))
                logs.append(best + jnp.log(total))
            outs.append(jnp.concatenate(parts, axis=1))
            log_ref[j, head : head + 1, :] = jnp.concatenate(logs, axis=1)
        mixed_ref[:, columns_at(j, group * PAIR)] = jnp.concatenate(outs, axis=0).T.astype(bf16)
        return carry

    lax.fori_loop(0, KV_HEADS // 2, attend, 0)


def router_kernel(
    tokens_ref, routes_ref, gains_ref, mixed_ref, output_ref, extra_ref,
    packet_ref, middle_ref, share_ref,
):
    width = tokens_ref.shape[1]

    def mix(c, carry):
        where = columns_at(c, TILE)
        branch = dot_turned(mixed_ref[...], output_ref[where, :])
        middle_ref[:, where] = tokens_ref[:, where].astype(f32) + residual_scale * branch
        return carry

    lax.fori_loop(0, width // TILE, mix, 0)
    middle = middle_ref[...]
    normed_two = (middle * row_scale_of(middle) * gains_ref[1:2, :]).astype(bf16)
    packet_ref[:, :width] = normed_two
    logits = dot(normed_two, extra_ref[...])
    lane = lax.broadcasted_iota(jnp.int32, logits.shape, 1)
    routed = lane == routes_ref[:, 0:1]
    for k in range(1, routes_ref.shape[1]):
        routed = routed | (lane == routes_ref[:, k : k + 1])
    best = jnp.max(jnp.where(routed, logits, masked_value), axis=1, keepdims=True)
    weights = jnp.where(routed, jnp.exp(jnp.where(routed, logits, best) - best), 0.0)
    shares = weights / jnp.sum(weights, axis=1, keepdims=True)
    share_ref[...] = shares
    high = shares.astype(bf16).astype(f32)
    packet_ref[:, width:] = (high + pltpu.roll(shares - high, EXPERTS, 1)).astype(bf16)


def column_of(row, lanes):
    return jnp.broadcast_to(row, (lanes, row.shape[1])).T


def middle_kernel(
    own_ref, near_top_ref, near_low_ref, far_top_ref, far_low_ref, packet_ref, middle_ref,
    cotangent_ref, share_ref, gains_ref, mixed_ref, output_ref, extra_ref,
    middle_grad_ref, mixed_grad_ref, pack_ref, back_ref, branch_ref, turned_ref,
):
    width = cotangent_ref.shape[1]
    half = own_ref.shape[0] // 2
    for place, near_ref, far_ref in (
        (pl.ds(0, half), near_top_ref, far_top_ref),
        (pl.ds(half, half), near_low_ref, far_low_ref),
    ):
        back_ref[place] = (
            own_ref[place].astype(f32) + near_ref[...].astype(f32) + far_ref[...].astype(f32)
        )
    shares = share_ref[...]
    share_grad = back_ref[:, width:]
    share_grad = share_grad + pltpu.roll(share_grad, EXTRA - EXPERTS, 1)
    weighted_mean = jnp.sum(shares * share_grad, axis=1, keepdims=True)
    logit_grad = (shares * (share_grad - weighted_mean)).astype(bf16)
    normed_grad = back_ref[:, :width] + dot_turned(logit_grad, extra_ref[...])
    middle = middle_ref[...]
    scale = row_scale_of(middle)
    scaled = middle * scale
    gain_grad = jnp.sum(normed_grad * scaled, axis=0, keepdims=True)
    weighted = normed_grad * gains_ref[1:2, :]
    correction = jnp.mean(weighted * middle, axis=1, keepdims=True)
    middle_grad = cotangent_ref[...].astype(f32) + scale * weighted - scaled * (scale * scale * correction)
    middle_grad_ref[...] = middle_grad
    branch_ref[...] = (residual_scale * middle_grad).astype(bf16)
    router_grad = dot(packet_ref[:, :width].T, logit_grad)
    lane = lax.broadcasted_iota(jnp.int32, router_grad.shape, 1)
    pack_ref[:, width:] = jnp.where(
        lane == EXPERTS, column_of(gain_grad, EXTRA), router_grad
    ).astype(bf16)
    turned_ref[...] = branch_ref[...].T

    def step(c, carry):
        where = columns_at(c, TILE)
        pack_ref[:, where] = dot(turned_ref[...], mixed_ref[:, where]).astype(bf16)
        mixed_grad_ref[:, where] = dot(branch_ref[...], output_ref[:, where]).astype(bf16)
        return carry

    lax.fori_loop(0, output_ref.shape[1] // TILE, step, 0)


def attention_back_kernel(
    length_ref, rotated_ref, mixed_grad_ref, log_ref, cosine_ref, sine_ref, grad_ref
):
    rows = rotated_ref.shape[0]
    head_columns, kv_columns = HEADS * HEAD_DIM, KV_HEADS * HEAD_DIM
    at_value = head_columns + kv_columns
    length = length_ref[0]
    group = HEADS // KV_HEADS
    block = rows // 2

    def attend(j, carry):
        wide = columns_at(j, group * PAIR)
        key_place = columns_at(j + head_columns // PAIR, PAIR)
        value_place = columns_at(j + at_value // PAIR, PAIR)
        queries, grads = rotated_ref[:, wide], mixed_grad_ref[:, wide]
        keys, values = rotated_ref[:, key_place], rotated_ref[:, value_place]
        keys_turned = keys.T
        query_grads, key_grads, value_grads = [], [], []
        for kv in range(2):
            key, value = head_of(keys, kv), head_of(values, kv)
            key_turned = keys_turned[kv * HEAD_DIM : (kv + 1) * HEAD_DIM]
            key_sums, value_sums = [], []
            for member in range(group):
                head = kv * group + member
                query, grad = head_of(queries, head), head_of(grads, head)
                query_parts = []
                for b in range(2):
                    reach = (b + 1) * block
                    query_block, grad_block = query[b * block : reach], grad[b * block : reach]
                    scores = scores_of(key[:reach], query_block, length, b * block)
                    chance = jnp.exp(scores - log_ref[j, head : head + 1, b * block : reach])
                    chance_grad = dot_turned(value[:reach], grad_block)
                    delta = jnp.sum(chance * chance_grad, axis=0, keepdims=True)
                    score_grad = (attention_scale * chance * (chance_grad - delta)).astype(bf16)
                    value_sums.append(dot(chance.astype(bf16), grad_block))
                    key_sums.append(dot(score_grad, query_block))
                    query_parts.append(dot(key_turned[:, :reach], score_grad))
                query_grads.append(jnp.concatenate(query_parts, axis=1))
            for sums, into in ((key_sums, key_grads), (value_sums, value_grads)):
                short = sum(sums[2::2], sums[0])
                long = sum(sums[3::2], sums[1])
                into.append(jnp.concatenate([short + long[:block], long[block:]], axis=0))
        query_grad = jnp.concatenate(query_grads, axis=0).T
        query_grad = query_grad * cosine_ref[...] - swap_halves(query_grad) * sine_ref[...]
        grad_ref[:, wide] = query_grad.astype(bf16)
        key_grad = jnp.concatenate(key_grads, axis=1)
        key_grad = key_grad * cosine_ref[:, :PAIR] - swap_halves(key_grad) * sine_ref[:, :PAIR]
        grad_ref[:, key_place] = key_grad.astype(bf16)
        grad_ref[:, value_place] = jnp.concatenate(value_grads, axis=1).astype(bf16)
        return carry

    lax.fori_loop(0, KV_HEADS // 2, attend, 0)


def inputs_kernel(
    tokens_ref, gains_ref, projected_ref, weight_ref, middle_grad_ref,
    grad_ref, pack_ref, normed_grad_ref, turned_ref,
):
    width = tokens_ref.shape[1]
    projections = projected_ref.shape[1]
    inputs = tokens_ref[...].astype(f32)
    scale = row_scale_of(inputs)
    scaled = inputs * scale
    turned_ref[...] = (scaled * gains_ref[0:1, :]).astype(bf16).T

    def to_weight(c, carry):
        where = columns_at(c, TILE)
        pack_ref[:, where] = dot(turned_ref[...], projected_ref[:, where]).astype(bf16)
        return carry

    def to_input(c, carry):
        where = columns_at(c, TILE)
        normed_grad_ref[:, where] = dot_turned(projected_ref[...], weight_ref[where, :])
        return carry

    lax.fori_loop(0, projections // TILE, to_weight, 0)
    lax.fori_loop(0, width // TILE, to_input, 0)
    normed_grad = normed_grad_ref[...]
    gain_grad = column_of(jnp.sum(normed_grad * scaled, axis=0, keepdims=True), EXTRA)
    lane = lax.broadcasted_iota(jnp.int32, gain_grad.shape, 1)
    pack_ref[:, projections:] = jnp.where(lane == 0, gain_grad, 0.0).astype(bf16)
    weighted = normed_grad * gains_ref[0:1, :]
    correction = jnp.mean(weighted * inputs, axis=1, keepdims=True)
    grad_ref[...] = middle_grad_ref[...] + scale * weighted - scaled * (scale * scale * correction)


def call_kernel(body, name, operands, out_shape, scratch, flops):
    specs, arrays = [], []
    for operand in operands:
        array, shape, index = operand
        if shape == "scalar":
            specs.append(pl.BlockSpec(memory_space=pltpu.SMEM))
        else:
            shape = array.shape if shape is None else shape
            index = (0,) * len(shape) if index is None else index
            specs.append(pl.BlockSpec(shape, lambda i, index=index: index))
        arrays.append(array)
    outs = [jax.ShapeDtypeStruct(shape, dtype) for shape, dtype in out_shape]
    return pl.pallas_call(
        body,
        grid=(1,),
        in_specs=specs,
        out_specs=[
            pl.BlockSpec(out.shape, lambda i, rank=len(out.shape): (0,) * rank) for out in outs
        ],
        out_shape=outs,
        scratch_shapes=[pltpu.VMEM(shape, dtype) for shape, dtype in scratch],
        compiler_params=pltpu.CompilerParams(vmem_limit_bytes=62 * 1024 * 1024),
        cost_estimate=pl.CostEstimate(
            flops=flops,
            bytes_accessed=sum(a.size * a.dtype.itemsize for a in arrays)
            + sum(o.size * o.dtype.itemsize for o in outs),
            transcendentals=0,
        ),
        name=name,
    )(*arrays)


def rope_lanes(row_count):
    cosine_table, sine_table = rope_tables(row_count)
    half_dim = HEAD_DIM // 2
    signed = jnp.concatenate([-sine_table[:, :half_dim], sine_table[:, half_dim:]], axis=1)
    repeats = TILE // HEAD_DIM
    return jnp.tile(cosine_table, (1, repeats)), jnp.tile(signed, (1, repeats))


def attention_forward(tokens, lengths, tables, gains, whole):
    rows, width = tokens.shape
    head_columns, kv_columns = HEADS * HEAD_DIM, KV_HEADS * HEAD_DIM
    projections = head_columns + 2 * kv_columns
    return call_kernel(
        attention_kernel,
        "attention_forward",
        [
            (lengths, "scalar", None), (tokens, None, None), (tables[0], None, None),
            (tables[1], None, None), (gains, None, None), (whole, (width, projections), (0, 0)),
        ],
        [
            ((rows, projections), bf16), ((rows, head_columns), bf16),
            ((KV_HEADS // 2, 2 * HEADS // KV_HEADS, rows), f32),
        ],
        [((rows, width), bf16)],
        8 * rows * width * head_columns,
    )


def output_blocks(whole):
    width = whole.shape[0]
    head_columns, kv_columns = HEADS * HEAD_DIM, KV_HEADS * HEAD_DIM
    at_output = head_columns + 2 * kv_columns
    return [
        (whole, (width, head_columns), (0, at_output // head_columns)),
        (whole, (width, EXTRA), (0, (at_output + head_columns) // EXTRA)),
    ]


def router_forward(tokens, routes, gains, mixed, whole):
    rows, width = tokens.shape
    return call_kernel(
        router_kernel,
        "router_forward",
        [(a, None, None) for a in (tokens, routes, gains, mixed)] + output_blocks(whole),
        [((rows, width + EXTRA), bf16), ((rows, width), f32), ((rows, EXTRA), f32)],
        [],
        2 * rows * width * mixed.shape[1],
    )


def middle_back(pieces, packet, middle, cotangent, shares, gains, mixed, whole):
    rows, width = cotangent.shape
    head_columns = HEADS * HEAD_DIM
    return call_kernel(
        middle_kernel,
        "middle_back",
        [(a, None, None) for a in (*pieces, packet, middle, cotangent, shares, gains, mixed)]
        + output_blocks(whole),
        [((rows, width), f32), ((rows, head_columns), bf16), ((width, head_columns + EXTRA), bf16)],
        [((rows, width + EXTRA), f32), ((rows, width), bf16), ((width, rows), bf16)],
        4 * rows * width * head_columns,
    )


def attention_back(lengths, rotated, mixed_grad, logs, tables):
    return call_kernel(
        attention_back_kernel,
        "attention_back",
        [
            (lengths, "scalar", None), (rotated, None, None), (mixed_grad, None, None),
            (logs, None, None), (tables[0], None, None), (tables[1], None, None),
        ],
        [(rotated.shape, bf16)],
        [],
        10 * rotated.shape[0] ** 2 * HEADS * HEAD_DIM,
    )[0]


def inputs_back(tokens, gains, projected_grad, whole, middle_grad):
    rows, width = tokens.shape
    projections = projected_grad.shape[1]
    return call_kernel(
        inputs_kernel,
        "inputs_back",
        [
            (tokens, None, None), (gains, None, None), (projected_grad, None, None),
            (whole, (width, projections), (0, 0)), (middle_grad, None, None),
        ],
        [((rows, width), f32), ((width, projections + EXTRA), bf16)],
        [((rows, width), f32), ((width, rows), bf16)],
        4 * rows * width * projections,
    )


def local(
    tokens,
    lengths,
    routes,
    attention_gain,
    query_weight,
    key_weight,
    value_weight,
    output_weight,
    expert_gain,
    router_weight,
    gate_weight,
    up_weight,
    down_weight,
    cotangent,
    *,
    count,
):
    links = Exchange(count)
    member, group, groups = links.member, links.group, links.groups
    row_count, width = tokens.shape
    shard = query_weight.shape[0]
    hidden = gate_weight.shape[2]
    head_columns, kv_columns = HEADS * HEAD_DIM, KV_HEADS * HEAD_DIM

    mine = jnp.stack([gate_weight, up_weight, down_weight.transpose(0, 2, 1)], axis=1)
    mine = mine.reshape(MEMBERS, LOCAL_EXPERTS, 3, shard, hidden)
    arrived = links.chip_parts(mine)

    packed = jnp.concatenate(
        [
            query_weight,
            key_weight,
            value_weight,
            output_weight.T,
            router_weight,
            attention_gain[:, None],
            expert_gain[:, None],
            jnp.zeros((shard, EXTRA - EXPERTS - 2), bf16),
        ],
        axis=1,
    )
    pack_width = packed.shape[1]
    column = links.direct_gather(packed).reshape(groups * shard, pack_width)
    arrived, column = lax.optimization_barrier((arrived, column))
    half = column.shape[0] // 2
    top, low = column[:half], column[half:]
    near_top, far_low = links.swap(top, 2), links.swap(low, 4)
    near_low, far_top = links.swap(low, 2), links.swap(top, 4)
    kept, other = links.keep_parts(arrived)
    kept, other, near_top, far_low = lax.optimization_barrier((kept, other, near_top, far_low))
    shelf = links.in_order(kept, other).transpose(1, 2, 0, 3, 4)
    shelf = shelf.reshape(LOCAL_EXPERTS, 3, MEMBERS * shard, hidden)
    cross_top, cross_low = links.swap(near_top, 4), links.swap(far_low, 2)
    top, low, near_top = lax.optimization_barrier((top, low, near_top))
    spread = {
        0: (top, low), 2: (near_top, near_low), 4: (far_top, far_low), 6: (cross_top, cross_low)
    }
    lines = [[m + MEMBERS * g for g in range(groups)] for m in range(MEMBERS)]
    own_full = [
        lax.all_gather(shelf[n], "fsdp", axis_index_groups=lines) for n in range(LOCAL_EXPERTS)
    ]
    whole = jnp.zeros((groups, MEMBERS, shard, pack_width), bf16)
    for k in range(MEMBERS):
        parts = spread[k & 6]
        if k & 1:
            parts = [links.swap(part, 1) for part in parts]
        part = jnp.concatenate(parts, axis=0).reshape(groups, shard, pack_width)
        whole = lax.dynamic_update_index_in_dim(whole, part, member ^ k, 1)
    whole = whole.reshape(width, pack_width)
    at_output = head_columns + 2 * kv_columns
    at_extra = at_output + head_columns
    gains = whole[:, at_extra + EXPERTS : at_extra + EXPERTS + 2].astype(f32).T

    late_cotangent, whole = lax.optimization_barrier((cotangent, whole))
    cot_near, cot_far = links.swap(late_cotangent, 2), links.swap(late_cotangent, 4)

    tables = rope_lanes(row_count)
    rotated, mixed, logs = attention_forward(tokens, lengths, tables, gains, whole)
    cot_near, cot_far, mixed = lax.optimization_barrier((cot_near, cot_far, mixed))
    packet, middle, shares = router_forward(tokens, routes, gains, mixed, whole)
    near, far = links.swap(packet, 2), links.swap(packet, 4)
    own_full[0], packet, cot_near, cot_far = lax.optimization_barrier(
        (own_full[0], packet, cot_near, cot_far)
    )
    cot_cross = links.cross_of(cot_near, cot_far)

    names = [
        jnp.stack([member, member ^ 1]).astype(jnp.int32) * LOCAL_EXPERTS + n
        for n in range(LOCAL_EXPERTS)
    ]
    rows_own = [(packet,)], [(cotangent,)]
    first_full = own_full[0], links.swap(own_full[0], 1)
    own_out, own_back, *zero = run_experts(names[0], *rows_own, first_full)
    near, far, cot_cross, own_back = lax.optimization_barrier((near, far, cot_cross, own_back))
    cross = links.cross_of(near, far)
    rows_chips = [cross, (near,), (far,)], [cot_cross, (cot_near,), (cot_far,)]
    chip_out, chip_back, *zero = run_experts(names[0], *rows_chips, first_full, zero, True)
    own_full[1], chip_back = lax.optimization_barrier((own_full[1], chip_back))
    second_full = own_full[1], links.swap(own_full[1], 1)
    chip_out, chip_back, *one = run_experts(
        names[1], *rows_chips, second_full, None, False, (chip_out, chip_back)
    )

    def join_cores(own, other):
        return (own.astype(f32) + links.swap(other, 1).astype(f32)).astype(bf16)

    def reduce_groups(total):
        return lax.psum_scatter(total, "fsdp", scatter_dimension=0, axis_index_groups=lines)

    zero = join_cores(*zero)
    zero, chip_back = lax.optimization_barrier((zero, chip_back))
    shelf_zero = reduce_groups(zero)
    half = row_count // 2
    cross_top, cross_low = links.send_cross(chip_back[0])
    near_top, far_low = links.swap(chip_back[1, :half], 2), links.swap(chip_back[2, half:], 4)
    own_out, own_back, *one = run_experts(
        names[1], *rows_own, second_full, one, True, (own_out, own_back)
    )
    cross_top, cross_low, near_top, far_low, own_back = lax.optimization_barrier(
        (cross_top, cross_low, near_top, far_low, own_back)
    )
    near_low = (chip_back[1, half:].astype(f32) + cross_low.astype(f32)).astype(bf16)
    far_top = (chip_back[2, :half].astype(f32) + cross_top.astype(f32)).astype(bf16)
    near_low, far_top, one = lax.optimization_barrier((near_low, far_top, one))
    near_low, far_top = links.swap(near_low, 2), links.swap(far_top, 4)
    one = join_cores(*one)
    back_pieces = near_top, near_low, far_top, far_low
    out_cross, back_pieces = lax.optimization_barrier((chip_out[0], back_pieces))
    out_cross = links.send_cross(out_cross)

    core, chip = member % 2, member // 2

    def pack_cores(pack):
        columns = pack.shape[1]
        pack = pack.reshape(groups, MEMBERS // 2, 2, shard, columns)
        own = lax.dynamic_index_in_dim(pack, core, 2, keepdims=False)
        other = links.swap(lax.dynamic_index_in_dim(pack, 1 - core, 2, keepdims=False), 1)

        joined = own.astype(f32) + other.astype(f32)
        return [
            lax.dynamic_index_in_dim(joined, chip ^ bits, 1, keepdims=False).reshape(
                groups * shard, columns
            )
            for bits in range(MEMBERS // 2)
        ]

    def pack_cross(parts):
        return links.send_cross(parts[3].astype(bf16))

    def pack_add(parts, cross):
        return links.add_cross(parts[1].astype(bf16), parts[2].astype(bf16), cross)

    def pack_end(parts, near, far):
        near, far = links.swap(near, 2), links.swap(far, 4)
        total = parts[0] + near.astype(f32) + far.astype(f32)
        return links.direct_reduce(total.reshape(groups, shard, total.shape[1]))

    middle_grad, mixed_grad, first_pack = middle_back(
        (own_back[0], *back_pieces), packet, middle, cotangent, shares, gains, mixed, whole
    )
    out_near, out_far = links.add_cross(chip_out[1], chip_out[2], out_cross)
    out_near, out_far, one, mixed_grad = lax.optimization_barrier(
        (out_near, out_far, one, mixed_grad)
    )
    shelf_one = reduce_groups(one)
    out_near, out_far = links.swap(out_near, 2), links.swap(out_far, 4)
    first_parts = pack_cores(first_pack)
    projected_grad = attention_back(lengths, rotated, mixed_grad, logs, tables)
    out_near, out_far, shelf_zero, first_parts, projected_grad = lax.optimization_barrier(
        (out_near, out_far, shelf_zero, first_parts, projected_grad)
    )
    first_cross = pack_cross(first_parts)
    grad_tokens, second_pack = inputs_back(tokens, gains, projected_grad, whole, middle_grad)
    first_near, first_far = pack_add(first_parts, first_cross)
    first_near, first_far, second_pack = lax.optimization_barrier(
        (first_near, first_far, second_pack)
    )
    second_parts = pack_cores(second_pack)
    first_total = pack_end(first_parts, first_near, first_far)
    second_near, second_far = pack_add(second_parts, pack_cross(second_parts))
    second_near, second_far, shelf_one = lax.optimization_barrier(
        (second_near, second_far, shelf_one)
    )
    second_total = pack_end(second_parts, second_near, second_far)
    out_pieces = (own_out[0], out_near, out_far)
    layer_out = (middle + sum(piece.astype(f32) for piece in out_pieces)).astype(bf16)
    shelf_grad = jnp.stack([shelf_zero, shelf_one])
    shelf_grad = shelf_grad.reshape(LOCAL_EXPERTS, 3, MEMBERS, shard, hidden)
    expert_shards = links.in_order(
        *links.keep_parts(links.chip_parts(shelf_grad.transpose(2, 0, 1, 3, 4)))
    ).astype(f32)
    expert_shards = expert_shards.reshape(EXPERTS, 3, shard, hidden)
    return (
        layer_out,
        grad_tokens,
        second_total[:, at_output],
        second_total[:, :head_columns],
        second_total[:, head_columns : head_columns + kv_columns],
        second_total[:, head_columns + kv_columns : at_output],
        first_total[:, :head_columns].T,
        first_total[:, head_columns + EXPERTS],
        first_total[:, head_columns : head_columns + EXPERTS],
        expert_shards[:, 0],
        expert_shards[:, 1],
        expert_shards[:, 2].transpose(0, 2, 1),
    )


def solution(mesh):
    count = mesh.shape["fsdp"]
    placed = (
        P("fsdp", None),
        P("fsdp"),
        P("fsdp", None),
        P("fsdp"),
        P("fsdp", None),
        P("fsdp", None),
        P("fsdp", None),
        P(None, "fsdp"),
        P("fsdp"),
        P("fsdp", None),
        P(None, "fsdp", None),
        P(None, "fsdp", None),
        P(None, None, "fsdp"),
        P("fsdp", None),
    )

    def body(*args):
        return local(*args, count=count)

    return jax.shard_map(
        body,
        mesh=mesh,
        in_specs=placed,
        out_specs=(
            P("fsdp", None),
            P("fsdp", None),
            P("fsdp"),
            P("fsdp", None),
            P("fsdp", None),
            P("fsdp", None),
            P(None, "fsdp"),
            P("fsdp"),
            P("fsdp", None),
            P(None, "fsdp", None),
            P(None, "fsdp", None),
            P(None, None, "fsdp"),
        ),
        check_vma=False,
    )
```

```python
import functools

import jax
import jax.numpy as jnp
from jax import lax
from jax.experimental import pallas as pl
from jax.experimental.pallas import tpu as pltpu
from jax.sharding import PartitionSpec as P

HEADS = 16
KV_HEADS = 8
HEAD_DIM = 64
EXPERTS = 16
MEMBERS = 8
LOCAL_EXPERTS = EXPERTS // MEMBERS
EXTRA = 128

norm_eps = 1e-06
attention_scale = 0.015625
residual_scale = 0.22
rope_base = 10000.0
masked_value = -1e30
f32 = jnp.float32
bf16 = jnp.bfloat16


def rope_tables(row_count):
    half_dim = HEAD_DIM // 2
    frequency = rope_base ** (-2.0 * jnp.arange(half_dim, dtype=jnp.float32) / HEAD_DIM)
    angles = jnp.arange(row_count, dtype=jnp.float32)[:, None] * frequency[None, :]
    angles = jnp.concatenate([angles, angles], axis=1)
    return (jnp.cos(angles), jnp.sin(angles))


class Exchange:
    def __init__(self, count):
        self.count = count
        self.groups = count // MEMBERS
        index = lax.axis_index("fsdp")
        self.member = index % MEMBERS
        self.group = index // MEMBERS

    def swap(self, value, bits):
        return lax.ppermute(value, "fsdp", [(i, i ^ bits) for i in range(self.count)])

    def direct_gather(self, piece):
        stack = jnp.zeros((self.groups,) + piece.shape, piece.dtype)
        for bits in range(self.groups):
            part = self.swap(piece, bits * MEMBERS) if bits else piece
            stack = lax.dynamic_update_index_in_dim(stack, part, self.group ^ bits, 0)
        return stack

    def direct_reduce(self, terms):
        total = lax.dynamic_index_in_dim(terms, self.group, 0, keepdims=False)
        for bits in range(1, self.groups):
            part = lax.dynamic_index_in_dim(terms, self.group ^ bits, 0, keepdims=False)
            total = total + self.swap(part.astype(bf16), bits * MEMBERS).astype(f32)
        return total

    def send_cross(self, block):
        half = block.shape[0] // 2
        return self.swap(block[:half], 2), self.swap(block[half:], 4)

    def add_cross(self, near, far, cross):
        half = near.shape[0] // 2
        cross_top, cross_low = cross
        near_low = (near[half:].astype(f32) + cross_low.astype(f32)).astype(bf16)
        far_top = (far[:half].astype(f32) + cross_top.astype(f32)).astype(bf16)
        return (
            jnp.concatenate([near[:half], near_low], axis=0),
            jnp.concatenate([far_top, far[half:]], axis=0),
        )

    def chip_parts(self, parts):
        chips = parts.reshape((MEMBERS // 2, 2) + parts.shape[1:])
        chip = self.member // 2
        found = []
        for bits in range(MEMBERS // 2):
            part = lax.dynamic_index_in_dim(chips, chip ^ bits, 0, keepdims=False)
            found.append(self.swap(part, 2 * bits) if bits else part)
        return found

    def keep_parts(self, found):
        chip, core = self.member // 2, self.member % 2
        arrived = jnp.zeros((MEMBERS // 2,) + found[0].shape, found[0].dtype)
        for bits, part in enumerate(found):
            arrived = lax.dynamic_update_index_in_dim(arrived, part, chip ^ bits, 0)
        kept = lax.dynamic_index_in_dim(arrived, core, 1, keepdims=False)
        other = self.swap(lax.dynamic_index_in_dim(arrived, 1 - core, 1, keepdims=False), 1)
        return kept, other

    def send_parts(self, parts):
        kept, other = self.keep_parts(self.chip_parts(parts))
        core = self.member % 2
        even = jnp.where(core == 0, kept, other)
        odd = jnp.where(core == 0, other, kept)
        return jnp.stack([even, odd], axis=1).reshape(parts.shape)


def dot(left, right):
    return jnp.dot(left, right, preferred_element_type=f32)


def dot_turned(left, right):
    return lax.dot_general(left, right, (((1,), (1,)), ((), ())), preferred_element_type=f32)


def expert_kernel(names_ref, *refs, layout, fresh, last, carried):
    refs = list(refs)
    experts = range(names_ref.shape[0])
    packet_parts = [[refs.pop(0) for _ in range(number)] for number in layout]
    cotangent_parts = [[refs.pop(0) for _ in range(number)] for number in layout]
    weight_parts = [refs.pop(0) for _ in experts]
    prior_refs = [None if fresh else refs.pop(0) for _ in experts]
    carried_out, carried_back = (refs.pop(0), refs.pop(0)) if carried else (None, None)
    out_ref, back_ref = refs.pop(0), refs.pop(0)
    result_refs = [refs.pop(0) for _ in experts]
    grad_refs = [refs.pop(0) for _ in experts] if last else result_refs
    packet_buffer, cotangent_buffer, weight_ref, packet_turned, cotangent_turned, sums = refs[:6]
    block_sem, weight_sem, prior_sem = refs[6:]
    rows, width = cotangent_buffer.shape[1:]
    groups, _, depth, _ = weight_parts[0].shape
    blocks = len(layout)
    at = pl.program_id(0)

    def block_copies(block):
        copies = []
        for kind, (parts, buffer) in enumerate(
            ((packet_parts, packet_buffer), (cotangent_parts, cotangent_buffer))
        ):
            size = rows // layout[block]
            for number, part in enumerate(parts[block]):
                place = buffer.at[block, pl.ds(number * size, size)]
                copies.append(
                    pltpu.make_async_copy(part, place, block_sem.at[block, 2 * kind + number])
                )
        return copies

    def weight_copies(n):
        return [
            pltpu.make_async_copy(
                weight_parts[n].at[g], weight_ref.at[n, :, pl.ds(g * depth, depth)], weight_sem.at[n, g]
            )
            for g in range(groups)
        ]

    def prior_copy(n):
        return pltpu.make_async_copy(prior_refs[n], grad_refs[n], prior_sem.at[n])

    @pl.when(at == 0)
    def _():
        for copy in block_copies(0):
            copy.start()
        for n in experts:
            for copy in weight_copies(n):
                copy.start()
        for n in experts:
            if fresh:
                grad_refs[n][...] = jnp.zeros_like(grad_refs[n])
            else:
                prior_copy(n).start()
        for block in range(1, blocks):
            for copy in block_copies(block):
                copy.start()
        for n in experts:
            for copy in weight_copies(n):
                copy.wait()

    for block in range(blocks):

        @pl.when(at == block)
        def _():
            for copy in block_copies(block):
                copy.wait()

    lane = lax.broadcasted_iota(jnp.int32, (rows, EXTRA), 1)
    normed = packet_buffer[at, :, :width]
    upstream = cotangent_buffer[at]
    shares = packet_buffer[at, :, width:].astype(f32)
    extra = jnp.zeros((rows, EXTRA), f32)
    packet_turned[...] = normed.T
    cotangent_turned[...] = upstream.T
    begun = []
    for n in experts:
        begun.append(
            (
                dot(normed, weight_ref[n, 0]),
                dot(normed, weight_ref[n, 1]),
                dot(upstream, weight_ref[n, 2]),
            )
        )
    if not fresh:

        @pl.when(at == 0)
        def _():
            for n in experts:
                prior_copy(n).wait()

    for n in experts:
        gate_pre, up_pre, inner_raw = begun[n]
        expert = names_ref[n]
        is_high, is_low = lane == expert, lane == expert + EXPERTS
        share = jnp.sum(jnp.where(is_high | is_low, shares, 0.0), axis=1, keepdims=True)
        sigmoid_gate = jax.nn.sigmoid(gate_pre)
        activated = gate_pre * sigmoid_gate
        inner = (activated * up_pre).astype(bf16).astype(f32)
        share_grad = residual_scale * jnp.sum(inner * inner_raw, axis=1, keepdims=True)
        scaled = share * residual_scale
        inner_grad = inner_raw * scaled
        gate_grad = (
            inner_grad * up_pre * (sigmoid_gate + activated * (1.0 - sigmoid_gate))
        ).astype(bf16)
        up_grad = (inner_grad * activated).astype(bf16)
        inner_shared = (inner * scaled).astype(bf16)
        out_term = dot_turned(inner_shared, weight_ref[n, 2])
        back_term = dot_turned(gate_grad, weight_ref[n, 0]) + dot_turned(up_grad, weight_ref[n, 1])
        if n == 0:
            sums[0], sums[1] = out_term, back_term
        else:
            sums[0] += out_term
            sums[1] += back_term
        grad_refs[n][0] += dot(packet_turned[...], gate_grad)
        grad_refs[n][1] += dot(packet_turned[...], up_grad)
        grad_refs[n][2] += dot(cotangent_turned[...], inner_shared)
        high = share_grad.astype(bf16).astype(f32)
        extra = extra + jnp.where(is_high, high, 0.0) + jnp.where(is_low, share_grad - high, 0.0)
    out_total, back_total = sums[0], sums[1]
    if carried:
        out_total = out_total + carried_out[0].astype(f32)
        back_total = back_total + carried_back[0, :, :width].astype(f32)
        extra = extra + carried_back[0, :, width:].astype(f32)
    out_ref[0] = out_total.astype(bf16)
    back_ref[0, :, :width] = back_total.astype(bf16)
    back_ref[0, :, width:] = extra.astype(bf16)

    if last:

        @pl.when(at == blocks - 1)
        def _():
            for n in experts:
                for g in range(groups):
                    result_refs[n][g] = grad_refs[n][:, pl.ds(g * depth, depth)].astype(bf16)


def run_experts(names, packets, cotangents, weights, priors=None, last=False, carried=None):
    layout = tuple(len(parts) for parts in packets)
    blocks = len(layout)
    rows = sum(part.shape[0] for part in packets[0])
    wide, width = packets[0][0].shape[1], cotangents[0][0].shape[1]
    groups, _, depth, hidden = weights[0].shape
    grad_shape = (3, width, hidden)
    fresh = priors is None
    count = len(weights)
    operands = [part for parts in packets for part in parts]
    operands += [part for parts in cotangents for part in parts]
    operands += list(weights) + list(priors or ())

    def whole(shape):
        return pl.BlockSpec(
            shape, lambda i, s, rank=len(shape): (0,) * rank, pipeline_mode=pl.Buffered(1)
        )

    term_specs = [
        pl.BlockSpec((1, rows, columns), lambda i, s: (i, 0, 0)) for columns in (width, wide)
    ]
    in_specs = [pl.BlockSpec(memory_space=pl.ANY)] * len(operands)
    if carried is not None:
        in_specs += term_specs
        operands += list(carried)
    grads = [((groups, 3, depth, hidden), bf16) if last else (grad_shape, f32)] * count
    scratch = [pltpu.VMEM(grad_shape, f32)] * (count if last else 0)
    scratch += [
        pltpu.VMEM((blocks, rows, wide), bf16),
        pltpu.VMEM((blocks, rows, width), bf16),
        pltpu.VMEM((count,) + grad_shape, bf16),
        pltpu.VMEM((width, rows), bf16),
        pltpu.VMEM((width, rows), bf16),
        pltpu.VMEM((2, rows, width), f32),
        pltpu.SemaphoreType.DMA((blocks, 4)),
        pltpu.SemaphoreType.DMA((count, groups)),
        pltpu.SemaphoreType.DMA((count,)),
    ]
    return pl.pallas_call(
        functools.partial(
            expert_kernel, layout=layout, fresh=fresh, last=last, carried=carried is not None
        ),
        grid_spec=pltpu.PrefetchScalarGridSpec(
            num_scalar_prefetch=1,
            grid=(blocks,),
            in_specs=in_specs,
            out_specs=term_specs + [whole(shape) for shape, _ in grads],
            scratch_shapes=scratch,
        ),
        out_shape=[
            jax.ShapeDtypeStruct((blocks, rows, columns), bf16) for columns in (width, wide)
        ]
        + [jax.ShapeDtypeStruct(shape, dtype) for shape, dtype in grads],
        compiler_params=pltpu.CompilerParams(vmem_limit_bytes=62 * 1024 * 1024),
        cost_estimate=pl.CostEstimate(
            flops=blocks * count * 9 * 2 * rows * width * hidden,
            bytes_accessed=blocks * rows * width * 8 + 18 * count * width * hidden,
            transcendentals=blocks * count * rows * hidden,
        ),
        name="experts",
    )(names, *operands)


TILE = 256
PAIR = 2 * HEAD_DIM


def columns_at(index, size):
    return pl.ds(pl.multiple_of(index * size, size), size)


def swap_halves(values):
    width, half_dim = values.shape[1], HEAD_DIM // 2
    lane = lax.broadcasted_iota(jnp.int32, values.shape, 1)
    return jnp.where(
        lane % HEAD_DIM < half_dim,
        pltpu.roll(values, width - half_dim, 1),
        pltpu.roll(values, half_dim, 1),
    )


def row_scale_of(values):
    return lax.rsqrt(jnp.mean(values * values, axis=1, keepdims=True) + norm_eps)


def scores_of(keys, queries, length, first_query):
    scores = attention_scale * dot_turned(keys, queries)
    key_at = lax.broadcasted_iota(jnp.int32, scores.shape, 0)
    query_at = lax.broadcasted_iota(jnp.int32, scores.shape, 1) + first_query
    return jnp.where((key_at <= query_at) & (key_at < length), scores, masked_value)


def head_of(block, index):
    return block[:, index * HEAD_DIM : (index + 1) * HEAD_DIM]


def attention_kernel(
    length_ref, tokens_ref, cosine_ref, sine_ref, gains_ref, weight_ref,
    rotated_ref, mixed_ref, log_ref, normed_ref,
):
    rows = tokens_ref.shape[0]
    head_columns, kv_columns = HEADS * HEAD_DIM, KV_HEADS * HEAD_DIM
    at_value = head_columns + kv_columns
    at_output = at_value + kv_columns
    length = length_ref[0]
    group = HEADS // KV_HEADS

    inputs = tokens_ref[...].astype(f32)
    normed_ref[...] = (inputs * row_scale_of(inputs) * gains_ref[0:1, :]).astype(bf16)

    def project_turned(c, carry):
        where = columns_at(c, TILE)
        value = dot(normed_ref[...], weight_ref[:, where])
        value = value * cosine_ref[...] + swap_halves(value) * sine_ref[...]
        rotated_ref[:, where] = value.astype(bf16)
        return carry

    def project(c, carry):
        where = columns_at(c, TILE)
        rotated_ref[:, where] = dot(normed_ref[...], weight_ref[:, where]).astype(bf16)
        return carry

    lax.fori_loop(0, at_value // TILE, project_turned, 0)
    lax.fori_loop(at_value // TILE, at_output // TILE, project, 0)

    block = rows // 2

    def attend(j, carry):
        queries = rotated_ref[:, columns_at(j, group * PAIR)]
        keys = rotated_ref[:, columns_at(j + head_columns // PAIR, PAIR)]
        values_turned = rotated_ref[:, columns_at(j + at_value // PAIR, PAIR)].T
        outs = []
        for head in range(2 * group):
            kv = head // group
            key, query = head_of(keys, kv), head_of(queries, head)
            value = values_turned[kv * HEAD_DIM : (kv + 1) * HEAD_DIM]
            parts, logs = [], []
            for b in range(2):
                reach = (b + 1) * block
                scores = scores_of(key[:reach], query[b * block : reach], length, b * block)
                best = jnp.max(scores, axis=0, keepdims=True)
                exponent = jnp.exp(scores - best)
                total = jnp.sum(exponent, axis=0, keepdims=True)
                chance = (exponent * (1.0 / total)).astype(bf16)
                parts.append(dot(value[:, :reach], chance))
                logs.append(best + jnp.log(total))
            outs.append(jnp.concatenate(parts, axis=1))
            log_ref[j, head : head + 1, :] = jnp.concatenate(logs, axis=1)
        mixed_ref[:, columns_at(j, group * PAIR)] = jnp.concatenate(outs, axis=0).T.astype(bf16)
        return carry

    lax.fori_loop(0, KV_HEADS // 2, attend, 0)


def router_kernel(
    tokens_ref, routes_ref, gains_ref, mixed_ref, output_ref, extra_ref,
    packet_ref, middle_ref, share_ref,
):
    width = tokens_ref.shape[1]

    def mix(c, carry):
        where = columns_at(c, TILE)
        branch = dot_turned(mixed_ref[...], output_ref[where, :])
        middle_ref[:, where] = tokens_ref[:, where].astype(f32) + residual_scale * branch
        return carry

    lax.fori_loop(0, width // TILE, mix, 0)
    middle = middle_ref[...]
    normed_two = (middle * row_scale_of(middle) * gains_ref[1:2, :]).astype(bf16)
    packet_ref[:, :width] = normed_two
    logits = dot(normed_two, extra_ref[...])
    lane = lax.broadcasted_iota(jnp.int32, logits.shape, 1)
    routed = lane == routes_ref[:, 0:1]
    for k in range(1, routes_ref.shape[1]):
        routed = routed | (lane == routes_ref[:, k : k + 1])
    best = jnp.max(jnp.where(routed, logits, masked_value), axis=1, keepdims=True)
    weights = jnp.where(routed, jnp.exp(jnp.where(routed, logits, best) - best), 0.0)
    shares = weights / jnp.sum(weights, axis=1, keepdims=True)
    share_ref[...] = shares
    high = shares.astype(bf16).astype(f32)
    packet_ref[:, width:] = (high + pltpu.roll(shares - high, EXPERTS, 1)).astype(bf16)


def column_of(row, lanes):
    return jnp.broadcast_to(row, (lanes, row.shape[1])).T


def middle_kernel(
    own_ref, near_top_ref, near_low_ref, far_top_ref, far_low_ref, packet_ref, middle_ref,
    cotangent_ref, share_ref, gains_ref, mixed_ref, output_ref, extra_ref,
    middle_grad_ref, mixed_grad_ref, pack_ref, back_ref, branch_ref, turned_ref,
):
    width = cotangent_ref.shape[1]
    half = own_ref.shape[0] // 2
    for place, near_ref, far_ref in (
        (pl.ds(0, half), near_top_ref, far_top_ref),
        (pl.ds(half, half), near_low_ref, far_low_ref),
    ):
        back_ref[place] = (
            own_ref[place].astype(f32) + near_ref[...].astype(f32) + far_ref[...].astype(f32)
        )
    shares = share_ref[...]
    share_grad = back_ref[:, width:]
    share_grad = share_grad + pltpu.roll(share_grad, EXTRA - EXPERTS, 1)
    weighted_mean = jnp.sum(shares * share_grad, axis=1, keepdims=True)
    logit_grad = (shares * (share_grad - weighted_mean)).astype(bf16)
    normed_grad = back_ref[:, :width] + dot_turned(logit_grad, extra_ref[...])
    middle = middle_ref[...]
    scale = row_scale_of(middle)
    scaled = middle * scale
    gain_grad = jnp.sum(normed_grad * scaled, axis=0, keepdims=True)
    weighted = normed_grad * gains_ref[1:2, :]
    correction = jnp.mean(weighted * middle, axis=1, keepdims=True)
    middle_grad = cotangent_ref[...].astype(f32) + scale * weighted - scaled * (scale * scale * correction)
    middle_grad_ref[...] = middle_grad
    branch_ref[...] = (residual_scale * middle_grad).astype(bf16)
    router_grad = dot(packet_ref[:, :width].T, logit_grad)
    lane = lax.broadcasted_iota(jnp.int32, router_grad.shape, 1)
    pack_ref[:, width:] = jnp.where(
        lane == EXPERTS, column_of(gain_grad, EXTRA), router_grad
    ).astype(bf16)
    turned_ref[...] = branch_ref[...].T

    def step(c, carry):
        where = columns_at(c, TILE)
        pack_ref[:, where] = dot(turned_ref[...], mixed_ref[:, where]).astype(bf16)
        mixed_grad_ref[:, where] = dot(branch_ref[...], output_ref[:, where]).astype(bf16)
        return carry

    lax.fori_loop(0, output_ref.shape[1] // TILE, step, 0)


def attention_back_kernel(
    length_ref, rotated_ref, mixed_grad_ref, log_ref, cosine_ref, sine_ref, grad_ref
):
    rows = rotated_ref.shape[0]
    head_columns, kv_columns = HEADS * HEAD_DIM, KV_HEADS * HEAD_DIM
    at_value = head_columns + kv_columns
    length = length_ref[0]
    group = HEADS // KV_HEADS
    block = rows // 2

    def attend(j, carry):
        wide = columns_at(j, group * PAIR)
        key_place = columns_at(j + head_columns // PAIR, PAIR)
        value_place = columns_at(j + at_value // PAIR, PAIR)
        queries, grads = rotated_ref[:, wide], mixed_grad_ref[:, wide]
        keys, values = rotated_ref[:, key_place], rotated_ref[:, value_place]
        keys_turned = keys.T
        query_grads, key_grads, value_grads = [], [], []
        for kv in range(2):
            key, value = head_of(keys, kv), head_of(values, kv)
            key_turned = keys_turned[kv * HEAD_DIM : (kv + 1) * HEAD_DIM]
            key_sums, value_sums = [], []
            for member in range(group):
                head = kv * group + member
                query, grad = head_of(queries, head), head_of(grads, head)
                query_parts = []
                for b in range(2):
                    reach = (b + 1) * block
                    query_block, grad_block = query[b * block : reach], grad[b * block : reach]
                    scores = scores_of(key[:reach], query_block, length, b * block)
                    chance = jnp.exp(scores - log_ref[j, head : head + 1, b * block : reach])
                    chance_grad = dot_turned(value[:reach], grad_block)
                    delta = jnp.sum(chance * chance_grad, axis=0, keepdims=True)
                    score_grad = (attention_scale * chance * (chance_grad - delta)).astype(bf16)
                    value_sums.append(dot(chance.astype(bf16), grad_block))
                    key_sums.append(dot(score_grad, query_block))
                    query_parts.append(dot(key_turned[:, :reach], score_grad))
                query_grads.append(jnp.concatenate(query_parts, axis=1))
            for sums, into in ((key_sums, key_grads), (value_sums, value_grads)):
                short = sum(sums[2::2], sums[0])
                long = sum(sums[3::2], sums[1])
                into.append(jnp.concatenate([short + long[:block], long[block:]], axis=0))
        query_grad = jnp.concatenate(query_grads, axis=0).T
        query_grad = query_grad * cosine_ref[...] - swap_halves(query_grad) * sine_ref[...]
        grad_ref[:, wide] = query_grad.astype(bf16)
        key_grad = jnp.concatenate(key_grads, axis=1)
        key_grad = key_grad * cosine_ref[:, :PAIR] - swap_halves(key_grad) * sine_ref[:, :PAIR]
        grad_ref[:, key_place] = key_grad.astype(bf16)
        grad_ref[:, value_place] = jnp.concatenate(value_grads, axis=1).astype(bf16)
        return carry

    lax.fori_loop(0, KV_HEADS // 2, attend, 0)


def inputs_kernel(
    tokens_ref, gains_ref, projected_ref, weight_ref, middle_grad_ref,
    grad_ref, pack_ref, normed_grad_ref, turned_ref,
):
    width = tokens_ref.shape[1]
    projections = projected_ref.shape[1]
    inputs = tokens_ref[...].astype(f32)
    scale = row_scale_of(inputs)
    scaled = inputs * scale
    turned_ref[...] = (scaled * gains_ref[0:1, :]).astype(bf16).T

    def to_weight(c, carry):
        where = columns_at(c, TILE)
        pack_ref[:, where] = dot(turned_ref[...], projected_ref[:, where]).astype(bf16)
        return carry

    def to_input(c, carry):
        where = columns_at(c, TILE)
        normed_grad_ref[:, where] = dot_turned(projected_ref[...], weight_ref[where, :])
        return carry

    lax.fori_loop(0, projections // TILE, to_weight, 0)
    lax.fori_loop(0, width // TILE, to_input, 0)
    normed_grad = normed_grad_ref[...]
    gain_grad = column_of(jnp.sum(normed_grad * scaled, axis=0, keepdims=True), EXTRA)
    lane = lax.broadcasted_iota(jnp.int32, gain_grad.shape, 1)
    pack_ref[:, projections:] = jnp.where(lane == 0, gain_grad, 0.0).astype(bf16)
    weighted = normed_grad * gains_ref[0:1, :]
    correction = jnp.mean(weighted * inputs, axis=1, keepdims=True)
    grad_ref[...] = middle_grad_ref[...] + scale * weighted - scaled * (scale * scale * correction)


def call_kernel(body, name, operands, out_shape, scratch, flops):
    specs, arrays = [], []
    for operand in operands:
        array, shape, index = operand
        if shape == "scalar":
            specs.append(pl.BlockSpec(memory_space=pltpu.SMEM))
        else:
            shape = array.shape if shape is None else shape
            index = (0,) * len(shape) if index is None else index
            specs.append(pl.BlockSpec(shape, lambda i, index=index: index))
        arrays.append(array)
    outs = [jax.ShapeDtypeStruct(shape, dtype) for shape, dtype in out_shape]
    return pl.pallas_call(
        body,
        grid=(1,),
        in_specs=specs,
        out_specs=[
            pl.BlockSpec(out.shape, lambda i, rank=len(out.shape): (0,) * rank) for out in outs
        ],
        out_shape=outs,
        scratch_shapes=[pltpu.VMEM(shape, dtype) for shape, dtype in scratch],
        compiler_params=pltpu.CompilerParams(vmem_limit_bytes=62 * 1024 * 1024),
        cost_estimate=pl.CostEstimate(
            flops=flops,
            bytes_accessed=sum(a.size * a.dtype.itemsize for a in arrays)
            + sum(o.size * o.dtype.itemsize for o in outs),
            transcendentals=0,
        ),
        name=name,
    )(*arrays)


def rope_lanes(row_count):
    cosine_table, sine_table = rope_tables(row_count)
    half_dim = HEAD_DIM // 2
    signed = jnp.concatenate([-sine_table[:, :half_dim], sine_table[:, half_dim:]], axis=1)
    repeats = TILE // HEAD_DIM
    return jnp.tile(cosine_table, (1, repeats)), jnp.tile(signed, (1, repeats))


def attention_forward(tokens, lengths, tables, gains, whole):
    rows, width = tokens.shape
    head_columns, kv_columns = HEADS * HEAD_DIM, KV_HEADS * HEAD_DIM
    projections = head_columns + 2 * kv_columns
    return call_kernel(
        attention_kernel,
        "attention_forward",
        [
            (lengths, "scalar", None), (tokens, None, None), (tables[0], None, None),
            (tables[1], None, None), (gains, None, None), (whole, (width, projections), (0, 0)),
        ],
        [
            ((rows, projections), bf16), ((rows, head_columns), bf16),
            ((KV_HEADS // 2, 2 * HEADS // KV_HEADS, rows), f32),
        ],
        [((rows, width), bf16)],
        8 * rows * width * head_columns,
    )


def output_blocks(whole):
    width = whole.shape[0]
    head_columns, kv_columns = HEADS * HEAD_DIM, KV_HEADS * HEAD_DIM
    at_output = head_columns + 2 * kv_columns
    return [
        (whole, (width, head_columns), (0, at_output // head_columns)),
        (whole, (width, EXTRA), (0, (at_output + head_columns) // EXTRA)),
    ]


def router_forward(tokens, routes, gains, mixed, whole):
    rows, width = tokens.shape
    return call_kernel(
        router_kernel,
        "router_forward",
        [(a, None, None) for a in (tokens, routes, gains, mixed)] + output_blocks(whole),
        [((rows, width + EXTRA), bf16), ((rows, width), f32), ((rows, EXTRA), f32)],
        [],
        2 * rows * width * mixed.shape[1],
    )


def middle_back(pieces, packet, middle, cotangent, shares, gains, mixed, whole):
    rows, width = cotangent.shape
    head_columns = HEADS * HEAD_DIM
    return call_kernel(
        middle_kernel,
        "middle_back",
        [(a, None, None) for a in (*pieces, packet, middle, cotangent, shares, gains, mixed)]
        + output_blocks(whole),
        [((rows, width), f32), ((rows, head_columns), bf16), ((width, head_columns + EXTRA), bf16)],
        [((rows, width + EXTRA), f32), ((rows, width), bf16), ((width, rows), bf16)],
        4 * rows * width * head_columns,
    )


def attention_back(lengths, rotated, mixed_grad, logs, tables):
    return call_kernel(
        attention_back_kernel,
        "attention_back",
        [
            (lengths, "scalar", None), (rotated, None, None), (mixed_grad, None, None),
            (logs, None, None), (tables[0], None, None), (tables[1], None, None),
        ],
        [(rotated.shape, bf16)],
        [],
        10 * rotated.shape[0] ** 2 * HEADS * HEAD_DIM,
    )[0]


def inputs_back(tokens, gains, projected_grad, whole, middle_grad):
    rows, width = tokens.shape
    projections = projected_grad.shape[1]
    return call_kernel(
        inputs_kernel,
        "inputs_back",
        [
            (tokens, None, None), (gains, None, None), (projected_grad, None, None),
            (whole, (width, projections), (0, 0)), (middle_grad, None, None),
        ],
        [((rows, width), f32), ((width, projections + EXTRA), bf16)],
        [((rows, width), f32), ((width, rows), bf16)],
        4 * rows * width * projections,
    )


def local(
    tokens,
    lengths,
    routes,
    attention_gain,
    query_weight,
    key_weight,
    value_weight,
    output_weight,
    expert_gain,
    router_weight,
    gate_weight,
    up_weight,
    down_weight,
    cotangent,
    *,
    count,
):
    links = Exchange(count)
    member, group, groups = links.member, links.group, links.groups
    row_count, width = tokens.shape
    shard = query_weight.shape[0]
    hidden = gate_weight.shape[2]
    head_columns, kv_columns = HEADS * HEAD_DIM, KV_HEADS * HEAD_DIM

    mine = jnp.stack([gate_weight, up_weight, down_weight.transpose(0, 2, 1)], axis=1)
    mine = mine.reshape(MEMBERS, LOCAL_EXPERTS, 3, shard, hidden)
    shelf = links.send_parts(mine).transpose(1, 2, 0, 3, 4)
    shelf = shelf.reshape(LOCAL_EXPERTS, 3, MEMBERS * shard, hidden)
    lines = [[m + MEMBERS * g for g in range(groups)] for m in range(MEMBERS)]
    own_full = [
        lax.all_gather(shelf[n], "fsdp", axis_index_groups=lines) for n in range(LOCAL_EXPERTS)
    ]

    packed = jnp.concatenate(
        [
            query_weight,
            key_weight,
            value_weight,
            output_weight.T,
            router_weight,
            attention_gain[:, None],
            expert_gain[:, None],
            jnp.zeros((shard, EXTRA - EXPERTS - 2), bf16),
        ],
        axis=1,
    )
    pack_width = packed.shape[1]
    column = links.direct_gather(packed).reshape(groups * shard, pack_width)
    half = column.shape[0] // 2
    near_top, far_low = links.swap(column[:half], 2), links.swap(column[half:], 4)
    near_low, far_top = links.swap(column[half:], 2), links.swap(column[:half], 4)
    cross_top, cross_low = links.swap(near_top, 4), links.swap(far_low, 2)
    spread = {
        0: (column,), 2: (near_top, near_low), 4: (far_top, far_low), 6: (cross_top, cross_low)
    }
    whole = jnp.zeros((groups, MEMBERS, shard, pack_width), bf16)
    for k in range(MEMBERS):
        parts = spread[k & 6]
        if k & 1:
            parts = [links.swap(part, 1) for part in parts]
        part = jnp.concatenate(parts, axis=0).reshape(groups, shard, pack_width)
        whole = lax.dynamic_update_index_in_dim(whole, part, member ^ k, 1)
    whole = whole.reshape(width, pack_width)
    at_output = head_columns + 2 * kv_columns
    at_extra = at_output + head_columns
    gains = whole[:, at_extra + EXPERTS : at_extra + EXPERTS + 2].astype(f32).T

    late_cotangent, whole = lax.optimization_barrier((cotangent, whole))
    cot_near, cot_far = links.swap(late_cotangent, 2), links.swap(late_cotangent, 4)

    tables = rope_lanes(row_count)
    rotated, mixed, logs = attention_forward(tokens, lengths, tables, gains, whole)
    half = row_count // 2
    cot_cross = cot_near[:half], cot_far[half:]
    cot_cross, mixed = lax.optimization_barrier((cot_cross, mixed))
    cot_cross = links.swap(cot_cross[0], 4), links.swap(cot_cross[1], 2)
    packet, middle, shares = router_forward(tokens, routes, gains, mixed, whole)
    near, far = links.swap(packet, 2), links.swap(packet, 4)
    own_full[0], packet = lax.optimization_barrier((own_full[0], packet))

    names = [
        jnp.stack([member, member ^ 1]).astype(jnp.int32) * LOCAL_EXPERTS + n
        for n in range(LOCAL_EXPERTS)
    ]
    rows_own = [(packet,)], [(cotangent,)]
    first_full = own_full[0], links.swap(own_full[0], 1)
    own_out, own_back, *zero = run_experts(names[0], *rows_own, first_full)
    near, far, cot_cross, own_back = lax.optimization_barrier((near, far, cot_cross, own_back))
    cross = links.swap(near[:half], 4), links.swap(far[half:], 2)
    rows_chips = [cross, (near,), (far,)], [cot_cross, (cot_near,), (cot_far,)]
    chip_out, chip_back, *zero = run_experts(names[0], *rows_chips, first_full, zero, True)
    own_full[1], chip_back = lax.optimization_barrier((own_full[1], chip_back))
    second_full = own_full[1], links.swap(own_full[1], 1)

    def join_cores(own, other):
        return (own.astype(f32) + links.swap(other, 1).astype(f32)).astype(bf16)

    def reduce_groups(total):
        return lax.psum_scatter(total, "fsdp", scatter_dimension=0, axis_index_groups=lines)

    zero, chip_out = lax.optimization_barrier((join_cores(*zero), chip_out))
    shelf_zero = reduce_groups(zero)
    chip_out, chip_back, *one = run_experts(
        names[1], *rows_chips, second_full, None, False, (chip_out, chip_back)
    )
    cross_top, cross_low = links.send_cross(chip_back[0])
    near_top, far_low = links.swap(chip_back[1, :half], 2), links.swap(chip_back[2, half:], 4)
    own_out, own_back, *one = run_experts(
        names[1], *rows_own, second_full, one, True, (own_out, own_back)
    )
    cross_top, cross_low, near_top, far_low, own_back = lax.optimization_barrier(
        (cross_top, cross_low, near_top, far_low, own_back)
    )
    near_low = (chip_back[1, half:].astype(f32) + cross_low.astype(f32)).astype(bf16)
    far_top = (chip_back[2, :half].astype(f32) + cross_top.astype(f32)).astype(bf16)
    near_low, far_top, one = lax.optimization_barrier((near_low, far_top, one))
    near_low, far_top = links.swap(near_low, 2), links.swap(far_top, 4)
    one = join_cores(*one)
    back_pieces = near_top, near_low, far_top, far_low
    out_cross, one, back_pieces = lax.optimization_barrier((chip_out[0], one, back_pieces))
    shelf_one = reduce_groups(one)
    out_cross = links.send_cross(out_cross)

    core, chip = member % 2, member // 2

    def pack_cores(pack):
        columns = pack.shape[1]
        pack = pack.reshape(groups, MEMBERS // 2, 2, shard, columns)
        own = lax.dynamic_index_in_dim(pack, core, 2, keepdims=False)
        other = links.swap(lax.dynamic_index_in_dim(pack, 1 - core, 2, keepdims=False), 1)

        joined = own.astype(f32) + other.astype(f32)
        return [
            lax.dynamic_index_in_dim(joined, chip ^ bits, 1, keepdims=False).reshape(
                groups * shard, columns
            )
            for bits in range(MEMBERS // 2)
        ]

    def pack_cross(parts):
        return links.send_cross(parts[3].astype(bf16))

    def pack_add(parts, cross):
        return links.add_cross(parts[1].astype(bf16), parts[2].astype(bf16), cross)

    def pack_sum(parts, near, far):
        near, far = links.swap(near, 2), links.swap(far, 4)
        return parts[0] + near.astype(f32) + far.astype(f32)

    middle_grad, mixed_grad, first_pack = middle_back(
        (own_back[0], *back_pieces), packet, middle, cotangent, shares, gains, mixed, whole
    )
    out_near, out_far = links.add_cross(chip_out[1], chip_out[2], out_cross)
    out_near, out_far, mixed_grad = lax.optimization_barrier((out_near, out_far, mixed_grad))
    out_near, out_far = links.swap(out_near, 2), links.swap(out_far, 4)
    first_parts = pack_cores(first_pack)
    projected_grad = attention_back(lengths, rotated, mixed_grad, logs, tables)
    shelf_zero, first_parts, projected_grad = lax.optimization_barrier(
        (shelf_zero, first_parts, projected_grad)
    )
    first_cross = pack_cross(first_parts)
    grad_tokens, second_pack = inputs_back(tokens, gains, projected_grad, whole, middle_grad)
    first_near, first_far = pack_add(first_parts, first_cross)
    first_near, first_far, second_pack, out_near, out_far, shelf_one = lax.optimization_barrier(
        (first_near, first_far, second_pack, out_near, out_far, shelf_one)
    )
    second_parts = pack_cores(second_pack)
    first_sum = pack_sum(first_parts, first_near, first_far)
    second_near, second_far = pack_add(second_parts, pack_cross(second_parts))
    second_sum = pack_sum(second_parts, second_near, second_far)
    pack_total = jnp.concatenate([second_sum, first_sum], axis=1)
    pack_total = links.direct_reduce(pack_total.reshape(groups, shard, pack_total.shape[1]))
    second_total = pack_total[:, : second_sum.shape[1]]
    first_total = pack_total[:, second_sum.shape[1] :]
    out_pieces = (own_out[0], out_near, out_far)
    layer_out = (middle + sum(piece.astype(f32) for piece in out_pieces)).astype(bf16)
    shelf_grad = jnp.stack([shelf_zero, shelf_one])
    shelf_grad = shelf_grad.reshape(LOCAL_EXPERTS, 3, MEMBERS, shard, hidden)
    expert_shards = links.send_parts(shelf_grad.transpose(2, 0, 1, 3, 4)).astype(f32)
    expert_shards = expert_shards.reshape(EXPERTS, 3, shard, hidden)
    return (
        layer_out,
        grad_tokens,
        second_total[:, at_output],
        second_total[:, :head_columns],
        second_total[:, head_columns : head_columns + kv_columns],
        second_total[:, head_columns + kv_columns : at_output],
        first_total[:, :head_columns].T,
        first_total[:, head_columns + EXPERTS],
        first_total[:, head_columns : head_columns + EXPERTS],
        expert_shards[:, 0],
        expert_shards[:, 1],
        expert_shards[:, 2].transpose(0, 2, 1),
    )


def solution(mesh):
    count = mesh.shape["fsdp"]
    placed = (
        P("fsdp", None),
        P("fsdp"),
        P("fsdp", None),
        P("fsdp"),
        P("fsdp", None),
        P("fsdp", None),
        P("fsdp", None),
        P(None, "fsdp"),
        P("fsdp"),
        P("fsdp", None),
        P(None, "fsdp", None),
        P(None, "fsdp", None),
        P(None, None, "fsdp"),
        P("fsdp", None),
    )

    def body(*args):
        return local(*args, count=count)

    return jax.shard_map(
        body,
        mesh=mesh,
        in_specs=placed,
        out_specs=(
            P("fsdp", None),
            P("fsdp", None),
            P("fsdp"),
            P("fsdp", None),
            P("fsdp", None),
            P("fsdp", None),
            P(None, "fsdp"),
            P("fsdp"),
            P("fsdp", None),
            P(None, "fsdp", None),
            P(None, "fsdp", None),
            P(None, None, "fsdp"),
        ),
        check_vma=False,
    )
```

```python
import functools

import jax
import jax.numpy as jnp
import numpy as np
from jax import lax
from jax.experimental import pallas as pl
from jax.experimental.pallas import tpu as pltpu
from jax.sharding import PartitionSpec as P

HEADS = 16
KV_HEADS = 8
HEAD_DIM = 64
EXPERTS = 16
MEMBERS = 8
LOCAL_EXPERTS = EXPERTS // MEMBERS
EXTRA = 128

norm_eps = 1e-06
attention_scale = 0.015625
residual_scale = 0.22
rope_base = 10000.0
masked_value = -1e30
f32 = jnp.float32
bf16 = jnp.bfloat16


def rope_tables(row_count):
    half_dim = HEAD_DIM // 2
    frequency = rope_base ** (-2.0 * np.arange(half_dim, dtype=np.float32) / np.float32(HEAD_DIM))
    angles = np.arange(row_count, dtype=np.float32)[:, None] * frequency.astype(np.float32)[None, :]
    angles = np.concatenate([angles, angles], axis=1)
    return (np.cos(angles), np.sin(angles))


class Exchange:
    def __init__(self, count):
        self.count = count
        self.groups = count // MEMBERS
        index = lax.axis_index("fsdp")
        self.member = index % MEMBERS
        self.group = index // MEMBERS

    def swap(self, value, bits):
        return lax.ppermute(value, "fsdp", [(i, i ^ bits) for i in range(self.count)])

    def direct_gather(self, piece):
        stack = jnp.zeros((self.groups,) + piece.shape, piece.dtype)
        for bits in range(self.groups):
            part = self.swap(piece, bits * MEMBERS) if bits else piece
            stack = lax.dynamic_update_index_in_dim(stack, part, self.group ^ bits, 0)
        return stack

    def direct_reduce(self, terms):
        total = lax.dynamic_index_in_dim(terms, self.group, 0, keepdims=False)
        for bits in range(1, self.groups):
            part = lax.dynamic_index_in_dim(terms, self.group ^ bits, 0, keepdims=False)
            total = total + self.swap(part.astype(bf16), bits * MEMBERS).astype(f32)
        return total

    def send_cross(self, block):
        half = block.shape[0] // 2
        return self.swap(block[:half], 2), self.swap(block[half:], 4)

    def add_cross(self, near, far, cross):
        half = near.shape[0] // 2
        cross_top, cross_low = cross
        near_low = (near[half:].astype(f32) + cross_low.astype(f32)).astype(bf16)
        far_top = (far[:half].astype(f32) + cross_top.astype(f32)).astype(bf16)
        return (
            jnp.concatenate([near[:half], near_low], axis=0),
            jnp.concatenate([far_top, far[half:]], axis=0),
        )

    def chip_parts(self, parts):
        chips = parts.reshape((MEMBERS // 2, 2) + parts.shape[1:])
        chip = self.member // 2
        found = []
        for bits in range(MEMBERS // 2):
            part = lax.dynamic_index_in_dim(chips, chip ^ bits, 0, keepdims=False)
            found.append(self.swap(part, 2 * bits) if bits else part)
        return found

    def keep_parts(self, found):
        chip, core = self.member // 2, self.member % 2
        arrived = jnp.zeros((MEMBERS // 2,) + found[0].shape, found[0].dtype)
        for bits, part in enumerate(found):
            arrived = lax.dynamic_update_index_in_dim(arrived, part, chip ^ bits, 0)
        kept = lax.dynamic_index_in_dim(arrived, core, 1, keepdims=False)
        other = self.swap(lax.dynamic_index_in_dim(arrived, 1 - core, 1, keepdims=False), 1)
        return kept, other

    def in_order(self, kept, other):
        core = self.member % 2
        even = jnp.where(core == 0, kept, other)
        odd = jnp.where(core == 0, other, kept)
        return jnp.stack([even, odd], axis=1).reshape((MEMBERS,) + kept.shape[1:])


def dot(left, right):
    return jnp.dot(left, right, preferred_element_type=f32)


def dot_turned(left, right):
    return lax.dot_general(left, right, (((1,), (1,)), ((), ())), preferred_element_type=f32)


def expert_kernel(names_ref, *refs, layout, fresh, last, carried):
    refs = list(refs)
    experts = range(names_ref.shape[0])
    packet_parts = [[refs.pop(0) for _ in range(number)] for number in layout]
    cotangent_parts = [[refs.pop(0) for _ in range(number)] for number in layout]
    weight_parts = [refs.pop(0) for _ in experts]
    prior_refs = [None if fresh else refs.pop(0) for _ in experts]
    carried_out, carried_back = (refs.pop(0), refs.pop(0)) if carried else (None, None)
    out_ref, back_ref = refs.pop(0), refs.pop(0)
    result_refs = [refs.pop(0) for _ in experts]
    grad_refs = [refs.pop(0) for _ in experts] if last else result_refs
    packet_buffer, cotangent_buffer, weight_ref, packet_turned, cotangent_turned, sums = refs[:6]
    block_sem, weight_sem, prior_sem = refs[6:]
    rows, width = cotangent_buffer.shape[1:]
    groups, _, depth, _ = weight_parts[0].shape
    blocks = len(layout)
    at = pl.program_id(0)

    def block_copies(block):
        copies = []
        for kind, (parts, buffer) in enumerate(
            ((packet_parts, packet_buffer), (cotangent_parts, cotangent_buffer))
        ):
            size = rows // layout[block]
            for number, part in enumerate(parts[block]):
                place = buffer.at[block, pl.ds(number * size, size)]
                copies.append(
                    pltpu.make_async_copy(part, place, block_sem.at[block, 2 * kind + number])
                )
        return copies

    def weight_copies(n):
        return [
            pltpu.make_async_copy(
                weight_parts[n].at[g], weight_ref.at[n, :, pl.ds(g * depth, depth)], weight_sem.at[n, g]
            )
            for g in range(groups)
        ]

    def prior_copy(n):
        return pltpu.make_async_copy(prior_refs[n], grad_refs[n], prior_sem.at[n])

    @pl.when(at == 0)
    def _():
        for copy in block_copies(0):
            copy.start()
        for n in experts:
            for copy in weight_copies(n):
                copy.start()
        for n in experts:
            if fresh:
                grad_refs[n][...] = jnp.zeros_like(grad_refs[n])
            else:
                prior_copy(n).start()
        for block in range(1, blocks):
            for copy in block_copies(block):
                copy.start()
        for n in experts:
            for copy in weight_copies(n):
                copy.wait()

    for block in range(blocks):

        @pl.when(at == block)
        def _():
            for copy in block_copies(block):
                copy.wait()

    lane = lax.broadcasted_iota(jnp.int32, (rows, EXTRA), 1)
    normed = packet_buffer[at, :, :width]
    upstream = cotangent_buffer[at]
    shares = packet_buffer[at, :, width:].astype(f32)
    extra = jnp.zeros((rows, EXTRA), f32)
    packet_turned[...] = normed.T
    cotangent_turned[...] = upstream.T
    begun = []
    for n in experts:
        begun.append(
            (
                dot(normed, weight_ref[n, 0]),
                dot(normed, weight_ref[n, 1]),
                dot(upstream, weight_ref[n, 2]),
            )
        )
    if not fresh:

        @pl.when(at == 0)
        def _():
            for n in experts:
                prior_copy(n).wait()

    for n in experts:
        gate_pre, up_pre, inner_raw = begun[n]
        expert = names_ref[n]
        is_high, is_low = lane == expert, lane == expert + EXPERTS
        share = jnp.sum(jnp.where(is_high | is_low, shares, 0.0), axis=1, keepdims=True)
        sigmoid_gate = jax.nn.sigmoid(gate_pre)
        activated = gate_pre * sigmoid_gate
        inner = (activated * up_pre).astype(bf16).astype(f32)
        share_grad = residual_scale * jnp.sum(inner * inner_raw, axis=1, keepdims=True)
        scaled = share * residual_scale
        inner_grad = inner_raw * scaled
        gate_grad = (
            inner_grad * up_pre * (sigmoid_gate + activated * (1.0 - sigmoid_gate))
        ).astype(bf16)
        up_grad = (inner_grad * activated).astype(bf16)
        inner_shared = (inner * scaled).astype(bf16)
        out_term = dot_turned(inner_shared, weight_ref[n, 2])
        back_term = dot_turned(gate_grad, weight_ref[n, 0]) + dot_turned(up_grad, weight_ref[n, 1])
        if n == 0:
            sums[0], sums[1] = out_term, back_term
        else:
            sums[0] += out_term
            sums[1] += back_term
        grad_refs[n][0] += dot(packet_turned[...], gate_grad)
        grad_refs[n][1] += dot(packet_turned[...], up_grad)
        grad_refs[n][2] += dot(cotangent_turned[...], inner_shared)
        high = share_grad.astype(bf16).astype(f32)
        extra = extra + jnp.where(is_high, high, 0.0) + jnp.where(is_low, share_grad - high, 0.0)
    out_total, back_total = sums[0], sums[1]
    if carried:
        out_total = out_total + carried_out[0].astype(f32)
        back_total = back_total + carried_back[0, :, :width].astype(f32)
        extra = extra + carried_back[0, :, width:].astype(f32)
    out_ref[0] = out_total.astype(bf16)
    back_ref[0, :, :width] = back_total.astype(bf16)
    back_ref[0, :, width:] = extra.astype(bf16)

    if last:

        @pl.when(at == blocks - 1)
        def _():
            for n in experts:
                for g in range(groups):
                    result_refs[n][g] = grad_refs[n][:, pl.ds(g * depth, depth)].astype(bf16)


def run_experts(names, packets, cotangents, weights, priors=None, last=False, carried=None):
    layout = tuple(len(parts) for parts in packets)
    blocks = len(layout)
    rows = sum(part.shape[0] for part in packets[0])
    wide, width = packets[0][0].shape[1], cotangents[0][0].shape[1]
    groups, _, depth, hidden = weights[0].shape
    grad_shape = (3, width, hidden)
    fresh = priors is None
    count = len(weights)
    operands = [part for parts in packets for part in parts]
    operands += [part for parts in cotangents for part in parts]
    operands += list(weights) + list(priors or ())

    def whole(shape):
        return pl.BlockSpec(
            shape, lambda i, s, rank=len(shape): (0,) * rank, pipeline_mode=pl.Buffered(1)
        )

    term_specs = [
        pl.BlockSpec((1, rows, columns), lambda i, s: (i, 0, 0)) for columns in (width, wide)
    ]
    in_specs = [pl.BlockSpec(memory_space=pl.ANY)] * len(operands)
    if carried is not None:
        in_specs += term_specs
        operands += list(carried)
    grads = [((groups, 3, depth, hidden), bf16) if last else (grad_shape, f32)] * count
    scratch = [pltpu.VMEM(grad_shape, f32)] * (count if last else 0)
    scratch += [
        pltpu.VMEM((blocks, rows, wide), bf16),
        pltpu.VMEM((blocks, rows, width), bf16),
        pltpu.VMEM((count,) + grad_shape, bf16),
        pltpu.VMEM((width, rows), bf16),
        pltpu.VMEM((width, rows), bf16),
        pltpu.VMEM((2, rows, width), f32),
        pltpu.SemaphoreType.DMA((blocks, 4)),
        pltpu.SemaphoreType.DMA((count, groups)),
        pltpu.SemaphoreType.DMA((count,)),
    ]
    return pl.pallas_call(
        functools.partial(
            expert_kernel, layout=layout, fresh=fresh, last=last, carried=carried is not None
        ),
        grid_spec=pltpu.PrefetchScalarGridSpec(
            num_scalar_prefetch=1,
            grid=(blocks,),
            in_specs=in_specs,
            out_specs=term_specs + [whole(shape) for shape, _ in grads],
            scratch_shapes=scratch,
        ),
        out_shape=[
            jax.ShapeDtypeStruct((blocks, rows, columns), bf16) for columns in (width, wide)
        ]
        + [jax.ShapeDtypeStruct(shape, dtype) for shape, dtype in grads],
        compiler_params=pltpu.CompilerParams(vmem_limit_bytes=62 * 1024 * 1024),
        cost_estimate=pl.CostEstimate(
            flops=blocks * count * 9 * 2 * rows * width * hidden,
            bytes_accessed=blocks * rows * width * 8 + 18 * count * width * hidden,
            transcendentals=blocks * count * rows * hidden,
        ),
        name="experts",
    )(names, *operands)


TILE = 256
PAIR = 2 * HEAD_DIM


def columns_at(index, size):
    return pl.ds(pl.multiple_of(index * size, size), size)


def swap_halves(values):
    width, half_dim = values.shape[1], HEAD_DIM // 2
    lane = lax.broadcasted_iota(jnp.int32, values.shape, 1)
    return jnp.where(
        lane % HEAD_DIM < half_dim,
        pltpu.roll(values, width - half_dim, 1),
        pltpu.roll(values, half_dim, 1),
    )


def row_scale_of(values):
    return lax.rsqrt(jnp.mean(values * values, axis=1, keepdims=True) + norm_eps)


def scores_of(keys, queries, length, first_query):
    scores = attention_scale * dot_turned(keys, queries)
    key_at = lax.broadcasted_iota(jnp.int32, scores.shape, 0)
    query_at = lax.broadcasted_iota(jnp.int32, scores.shape, 1) + first_query
    return jnp.where((key_at <= query_at) & (key_at < length), scores, masked_value)


def head_of(block, index):
    return block[:, index * HEAD_DIM : (index + 1) * HEAD_DIM]


def attention_kernel(
    length_ref, tokens_ref, cosine_ref, sine_ref, gains_ref, weight_ref,
    rotated_ref, mixed_ref, log_ref, normed_ref,
):
    rows = tokens_ref.shape[0]
    head_columns, kv_columns = HEADS * HEAD_DIM, KV_HEADS * HEAD_DIM
    at_value = head_columns + kv_columns
    at_output = at_value + kv_columns
    length = length_ref[0]
    group = HEADS // KV_HEADS

    inputs = tokens_ref[...].astype(f32)
    normed_ref[...] = (inputs * row_scale_of(inputs) * gains_ref[0:1, :]).astype(bf16)

    def project_turned(c, carry):
        where = columns_at(c, TILE)
        value = dot(normed_ref[...], weight_ref[:, where])
        value = value * cosine_ref[...] + swap_halves(value) * sine_ref[...]
        rotated_ref[:, where] = value.astype(bf16)
        return carry

    def project(c, carry):
        where = columns_at(c, TILE)
        rotated_ref[:, where] = dot(normed_ref[...], weight_ref[:, where]).astype(bf16)
        return carry

    lax.fori_loop(0, at_value // TILE, project_turned, 0)
    lax.fori_loop(at_value // TILE, at_output // TILE, project, 0)

    block = rows // 2

    def attend(j, carry):
        queries = rotated_ref[:, columns_at(j, group * PAIR)]
        keys = rotated_ref[:, columns_at(j + head_columns // PAIR, PAIR)]
        values_turned = rotated_ref[:, columns_at(j + at_value // PAIR, PAIR)].T
        outs = []
        for head in range(2 * group):
            kv = head // group
            key, query = head_of(keys, kv), head_of(queries, head)
            value = values_turned[kv * HEAD_DIM : (kv + 1) * HEAD_DIM]
            parts, logs = [], []
            for b in range(2):
                reach = (b + 1) * block
                scores = scores_of(key[:reach], query[b * block : reach], length, b * block)
                best = jnp.max(scores, axis=0, keepdims=True)
                exponent = jnp.exp(scores - best)
                total = jnp.sum(exponent, axis=0, keepdims=True)
                chance = (exponent * (1.0 / total)).astype(bf16)
                parts.append(dot(value[:, :reach], chance))
                logs.append(best + jnp.log(total))
            outs.append(jnp.concatenate(parts, axis=1))
            log_ref[j, head : head + 1, :] = jnp.concatenate(logs, axis=1)
        mixed_ref[:, columns_at(j, group * PAIR)] = jnp.concatenate(outs, axis=0).T.astype(bf16)
        return carry

    lax.fori_loop(0, KV_HEADS // 2, attend, 0)


def router_kernel(
    tokens_ref, routes_ref, gains_ref, mixed_ref, output_ref, extra_ref,
    packet_ref, middle_ref, share_ref,
):
    width = tokens_ref.shape[1]

    def mix(c, carry):
        where = columns_at(c, TILE)
        branch = dot_turned(mixed_ref[...], output_ref[where, :])
        middle_ref[:, where] = tokens_ref[:, where].astype(f32) + residual_scale * branch
        return carry

    lax.fori_loop(0, width // TILE, mix, 0)
    middle = middle_ref[...]
    normed_two = (middle * row_scale_of(middle) * gains_ref[1:2, :]).astype(bf16)
    packet_ref[:, :width] = normed_two
    logits = dot(normed_two, extra_ref[...])
    lane = lax.broadcasted_iota(jnp.int32, logits.shape, 1)
    routed = lane == routes_ref[:, 0:1]
    for k in range(1, routes_ref.shape[1]):
        routed = routed | (lane == routes_ref[:, k : k + 1])
    best = jnp.max(jnp.where(routed, logits, masked_value), axis=1, keepdims=True)
    weights = jnp.where(routed, jnp.exp(jnp.where(routed, logits, best) - best), 0.0)
    shares = weights / jnp.sum(weights, axis=1, keepdims=True)
    share_ref[...] = shares
    high = shares.astype(bf16).astype(f32)
    packet_ref[:, width:] = (high + pltpu.roll(shares - high, EXPERTS, 1)).astype(bf16)


def column_of(row, lanes):
    return jnp.broadcast_to(row, (lanes, row.shape[1])).T


def middle_kernel(
    own_ref, near_top_ref, near_low_ref, far_top_ref, far_low_ref, packet_ref, middle_ref,
    cotangent_ref, share_ref, gains_ref, mixed_ref, output_ref, extra_ref,
    middle_grad_ref, mixed_grad_ref, pack_ref, back_ref, branch_ref, turned_ref,
):
    width = cotangent_ref.shape[1]
    half = own_ref.shape[0] // 2
    for place, near_ref, far_ref in (
        (pl.ds(0, half), near_top_ref, far_top_ref),
        (pl.ds(half, half), near_low_ref, far_low_ref),
    ):
        back_ref[place] = (
            own_ref[place].astype(f32) + near_ref[...].astype(f32) + far_ref[...].astype(f32)
        )
    shares = share_ref[...]
    share_grad = back_ref[:, width:]
    share_grad = share_grad + pltpu.roll(share_grad, EXTRA - EXPERTS, 1)
    weighted_mean = jnp.sum(shares * share_grad, axis=1, keepdims=True)
    logit_grad = (shares * (share_grad - weighted_mean)).astype(bf16)
    normed_grad = back_ref[:, :width] + dot_turned(logit_grad, extra_ref[...])
    middle = middle_ref[...]
    scale = row_scale_of(middle)
    scaled = middle * scale
    gain_grad = jnp.sum(normed_grad * scaled, axis=0, keepdims=True)
    weighted = normed_grad * gains_ref[1:2, :]
    correction = jnp.mean(weighted * middle, axis=1, keepdims=True)
    middle_grad = cotangent_ref[...].astype(f32) + scale * weighted - scaled * (scale * scale * correction)
    middle_grad_ref[...] = middle_grad
    branch_ref[...] = (residual_scale * middle_grad).astype(bf16)
    router_grad = dot(packet_ref[:, :width].T, logit_grad)
    lane = lax.broadcasted_iota(jnp.int32, router_grad.shape, 1)
    pack_ref[:, width:] = jnp.where(
        lane == EXPERTS, column_of(gain_grad, EXTRA), router_grad
    ).astype(bf16)
    turned_ref[...] = branch_ref[...].T

    def step(c, carry):
        where = columns_at(c, TILE)
        pack_ref[:, where] = dot(turned_ref[...], mixed_ref[:, where]).astype(bf16)
        mixed_grad_ref[:, where] = dot(branch_ref[...], output_ref[:, where]).astype(bf16)
        return carry

    lax.fori_loop(0, output_ref.shape[1] // TILE, step, 0)


def attention_back_kernel(
    length_ref, rotated_ref, mixed_grad_ref, log_ref, cosine_ref, sine_ref, grad_ref
):
    rows = rotated_ref.shape[0]
    head_columns, kv_columns = HEADS * HEAD_DIM, KV_HEADS * HEAD_DIM
    at_value = head_columns + kv_columns
    length = length_ref[0]
    group = HEADS // KV_HEADS
    block = rows // 2

    def attend(j, carry):
        wide = columns_at(j, group * PAIR)
        key_place = columns_at(j + head_columns // PAIR, PAIR)
        value_place = columns_at(j + at_value // PAIR, PAIR)
        queries, grads = rotated_ref[:, wide], mixed_grad_ref[:, wide]
        keys, values = rotated_ref[:, key_place], rotated_ref[:, value_place]
        keys_turned = keys.T
        query_grads, key_grads, value_grads = [], [], []
        for kv in range(2):
            key, value = head_of(keys, kv), head_of(values, kv)
            key_turned = keys_turned[kv * HEAD_DIM : (kv + 1) * HEAD_DIM]
            key_sums, value_sums = [], []
            for member in range(group):
                head = kv * group + member
                query, grad = head_of(queries, head), head_of(grads, head)
                query_parts = []
                for b in range(2):
                    reach = (b + 1) * block
                    query_block, grad_block = query[b * block : reach], grad[b * block : reach]
                    scores = scores_of(key[:reach], query_block, length, b * block)
                    chance = jnp.exp(scores - log_ref[j, head : head + 1, b * block : reach])
                    chance_grad = dot_turned(value[:reach], grad_block)
                    delta = jnp.sum(chance * chance_grad, axis=0, keepdims=True)
                    score_grad = (attention_scale * chance * (chance_grad - delta)).astype(bf16)
                    value_sums.append(dot(chance.astype(bf16), grad_block))
                    key_sums.append(dot(score_grad, query_block))
                    query_parts.append(dot(key_turned[:, :reach], score_grad))
                query_grads.append(jnp.concatenate(query_parts, axis=1))
            for sums, into in ((key_sums, key_grads), (value_sums, value_grads)):
                short = sum(sums[2::2], sums[0])
                long = sum(sums[3::2], sums[1])
                into.append(jnp.concatenate([short + long[:block], long[block:]], axis=0))
        query_grad = jnp.concatenate(query_grads, axis=0).T
        query_grad = query_grad * cosine_ref[...] - swap_halves(query_grad) * sine_ref[...]
        grad_ref[:, wide] = query_grad.astype(bf16)
        key_grad = jnp.concatenate(key_grads, axis=1)
        key_grad = key_grad * cosine_ref[:, :PAIR] - swap_halves(key_grad) * sine_ref[:, :PAIR]
        grad_ref[:, key_place] = key_grad.astype(bf16)
        grad_ref[:, value_place] = jnp.concatenate(value_grads, axis=1).astype(bf16)
        return carry

    lax.fori_loop(0, KV_HEADS // 2, attend, 0)


def inputs_kernel(
    tokens_ref, gains_ref, projected_ref, weight_ref, middle_grad_ref,
    grad_ref, pack_ref, normed_grad_ref, turned_ref,
):
    width = tokens_ref.shape[1]
    projections = projected_ref.shape[1]
    inputs = tokens_ref[...].astype(f32)
    scale = row_scale_of(inputs)
    scaled = inputs * scale
    turned_ref[...] = (scaled * gains_ref[0:1, :]).astype(bf16).T

    def to_weight(c, carry):
        where = columns_at(c, TILE)
        pack_ref[:, where] = dot(turned_ref[...], projected_ref[:, where]).astype(bf16)
        return carry

    def to_input(c, carry):
        where = columns_at(c, TILE)
        normed_grad_ref[:, where] = dot_turned(projected_ref[...], weight_ref[where, :])
        return carry

    lax.fori_loop(0, projections // TILE, to_weight, 0)
    lax.fori_loop(0, width // TILE, to_input, 0)
    normed_grad = normed_grad_ref[...]
    gain_grad = column_of(jnp.sum(normed_grad * scaled, axis=0, keepdims=True), EXTRA)
    lane = lax.broadcasted_iota(jnp.int32, gain_grad.shape, 1)
    pack_ref[:, projections:] = jnp.where(lane == 0, gain_grad, 0.0).astype(bf16)
    weighted = normed_grad * gains_ref[0:1, :]
    correction = jnp.mean(weighted * inputs, axis=1, keepdims=True)
    grad_ref[...] = middle_grad_ref[...] + scale * weighted - scaled * (scale * scale * correction)


def call_kernel(body, name, operands, out_shape, scratch, flops):
    specs, arrays = [], []
    for operand in operands:
        array, shape, index = operand
        if shape == "scalar":
            specs.append(pl.BlockSpec(memory_space=pltpu.SMEM))
        else:
            shape = array.shape if shape is None else shape
            index = (0,) * len(shape) if index is None else index
            specs.append(pl.BlockSpec(shape, lambda i, index=index: index))
        arrays.append(array)
    outs = [jax.ShapeDtypeStruct(shape, dtype) for shape, dtype in out_shape]
    return pl.pallas_call(
        body,
        grid=(1,),
        in_specs=specs,
        out_specs=[
            pl.BlockSpec(out.shape, lambda i, rank=len(out.shape): (0,) * rank) for out in outs
        ],
        out_shape=outs,
        scratch_shapes=[pltpu.VMEM(shape, dtype) for shape, dtype in scratch],
        compiler_params=pltpu.CompilerParams(vmem_limit_bytes=62 * 1024 * 1024),
        cost_estimate=pl.CostEstimate(
            flops=flops,
            bytes_accessed=sum(a.size * a.dtype.itemsize for a in arrays)
            + sum(o.size * o.dtype.itemsize for o in outs),
            transcendentals=0,
        ),
        name=name,
    )(*arrays)


def rope_lanes(row_count):
    cosine_table, sine_table = rope_tables(row_count)
    half_dim = HEAD_DIM // 2
    signed = np.concatenate([-sine_table[:, :half_dim], sine_table[:, half_dim:]], axis=1)
    repeats = TILE // HEAD_DIM
    return jnp.asarray(np.tile(cosine_table, (1, repeats))), jnp.asarray(np.tile(signed, (1, repeats)))


def attention_forward(tokens, lengths, tables, gains, whole):
    rows, width = tokens.shape
    head_columns, kv_columns = HEADS * HEAD_DIM, KV_HEADS * HEAD_DIM
    projections = head_columns + 2 * kv_columns
    return call_kernel(
        attention_kernel,
        "attention_forward",
        [
            (lengths, "scalar", None), (tokens, None, None), (tables[0], None, None),
            (tables[1], None, None), (gains, None, None), (whole, (width, projections), (0, 0)),
        ],
        [
            ((rows, projections), bf16), ((rows, head_columns), bf16),
            ((KV_HEADS // 2, 2 * HEADS // KV_HEADS, rows), f32),
        ],
        [((rows, width), bf16)],
        8 * rows * width * head_columns,
    )


def output_blocks(whole):
    width = whole.shape[0]
    head_columns, kv_columns = HEADS * HEAD_DIM, KV_HEADS * HEAD_DIM
    at_output = head_columns + 2 * kv_columns
    return [
        (whole, (width, head_columns), (0, at_output // head_columns)),
        (whole, (width, EXTRA), (0, (at_output + head_columns) // EXTRA)),
    ]


def router_forward(tokens, routes, gains, mixed, whole):
    rows, width = tokens.shape
    return call_kernel(
        router_kernel,
        "router_forward",
        [(a, None, None) for a in (tokens, routes, gains, mixed)] + output_blocks(whole),
        [((rows, width + EXTRA), bf16), ((rows, width), f32), ((rows, EXTRA), f32)],
        [],
        2 * rows * width * mixed.shape[1],
    )


def middle_back(pieces, packet, middle, cotangent, shares, gains, mixed, whole):
    rows, width = cotangent.shape
    head_columns = HEADS * HEAD_DIM
    return call_kernel(
        middle_kernel,
        "middle_back",
        [(a, None, None) for a in (*pieces, packet, middle, cotangent, shares, gains, mixed)]
        + output_blocks(whole),
        [((rows, width), f32), ((rows, head_columns), bf16), ((width, head_columns + EXTRA), bf16)],
        [((rows, width + EXTRA), f32), ((rows, width), bf16), ((width, rows), bf16)],
        4 * rows * width * head_columns,
    )


def attention_back(lengths, rotated, mixed_grad, logs, tables):
    return call_kernel(
        attention_back_kernel,
        "attention_back",
        [
            (lengths, "scalar", None), (rotated, None, None), (mixed_grad, None, None),
            (logs, None, None), (tables[0], None, None), (tables[1], None, None),
        ],
        [(rotated.shape, bf16)],
        [],
        10 * rotated.shape[0] ** 2 * HEADS * HEAD_DIM,
    )[0]


def inputs_back(tokens, gains, projected_grad, whole, middle_grad):
    rows, width = tokens.shape
    projections = projected_grad.shape[1]
    return call_kernel(
        inputs_kernel,
        "inputs_back",
        [
            (tokens, None, None), (gains, None, None), (projected_grad, None, None),
            (whole, (width, projections), (0, 0)), (middle_grad, None, None),
        ],
        [((rows, width), f32), ((width, projections + EXTRA), bf16)],
        [((rows, width), f32), ((width, rows), bf16)],
        4 * rows * width * projections,
    )


def local(
    tokens,
    lengths,
    routes,
    attention_gain,
    query_weight,
    key_weight,
    value_weight,
    output_weight,
    expert_gain,
    router_weight,
    gate_weight,
    up_weight,
    down_weight,
    cotangent,
    *,
    count,
):
    links = Exchange(count)
    member, group, groups = links.member, links.group, links.groups
    row_count, width = tokens.shape
    shard = query_weight.shape[0]
    hidden = gate_weight.shape[2]
    head_columns, kv_columns = HEADS * HEAD_DIM, KV_HEADS * HEAD_DIM

    packed = jnp.concatenate(
        [
            query_weight,
            key_weight,
            value_weight,
            output_weight.T,
            router_weight,
            attention_gain[:, None],
            expert_gain[:, None],
            jnp.zeros((shard, EXTRA - EXPERTS - 2), bf16),
        ],
        axis=1,
    )
    pack_width = packed.shape[1]
    column = links.direct_gather(packed).reshape(groups * shard, pack_width)

    mine = jnp.stack([gate_weight, up_weight, down_weight.transpose(0, 2, 1)], axis=1)
    mine = mine.reshape(MEMBERS, LOCAL_EXPERTS, 3, shard, hidden)
    kept, other = links.keep_parts(links.chip_parts(mine))
    other, column = lax.optimization_barrier((other, column))
    shelf = links.in_order(kept, other).transpose(1, 2, 0, 3, 4)
    shelf = shelf.reshape(LOCAL_EXPERTS, 3, MEMBERS * shard, hidden)
    lines = [[m + MEMBERS * g for g in range(groups)] for m in range(MEMBERS)]
    own_full = [
        lax.all_gather(shelf[n], "fsdp", axis_index_groups=lines) for n in range(LOCAL_EXPERTS)
    ]

    half = column.shape[0] // 2
    near_top, far_low = links.swap(column[:half], 2), links.swap(column[half:], 4)
    near_low, far_top = links.swap(column[half:], 2), links.swap(column[:half], 4)
    cross_top, cross_low = links.swap(near_top, 4), links.swap(far_low, 2)
    spread = {
        0: (column,), 2: (near_top, near_low), 4: (far_top, far_low), 6: (cross_top, cross_low)
    }
    whole = jnp.zeros((groups, MEMBERS, shard, pack_width), bf16)
    for k in range(MEMBERS):
        parts = spread[k & 6]
        if k & 1:
            parts = [links.swap(part, 1) for part in parts]
        part = jnp.concatenate(parts, axis=0).reshape(groups, shard, pack_width)
        whole = lax.dynamic_update_index_in_dim(whole, part, member ^ k, 1)
    whole = whole.reshape(width, pack_width)
    at_output = head_columns + 2 * kv_columns
    at_extra = at_output + head_columns
    gains = whole[:, at_extra + EXPERTS : at_extra + EXPERTS + 2].astype(f32).T

    late_cotangent, whole = lax.optimization_barrier((cotangent, whole))
    cot_near, cot_far = links.swap(late_cotangent, 2), links.swap(late_cotangent, 4)

    tables = rope_lanes(row_count)
    rotated, mixed, logs = attention_forward(tokens, lengths, tables, gains, whole)
    half = row_count // 2
    cot_cross = cot_near[:half], cot_far[half:]
    cot_cross, mixed = lax.optimization_barrier((cot_cross, mixed))
    cot_cross = links.swap(cot_cross[0], 4), links.swap(cot_cross[1], 2)
    packet, middle, shares = router_forward(tokens, routes, gains, mixed, whole)
    near, far = links.swap(packet, 2), links.swap(packet, 4)
    own_full[0], cot_cross, packet = lax.optimization_barrier((own_full[0], cot_cross, packet))

    names = [
        jnp.stack([member, member ^ 1]).astype(jnp.int32) * LOCAL_EXPERTS + n
        for n in range(LOCAL_EXPERTS)
    ]
    rows_own = [(packet,)], [(cotangent,)]
    first_full = own_full[0], links.swap(own_full[0], 1)
    own_out, own_back, *zero = run_experts(names[0], *rows_own, first_full)
    near, far, own_back = lax.optimization_barrier((near, far, own_back))
    cross = links.swap(near[:half], 4), links.swap(far[half:], 2)
    rows_chips = [cross, (near,), (far,)], [cot_cross, (cot_near,), (cot_far,)]
    chip_out, chip_back, *zero = run_experts(names[0], *rows_chips, first_full, zero, True)
    own_full[1], chip_back = lax.optimization_barrier((own_full[1], chip_back))
    second_full = own_full[1], links.swap(own_full[1], 1)

    def join_cores(own, other):
        return (own.astype(f32) + links.swap(other, 1).astype(f32)).astype(bf16)

    def reduce_groups(total):
        return lax.psum_scatter(total, "fsdp", scatter_dimension=0, axis_index_groups=lines)

    zero, chip_out = lax.optimization_barrier((join_cores(*zero), chip_out))
    shelf_zero = reduce_groups(zero)
    chip_out, chip_back, *one = run_experts(
        names[1], *rows_chips, second_full, None, False, (chip_out, chip_back)
    )
    cross_top, cross_low = links.send_cross(chip_back[0])
    near_top, far_low = links.swap(chip_back[1, :half], 2), links.swap(chip_back[2, half:], 4)
    own_out, own_back, *one = run_experts(
        names[1], *rows_own, second_full, one, True, (own_out, own_back)
    )
    cross_top, cross_low, near_top, far_low, own_back = lax.optimization_barrier(
        (cross_top, cross_low, near_top, far_low, own_back)
    )
    near_low = (chip_back[1, half:].astype(f32) + cross_low.astype(f32)).astype(bf16)
    far_top = (chip_back[2, :half].astype(f32) + cross_top.astype(f32)).astype(bf16)
    near_low, far_top, one = lax.optimization_barrier((near_low, far_top, one))
    near_low, far_top = links.swap(near_low, 2), links.swap(far_top, 4)
    one = join_cores(*one)
    back_pieces = near_top, near_low, far_top, far_low
    out_cross, one, back_pieces = lax.optimization_barrier((chip_out[0], one, back_pieces))
    shelf_one = reduce_groups(one)
    out_cross = links.send_cross(out_cross)

    core, chip = member % 2, member // 2

    def pack_cores(pack):
        columns = pack.shape[1]
        pack = pack.reshape(groups, MEMBERS // 2, 2, shard, columns)
        own = lax.dynamic_index_in_dim(pack, core, 2, keepdims=False)
        other = links.swap(lax.dynamic_index_in_dim(pack, 1 - core, 2, keepdims=False), 1)

        joined = own.astype(f32) + other.astype(f32)
        return [
            lax.dynamic_index_in_dim(joined, chip ^ bits, 1, keepdims=False).reshape(
                groups * shard, columns
            )
            for bits in range(MEMBERS // 2)
        ]

    def pack_cross(parts):
        return links.send_cross(parts[3].astype(bf16))

    def pack_add(parts, cross):
        return links.add_cross(parts[1].astype(bf16), parts[2].astype(bf16), cross)

    def pack_sum(parts, near, far):
        near, far = links.swap(near, 2), links.swap(far, 4)
        return parts[0] + near.astype(f32) + far.astype(f32)

    middle_grad, mixed_grad, first_pack = middle_back(
        (own_back[0], *back_pieces), packet, middle, cotangent, shares, gains, mixed, whole
    )
    out_near, out_far = links.add_cross(chip_out[1], chip_out[2], out_cross)
    out_near, out_far, mixed_grad = lax.optimization_barrier((out_near, out_far, mixed_grad))
    out_near, out_far = links.swap(out_near, 2), links.swap(out_far, 4)
    first_parts = pack_cores(first_pack)
    projected_grad = attention_back(lengths, rotated, mixed_grad, logs, tables)
    shelf_zero, first_parts, projected_grad = lax.optimization_barrier(
        (shelf_zero, first_parts, projected_grad)
    )
    first_cross = pack_cross(first_parts)
    grad_tokens, second_pack = inputs_back(tokens, gains, projected_grad, whole, middle_grad)
    first_near, first_far = pack_add(first_parts, first_cross)
    first_near, first_far, second_pack, out_near, out_far, shelf_one = lax.optimization_barrier(
        (first_near, first_far, second_pack, out_near, out_far, shelf_one)
    )
    second_parts = pack_cores(second_pack)
    first_sum = pack_sum(first_parts, first_near, first_far)
    shelf_grad = jnp.stack([shelf_zero, shelf_one])
    shelf_grad = shelf_grad.reshape(LOCAL_EXPERTS, 3, MEMBERS, shard, hidden)
    shelf_grad = shelf_grad.transpose(2, 0, 1, 3, 4)
    second_parts, shelf_grad = lax.optimization_barrier((second_parts, shelf_grad))
    second_near, second_far = pack_add(second_parts, pack_cross(second_parts))
    second_sum = pack_sum(second_parts, second_near, second_far)
    pack_total = jnp.concatenate([second_sum, first_sum], axis=1)
    pack_total = links.direct_reduce(pack_total.reshape(groups, shard, pack_total.shape[1]))
    second_total = pack_total[:, : second_sum.shape[1]]
    first_total = pack_total[:, second_sum.shape[1] :]
    expert_shards = links.in_order(*links.keep_parts(links.chip_parts(shelf_grad))).astype(f32)
    expert_shards = expert_shards.reshape(EXPERTS, 3, shard, hidden)
    out_pieces = (own_out[0], out_near, out_far)
    layer_out = (middle + sum(piece.astype(f32) for piece in out_pieces)).astype(bf16)
    return (
        layer_out,
        grad_tokens,
        second_total[:, at_output],
        second_total[:, :head_columns],
        second_total[:, head_columns : head_columns + kv_columns],
        second_total[:, head_columns + kv_columns : at_output],
        first_total[:, :head_columns].T,
        first_total[:, head_columns + EXPERTS],
        first_total[:, head_columns : head_columns + EXPERTS],
        expert_shards[:, 0],
        expert_shards[:, 1],
        expert_shards[:, 2].transpose(0, 2, 1),
    )


def solution(mesh):
    count = mesh.shape["fsdp"]
    placed = (
        P("fsdp", None),
        P("fsdp"),
        P("fsdp", None),
        P("fsdp"),
        P("fsdp", None),
        P("fsdp", None),
        P("fsdp", None),
        P(None, "fsdp"),
        P("fsdp"),
        P("fsdp", None),
        P(None, "fsdp", None),
        P(None, "fsdp", None),
        P(None, None, "fsdp"),
        P("fsdp", None),
    )

    def body(*args):
        return local(*args, count=count)

    return jax.shard_map(
        body,
        mesh=mesh,
        in_specs=placed,
        out_specs=(
            P("fsdp", None),
            P("fsdp", None),
            P("fsdp"),
            P("fsdp", None),
            P("fsdp", None),
            P("fsdp", None),
            P(None, "fsdp"),
            P("fsdp"),
            P("fsdp", None),
            P(None, "fsdp", None),
            P(None, "fsdp", None),
            P(None, None, "fsdp"),
        ),
        check_vma=False,
    )
```

```python
import functools

import jax
import jax.numpy as jnp
import numpy as np
from jax import lax
from jax.experimental import pallas as pl
from jax.experimental.pallas import tpu as pltpu
from jax.sharding import PartitionSpec as P

HEADS = 16
KV_HEADS = 8
HEAD_DIM = 64
EXPERTS = 16
MEMBERS = 8
LOCAL_EXPERTS = EXPERTS // MEMBERS
EXTRA = 128

norm_eps = 1e-06
attention_scale = 0.015625
residual_scale = 0.22
rope_base = 10000.0
masked_value = -1e30
f32 = jnp.float32
bf16 = jnp.bfloat16


def rope_tables(row_count):
    half_dim = HEAD_DIM // 2
    frequency = rope_base ** (-2.0 * np.arange(half_dim, dtype=np.float32) / np.float32(HEAD_DIM))
    angles = np.arange(row_count, dtype=np.float32)[:, None] * frequency.astype(np.float32)[None, :]
    angles = np.concatenate([angles, angles], axis=1)
    return (np.cos(angles), np.sin(angles))


class Exchange:
    def __init__(self, count):
        self.count = count
        self.groups = count // MEMBERS
        index = lax.axis_index("fsdp")
        self.member = index % MEMBERS
        self.group = index // MEMBERS

    def swap(self, value, bits):
        return lax.ppermute(value, "fsdp", [(i, i ^ bits) for i in range(self.count)])

    def direct_gather(self, piece):
        stack = jnp.zeros((self.groups,) + piece.shape, piece.dtype)
        for bits in range(self.groups):
            part = self.swap(piece, bits * MEMBERS) if bits else piece
            stack = lax.dynamic_update_index_in_dim(stack, part, self.group ^ bits, 0)
        return stack

    def direct_reduce(self, terms):
        total = lax.dynamic_index_in_dim(terms, self.group, 0, keepdims=False)
        for bits in range(1, self.groups):
            part = lax.dynamic_index_in_dim(terms, self.group ^ bits, 0, keepdims=False)
            total = total + self.swap(part.astype(bf16), bits * MEMBERS).astype(f32)
        return total

    def to_sides(self, top, low):
        near_top, far_low = self.swap(top, 2), self.swap(low, 4)
        near_low, far_top = self.swap(low, 2), self.swap(top, 4)
        return (near_top, near_low), (far_top, far_low)

    def to_cross(self, near, far):
        return self.swap(near[0], 4), self.swap(far[1], 2)

    def send_cross(self, block):
        half = block.shape[0] // 2
        return self.swap(block[:half], 2), self.swap(block[half:], 4)

    def add_cross(self, near, far, cross):
        half = near.shape[0] // 2
        cross_top, cross_low = cross
        near_low = (near[half:].astype(f32) + cross_low.astype(f32)).astype(bf16)
        far_top = (far[:half].astype(f32) + cross_top.astype(f32)).astype(bf16)
        return (
            jnp.concatenate([near[:half], near_low], axis=0),
            jnp.concatenate([far_top, far[half:]], axis=0),
        )

    def chip_parts(self, parts):
        chips = parts.reshape((MEMBERS // 2, 2) + parts.shape[1:])
        chip = self.member // 2
        found = []
        for bits in range(MEMBERS // 2):
            part = lax.dynamic_index_in_dim(chips, chip ^ bits, 0, keepdims=False)
            found.append(self.swap(part, 2 * bits) if bits else part)
        return found

    def keep_parts(self, found):
        chip, core = self.member // 2, self.member % 2
        arrived = jnp.zeros((MEMBERS // 2,) + found[0].shape, found[0].dtype)
        for bits, part in enumerate(found):
            arrived = lax.dynamic_update_index_in_dim(arrived, part, chip ^ bits, 0)
        kept = lax.dynamic_index_in_dim(arrived, core, 1, keepdims=False)
        other = self.swap(lax.dynamic_index_in_dim(arrived, 1 - core, 1, keepdims=False), 1)
        return kept, other

    def in_order(self, kept, other):
        core = self.member % 2
        even = jnp.where(core == 0, kept, other)
        odd = jnp.where(core == 0, other, kept)
        return jnp.stack([even, odd], axis=1).reshape((MEMBERS,) + kept.shape[1:])


def dot(left, right):
    return jnp.dot(left, right, preferred_element_type=f32)


def dot_turned(left, right):
    return lax.dot_general(left, right, (((1,), (1,)), ((), ())), preferred_element_type=f32)


def expert_kernel(names_ref, *refs, layout, fresh, last, carried):
    refs = list(refs)
    experts = range(names_ref.shape[0])
    packet_parts = [[refs.pop(0) for _ in range(number)] for number in layout]
    cotangent_parts = [[refs.pop(0) for _ in range(number)] for number in layout]
    weight_parts = [refs.pop(0) for _ in experts]
    prior_refs = [None if fresh else refs.pop(0) for _ in experts]
    carried_out, carried_back = (refs.pop(0), refs.pop(0)) if carried else (None, None)
    out_ref, back_ref = refs.pop(0), refs.pop(0)
    result_refs = [refs.pop(0) for _ in experts]
    grad_refs = [refs.pop(0) for _ in experts] if last else result_refs
    packet_buffer, cotangent_buffer, weight_ref, packet_turned, cotangent_turned, sums = refs[:6]
    block_sem, weight_sem, prior_sem = refs[6:]
    rows, width = cotangent_buffer.shape[1:]
    groups, _, depth, _ = weight_parts[0].shape
    blocks = len(layout)
    at = pl.program_id(0)

    def block_copies(block):
        copies = []
        for kind, (parts, buffer) in enumerate(
            ((packet_parts, packet_buffer), (cotangent_parts, cotangent_buffer))
        ):
            size = rows // layout[block]
            for number, part in enumerate(parts[block]):
                place = buffer.at[block, pl.ds(number * size, size)]
                copies.append(
                    pltpu.make_async_copy(part, place, block_sem.at[block, 2 * kind + number])
                )
        return copies

    def weight_copies(n):
        return [
            pltpu.make_async_copy(
                weight_parts[n].at[g], weight_ref.at[n, :, pl.ds(g * depth, depth)], weight_sem.at[n, g]
            )
            for g in range(groups)
        ]

    def prior_copy(n):
        return pltpu.make_async_copy(prior_refs[n], grad_refs[n], prior_sem.at[n])

    @pl.when(at == 0)
    def _():
        for copy in block_copies(0):
            copy.start()
        for n in experts:
            for copy in weight_copies(n):
                copy.start()
        for n in experts:
            if fresh:
                grad_refs[n][...] = jnp.zeros_like(grad_refs[n])
            else:
                prior_copy(n).start()
        for block in range(1, blocks):
            for copy in block_copies(block):
                copy.start()
    for block in range(blocks):

        @pl.when(at == block)
        def _():
            for copy in block_copies(block):
                copy.wait()

    lane = lax.broadcasted_iota(jnp.int32, (rows, EXTRA), 1)
    normed = packet_buffer[at, :, :width]
    upstream = cotangent_buffer[at]
    shares = packet_buffer[at, :, width:].astype(f32)
    extra = jnp.zeros((rows, EXTRA), f32)
    packet_turned[...] = normed.T
    cotangent_turned[...] = upstream.T
    begun = []
    for n in experts:

        @pl.when(at == 0)
        def _():
            for copy in weight_copies(n):
                copy.wait()

        begun.append(
            (
                dot(normed, weight_ref[n, 0]),
                dot(normed, weight_ref[n, 1]),
                dot(upstream, weight_ref[n, 2]),
            )
        )
    if not fresh:

        @pl.when(at == 0)
        def _():
            for n in experts:
                prior_copy(n).wait()

    for n in experts:
        gate_pre, up_pre, inner_raw = begun[n]
        expert = names_ref[n]
        is_high, is_low = lane == expert, lane == expert + EXPERTS
        share = jnp.sum(jnp.where(is_high | is_low, shares, 0.0), axis=1, keepdims=True)
        sigmoid_gate = jax.nn.sigmoid(gate_pre)
        activated = gate_pre * sigmoid_gate
        inner = (activated * up_pre).astype(bf16).astype(f32)
        share_grad = residual_scale * jnp.sum(inner * inner_raw, axis=1, keepdims=True)
        scaled = share * residual_scale
        inner_grad = inner_raw * scaled
        gate_grad = (
            inner_grad * up_pre * (sigmoid_gate + activated * (1.0 - sigmoid_gate))
        ).astype(bf16)
        up_grad = (inner_grad * activated).astype(bf16)
        inner_shared = (inner * scaled).astype(bf16)
        out_term = dot_turned(inner_shared, weight_ref[n, 2])
        back_term = dot_turned(gate_grad, weight_ref[n, 0]) + dot_turned(up_grad, weight_ref[n, 1])
        if n == 0:
            sums[0], sums[1] = out_term, back_term
        else:
            sums[0] += out_term
            sums[1] += back_term
        grad_refs[n][0] += dot(packet_turned[...], gate_grad)
        grad_refs[n][1] += dot(packet_turned[...], up_grad)
        grad_refs[n][2] += dot(cotangent_turned[...], inner_shared)
        high = share_grad.astype(bf16).astype(f32)
        extra = extra + jnp.where(is_high, high, 0.0) + jnp.where(is_low, share_grad - high, 0.0)
    out_total, back_total = sums[0], sums[1]
    if carried:
        out_total = out_total + carried_out[0].astype(f32)
        back_total = back_total + carried_back[0, :, :width].astype(f32)
        extra = extra + carried_back[0, :, width:].astype(f32)
    out_ref[0] = out_total.astype(bf16)
    back_ref[0, :, :width] = back_total.astype(bf16)
    back_ref[0, :, width:] = extra.astype(bf16)

    if last:

        @pl.when(at == blocks - 1)
        def _():
            for n in experts:
                for g in range(groups):
                    result_refs[n][g] = grad_refs[n][:, pl.ds(g * depth, depth)].astype(bf16)


def run_experts(names, packets, cotangents, weights, priors=None, last=False, carried=None):
    layout = tuple(len(parts) for parts in packets)
    blocks = len(layout)
    rows = sum(part.shape[0] for part in packets[0])
    wide, width = packets[0][0].shape[1], cotangents[0][0].shape[1]
    groups, _, depth, hidden = weights[0].shape
    grad_shape = (3, width, hidden)
    fresh = priors is None
    count = len(weights)
    operands = [part for parts in packets for part in parts]
    operands += [part for parts in cotangents for part in parts]
    operands += list(weights) + list(priors or ())

    def whole(shape):
        return pl.BlockSpec(
            shape, lambda i, s, rank=len(shape): (0,) * rank, pipeline_mode=pl.Buffered(1)
        )

    term_specs = [
        pl.BlockSpec((1, rows, columns), lambda i, s: (i, 0, 0)) for columns in (width, wide)
    ]
    in_specs = [pl.BlockSpec(memory_space=pl.ANY)] * len(operands)
    if carried is not None:
        in_specs += term_specs
        operands += list(carried)
    grads = [((groups, 3, depth, hidden), bf16) if last else (grad_shape, f32)] * count
    scratch = [pltpu.VMEM(grad_shape, f32)] * (count if last else 0)
    scratch += [
        pltpu.VMEM((blocks, rows, wide), bf16),
        pltpu.VMEM((blocks, rows, width), bf16),
        pltpu.VMEM((count,) + grad_shape, bf16),
        pltpu.VMEM((width, rows), bf16),
        pltpu.VMEM((width, rows), bf16),
        pltpu.VMEM((2, rows, width), f32),
        pltpu.SemaphoreType.DMA((blocks, 4)),
        pltpu.SemaphoreType.DMA((count, groups)),
        pltpu.SemaphoreType.DMA((count,)),
    ]
    return pl.pallas_call(
        functools.partial(
            expert_kernel, layout=layout, fresh=fresh, last=last, carried=carried is not None
        ),
        grid_spec=pltpu.PrefetchScalarGridSpec(
            num_scalar_prefetch=1,
            grid=(blocks,),
            in_specs=in_specs,
            out_specs=term_specs + [whole(shape) for shape, _ in grads],
            scratch_shapes=scratch,
        ),
        out_shape=[
            jax.ShapeDtypeStruct((blocks, rows, columns), bf16) for columns in (width, wide)
        ]
        + [jax.ShapeDtypeStruct(shape, dtype) for shape, dtype in grads],
        compiler_params=pltpu.CompilerParams(vmem_limit_bytes=62 * 1024 * 1024),
        cost_estimate=pl.CostEstimate(
            flops=blocks * count * 9 * 2 * rows * width * hidden,
            bytes_accessed=blocks * rows * width * 8 + 18 * count * width * hidden,
            transcendentals=blocks * count * rows * hidden,
        ),
        name="experts",
    )(names, *operands)


TILE = 256
PAIR = 2 * HEAD_DIM


def columns_at(index, size):
    return pl.ds(pl.multiple_of(index * size, size), size)


def swap_halves(values):
    width, half_dim = values.shape[1], HEAD_DIM // 2
    lane = lax.broadcasted_iota(jnp.int32, values.shape, 1)
    return jnp.where(
        lane % HEAD_DIM < half_dim,
        pltpu.roll(values, width - half_dim, 1),
        pltpu.roll(values, half_dim, 1),
    )


def row_scale_of(values):
    return lax.rsqrt(jnp.mean(values * values, axis=1, keepdims=True) + norm_eps)


def scores_of(keys, queries, length, first_query):
    scores = attention_scale * dot_turned(keys, queries)
    key_at = lax.broadcasted_iota(jnp.int32, scores.shape, 0)
    query_at = lax.broadcasted_iota(jnp.int32, scores.shape, 1) + first_query
    return jnp.where((key_at <= query_at) & (key_at < length), scores, masked_value)


def head_of(block, index):
    return block[:, index * HEAD_DIM : (index + 1) * HEAD_DIM]


def attention_kernel(
    length_ref, tokens_ref, cosine_ref, sine_ref, gains_ref, weight_ref,
    rotated_ref, mixed_ref, log_ref, normed_ref,
):
    rows = tokens_ref.shape[0]
    head_columns, kv_columns = HEADS * HEAD_DIM, KV_HEADS * HEAD_DIM
    at_value = head_columns + kv_columns
    at_output = at_value + kv_columns
    length = length_ref[0]
    group = HEADS // KV_HEADS

    inputs = tokens_ref[...].astype(f32)
    normed_ref[...] = (inputs * row_scale_of(inputs) * gains_ref[0:1, :]).astype(bf16)

    def project_turned(c, carry):
        where = columns_at(c, TILE)
        value = dot(normed_ref[...], weight_ref[:, where])
        value = value * cosine_ref[...] + swap_halves(value) * sine_ref[...]
        rotated_ref[:, where] = value.astype(bf16)
        return carry

    def project(c, carry):
        where = columns_at(c, TILE)
        rotated_ref[:, where] = dot(normed_ref[...], weight_ref[:, where]).astype(bf16)
        return carry

    lax.fori_loop(0, at_value // TILE, project_turned, 0)
    lax.fori_loop(at_value // TILE, at_output // TILE, project, 0)

    block = rows // 2

    def attend(j, carry):
        queries = rotated_ref[:, columns_at(j, group * PAIR)]
        keys = rotated_ref[:, columns_at(j + head_columns // PAIR, PAIR)]
        values_turned = rotated_ref[:, columns_at(j + at_value // PAIR, PAIR)].T
        outs = []
        for head in range(2 * group):
            kv = head // group
            key, query = head_of(keys, kv), head_of(queries, head)
            value = values_turned[kv * HEAD_DIM : (kv + 1) * HEAD_DIM]
            parts, logs = [], []
            for b in range(2):
                reach = (b + 1) * block
                scores = scores_of(key[:reach], query[b * block : reach], length, b * block)
                best = jnp.max(scores, axis=0, keepdims=True)
                exponent = jnp.exp(scores - best)
                total = jnp.sum(exponent, axis=0, keepdims=True)
                chance = (exponent * (1.0 / total)).astype(bf16)
                parts.append(dot(value[:, :reach], chance))
                logs.append(best + jnp.log(total))
            outs.append(jnp.concatenate(parts, axis=1))
            log_ref[j, head : head + 1, :] = jnp.concatenate(logs, axis=1)
        mixed_ref[:, columns_at(j, group * PAIR)] = jnp.concatenate(outs, axis=0).T.astype(bf16)
        return carry

    lax.fori_loop(0, KV_HEADS // 2, attend, 0)


def router_kernel(
    tokens_ref, routes_ref, gains_ref, mixed_ref, output_ref, extra_ref,
    packet_top_ref, packet_low_ref, middle_ref, share_ref,
):
    rows, width = tokens_ref.shape
    half = rows // 2

    def mix(c, carry):
        where = columns_at(c, TILE)
        branch = dot_turned(mixed_ref[...], output_ref[where, :])
        middle_ref[:, where] = tokens_ref[:, where].astype(f32) + residual_scale * branch
        return carry

    lax.fori_loop(0, width // TILE, mix, 0)
    middle = middle_ref[...]
    normed_two = (middle * row_scale_of(middle) * gains_ref[1:2, :]).astype(bf16)
    packet_top_ref[:, :width] = normed_two[:half]
    packet_low_ref[:, :width] = normed_two[half:]
    logits = dot(normed_two, extra_ref[...])
    lane = lax.broadcasted_iota(jnp.int32, logits.shape, 1)
    routed = lane == routes_ref[:, 0:1]
    for k in range(1, routes_ref.shape[1]):
        routed = routed | (lane == routes_ref[:, k : k + 1])
    best = jnp.max(jnp.where(routed, logits, masked_value), axis=1, keepdims=True)
    weights = jnp.where(routed, jnp.exp(jnp.where(routed, logits, best) - best), 0.0)
    shares = weights / jnp.sum(weights, axis=1, keepdims=True)
    share_ref[...] = shares
    high = shares.astype(bf16).astype(f32)
    both = (high + pltpu.roll(shares - high, EXPERTS, 1)).astype(bf16)
    packet_top_ref[:, width:] = both[:half]
    packet_low_ref[:, width:] = both[half:]


def column_of(row, lanes):
    return jnp.broadcast_to(row, (lanes, row.shape[1])).T


def middle_kernel(
    own_ref, near_top_ref, near_low_ref, far_top_ref, far_low_ref, packet_top_ref,
    packet_low_ref, middle_ref, cotangent_ref, share_ref, gains_ref, mixed_ref, output_ref, extra_ref,
    middle_grad_ref, mixed_grad_ref, pack_ref, back_ref, branch_ref, turned_ref,
):
    width = cotangent_ref.shape[1]
    half = own_ref.shape[0] // 2
    for place, near_ref, far_ref in (
        (pl.ds(0, half), near_top_ref, far_top_ref),
        (pl.ds(half, half), near_low_ref, far_low_ref),
    ):
        back_ref[place] = (
            own_ref[place].astype(f32) + near_ref[...].astype(f32) + far_ref[...].astype(f32)
        )
    shares = share_ref[...]
    share_grad = back_ref[:, width:]
    share_grad = share_grad + pltpu.roll(share_grad, EXTRA - EXPERTS, 1)
    weighted_mean = jnp.sum(shares * share_grad, axis=1, keepdims=True)
    logit_grad = (shares * (share_grad - weighted_mean)).astype(bf16)
    normed_grad = back_ref[:, :width] + dot_turned(logit_grad, extra_ref[...])
    middle = middle_ref[...]
    scale = row_scale_of(middle)
    scaled = middle * scale
    gain_grad = jnp.sum(normed_grad * scaled, axis=0, keepdims=True)
    weighted = normed_grad * gains_ref[1:2, :]
    correction = jnp.mean(weighted * middle, axis=1, keepdims=True)
    middle_grad = cotangent_ref[...].astype(f32) + scale * weighted - scaled * (scale * scale * correction)
    middle_grad_ref[...] = middle_grad
    branch_ref[...] = (residual_scale * middle_grad).astype(bf16)
    router_grad = dot(packet_top_ref[:, :width].T, logit_grad[:half]) + dot(
        packet_low_ref[:, :width].T, logit_grad[half:]
    )
    lane = lax.broadcasted_iota(jnp.int32, router_grad.shape, 1)
    pack_ref[:, width:] = jnp.where(
        lane == EXPERTS, column_of(gain_grad, EXTRA), router_grad
    ).astype(bf16)
    turned_ref[...] = branch_ref[...].T

    def step(c, carry):
        where = columns_at(c, TILE)
        pack_ref[:, where] = dot(turned_ref[...], mixed_ref[:, where]).astype(bf16)
        mixed_grad_ref[:, where] = dot(branch_ref[...], output_ref[:, where]).astype(bf16)
        return carry

    lax.fori_loop(0, output_ref.shape[1] // TILE, step, 0)


def attention_back_kernel(
    length_ref, rotated_ref, mixed_grad_ref, log_ref, cosine_ref, sine_ref, grad_ref
):
    rows = rotated_ref.shape[0]
    head_columns, kv_columns = HEADS * HEAD_DIM, KV_HEADS * HEAD_DIM
    at_value = head_columns + kv_columns
    length = length_ref[0]
    group = HEADS // KV_HEADS
    block = rows // 2

    def attend(j, carry):
        wide = columns_at(j, group * PAIR)
        key_place = columns_at(j + head_columns // PAIR, PAIR)
        value_place = columns_at(j + at_value // PAIR, PAIR)
        queries, grads = rotated_ref[:, wide], mixed_grad_ref[:, wide]
        keys, values = rotated_ref[:, key_place], rotated_ref[:, value_place]
        keys_turned = keys.T
        query_grads, key_grads, value_grads = [], [], []
        for kv in range(2):
            key, value = head_of(keys, kv), head_of(values, kv)
            key_turned = keys_turned[kv * HEAD_DIM : (kv + 1) * HEAD_DIM]
            key_sums, value_sums = [], []
            for member in range(group):
                head = kv * group + member
                query, grad = head_of(queries, head), head_of(grads, head)
                query_parts = []
                for b in range(2):
                    reach = (b + 1) * block
                    query_block, grad_block = query[b * block : reach], grad[b * block : reach]
                    scores = scores_of(key[:reach], query_block, length, b * block)
                    chance = jnp.exp(scores - log_ref[j, head : head + 1, b * block : reach])
                    chance_grad = dot_turned(value[:reach], grad_block)
                    delta = jnp.sum(chance * chance_grad, axis=0, keepdims=True)
                    score_grad = (attention_scale * chance * (chance_grad - delta)).astype(bf16)
                    value_sums.append(dot(chance.astype(bf16), grad_block))
                    key_sums.append(dot(score_grad, query_block))
                    query_parts.append(dot(key_turned[:, :reach], score_grad))
                query_grads.append(jnp.concatenate(query_parts, axis=1))
            for sums, into in ((key_sums, key_grads), (value_sums, value_grads)):
                short = sum(sums[2::2], sums[0])
                long = sum(sums[3::2], sums[1])
                into.append(jnp.concatenate([short + long[:block], long[block:]], axis=0))
        query_grad = jnp.concatenate(query_grads, axis=0).T
        query_grad = query_grad * cosine_ref[...] - swap_halves(query_grad) * sine_ref[...]
        grad_ref[:, wide] = query_grad.astype(bf16)
        key_grad = jnp.concatenate(key_grads, axis=1)
        key_grad = key_grad * cosine_ref[:, :PAIR] - swap_halves(key_grad) * sine_ref[:, :PAIR]
        grad_ref[:, key_place] = key_grad.astype(bf16)
        grad_ref[:, value_place] = jnp.concatenate(value_grads, axis=1).astype(bf16)
        return carry

    lax.fori_loop(0, KV_HEADS // 2, attend, 0)


def inputs_kernel(
    tokens_ref, gains_ref, projected_ref, weight_ref, middle_grad_ref,
    grad_ref, pack_ref, normed_grad_ref, turned_ref,
):
    width = tokens_ref.shape[1]
    projections = projected_ref.shape[1]
    inputs = tokens_ref[...].astype(f32)
    scale = row_scale_of(inputs)
    scaled = inputs * scale
    turned_ref[...] = (scaled * gains_ref[0:1, :]).astype(bf16).T

    def to_weight(c, carry):
        where = columns_at(c, TILE)
        pack_ref[:, where] = dot(turned_ref[...], projected_ref[:, where]).astype(bf16)
        return carry

    def to_input(c, carry):
        where = columns_at(c, TILE)
        normed_grad_ref[:, where] = dot_turned(projected_ref[...], weight_ref[where, :])
        return carry

    lax.fori_loop(0, projections // TILE, to_weight, 0)
    lax.fori_loop(0, width // TILE, to_input, 0)
    normed_grad = normed_grad_ref[...]
    gain_grad = column_of(jnp.sum(normed_grad * scaled, axis=0, keepdims=True), EXTRA)
    lane = lax.broadcasted_iota(jnp.int32, gain_grad.shape, 1)
    pack_ref[:, projections:] = jnp.where(lane == 0, gain_grad, 0.0).astype(bf16)
    weighted = normed_grad * gains_ref[0:1, :]
    correction = jnp.mean(weighted * inputs, axis=1, keepdims=True)
    grad_ref[...] = middle_grad_ref[...] + scale * weighted - scaled * (scale * scale * correction)


def call_kernel(body, name, operands, out_shape, scratch, flops):
    specs, arrays = [], []
    for operand in operands:
        array, shape, index = operand
        if shape == "scalar":
            specs.append(pl.BlockSpec(memory_space=pltpu.SMEM))
        else:
            shape = array.shape if shape is None else shape
            index = (0,) * len(shape) if index is None else index
            specs.append(pl.BlockSpec(shape, lambda i, index=index: index))
        arrays.append(array)
    outs = [jax.ShapeDtypeStruct(shape, dtype) for shape, dtype in out_shape]
    return pl.pallas_call(
        body,
        grid=(1,),
        in_specs=specs,
        out_specs=[
            pl.BlockSpec(out.shape, lambda i, rank=len(out.shape): (0,) * rank) for out in outs
        ],
        out_shape=outs,
        scratch_shapes=[pltpu.VMEM(shape, dtype) for shape, dtype in scratch],
        compiler_params=pltpu.CompilerParams(vmem_limit_bytes=62 * 1024 * 1024),
        cost_estimate=pl.CostEstimate(
            flops=flops,
            bytes_accessed=sum(a.size * a.dtype.itemsize for a in arrays)
            + sum(o.size * o.dtype.itemsize for o in outs),
            transcendentals=0,
        ),
        name=name,
    )(*arrays)


def rope_lanes(row_count):
    cosine_table, sine_table = rope_tables(row_count)
    half_dim = HEAD_DIM // 2
    signed = np.concatenate([-sine_table[:, :half_dim], sine_table[:, half_dim:]], axis=1)
    repeats = TILE // HEAD_DIM
    return jnp.asarray(np.tile(cosine_table, (1, repeats))), jnp.asarray(np.tile(signed, (1, repeats)))


def attention_forward(tokens, lengths, tables, gains, whole):
    rows, width = tokens.shape
    head_columns, kv_columns = HEADS * HEAD_DIM, KV_HEADS * HEAD_DIM
    projections = head_columns + 2 * kv_columns
    return call_kernel(
        attention_kernel,
        "attention_forward",
        [
            (lengths, "scalar", None), (tokens, None, None), (tables[0], None, None),
            (tables[1], None, None), (gains, None, None), (whole, (width, projections), (0, 0)),
        ],
        [
            ((rows, projections), bf16), ((rows, head_columns), bf16),
            ((KV_HEADS // 2, 2 * HEADS // KV_HEADS, rows), f32),
        ],
        [((rows, width), bf16)],
        8 * rows * width * head_columns,
    )


def output_blocks(whole):
    width = whole.shape[0]
    head_columns, kv_columns = HEADS * HEAD_DIM, KV_HEADS * HEAD_DIM
    at_output = head_columns + 2 * kv_columns
    return [
        (whole, (width, head_columns), (0, at_output // head_columns)),
        (whole, (width, EXTRA), (0, (at_output + head_columns) // EXTRA)),
    ]


def router_forward(tokens, routes, gains, mixed, whole):
    rows, width = tokens.shape
    return call_kernel(
        router_kernel,
        "router_forward",
        [(a, None, None) for a in (tokens, routes, gains, mixed)] + output_blocks(whole),
        [((rows // 2, width + EXTRA), bf16)] * 2 + [((rows, width), f32), ((rows, EXTRA), f32)],
        [],
        2 * rows * width * mixed.shape[1],
    )


def middle_back(pieces, packets, middle, cotangent, shares, gains, mixed, whole):
    rows, width = cotangent.shape
    head_columns = HEADS * HEAD_DIM
    return call_kernel(
        middle_kernel,
        "middle_back",
        [(a, None, None) for a in (*pieces, *packets, middle, cotangent, shares, gains, mixed)]
        + output_blocks(whole),
        [((rows, width), f32), ((rows, head_columns), bf16), ((width, head_columns + EXTRA), bf16)],
        [((rows, width + EXTRA), f32), ((rows, width), bf16), ((width, rows), bf16)],
        4 * rows * width * head_columns,
    )


def attention_back(lengths, rotated, mixed_grad, logs, tables):
    return call_kernel(
        attention_back_kernel,
        "attention_back",
        [
            (lengths, "scalar", None), (rotated, None, None), (mixed_grad, None, None),
            (logs, None, None), (tables[0], None, None), (tables[1], None, None),
        ],
        [(rotated.shape, bf16)],
        [],
        10 * rotated.shape[0] ** 2 * HEADS * HEAD_DIM,
    )[0]


def inputs_back(tokens, gains, projected_grad, whole, middle_grad):
    rows, width = tokens.shape
    projections = projected_grad.shape[1]
    return call_kernel(
        inputs_kernel,
        "inputs_back",
        [
            (tokens, None, None), (gains, None, None), (projected_grad, None, None),
            (whole, (width, projections), (0, 0)), (middle_grad, None, None),
        ],
        [((rows, width), f32), ((width, projections + EXTRA), bf16)],
        [((rows, width), f32), ((width, rows), bf16)],
        4 * rows * width * projections,
    )


def local(
    tokens,
    lengths,
    routes,
    attention_gain,
    query_weight,
    key_weight,
    value_weight,
    output_weight,
    expert_gain,
    router_weight,
    gate_weight,
    up_weight,
    down_weight,
    cotangent,
    *,
    count,
):
    links = Exchange(count)
    member, group, groups = links.member, links.group, links.groups
    row_count, width = tokens.shape
    shard = query_weight.shape[0]
    hidden = gate_weight.shape[2]
    head_columns, kv_columns = HEADS * HEAD_DIM, KV_HEADS * HEAD_DIM

    packed = jnp.concatenate(
        [
            query_weight,
            key_weight,
            value_weight,
            output_weight.T,
            router_weight,
            attention_gain[:, None],
            expert_gain[:, None],
            jnp.zeros((shard, EXTRA - EXPERTS - 2), bf16),
        ],
        axis=1,
    )
    pack_width = packed.shape[1]
    column = links.direct_gather(packed).reshape(groups * shard, pack_width)

    mine = jnp.stack([gate_weight, up_weight, down_weight.transpose(0, 2, 1)], axis=1)
    mine = mine.reshape(MEMBERS, LOCAL_EXPERTS, 3, shard, hidden)
    kept, other = links.keep_parts(links.chip_parts(mine))
    other, column = lax.optimization_barrier((other, column))
    shelf = links.in_order(kept, other).transpose(1, 2, 0, 3, 4)
    shelf = shelf.reshape(LOCAL_EXPERTS, 3, MEMBERS * shard, hidden)
    lines = [[m + MEMBERS * g for g in range(groups)] for m in range(MEMBERS)]
    own_full = [
        lax.all_gather(shelf[n], "fsdp", axis_index_groups=lines) for n in range(LOCAL_EXPERTS)
    ]

    half = column.shape[0] // 2
    side_near, side_far = links.to_sides(column[:half], column[half:])
    spread = {0: (column,), 2: side_near, 4: side_far, 6: links.to_cross(side_near, side_far)}
    whole = jnp.zeros((groups, MEMBERS, shard, pack_width), bf16)
    for k in range(MEMBERS):
        parts = spread[k & 6]
        if k & 1:
            parts = [links.swap(part, 1) for part in parts]
        part = jnp.concatenate(parts, axis=0).reshape(groups, shard, pack_width)
        whole = lax.dynamic_update_index_in_dim(whole, part, member ^ k, 1)
    whole = whole.reshape(width, pack_width)
    at_output = head_columns + 2 * kv_columns
    at_extra = at_output + head_columns
    gains = whole[:, at_extra + EXPERTS : at_extra + EXPERTS + 2].astype(f32).T

    half = row_count // 2
    cot_own = cotangent[:half], cotangent[half:]
    cot_late, whole = lax.optimization_barrier((cot_own, whole))
    cot_near, cot_far = links.to_sides(*cot_late)

    tables = rope_lanes(row_count)
    rotated, mixed, logs = attention_forward(tokens, lengths, tables, gains, whole)
    cot_near, cot_far, mixed = lax.optimization_barrier((cot_near, cot_far, mixed))
    cot_cross = links.to_cross(cot_near, cot_far)
    *packet, middle, shares = router_forward(tokens, routes, gains, mixed, whole)
    near, far = links.to_sides(*packet)
    own_full[0], cot_cross, packet = lax.optimization_barrier((own_full[0], cot_cross, packet))

    names = [
        jnp.stack([member, member ^ 1]).astype(jnp.int32) * LOCAL_EXPERTS + n
        for n in range(LOCAL_EXPERTS)
    ]
    rows_own = [packet], [cot_own]
    first_full = own_full[0], links.swap(own_full[0], 1)
    own_out, own_back, *zero = run_experts(names[0], *rows_own, first_full)
    near, far, own_back = lax.optimization_barrier((near, far, own_back))
    cross = links.to_cross(near, far)
    rows_chips = [cross, near, far], [cot_cross, cot_near, cot_far]
    chip_out, chip_back, *zero = run_experts(names[0], *rows_chips, first_full, zero, True)
    own_full[1], chip_back = lax.optimization_barrier((own_full[1], chip_back))
    second_full = own_full[1], links.swap(own_full[1], 1)

    def join_cores(own, other):
        return (own.astype(f32) + links.swap(other, 1).astype(f32)).astype(bf16)

    def reduce_groups(total):
        return lax.psum_scatter(total, "fsdp", scatter_dimension=0, axis_index_groups=lines)

    zero, chip_out = lax.optimization_barrier((join_cores(*zero), chip_out))
    shelf_zero = reduce_groups(zero)
    chip_out, chip_back, *one = run_experts(
        names[1], *rows_chips, second_full, None, False, (chip_out, chip_back)
    )
    cross_top, cross_low = links.send_cross(chip_back[0])
    near_top, far_low = links.swap(chip_back[1, :half], 2), links.swap(chip_back[2, half:], 4)
    own_out, own_back, *one = run_experts(
        names[1], *rows_own, second_full, one, True, (own_out, own_back)
    )
    cross_top, cross_low, near_top, far_low, own_back = lax.optimization_barrier(
        (cross_top, cross_low, near_top, far_low, own_back)
    )
    near_low = (chip_back[1, half:].astype(f32) + cross_low.astype(f32)).astype(bf16)
    far_top = (chip_back[2, :half].astype(f32) + cross_top.astype(f32)).astype(bf16)
    near_low, far_top, one = lax.optimization_barrier((near_low, far_top, one))
    near_low, far_top = links.swap(near_low, 2), links.swap(far_top, 4)
    one = join_cores(*one)
    back_pieces = near_top, near_low, far_top, far_low
    out_cross, one, back_pieces = lax.optimization_barrier((chip_out[0], one, back_pieces))
    shelf_one = reduce_groups(one)
    out_cross = links.send_cross(out_cross)

    core, chip = member % 2, member // 2

    def pack_cores(pack):
        columns = pack.shape[1]
        pack = pack.reshape(groups, MEMBERS // 2, 2, shard, columns)
        own = lax.dynamic_index_in_dim(pack, core, 2, keepdims=False)
        other = links.swap(lax.dynamic_index_in_dim(pack, 1 - core, 2, keepdims=False), 1)

        joined = own.astype(f32) + other.astype(f32)
        return [
            lax.dynamic_index_in_dim(joined, chip ^ bits, 1, keepdims=False).reshape(
                groups * shard, columns
            )
            for bits in range(MEMBERS // 2)
        ]

    def pack_cross(parts):
        return links.send_cross(parts[3].astype(bf16))

    def pack_add(parts, cross):
        return links.add_cross(parts[1].astype(bf16), parts[2].astype(bf16), cross)

    middle_grad, mixed_grad, first_pack = middle_back(
        (own_back[0], *back_pieces), packet, middle, cotangent, shares, gains, mixed, whole
    )
    out_near, out_far = links.add_cross(chip_out[1], chip_out[2], out_cross)
    out_near, out_far, mixed_grad = lax.optimization_barrier((out_near, out_far, mixed_grad))
    out_near, out_far = links.swap(out_near, 2), links.swap(out_far, 4)
    first_parts = pack_cores(first_pack)
    projected_grad = attention_back(lengths, rotated, mixed_grad, logs, tables)
    shelf_zero, first_parts, projected_grad = lax.optimization_barrier(
        (shelf_zero, first_parts, projected_grad)
    )
    first_cross = pack_cross(first_parts)
    grad_tokens, second_pack = inputs_back(tokens, gains, projected_grad, whole, middle_grad)
    first_near, first_far = pack_add(first_parts, first_cross)
    first_near, first_far, second_pack, out_near, out_far, shelf_one = lax.optimization_barrier(
        (first_near, first_far, second_pack, out_near, out_far, shelf_one)
    )
    second_parts = pack_cores(second_pack)
    first_near, first_far = links.swap(first_near, 2), links.swap(first_far, 4)
    first_sum = first_parts[0] + first_near.astype(f32) + first_far.astype(f32)
    shelf_grad = jnp.stack([shelf_zero, shelf_one])
    shelf_grad = shelf_grad.reshape(LOCAL_EXPERTS, 3, MEMBERS, shard, hidden)
    shelf_grad = shelf_grad.transpose(2, 0, 1, 3, 4)
    second_near, second_far = pack_add(second_parts, pack_cross(second_parts))
    second_near, second_far = links.swap(second_near, 2), links.swap(second_far, 4)
    second_near, second_far, shelf_grad = lax.optimization_barrier(
        (second_near, second_far, shelf_grad)
    )
    second_sum = second_parts[0] + second_near.astype(f32) + second_far.astype(f32)
    pack_total = jnp.concatenate([second_sum, first_sum], axis=1)
    pack_total = links.direct_reduce(pack_total.reshape(groups, shard, pack_total.shape[1]))
    second_total = pack_total[:, : second_sum.shape[1]]
    first_total = pack_total[:, second_sum.shape[1] :]
    expert_shards = links.in_order(*links.keep_parts(links.chip_parts(shelf_grad))).astype(f32)
    expert_shards = expert_shards.reshape(EXPERTS, 3, shard, hidden)
    out_pieces = (own_out[0], out_near, out_far)
    layer_out = (middle + sum(piece.astype(f32) for piece in out_pieces)).astype(bf16)
    return (
        layer_out,
        grad_tokens,
        second_total[:, at_output],
        second_total[:, :head_columns],
        second_total[:, head_columns : head_columns + kv_columns],
        second_total[:, head_columns + kv_columns : at_output],
        first_total[:, :head_columns].T,
        first_total[:, head_columns + EXPERTS],
        first_total[:, head_columns : head_columns + EXPERTS],
        expert_shards[:, 0],
        expert_shards[:, 1],
        expert_shards[:, 2].transpose(0, 2, 1),
    )


def solution(mesh):
    count = mesh.shape["fsdp"]
    placed = (
        P("fsdp", None),
        P("fsdp"),
        P("fsdp", None),
        P("fsdp"),
        P("fsdp", None),
        P("fsdp", None),
        P("fsdp", None),
        P(None, "fsdp"),
        P("fsdp"),
        P("fsdp", None),
        P(None, "fsdp", None),
        P(None, "fsdp", None),
        P(None, None, "fsdp"),
        P("fsdp", None),
    )

    def body(*args):
        return local(*args, count=count)

    return jax.shard_map(
        body,
        mesh=mesh,
        in_specs=placed,
        out_specs=(
            P("fsdp", None),
            P("fsdp", None),
            P("fsdp"),
            P("fsdp", None),
            P("fsdp", None),
            P("fsdp", None),
            P(None, "fsdp"),
            P("fsdp"),
            P("fsdp", None),
            P(None, "fsdp", None),
            P(None, "fsdp", None),
            P(None, None, "fsdp"),
        ),
        check_vma=False,
    )
```

```python
import functools

import jax
import jax.numpy as jnp
import numpy as np
from jax import lax
from jax.experimental import pallas as pl
from jax.experimental.pallas import tpu as pltpu
from jax.sharding import PartitionSpec as P

HEADS = 16
KV_HEADS = 8
HEAD_DIM = 64
EXPERTS = 16
MEMBERS = 8
LOCAL_EXPERTS = EXPERTS // MEMBERS
EXTRA = 128

norm_eps = 1e-06
attention_scale = 0.015625
residual_scale = 0.22
rope_base = 10000.0
masked_value = -1e30
f32 = jnp.float32
bf16 = jnp.bfloat16


def rope_tables(row_count):
    half_dim = HEAD_DIM // 2
    frequency = rope_base ** (-2.0 * np.arange(half_dim, dtype=np.float32) / np.float32(HEAD_DIM))
    angles = np.arange(row_count, dtype=np.float32)[:, None] * frequency.astype(np.float32)[None, :]
    angles = np.concatenate([angles, angles], axis=1)
    return (np.cos(angles), np.sin(angles))


class Exchange:
    def __init__(self, count):
        self.count = count
        self.groups = count // MEMBERS
        index = lax.axis_index("fsdp")
        self.member = index % MEMBERS
        self.group = index // MEMBERS

    def swap(self, value, bits):
        return lax.ppermute(value, "fsdp", [(i, i ^ bits) for i in range(self.count)])

    def direct_gather(self, piece):
        stack = jnp.zeros((self.groups,) + piece.shape, piece.dtype)
        for bits in range(self.groups):
            part = self.swap(piece, bits * MEMBERS) if bits else piece
            stack = lax.dynamic_update_index_in_dim(stack, part, self.group ^ bits, 0)
        return stack

    def direct_reduce(self, terms):
        total = lax.dynamic_index_in_dim(terms, self.group, 0, keepdims=False)
        for bits in range(1, self.groups):
            part = lax.dynamic_index_in_dim(terms, self.group ^ bits, 0, keepdims=False)
            total = total + self.swap(part.astype(bf16), bits * MEMBERS).astype(f32)
        return total

    def to_sides(self, top, low):
        near_top, far_low = self.swap(top, 2), self.swap(low, 4)
        near_low, far_top = self.swap(low, 2), self.swap(top, 4)
        return (near_top, near_low), (far_top, far_low)

    def to_cross(self, near, far):
        return self.swap(near[0], 4), self.swap(far[1], 2)

    def send_cross(self, block):
        half = block.shape[0] // 2
        return self.swap(block[:half], 2), self.swap(block[half:], 4)

    def add_cross(self, near, far, cross):
        half = near.shape[0] // 2
        cross_top, cross_low = cross
        near_low = (near[half:].astype(f32) + cross_low.astype(f32)).astype(bf16)
        far_top = (far[:half].astype(f32) + cross_top.astype(f32)).astype(bf16)
        return (
            jnp.concatenate([near[:half], near_low], axis=0),
            jnp.concatenate([far_top, far[half:]], axis=0),
        )

    def chip_parts(self, parts):
        chips = parts.reshape((MEMBERS // 2, 2) + parts.shape[1:])
        chip = self.member // 2
        found = []
        for bits in range(MEMBERS // 2):
            part = lax.dynamic_index_in_dim(chips, chip ^ bits, 0, keepdims=False)
            found.append(self.swap(part, 2 * bits) if bits else part)
        return found

    def keep_parts(self, found):
        chip, core = self.member // 2, self.member % 2
        arrived = jnp.zeros((MEMBERS // 2,) + found[0].shape, found[0].dtype)
        for bits, part in enumerate(found):
            arrived = lax.dynamic_update_index_in_dim(arrived, part, chip ^ bits, 0)
        kept = lax.dynamic_index_in_dim(arrived, core, 1, keepdims=False)
        other = self.swap(lax.dynamic_index_in_dim(arrived, 1 - core, 1, keepdims=False), 1)
        return kept, other

    def in_order(self, kept, other):
        core = self.member % 2
        even = jnp.where(core == 0, kept, other)
        odd = jnp.where(core == 0, other, kept)
        return jnp.stack([even, odd], axis=1).reshape((MEMBERS,) + kept.shape[1:])


def dot(left, right):
    return jnp.dot(left, right, preferred_element_type=f32)


def dot_turned(left, right):
    return lax.dot_general(left, right, (((1,), (1,)), ((), ())), preferred_element_type=f32)


def expert_kernel(names_ref, *refs, layout, fresh, last, carried):
    refs = list(refs)
    experts = range(names_ref.shape[0])
    packet_parts = [[refs.pop(0) for _ in range(number)] for number in layout]
    cotangent_parts = [[refs.pop(0) for _ in range(number)] for number in layout]
    weight_parts = [refs.pop(0) for _ in experts]
    prior_refs = [None if fresh else refs.pop(0) for _ in experts]
    carried_out, carried_back = (refs.pop(0), refs.pop(0)) if carried else (None, None)
    out_ref, back_ref = refs.pop(0), refs.pop(0)
    result_refs = [refs.pop(0) for _ in experts]
    grad_refs = [refs.pop(0) for _ in experts] if last else result_refs
    packet_buffer, cotangent_buffer, weight_ref, packet_turned, cotangent_turned, sums = refs[:6]
    block_sem, weight_sem, prior_sem = refs[6:]
    rows, width = cotangent_buffer.shape[1:]
    groups, _, depth, _ = weight_parts[0].shape
    blocks = len(layout)
    at = pl.program_id(0)

    def block_copies(block):
        copies = []
        for kind, (parts, buffer) in enumerate(
            ((packet_parts, packet_buffer), (cotangent_parts, cotangent_buffer))
        ):
            size = rows // layout[block]
            for number, part in enumerate(parts[block]):
                place = buffer.at[block, pl.ds(number * size, size)]
                copies.append(
                    pltpu.make_async_copy(part, place, block_sem.at[block, 2 * kind + number])
                )
        return copies

    def weight_copies(n):
        return [
            pltpu.make_async_copy(
                weight_parts[n].at[g], weight_ref.at[n, :, pl.ds(g * depth, depth)], weight_sem.at[n, g]
            )
            for g in range(groups)
        ]

    def prior_copy(n):
        return pltpu.make_async_copy(prior_refs[n], grad_refs[n], prior_sem.at[n])

    @pl.when(at == 0)
    def _():
        for copy in block_copies(0):
            copy.start()
        for n in experts:
            for copy in weight_copies(n):
                copy.start()
        for n in experts:
            if fresh:
                grad_refs[n][...] = jnp.zeros_like(grad_refs[n])
            else:
                prior_copy(n).start()
        for block in range(1, blocks):
            for copy in block_copies(block):
                copy.start()
        for n in experts:
            for copy in weight_copies(n):
                copy.wait()
    for block in range(blocks):

        @pl.when(at == block)
        def _():
            for copy in block_copies(block):
                copy.wait()

    lane = lax.broadcasted_iota(jnp.int32, (rows, EXTRA), 1)
    normed = packet_buffer[at, :, :width]
    upstream = cotangent_buffer[at]
    shares = packet_buffer[at, :, width:].astype(f32)
    extra = jnp.zeros((rows, EXTRA), f32)
    packet_turned[...] = normed.T
    cotangent_turned[...] = upstream.T
    begun = []
    for n in experts:
        begun.append(
            (
                dot(normed, weight_ref[n, 0]),
                dot(normed, weight_ref[n, 1]),
                dot(upstream, weight_ref[n, 2]),
            )
        )
    if not fresh:

        @pl.when(at == 0)
        def _():
            for n in experts:
                prior_copy(n).wait()

    for n in experts:
        gate_pre, up_pre, inner_raw = begun[n]
        expert = names_ref[n]
        is_high, is_low = lane == expert, lane == expert + EXPERTS
        share = jnp.sum(jnp.where(is_high | is_low, shares, 0.0), axis=1, keepdims=True)
        sigmoid_gate = jax.nn.sigmoid(gate_pre)
        activated = gate_pre * sigmoid_gate
        inner = (activated * up_pre).astype(bf16).astype(f32)
        share_grad = residual_scale * jnp.sum(inner * inner_raw, axis=1, keepdims=True)
        scaled = share * residual_scale
        inner_grad = inner_raw * scaled
        gate_grad = (
            inner_grad * up_pre * (sigmoid_gate + activated * (1.0 - sigmoid_gate))
        ).astype(bf16)
        up_grad = (inner_grad * activated).astype(bf16)
        inner_shared = (inner * scaled).astype(bf16)
        out_term = dot_turned(inner_shared, weight_ref[n, 2])
        back_term = dot_turned(gate_grad, weight_ref[n, 0]) + dot_turned(up_grad, weight_ref[n, 1])
        if n == 0:
            sums[0], sums[1] = out_term, back_term
        else:
            sums[0] += out_term
            sums[1] += back_term
        grad_refs[n][0] += dot(packet_turned[...], gate_grad)
        grad_refs[n][1] += dot(packet_turned[...], up_grad)
        grad_refs[n][2] += dot(cotangent_turned[...], inner_shared)
        high = share_grad.astype(bf16).astype(f32)
        extra = extra + jnp.where(is_high, high, 0.0) + jnp.where(is_low, share_grad - high, 0.0)
    out_total, back_total = sums[0], sums[1]
    if carried:
        out_total = out_total + carried_out[0].astype(f32)
        back_total = back_total + carried_back[0, :, :width].astype(f32)
        extra = extra + carried_back[0, :, width:].astype(f32)
    out_ref[0] = out_total.astype(bf16)
    back_ref[0, :, :width] = back_total.astype(bf16)
    back_ref[0, :, width:] = extra.astype(bf16)

    if last:

        @pl.when(at == blocks - 1)
        def _():
            for n in experts:
                for g in range(groups):
                    result_refs[n][g] = grad_refs[n][:, pl.ds(g * depth, depth)].astype(bf16)


def run_experts(names, packets, cotangents, weights, priors=None, last=False, carried=None):
    layout = tuple(len(parts) for parts in packets)
    blocks = len(layout)
    rows = sum(part.shape[0] for part in packets[0])
    wide, width = packets[0][0].shape[1], cotangents[0][0].shape[1]
    groups, _, depth, hidden = weights[0].shape
    grad_shape = (3, width, hidden)
    fresh = priors is None
    count = len(weights)
    operands = [part for parts in packets for part in parts]
    operands += [part for parts in cotangents for part in parts]
    operands += list(weights) + list(priors or ())

    def whole(shape):
        return pl.BlockSpec(
            shape, lambda i, s, rank=len(shape): (0,) * rank, pipeline_mode=pl.Buffered(1)
        )

    term_specs = [
        pl.BlockSpec((1, rows, columns), lambda i, s: (i, 0, 0)) for columns in (width, wide)
    ]
    in_specs = [pl.BlockSpec(memory_space=pl.ANY)] * len(operands)
    if carried is not None:
        in_specs += term_specs
        operands += list(carried)
    grads = [((groups, 3, depth, hidden), bf16) if last else (grad_shape, f32)] * count
    scratch = [pltpu.VMEM(grad_shape, f32)] * (count if last else 0)
    scratch += [
        pltpu.VMEM((blocks, rows, wide), bf16),
        pltpu.VMEM((blocks, rows, width), bf16),
        pltpu.VMEM((count,) + grad_shape, bf16),
        pltpu.VMEM((width, rows), bf16),
        pltpu.VMEM((width, rows), bf16),
        pltpu.VMEM((2, rows, width), f32),
        pltpu.SemaphoreType.DMA((blocks, 4)),
        pltpu.SemaphoreType.DMA((count, groups)),
        pltpu.SemaphoreType.DMA((count,)),
    ]
    return pl.pallas_call(
        functools.partial(
            expert_kernel, layout=layout, fresh=fresh, last=last, carried=carried is not None
        ),
        grid_spec=pltpu.PrefetchScalarGridSpec(
            num_scalar_prefetch=1,
            grid=(blocks,),
            in_specs=in_specs,
            out_specs=term_specs + [whole(shape) for shape, _ in grads],
            scratch_shapes=scratch,
        ),
        out_shape=[
            jax.ShapeDtypeStruct((blocks, rows, columns), bf16) for columns in (width, wide)
        ]
        + [jax.ShapeDtypeStruct(shape, dtype) for shape, dtype in grads],
        compiler_params=pltpu.CompilerParams(vmem_limit_bytes=62 * 1024 * 1024),
        cost_estimate=pl.CostEstimate(
            flops=blocks * count * 9 * 2 * rows * width * hidden,
            bytes_accessed=blocks * rows * width * 8 + 18 * count * width * hidden,
            transcendentals=blocks * count * rows * hidden,
        ),
        name="experts",
    )(names, *operands)


TILE = 256
PAIR = 2 * HEAD_DIM


def columns_at(index, size):
    return pl.ds(pl.multiple_of(index * size, size), size)


def swap_halves(values):
    width, half_dim = values.shape[1], HEAD_DIM // 2
    lane = lax.broadcasted_iota(jnp.int32, values.shape, 1)
    return jnp.where(
        lane % HEAD_DIM < half_dim,
        pltpu.roll(values, width - half_dim, 1),
        pltpu.roll(values, half_dim, 1),
    )


def row_scale_of(values):
    return lax.rsqrt(jnp.mean(values * values, axis=1, keepdims=True) + norm_eps)


def scores_of(keys, queries, length, first_query):
    scores = attention_scale * dot_turned(keys, queries)
    key_at = lax.broadcasted_iota(jnp.int32, scores.shape, 0)
    query_at = lax.broadcasted_iota(jnp.int32, scores.shape, 1) + first_query
    return jnp.where((key_at <= query_at) & (key_at < length), scores, masked_value)


def head_of(block, index):
    return block[:, index * HEAD_DIM : (index + 1) * HEAD_DIM]


def attention_kernel(
    length_ref, tokens_ref, cosine_ref, sine_ref, gains_ref, weight_ref,
    rotated_ref, mixed_ref, log_ref, normed_ref,
):
    rows = tokens_ref.shape[0]
    head_columns, kv_columns = HEADS * HEAD_DIM, KV_HEADS * HEAD_DIM
    at_value = head_columns + kv_columns
    at_output = at_value + kv_columns
    length = length_ref[0]
    group = HEADS // KV_HEADS

    inputs = tokens_ref[...].astype(f32)
    normed_ref[...] = (inputs * row_scale_of(inputs) * gains_ref[0:1, :]).astype(bf16)

    def project_turned(c, carry):
        where = columns_at(c, TILE)
        value = dot(normed_ref[...], weight_ref[:, where])
        value = value * cosine_ref[...] + swap_halves(value) * sine_ref[...]
        rotated_ref[:, where] = value.astype(bf16)
        return carry

    def project(c, carry):
        where = columns_at(c, TILE)
        rotated_ref[:, where] = dot(normed_ref[...], weight_ref[:, where]).astype(bf16)
        return carry

    lax.fori_loop(0, at_value // TILE, project_turned, 0)
    lax.fori_loop(at_value // TILE, at_output // TILE, project, 0)

    block = rows // 2

    def attend(j, carry):
        queries = rotated_ref[:, columns_at(j, group * PAIR)]
        keys = rotated_ref[:, columns_at(j + head_columns // PAIR, PAIR)]
        values_turned = rotated_ref[:, columns_at(j + at_value // PAIR, PAIR)].T
        outs = []
        for head in range(2 * group):
            kv = head // group
            key, query = head_of(keys, kv), head_of(queries, head)
            value = values_turned[kv * HEAD_DIM : (kv + 1) * HEAD_DIM]
            parts, logs = [], []
            for b in range(2):
                reach = (b + 1) * block
                scores = scores_of(key[:reach], query[b * block : reach], length, b * block)
                best = jnp.max(scores, axis=0, keepdims=True)
                exponent = jnp.exp(scores - best)
                total = jnp.sum(exponent, axis=0, keepdims=True)
                chance = (exponent * (1.0 / total)).astype(bf16)
                parts.append(dot(value[:, :reach], chance))
                logs.append(best + jnp.log(total))
            outs.append(jnp.concatenate(parts, axis=1))
            log_ref[j, head : head + 1, :] = jnp.concatenate(logs, axis=1)
        mixed_ref[:, columns_at(j, group * PAIR)] = jnp.concatenate(outs, axis=0).T.astype(bf16)
        return carry

    lax.fori_loop(0, KV_HEADS // 2, attend, 0)


def router_kernel(
    tokens_ref, routes_ref, gains_ref, mixed_ref, output_ref, extra_ref,
    packet_top_ref, packet_low_ref, middle_ref, share_ref,
):
    rows, width = tokens_ref.shape
    half = rows // 2

    def mix(c, carry):
        where = columns_at(c, TILE)
        branch = dot_turned(mixed_ref[...], output_ref[where, :])
        middle_ref[:, where] = tokens_ref[:, where].astype(f32) + residual_scale * branch
        return carry

    lax.fori_loop(0, width // TILE, mix, 0)
    middle = middle_ref[...]
    normed_two = (middle * row_scale_of(middle) * gains_ref[1:2, :]).astype(bf16)
    packet_top_ref[:, :width] = normed_two[:half]
    packet_low_ref[:, :width] = normed_two[half:]
    logits = dot(normed_two, extra_ref[...])
    lane = lax.broadcasted_iota(jnp.int32, logits.shape, 1)
    routed = lane == routes_ref[:, 0:1]
    for k in range(1, routes_ref.shape[1]):
        routed = routed | (lane == routes_ref[:, k : k + 1])
    best = jnp.max(jnp.where(routed, logits, masked_value), axis=1, keepdims=True)
    weights = jnp.where(routed, jnp.exp(jnp.where(routed, logits, best) - best), 0.0)
    shares = weights / jnp.sum(weights, axis=1, keepdims=True)
    share_ref[...] = shares
    high = shares.astype(bf16).astype(f32)
    both = (high + pltpu.roll(shares - high, EXPERTS, 1)).astype(bf16)
    packet_top_ref[:, width:] = both[:half]
    packet_low_ref[:, width:] = both[half:]


def column_of(row, lanes):
    return jnp.broadcast_to(row, (lanes, row.shape[1])).T


def middle_kernel(
    own_ref, near_top_ref, near_low_ref, far_top_ref, far_low_ref, packet_top_ref,
    packet_low_ref, middle_ref, cotangent_ref, share_ref, gains_ref, mixed_ref, output_ref, extra_ref,
    middle_grad_ref, mixed_grad_ref, pack_ref, back_ref, branch_ref, turned_ref,
):
    width = cotangent_ref.shape[1]
    half = own_ref.shape[0] // 2
    for place, near_ref, far_ref in (
        (pl.ds(0, half), near_top_ref, far_top_ref),
        (pl.ds(half, half), near_low_ref, far_low_ref),
    ):
        back_ref[place] = (
            own_ref[place].astype(f32) + near_ref[...].astype(f32) + far_ref[...].astype(f32)
        )
    shares = share_ref[...]
    share_grad = back_ref[:, width:]
    share_grad = share_grad + pltpu.roll(share_grad, EXTRA - EXPERTS, 1)
    weighted_mean = jnp.sum(shares * share_grad, axis=1, keepdims=True)
    logit_grad = (shares * (share_grad - weighted_mean)).astype(bf16)
    normed_grad = back_ref[:, :width] + dot_turned(logit_grad, extra_ref[...])
    middle = middle_ref[...]
    scale = row_scale_of(middle)
    scaled = middle * scale
    gain_grad = jnp.sum(normed_grad * scaled, axis=0, keepdims=True)
    weighted = normed_grad * gains_ref[1:2, :]
    correction = jnp.mean(weighted * middle, axis=1, keepdims=True)
    middle_grad = cotangent_ref[...].astype(f32) + scale * weighted - scaled * (scale * scale * correction)
    middle_grad_ref[...] = middle_grad
    branch_ref[...] = (residual_scale * middle_grad).astype(bf16)
    router_grad = dot(packet_top_ref[:, :width].T, logit_grad[:half]) + dot(
        packet_low_ref[:, :width].T, logit_grad[half:]
    )
    lane = lax.broadcasted_iota(jnp.int32, router_grad.shape, 1)
    pack_ref[:, width:] = jnp.where(
        lane == EXPERTS, column_of(gain_grad, EXTRA), router_grad
    ).astype(bf16)
    turned_ref[...] = branch_ref[...].T

    def step(c, carry):
        where = columns_at(c, TILE)
        pack_ref[:, where] = dot(turned_ref[...], mixed_ref[:, where]).astype(bf16)
        mixed_grad_ref[:, where] = dot(branch_ref[...], output_ref[:, where]).astype(bf16)
        return carry

    lax.fori_loop(0, output_ref.shape[1] // TILE, step, 0)


def attention_back_kernel(
    length_ref, rotated_ref, mixed_grad_ref, log_ref, cosine_ref, sine_ref, grad_ref
):
    rows = rotated_ref.shape[0]
    head_columns, kv_columns = HEADS * HEAD_DIM, KV_HEADS * HEAD_DIM
    at_value = head_columns + kv_columns
    length = length_ref[0]
    group = HEADS // KV_HEADS
    block = rows // 2

    def attend(j, carry):
        wide = columns_at(j, group * PAIR)
        key_place = columns_at(j + head_columns // PAIR, PAIR)
        value_place = columns_at(j + at_value // PAIR, PAIR)
        queries, grads = rotated_ref[:, wide], mixed_grad_ref[:, wide]
        keys, values = rotated_ref[:, key_place], rotated_ref[:, value_place]
        keys_turned = keys.T
        query_grads, key_grads, value_grads = [], [], []
        for kv in range(2):
            key, value = head_of(keys, kv), head_of(values, kv)
            key_turned = keys_turned[kv * HEAD_DIM : (kv + 1) * HEAD_DIM]
            key_sums, value_sums = [], []
            for member in range(group):
                head = kv * group + member
                query, grad = head_of(queries, head), head_of(grads, head)
                query_parts = []
                for b in range(2):
                    reach = (b + 1) * block
                    query_block, grad_block = query[b * block : reach], grad[b * block : reach]
                    scores = scores_of(key[:reach], query_block, length, b * block)
                    chance = jnp.exp(scores - log_ref[j, head : head + 1, b * block : reach])
                    chance_grad = dot_turned(value[:reach], grad_block)
                    delta = jnp.sum(chance * chance_grad, axis=0, keepdims=True)
                    score_grad = (attention_scale * chance * (chance_grad - delta)).astype(bf16)
                    value_sums.append(dot(chance.astype(bf16), grad_block))
                    key_sums.append(dot(score_grad, query_block))
                    query_parts.append(dot(key_turned[:, :reach], score_grad))
                query_grads.append(jnp.concatenate(query_parts, axis=1))
            for sums, into in ((key_sums, key_grads), (value_sums, value_grads)):
                short = sum(sums[2::2], sums[0])
                long = sum(sums[3::2], sums[1])
                into.append(jnp.concatenate([short + long[:block], long[block:]], axis=0))
        query_grad = jnp.concatenate(query_grads, axis=0).T
        query_grad = query_grad * cosine_ref[...] - swap_halves(query_grad) * sine_ref[...]
        grad_ref[:, wide] = query_grad.astype(bf16)
        key_grad = jnp.concatenate(key_grads, axis=1)
        key_grad = key_grad * cosine_ref[:, :PAIR] - swap_halves(key_grad) * sine_ref[:, :PAIR]
        grad_ref[:, key_place] = key_grad.astype(bf16)
        grad_ref[:, value_place] = jnp.concatenate(value_grads, axis=1).astype(bf16)
        return carry

    lax.fori_loop(0, KV_HEADS // 2, attend, 0)


def inputs_kernel(
    tokens_ref, gains_ref, projected_ref, weight_ref, middle_grad_ref,
    grad_ref, pack_ref, normed_grad_ref, turned_ref,
):
    width = tokens_ref.shape[1]
    projections = projected_ref.shape[1]
    inputs = tokens_ref[...].astype(f32)
    scale = row_scale_of(inputs)
    scaled = inputs * scale
    turned_ref[...] = (scaled * gains_ref[0:1, :]).astype(bf16).T

    def to_weight(c, carry):
        where = columns_at(c, TILE)
        pack_ref[:, where] = dot(turned_ref[...], projected_ref[:, where]).astype(bf16)
        return carry

    def to_input(c, carry):
        where = columns_at(c, TILE)
        normed_grad_ref[:, where] = dot_turned(projected_ref[...], weight_ref[where, :])
        return carry

    lax.fori_loop(0, projections // TILE, to_weight, 0)
    lax.fori_loop(0, width // TILE, to_input, 0)
    normed_grad = normed_grad_ref[...]
    gain_grad = column_of(jnp.sum(normed_grad * scaled, axis=0, keepdims=True), EXTRA)
    lane = lax.broadcasted_iota(jnp.int32, gain_grad.shape, 1)
    pack_ref[:, projections:] = jnp.where(lane == 0, gain_grad, 0.0).astype(bf16)
    weighted = normed_grad * gains_ref[0:1, :]
    correction = jnp.mean(weighted * inputs, axis=1, keepdims=True)
    grad_ref[...] = middle_grad_ref[...] + scale * weighted - scaled * (scale * scale * correction)


def call_kernel(body, name, operands, out_shape, scratch, flops):
    specs, arrays = [], []
    for operand in operands:
        array, shape, index = operand
        if shape == "scalar":
            specs.append(pl.BlockSpec(memory_space=pltpu.SMEM))
        else:
            shape = array.shape if shape is None else shape
            index = (0,) * len(shape) if index is None else index
            specs.append(pl.BlockSpec(shape, lambda i, index=index: index))
        arrays.append(array)
    outs = [jax.ShapeDtypeStruct(shape, dtype) for shape, dtype in out_shape]
    return pl.pallas_call(
        body,
        grid=(1,),
        in_specs=specs,
        out_specs=[
            pl.BlockSpec(out.shape, lambda i, rank=len(out.shape): (0,) * rank) for out in outs
        ],
        out_shape=outs,
        scratch_shapes=[pltpu.VMEM(shape, dtype) for shape, dtype in scratch],
        compiler_params=pltpu.CompilerParams(vmem_limit_bytes=62 * 1024 * 1024),
        cost_estimate=pl.CostEstimate(
            flops=flops,
            bytes_accessed=sum(a.size * a.dtype.itemsize for a in arrays)
            + sum(o.size * o.dtype.itemsize for o in outs),
            transcendentals=0,
        ),
        name=name,
    )(*arrays)


def rope_lanes(row_count):
    cosine_table, sine_table = rope_tables(row_count)
    half_dim = HEAD_DIM // 2
    signed = np.concatenate([-sine_table[:, :half_dim], sine_table[:, half_dim:]], axis=1)
    repeats = TILE // HEAD_DIM
    return jnp.asarray(np.tile(cosine_table, (1, repeats))), jnp.asarray(np.tile(signed, (1, repeats)))


def attention_forward(tokens, lengths, tables, gains, whole):
    rows, width = tokens.shape
    head_columns, kv_columns = HEADS * HEAD_DIM, KV_HEADS * HEAD_DIM
    projections = head_columns + 2 * kv_columns
    return call_kernel(
        attention_kernel,
        "attention_forward",
        [
            (lengths, "scalar", None), (tokens, None, None), (tables[0], None, None),
            (tables[1], None, None), (gains, None, None), (whole, (width, projections), (0, 0)),
        ],
        [
            ((rows, projections), bf16), ((rows, head_columns), bf16),
            ((KV_HEADS // 2, 2 * HEADS // KV_HEADS, rows), f32),
        ],
        [((rows, width), bf16)],
        8 * rows * width * head_columns,
    )


def output_blocks(whole):
    width = whole.shape[0]
    head_columns, kv_columns = HEADS * HEAD_DIM, KV_HEADS * HEAD_DIM
    at_output = head_columns + 2 * kv_columns
    return [
        (whole, (width, head_columns), (0, at_output // head_columns)),
        (whole, (width, EXTRA), (0, (at_output + head_columns) // EXTRA)),
    ]


def router_forward(tokens, routes, gains, mixed, whole):
    rows, width = tokens.shape
    return call_kernel(
        router_kernel,
        "router_forward",
        [(a, None, None) for a in (tokens, routes, gains, mixed)] + output_blocks(whole),
        [((rows // 2, width + EXTRA), bf16)] * 2 + [((rows, width), f32), ((rows, EXTRA), f32)],
        [],
        2 * rows * width * mixed.shape[1],
    )


def middle_back(pieces, packets, middle, cotangent, shares, gains, mixed, whole):
    rows, width = cotangent.shape
    head_columns = HEADS * HEAD_DIM
    return call_kernel(
        middle_kernel,
        "middle_back",
        [(a, None, None) for a in (*pieces, *packets, middle, cotangent, shares, gains, mixed)]
        + output_blocks(whole),
        [((rows, width), f32), ((rows, head_columns), bf16), ((width, head_columns + EXTRA), bf16)],
        [((rows, width + EXTRA), f32), ((rows, width), bf16), ((width, rows), bf16)],
        4 * rows * width * head_columns,
    )


def attention_back(lengths, rotated, mixed_grad, logs, tables):
    return call_kernel(
        attention_back_kernel,
        "attention_back",
        [
            (lengths, "scalar", None), (rotated, None, None), (mixed_grad, None, None),
            (logs, None, None), (tables[0], None, None), (tables[1], None, None),
        ],
        [(rotated.shape, bf16)],
        [],
        10 * rotated.shape[0] ** 2 * HEADS * HEAD_DIM,
    )[0]


def inputs_back(tokens, gains, projected_grad, whole, middle_grad):
    rows, width = tokens.shape
    projections = projected_grad.shape[1]
    return call_kernel(
        inputs_kernel,
        "inputs_back",
        [
            (tokens, None, None), (gains, None, None), (projected_grad, None, None),
            (whole, (width, projections), (0, 0)), (middle_grad, None, None),
        ],
        [((rows, width), f32), ((width, projections + EXTRA), bf16)],
        [((rows, width), f32), ((width, rows), bf16)],
        4 * rows * width * projections,
    )


def local(
    tokens,
    lengths,
    routes,
    attention_gain,
    query_weight,
    key_weight,
    value_weight,
    output_weight,
    expert_gain,
    router_weight,
    gate_weight,
    up_weight,
    down_weight,
    cotangent,
    *,
    count,
):
    links = Exchange(count)
    member, group, groups = links.member, links.group, links.groups
    row_count, width = tokens.shape
    shard = query_weight.shape[0]
    hidden = gate_weight.shape[2]
    head_columns, kv_columns = HEADS * HEAD_DIM, KV_HEADS * HEAD_DIM

    packed = jnp.concatenate(
        [
            query_weight,
            key_weight,
            value_weight,
            output_weight.T,
            router_weight,
            attention_gain[:, None],
            expert_gain[:, None],
            jnp.zeros((shard, EXTRA - EXPERTS - 2), bf16),
        ],
        axis=1,
    )
    pack_width = packed.shape[1]
    column = links.direct_gather(packed).reshape(groups * shard, pack_width)

    mine = jnp.stack([gate_weight, up_weight, down_weight.transpose(0, 2, 1)], axis=1)
    mine = mine.reshape(MEMBERS, LOCAL_EXPERTS, 3, shard, hidden)
    kept, other = links.keep_parts(links.chip_parts(mine))
    other, column = lax.optimization_barrier((other, column))
    shelf = links.in_order(kept, other).transpose(1, 2, 0, 3, 4)
    shelf = shelf.reshape(LOCAL_EXPERTS, 3, MEMBERS * shard, hidden)
    lines = [[m + MEMBERS * g for g in range(groups)] for m in range(MEMBERS)]
    own_full = [
        lax.all_gather(shelf[n], "fsdp", axis_index_groups=lines) for n in range(LOCAL_EXPERTS)
    ]

    half = column.shape[0] // 2
    side_near, side_far = links.to_sides(column[:half], column[half:])
    spread = {0: (column,), 2: side_near, 4: side_far, 6: links.to_cross(side_near, side_far)}
    whole = jnp.zeros((groups, MEMBERS, shard, pack_width), bf16)
    for k in range(MEMBERS):
        parts = spread[k & 6]
        if k & 1:
            parts = [links.swap(part, 1) for part in parts]
        part = jnp.concatenate(parts, axis=0).reshape(groups, shard, pack_width)
        whole = lax.dynamic_update_index_in_dim(whole, part, member ^ k, 1)
    whole = whole.reshape(width, pack_width)
    at_output = head_columns + 2 * kv_columns
    at_extra = at_output + head_columns
    gains = whole[:, at_extra + EXPERTS : at_extra + EXPERTS + 2].astype(f32).T

    half = row_count // 2
    cot_own = cotangent[:half], cotangent[half:]
    cot_late, _ = lax.optimization_barrier((cot_own, spread[6]))
    cot_near, cot_far = links.to_sides(*cot_late)

    tables = rope_lanes(row_count)
    rotated, mixed, logs = attention_forward(tokens, lengths, tables, gains, whole)
    cot_near, cot_far, mixed = lax.optimization_barrier((cot_near, cot_far, mixed))
    cot_cross = links.to_cross(cot_near, cot_far)
    *packet, middle, shares = router_forward(tokens, routes, gains, mixed, whole)
    near, far = links.to_sides(*packet)
    own_full[0], cot_cross, packet = lax.optimization_barrier((own_full[0], cot_cross, packet))

    names = [
        jnp.stack([member, member ^ 1]).astype(jnp.int32) * LOCAL_EXPERTS + n
        for n in range(LOCAL_EXPERTS)
    ]
    rows_own = [packet], [cot_own]
    first_full = own_full[0], links.swap(own_full[0], 1)
    own_out, own_back, *zero = run_experts(names[0], *rows_own, first_full)
    near, far, own_back = lax.optimization_barrier((near, far, own_back))
    cross = links.to_cross(near, far)
    rows_chips = [cross, near, far], [cot_cross, cot_near, cot_far]
    chip_out, chip_back, *zero = run_experts(names[0], *rows_chips, first_full, zero, True)
    own_full[1], chip_back = lax.optimization_barrier((own_full[1], chip_back))
    second_full = own_full[1], links.swap(own_full[1], 1)

    def join_cores(own, other):
        return (own.astype(f32) + links.swap(other, 1).astype(f32)).astype(bf16)

    def reduce_groups(total):
        return lax.psum_scatter(total, "fsdp", scatter_dimension=0, axis_index_groups=lines)

    zero, chip_out = lax.optimization_barrier((join_cores(*zero), chip_out))
    shelf_zero = reduce_groups(zero)
    chip_out, chip_back, *one = run_experts(
        names[1], *rows_chips, second_full, None, False, (chip_out, chip_back)
    )
    cross_top, cross_low = links.send_cross(chip_back[0])
    near_top, far_low = links.swap(chip_back[1, :half], 2), links.swap(chip_back[2, half:], 4)
    own_out, own_back, *one = run_experts(
        names[1], *rows_own, second_full, one, True, (own_out, own_back)
    )
    cross_top, cross_low, near_top, far_low, own_back = lax.optimization_barrier(
        (cross_top, cross_low, near_top, far_low, own_back)
    )
    near_low = (chip_back[1, half:].astype(f32) + cross_low.astype(f32)).astype(bf16)
    far_top = (chip_back[2, :half].astype(f32) + cross_top.astype(f32)).astype(bf16)
    near_low, far_top, one = lax.optimization_barrier((near_low, far_top, one))
    near_low, far_top = links.swap(near_low, 2), links.swap(far_top, 4)
    one = join_cores(*one)
    back_pieces = near_top, near_low, far_top, far_low
    out_cross, one, back_pieces = lax.optimization_barrier((chip_out[0], one, back_pieces))
    shelf_one = reduce_groups(one)
    out_cross = links.send_cross(out_cross)

    core, chip = member % 2, member // 2

    def pack_cores(pack):
        columns = pack.shape[1]
        pack = pack.reshape(groups, MEMBERS // 2, 2, shard, columns)
        own = lax.dynamic_index_in_dim(pack, core, 2, keepdims=False)
        other = links.swap(lax.dynamic_index_in_dim(pack, 1 - core, 2, keepdims=False), 1)

        joined = own.astype(f32) + other.astype(f32)
        return [
            lax.dynamic_index_in_dim(joined, chip ^ bits, 1, keepdims=False).reshape(
                groups * shard, columns
            )
            for bits in range(MEMBERS // 2)
        ]

    def pack_cross(parts):
        return links.send_cross(parts[3].astype(bf16))

    def pack_add(parts, cross):
        return links.add_cross(parts[1].astype(bf16), parts[2].astype(bf16), cross)

    middle_grad, mixed_grad, first_pack = middle_back(
        (own_back[0], *back_pieces), packet, middle, cotangent, shares, gains, mixed, whole
    )
    out_near, out_far = links.add_cross(chip_out[1], chip_out[2], out_cross)
    out_near, out_far, mixed_grad = lax.optimization_barrier((out_near, out_far, mixed_grad))
    out_near, out_far = links.swap(out_near, 2), links.swap(out_far, 4)
    first_parts = pack_cores(first_pack)
    projected_grad = attention_back(lengths, rotated, mixed_grad, logs, tables)
    shelf_zero, first_parts, projected_grad = lax.optimization_barrier(
        (shelf_zero, first_parts, projected_grad)
    )
    first_cross = pack_cross(first_parts)
    grad_tokens, second_pack = inputs_back(tokens, gains, projected_grad, whole, middle_grad)
    first_near, first_far = pack_add(first_parts, first_cross)
    first_near, first_far, second_pack, out_near, out_far, shelf_one = lax.optimization_barrier(
        (first_near, first_far, second_pack, out_near, out_far, shelf_one)
    )
    second_parts = pack_cores(second_pack)
    first_near, first_far = links.swap(first_near, 2), links.swap(first_far, 4)
    first_sum = first_parts[0] + first_near.astype(f32) + first_far.astype(f32)
    shelf_grad = jnp.stack([shelf_zero, shelf_one])
    shelf_grad = shelf_grad.reshape(LOCAL_EXPERTS, 3, MEMBERS, shard, hidden)
    shelf_grad = shelf_grad.transpose(2, 0, 1, 3, 4)
    second_near, second_far = pack_add(second_parts, pack_cross(second_parts))
    second_near, second_far = links.swap(second_near, 2), links.swap(second_far, 4)
    second_near, second_far, shelf_grad = lax.optimization_barrier(
        (second_near, second_far, shelf_grad)
    )
    second_sum = second_parts[0] + second_near.astype(f32) + second_far.astype(f32)
    pack_total = jnp.concatenate([second_sum, first_sum], axis=1)
    pack_total = links.direct_reduce(pack_total.reshape(groups, shard, pack_total.shape[1]))
    second_total = pack_total[:, : second_sum.shape[1]]
    first_total = pack_total[:, second_sum.shape[1] :]
    expert_shards = links.in_order(*links.keep_parts(links.chip_parts(shelf_grad))).astype(f32)
    expert_shards = expert_shards.reshape(EXPERTS, 3, shard, hidden)
    out_pieces = (own_out[0], out_near, out_far)
    layer_out = (middle + sum(piece.astype(f32) for piece in out_pieces)).astype(bf16)
    return (
        layer_out,
        grad_tokens,
        second_total[:, at_output],
        second_total[:, :head_columns],
        second_total[:, head_columns : head_columns + kv_columns],
        second_total[:, head_columns + kv_columns : at_output],
        first_total[:, :head_columns].T,
        first_total[:, head_columns + EXPERTS],
        first_total[:, head_columns : head_columns + EXPERTS],
        expert_shards[:, 0],
        expert_shards[:, 1],
        expert_shards[:, 2].transpose(0, 2, 1),
    )


def solution(mesh):
    count = mesh.shape["fsdp"]
    placed = (
        P("fsdp", None),
        P("fsdp"),
        P("fsdp", None),
        P("fsdp"),
        P("fsdp", None),
        P("fsdp", None),
        P("fsdp", None),
        P(None, "fsdp"),
        P("fsdp"),
        P("fsdp", None),
        P(None, "fsdp", None),
        P(None, "fsdp", None),
        P(None, None, "fsdp"),
        P("fsdp", None),
    )

    def body(*args):
        return local(*args, count=count)

    return jax.shard_map(
        body,
        mesh=mesh,
        in_specs=placed,
        out_specs=(
            P("fsdp", None),
            P("fsdp", None),
            P("fsdp"),
            P("fsdp", None),
            P("fsdp", None),
            P("fsdp", None),
            P(None, "fsdp"),
            P("fsdp"),
            P("fsdp", None),
            P(None, "fsdp", None),
            P(None, "fsdp", None),
            P(None, None, "fsdp"),
        ),
        check_vma=False,
    )
```
